32 devices in a mesh: seq: 4 (over x, core), ctx: 8 (over z, y).
Axes of the slice: x: 2, y: 2, z: 4, core: 2. Of those that a mesh axis runs over, the one named last changes fastest.
Arguments:
- tokens: bfloat16 [4, 1024, 1024], P('seq', 'ctx'), may hold values from -6 to 6
- encoder_states: bfloat16 [4, 256, 1024], P('seq', 'ctx'), may hold values from -6 to 6
- cotangent: bfloat16 [4, 1024, 1024], P('seq', 'ctx'), may hold values from -6 to 6
- target_lengths: int32 [4], P('seq'), may hold values from 512 to 1024, as said below
- source_lengths: int32 [4], P('seq'), may hold values from 225 to 256, as said below
- block_table: int32 [8, 2], replicated, may hold values from 0 to 15, as said below
- self_qkv: bfloat16 [1024, 3072], P('seq'), may hold values from -0.1875 to 0.1875
- self_out: bfloat16 [1024, 1024], P('seq'), may hold values from -3 to 3
- cross_q: bfloat16 [1024, 1024], P('seq'), may hold values from -0.1875 to 0.1875
- cross_kv: bfloat16 [1024, 2048], P('seq'), may hold values from -0.1875 to 0.1875
- cross_out: bfloat16 [1024, 1024], P('seq'), may hold values from -3 to 3
- mlp_up: bfloat16 [1024, 8192], P('seq'), may hold values from -0.1875 to 0.1875
- mlp_down: bfloat16 [8192, 1024], P('seq'), may hold values from -0.0625 to 0.0625
- norm_gain: float32 [3, 1024], replicated, may hold values from 0.1 to 1.9
- norm_bias: float32 [3, 1024], replicated, may hold values from -1.5 to 1.5
- clip_limit: float32 [2, 16], replicated, may hold values from 2 to 16
Outputs:
- output: bfloat16 [4, 1024, 1024], P('seq', 'ctx')
- grad_tokens: float32 [4, 1024, 1024], P('seq', 'ctx')
- grad_encoder: float32 [4, 256, 1024], P('seq', 'ctx')
- grad_self_qkv: float32 [1024, 3072], P(('seq', 'ctx'))
- grad_self_out: float32 [1024, 1024], P(('seq', 'ctx'))
- grad_cross_q: float32 [1024, 1024], P(('seq', 'ctx'))
- grad_cross_kv: float32 [1024, 2048], P(('seq', 'ctx'))
- grad_cross_out: float32 [1024, 1024], P(('seq', 'ctx'))
- grad_mlp_up: float32 [1024, 8192], P(('seq', 'ctx'))
- grad_mlp_down: float32 [8192, 1024], P(('seq', 'ctx'))
- grad_norm_gain: float32 [3, 1024], P(None, ('seq', 'ctx'))
- grad_norm_bias: float32 [3, 1024], P(None, ('seq', 'ctx'))
- clipped_self: bfloat16 [1024, 2048], P('seq')
- clipped_cross: bfloat16 [1024, 2048], P('seq')
- head_peaks: float32 [2, 16], replicated
The draws below stay inside these ranges and needn't reach their ends.
Inputs may be any that keep to these rules, and one draw needn't show every extreme that they name: `block_table`: row j names the two blocks of 64 positions held by device j of ctx; they are b and 15 - b for some b, and every block is named once. `target_lengths`: in every draw one slot is 1024 long. `source_lengths`: in every draw one sequence has all 256 states.
All inputs are finite; a program needn't handle non-finite values.
Results may differ from the reference program's by a relative error of at most 0.025.
Values may be sent and summed in bfloat16 or wider, within the bound.
A program may use at most 384 MiB of HBM per device.

```python
import math
import jax
import jax.numpy as jnp
from jax import lax

D = 1024
H = 16
HD = 64
FF = 8192
TOK_DEV = 128
SRC = 256
BLOCKS = 16
SEQ_LEN = 1024
SLOTS = 4
SRC_DEV = 32


def draw_target_lengths(key, part):
    lengths = jax.random.randint(jax.random.fold_in(key, 11), (SLOTS,), SEQ_LEN // 2, SEQ_LEN + 1)
    longest = jax.random.randint(jax.random.fold_in(key, 12), (), 0, SLOTS)
    return jnp.where(jnp.arange(SLOTS) == longest, SEQ_LEN, lengths).astype(jnp.int32)


def draw_source_lengths(key, part):
    shortfall = jax.random.randint(jax.random.fold_in(key, 21), (SLOTS,), 0, SRC_DEV)
    longest = jax.random.randint(jax.random.fold_in(key, 22), (), 0, SLOTS)
    return jnp.where(jnp.arange(SLOTS) == longest, SRC, SRC - shortfall).astype(jnp.int32)


def draw_block_table(key, part):
    pairs = jax.random.permutation(jax.random.fold_in(key, 31), BLOCKS // 2).astype(jnp.int32)
    flips = jax.random.randint(jax.random.fold_in(key, 32), (BLOCKS // 2,), 0, 2)
    mirror = BLOCKS - 1 - pairs
    leading = jnp.where(flips == 1, mirror, pairs)
    trailing = jnp.where(flips == 1, pairs, mirror)
    return jnp.stack([leading, trailing], axis=1).astype(jnp.int32)


def level_of(rng, shape, cuts, smallest, largest):
    def one(dim, parts):
        heights = jax.random.uniform(jax.random.fold_in(jax.random.fold_in(rng, 6), dim), (parts,), jnp.float32, smallest / len(cuts), largest / len(cuts))
        return jnp.repeat(jnp.exp(heights), shape[dim] // parts).reshape((-1,) + (1,) * (len(shape) - dim - 1))

    factor_of = one(*cuts[0])
    for cut in cuts[1:]:
        factor_of = factor_of * one(*cut)
    return factor_of


def centred(key, shape, scale, most, split=(), kind=jnp.bfloat16):
    level = level_of(key, shape, split, -0.22, 0.18) if split else 1.0
    result = jax.random.normal(key, shape, jnp.float32) * scale * level
    return jnp.minimum(jnp.maximum(result, -most), most).astype(kind)


def setup_inputs(seed: int = 0) -> dict:
    key_of = jax.random.split(jax.random.key(seed), 17)
    tokens = centred(key_of[0], (SLOTS, SEQ_LEN, D), 1.0, 6.0, ((0, 4), (1, 8)))
    encoder_states = centred(key_of[1], (SLOTS, SRC, D), 1.0, 6.0, ((0, 4), (1, 8)))
    cotangent = centred(key_of[2], (SLOTS, SEQ_LEN, D), 1.0, 6.0, ((0, 4), (1, 8)))
    target_lengths = draw_target_lengths(jax.random.fold_in(key_of[16], 71), 0)
    source_lengths = draw_source_lengths(jax.random.fold_in(key_of[16], 71), 0)
    block_table = draw_block_table(jax.random.fold_in(key_of[16], 71), 0)
    self_qkv = centred(key_of[6], (D, 3 * D), D ** -0.5, 0.1875, ((0, 4),))
    self_out = centred(key_of[7], (D, D), (max(D // 256, 1)) ** -0.5, 3.0, ((0, 4),))
    cross_q = centred(key_of[8], (D, D), D ** -0.5, 0.1875, ((0, 4),))
    cross_kv = centred(key_of[9], (D, 2 * D), D ** -0.5, 0.1875, ((0, 4),))
    cross_out = centred(key_of[10], (D, D), (max(D // 256, 1)) ** -0.5, 3.0, ((0, 4),))
    mlp_up = centred(key_of[11], (D, FF), D ** -0.5, 0.1875, ((0, 4),))
    mlp_down = centred(key_of[12], (FF, D), FF ** -0.5, 0.0625, ((0, 4),))
    norm_gain = jnp.clip(1.0 + 0.18 * jax.random.normal(key_of[13], (3, D), jnp.float32), 0.1, 1.9)
    norm_bias = centred(key_of[14], (3, D), 0.3, 1.5, (), jnp.float32)
    clip_limit = jnp.clip(jnp.exp(jax.random.uniform(key_of[15], (2, H), jnp.float32, math.log(2.0), math.log(16.0))), 2.0, 16.0)
    return dict(tokens=tokens, encoder_states=encoder_states, cotangent=cotangent, target_lengths=target_lengths, source_lengths=source_lengths, block_table=block_table, self_qkv=self_qkv, self_out=self_out, cross_q=cross_q, cross_kv=cross_kv, cross_out=cross_out, mlp_up=mlp_up, mlp_down=mlp_down, norm_gain=norm_gain, norm_bias=norm_bias, clip_limit=clip_limit)


@jax.custom_vjp
def low(v):
    return lax.optimization_barrier(v.astype(jnp.bfloat16)).astype(jnp.float32)

@jax.custom_vjp
def low_back(v):
    return v

def low_keep(v):
    return (low(v), None)

def low_pass(kept, grad):
    return (grad,)

def back_keep(v):
    return (v, None)

def back_low(kept, grad):
    return (low(grad),)
low.defvjp(low_keep, low_pass)
low_back.defvjp(back_keep, back_low)
masked_score = -1000000000.0
norm_eps = 1e-05

def product(left, right):
    return jnp.dot(left, right, precision=lax.Precision.HIGHEST)

def block_size(count):
    return max((step for step in range(1, min(count, 512) + 1) if count % step == 0))

def layer_norm(values, gain, bias):
    centered = values - lax.optimization_barrier(jnp.mean(values, axis=-1, keepdims=True))
    spread = lax.optimization_barrier(jnp.mean(centered * centered, axis=-1, keepdims=True))
    return centered * lax.rsqrt(spread + norm_eps) * gain + bias

def positions_of(block_table):
    half = TOK_DEV // 2
    offsets = jnp.arange(half, dtype=jnp.int32)
    return (block_table[:, :, None] * half + offsets[None, None, :]).reshape(-1).astype(jnp.int32)

def attention(query, keys, values, query_pos, query_ok, key_pos, key_limit, causal):
    rows = query.shape[0]
    step = block_size(rows)
    width = H * HD
    key_heads = keys.reshape(-1, H, HD)
    value_heads = values.reshape(-1, H, HD)
    keys_live = key_pos < key_limit

    def one_block(block):
        query_rows, block_pos, block_ok = block
        query_heads = query_rows.reshape(step, H, HD)
        allowed = jnp.broadcast_to(keys_live[None, :], (step, key_pos.shape[0]))
        if causal:
            allowed = allowed & (key_pos[None, :] <= block_pos[:, None])
        scores = low_back(jnp.einsum('qhd,khd->hqk', query_heads, key_heads, precision=lax.Precision.HIGHEST) * HD ** (-0.5))
        scores = jnp.where(allowed[None], scores, masked_score)
        top = lax.optimization_barrier(jnp.max(scores, axis=-1, keepdims=True))
        expos = jnp.exp(scores - top)
        probs = expos / lax.optimization_barrier(jnp.sum(expos, axis=-1, keepdims=True))
        mixed = jnp.einsum('hqk,khd->qhd', low(probs), value_heads, precision=lax.Precision.HIGHEST).reshape(step, width)
        counted = jnp.where((allowed & block_ok[:, None])[None], scores, masked_score)
        return (mixed, lax.optimization_barrier(jnp.max(counted, axis=(1, 2))))
    mixed, peaks = lax.map(jax.checkpoint(one_block), (query.reshape(-1, step, width), query_pos.reshape(-1, step), query_ok.reshape(-1, step)))
    return (low_back(low(mixed.reshape(rows, width))), lax.optimization_barrier(jnp.max(peaks, axis=0)))

def decoder_slot(inputs, source, length, source_length, positions, weights):
    w_qkv, w_out, w_cq, w_ckv, w_co, w_up, w_down, gain, bias = weights
    width = H * HD
    query_ok = positions < length
    first = low(layer_norm(inputs, gain[0], bias[0]))
    projected = low_back(low(product(first, w_qkv)))
    self_mix, self_peak = attention(projected[:, :width], projected[:, width:2 * width], projected[:, 2 * width:], positions, query_ok, positions, length, True)
    first_sum = inputs + low_back(product(self_mix, w_out))
    second = low(layer_norm(first_sum, gain[1], bias[1]))
    cross_query = low_back(low(product(second, w_cq)))
    source_kv = low_back(low(product(source, w_ckv)))
    source_positions = jnp.arange(SRC, dtype=jnp.int32)
    cross_mix, cross_peak = attention(cross_query, source_kv[:, :width], source_kv[:, width:], positions, query_ok, source_positions, source_length, False)
    second_sum = first_sum + low_back(product(cross_mix, w_co))
    third = low(layer_norm(second_sum, gain[2], bias[2]))
    hidden = low(jax.nn.gelu(low_back(product(third, w_up))))
    third_sum = second_sum + low_back(product(hidden, w_down))
    return (jnp.where(query_ok[:, None], third_sum, 0.0), jnp.stack([self_peak, cross_peak]))

def reference(tokens, encoder_states, cotangent, target_lengths, source_lengths, block_table, self_qkv, self_out, cross_q, cross_kv, cross_out, mlp_up, mlp_down, norm_gain, norm_bias, clip_limit):
    positions = positions_of(block_table)
    width = H * HD

    def forward(inputs, source, w_qkv, w_out, w_cq, w_ckv, w_co, w_up, w_down, gain, bias):
        weights = (w_qkv, w_out, w_cq, w_ckv, w_co, w_up, w_down, gain, bias)

        def one_slot(slot):
            slot_inputs, slot_source, length, source_length = slot
            return decoder_slot(slot_inputs, slot_source, length, source_length, positions, weights)
        results, peaks = lax.map(one_slot, (inputs, source, target_lengths, source_lengths))
        return (results, lax.optimization_barrier(jnp.max(peaks, axis=0)))
    results, pullback, peaks = jax.vjp(forward, tokens.astype(jnp.float32), encoder_states.astype(jnp.float32), self_qkv.astype(jnp.float32), self_out.astype(jnp.float32), cross_q.astype(jnp.float32), cross_kv.astype(jnp.float32), cross_out.astype(jnp.float32), mlp_up.astype(jnp.float32), mlp_down.astype(jnp.float32), norm_gain.astype(jnp.float32), norm_bias.astype(jnp.float32), has_aux=True)
    grads = pullback(cotangent.astype(jnp.float32))
    factors = jnp.sqrt(clip_limit / jnp.maximum(peaks, clip_limit))
    columns = jnp.repeat(factors, HD, axis=1)
    qkv_wide = self_qkv.astype(jnp.float32)
    clipped_self = jnp.concatenate([qkv_wide[:, :width] * columns[0], qkv_wide[:, width:2 * width] * columns[0]], axis=1).astype(jnp.bfloat16)
    clipped_cross = jnp.concatenate([cross_q.astype(jnp.float32) * columns[1], cross_kv[:, :width].astype(jnp.float32) * columns[1]], axis=1).astype(jnp.bfloat16)
    return (results.astype(jnp.bfloat16), grads[0], grads[1], grads[2], grads[3], grads[4], grads[5], grads[6], grads[7], grads[8], grads[9], grads[10], clipped_self, clipped_cross, peaks)
```

```python
import functools

import jax
import jax.numpy as jnp
from jax import lax
from jax.experimental import pallas as pl
from jax.experimental.pallas import tpu as pltpu
from jax.sharding import PartitionSpec as P

H = 16
HD = 64


masked_score = -1000000000.0
norm_eps = 1e-05


def block_size(count):
    return max((step for step in range(1, min(count, 512) + 1) if count % step == 0))


def layer_norm(values, gain, bias):
    centered = values - jnp.mean(values, axis=-1, keepdims=True)
    spread = jnp.mean(centered * centered, axis=-1, keepdims=True)
    return centered * lax.rsqrt(spread + norm_eps) * gain + bias


def allowed_pairs(query_pos, key_pos, key_limit, causal):
    allowed = jnp.broadcast_to(
        (key_pos < key_limit)[None, :], (query_pos.shape[0], key_pos.shape[0])
    )
    if causal:
        allowed = allowed & (key_pos[None, :] <= query_pos[:, None])
    return allowed


def head_scores(query_heads, key_rows):
    key_heads = key_rows.reshape(key_rows.shape[0], H, HD)
    return jnp.einsum(
        "qhd,khd->hqk", query_heads, key_heads, preferred_element_type=jnp.float32
    ) * HD ** (-0.5)


def softmax_stats(query_heads, kv_rows, key_pos, query_pos, query_ok, key_limit, causal):
    count = kv_rows.shape[0]
    step = block_size(count)
    width = H * HD
    rows = query_heads.shape[0]

    def softmax_visit(carry, block):
        top, total, peak = carry
        block_rows, block_pos = block
        allowed = allowed_pairs(query_pos, block_pos, key_limit, causal)
        scores = jnp.where(
            allowed[None], head_scores(query_heads, block_rows[:, :width]), masked_score
        )
        new_top = jnp.maximum(top, jnp.max(scores, axis=-1))
        total = total * jnp.exp(top - new_top) + jnp.sum(
            jnp.exp(scores - new_top[..., None]), axis=-1
        )
        counted = jnp.where((allowed & query_ok[:, None])[None], scores, masked_score)
        peak = jnp.maximum(peak, jnp.max(counted, axis=(1, 2)))
        return ((new_top, total, peak), None)

    start = (
        jnp.full((H, rows), -jnp.inf, jnp.float32),
        jnp.zeros((H, rows), jnp.float32),
        jnp.full((H,), masked_score, jnp.float32),
    )
    blocks = (kv_rows.reshape(count // step, step, 2 * width), key_pos.reshape(count // step, step))
    return lax.scan(softmax_visit, start, blocks)[0]


def attend_values(query_heads, kv_rows, key_pos, query_pos, key_limit, causal, top, total):
    count = kv_rows.shape[0]
    step = block_size(count)
    width = H * HD
    rows = query_heads.shape[0]

    def attend_visit(acc, block):
        block_rows, block_pos = block
        allowed = allowed_pairs(query_pos, block_pos, key_limit, causal)
        scores = jnp.where(
            allowed[None], head_scores(query_heads, block_rows[:, :width]), masked_score
        )
        weights = (jnp.exp(scores - top[..., None]) / total[..., None]).astype(jnp.bfloat16)
        value_heads = block_rows[:, width:].reshape(step, H, HD)
        return (
            acc
            + jnp.einsum("hqk,khd->qhd", weights, value_heads, preferred_element_type=jnp.float32),
            None,
        )

    blocks = (kv_rows.reshape(count // step, step, 2 * width), key_pos.reshape(count // step, step))
    acc = lax.scan(attend_visit, jnp.zeros((rows, H, HD), jnp.float32), blocks)[0]
    return acc.reshape(rows, width)


def query_grads(
    query_heads, kv_rows, key_pos, query_pos, key_limit, causal, top, total, grad_heads, delta
):
    count = kv_rows.shape[0]
    step = block_size(count)
    width = H * HD
    rows = query_heads.shape[0]

    def query_visit(acc, block):
        block_rows, block_pos = block
        allowed = allowed_pairs(query_pos, block_pos, key_limit, causal)
        scores = jnp.where(
            allowed[None], head_scores(query_heads, block_rows[:, :width]), masked_score
        )
        probs = jnp.exp(scores - top[..., None]) / total[..., None]
        value_heads = block_rows[:, width:].reshape(step, H, HD)
        dprobs = jnp.einsum(
            "qhd,khd->hqk", grad_heads, value_heads, preferred_element_type=jnp.float32
        )
        dscores = (probs * (dprobs - delta[..., None])).astype(jnp.bfloat16)
        key_heads = block_rows[:, :width].reshape(step, H, HD)
        return (
            acc
            + jnp.einsum("hqk,khd->qhd", dscores, key_heads, preferred_element_type=jnp.float32),
            None,
        )

    blocks = (kv_rows.reshape(count // step, step, 2 * width), key_pos.reshape(count // step, step))
    acc = lax.scan(query_visit, jnp.zeros((rows, H, HD), jnp.float32), blocks)[0]
    return acc.reshape(rows, width) * HD ** (-0.5)


def key_grads(
    query_heads,
    kv_rows,
    key_pos,
    query_pos,
    key_limit,
    causal,
    top,
    total,
    grad_heads,
    delta,
    start,
    count,
):
    step = block_size(count)
    width = H * HD

    def piece(index):
        offset = start + index * step
        block_rows = lax.dynamic_slice_in_dim(kv_rows, offset, step, 0)
        block_pos = lax.dynamic_slice_in_dim(key_pos, offset, step, 0)
        allowed = allowed_pairs(query_pos, block_pos, key_limit, causal)
        scores = jnp.where(
            allowed[None], head_scores(query_heads, block_rows[:, :width]), masked_score
        )
        probs = jnp.exp(scores - top[..., None]) / total[..., None]
        value_heads = block_rows[:, width:].reshape(step, H, HD)
        dprobs = jnp.einsum(
            "qhd,khd->hqk", grad_heads, value_heads, preferred_element_type=jnp.float32
        )
        dscores = (probs * (dprobs - delta[..., None])).astype(jnp.bfloat16)
        dkeys = jnp.einsum(
            "hqk,qhd->khd", dscores, query_heads, preferred_element_type=jnp.float32
        ).reshape(step, width) * HD ** (-0.5)
        dvalues = jnp.einsum(
            "hqk,qhd->khd",
            probs.astype(jnp.bfloat16),
            grad_heads,
            preferred_element_type=jnp.float32,
        ).reshape(step, width)
        return jnp.concatenate([dkeys, dvalues], axis=1)

    return lax.map(piece, jnp.arange(count // step, dtype=jnp.int32)).reshape(count, 2 * width)


def split_rows(grad, seq_count, ctx_count):
    return grad.reshape(
        (seq_count, ctx_count, grad.shape[0] // (seq_count * ctx_count)) + grad.shape[1:]
    )


def join_rows(grad):
    return grad.reshape((grad.shape[2],) + grad.shape[3:])


def general_device(
    tokens,
    encoder_states,
    cotangent,
    target_lengths,
    source_lengths,
    block_table,
    self_qkv,
    self_out,
    cross_q,
    cross_kv,
    cross_out,
    mlp_up,
    mlp_down,
    norm_gain,
    norm_bias,
    clip_limit,
):
    rows = tokens.shape[1]
    width = H * HD
    half = rows // 2
    source_rows = encoder_states.shape[1]
    seq_count = lax.axis_size("seq")
    ctx_count = lax.axis_size("ctx")
    all_positions = (
        block_table[:, :, None] * half + jnp.arange(half, dtype=jnp.int32)[None, None, :]
    ).reshape(-1)
    own_positions = lax.dynamic_slice_in_dim(all_positions, lax.axis_index("ctx") * rows, rows, 0)
    length = target_lengths[0]
    source_length = source_lengths[0]
    query_ok = own_positions < length
    valid_rows = query_ok[:, None]
    source_positions = jnp.arange(source_rows * ctx_count, dtype=jnp.int32)
    w_qkv, w_out, w_cq, w_ckv, w_co = (
        lax.all_gather(self_qkv, "seq", axis=0, tiled=True),
        lax.all_gather(self_out, "seq", axis=0, tiled=True),
        lax.all_gather(cross_q, "seq", axis=0, tiled=True),
        lax.all_gather(cross_kv, "seq", axis=0, tiled=True),
        lax.all_gather(cross_out, "seq", axis=0, tiled=True),
    )
    inputs = tokens[0].astype(jnp.float32)
    first_norm, first_back = jax.vjp(layer_norm, inputs, norm_gain[0], norm_bias[0])
    first_low = first_norm.astype(jnp.bfloat16)
    projected = jnp.dot(first_low, w_qkv, preferred_element_type=jnp.float32).astype(jnp.bfloat16)
    self_query = projected[:, :width].reshape(rows, H, HD)
    source_kv = jnp.dot(encoder_states[0], w_ckv, preferred_element_type=jnp.float32).astype(
        jnp.bfloat16
    )
    self_kv, cross_kvs = (
        lax.all_gather(projected[:, width:], "ctx", axis=0, tiled=True),
        lax.all_gather(source_kv, "ctx", axis=0, tiled=True),
    )
    self_top, self_total, self_peak = softmax_stats(
        self_query, self_kv, all_positions, own_positions, query_ok, length, True
    )
    self_mix = attend_values(
        self_query, self_kv, all_positions, own_positions, length, True, self_top, self_total
    )
    self_low = self_mix.astype(jnp.bfloat16)
    first_sum = inputs + jnp.dot(self_low, w_out, preferred_element_type=jnp.float32)
    second_norm, second_back = jax.vjp(layer_norm, first_sum, norm_gain[1], norm_bias[1])
    second_low = second_norm.astype(jnp.bfloat16)
    cross_rows = jnp.dot(second_low, w_cq, preferred_element_type=jnp.float32).astype(jnp.bfloat16)
    cross_query = cross_rows.reshape(rows, H, HD)
    cross_top, cross_total, cross_peak = softmax_stats(
        cross_query, cross_kvs, source_positions, own_positions, query_ok, source_length, False
    )
    cross_mix = attend_values(
        cross_query,
        cross_kvs,
        source_positions,
        own_positions,
        source_length,
        False,
        cross_top,
        cross_total,
    )
    cross_low = cross_mix.astype(jnp.bfloat16)
    second_sum = first_sum + jnp.dot(cross_low, w_co, preferred_element_type=jnp.float32)
    third_norm, third_back = jax.vjp(layer_norm, second_sum, norm_gain[2], norm_bias[2])
    third_low = third_norm.astype(jnp.bfloat16)
    w_up, w_down = (
        lax.all_gather(mlp_up, "seq", axis=0, tiled=True),
        lax.all_gather(mlp_down, "seq", axis=0, tiled=True),
    )
    hidden_pre = jnp.dot(third_low, w_up, preferred_element_type=jnp.float32)
    hidden_act, gelu_back = jax.vjp(jax.nn.gelu, hidden_pre)
    hidden_low = hidden_act.astype(jnp.bfloat16)
    third_sum = second_sum + jnp.dot(hidden_low, w_down, preferred_element_type=jnp.float32)
    output_rows = jnp.where(valid_rows, third_sum, 0.0).astype(jnp.bfloat16)
    peaks = lax.pmax(jnp.stack([self_peak, cross_peak]), ("seq", "ctx"))
    grad_rows = jnp.where(valid_rows, cotangent[0].astype(jnp.float32), 0.0)
    mlp_branch = grad_rows.astype(jnp.bfloat16)
    grad_down = jnp.einsum("rf,rd->fd", hidden_low, mlp_branch, preferred_element_type=jnp.float32)
    grad_act = jnp.einsum("rd,fd->rf", mlp_branch, w_down, preferred_element_type=jnp.float32)
    grad_pre = gelu_back(grad_act)[0].astype(jnp.bfloat16)
    grad_up = jnp.einsum("rd,rf->df", third_low, grad_pre, preferred_element_type=jnp.float32)
    back_third, gain_three, bias_three = third_back(
        jnp.einsum("rf,df->rd", grad_pre, w_up, preferred_element_type=jnp.float32)
    )
    up_part, down_part = (
        lax.psum_scatter(
            split_rows(grad_up, seq_count, ctx_count).astype(jnp.bfloat16),
            "ctx",
            scatter_dimension=1,
            tiled=True,
        ).astype(jnp.float32),
        lax.psum_scatter(
            split_rows(grad_down, seq_count, ctx_count).astype(jnp.bfloat16),
            "ctx",
            scatter_dimension=1,
            tiled=True,
        ).astype(jnp.float32),
    )
    up_shard, down_shard = (
        lax.psum_scatter(
            up_part.astype(jnp.bfloat16), "seq", scatter_dimension=0, tiled=True
        ).astype(jnp.float32),
        lax.psum_scatter(
            down_part.astype(jnp.bfloat16), "seq", scatter_dimension=0, tiled=True
        ).astype(jnp.float32),
    )
    grad_second = grad_rows + back_third
    cross_branch = grad_second.astype(jnp.bfloat16)
    grad_co = jnp.einsum("rd,re->de", cross_low, cross_branch, preferred_element_type=jnp.float32)
    cross_heads_grad = (
        jnp.einsum("re,de->rd", cross_branch, w_co, preferred_element_type=jnp.float32)
        .astype(jnp.bfloat16)
        .reshape(rows, H, HD)
    )
    cross_delta = jnp.einsum(
        "qhd,qhd->hq", cross_heads_grad.astype(jnp.float32), cross_mix.reshape(rows, H, HD)
    )
    grad_cross_rows = query_grads(
        cross_query,
        cross_kvs,
        source_positions,
        own_positions,
        source_length,
        False,
        cross_top,
        cross_total,
        cross_heads_grad,
        cross_delta,
    ).astype(jnp.bfloat16)
    grad_source_kv = lax.psum_scatter(
        key_grads(
            cross_query,
            cross_kvs,
            source_positions,
            own_positions,
            source_length,
            False,
            cross_top,
            cross_total,
            cross_heads_grad,
            cross_delta,
            jnp.int32(0),
            source_rows * lax.axis_size("ctx"),
        ).astype(jnp.bfloat16),
        "ctx",
        scatter_dimension=0,
        tiled=True,
    )
    grad_cq = jnp.einsum(
        "rd,re->de", second_low, grad_cross_rows, preferred_element_type=jnp.float32
    )
    grad_ckv = jnp.einsum(
        "sd,se->de", encoder_states[0], grad_source_kv, preferred_element_type=jnp.float32
    )
    grad_source = jnp.einsum("se,de->sd", grad_source_kv, w_ckv, preferred_element_type=jnp.float32)
    back_second, gain_two, bias_two = second_back(
        jnp.einsum("re,de->rd", grad_cross_rows, w_cq, preferred_element_type=jnp.float32)
    )
    grad_first = grad_second + back_second
    self_branch = grad_first.astype(jnp.bfloat16)
    grad_so = jnp.einsum("rd,re->de", self_low, self_branch, preferred_element_type=jnp.float32)
    self_heads_grad = (
        jnp.einsum("re,de->rd", self_branch, w_out, preferred_element_type=jnp.float32)
        .astype(jnp.bfloat16)
        .reshape(rows, H, HD)
    )
    self_delta = jnp.einsum(
        "qhd,qhd->hq", self_heads_grad.astype(jnp.float32), self_mix.reshape(rows, H, HD)
    )
    grad_query = query_grads(
        self_query,
        self_kv,
        all_positions,
        own_positions,
        length,
        True,
        self_top,
        self_total,
        self_heads_grad,
        self_delta,
    ).astype(jnp.bfloat16)
    grad_kv = lax.psum_scatter(
        key_grads(
            self_query,
            self_kv,
            all_positions,
            own_positions,
            length,
            True,
            self_top,
            self_total,
            self_heads_grad,
            self_delta,
            jnp.int32(0),
            rows * lax.axis_size("ctx"),
        ).astype(jnp.bfloat16),
        "ctx",
        scatter_dimension=0,
        tiled=True,
    )
    grad_projected = jnp.concatenate([grad_query, grad_kv], axis=1)
    grad_qkv = jnp.einsum(
        "rd,re->de", first_low, grad_projected, preferred_element_type=jnp.float32
    )
    back_first, gain_one, bias_one = first_back(
        jnp.einsum("re,de->rd", grad_projected, w_qkv, preferred_element_type=jnp.float32)
    )
    grad_inputs = grad_first + back_first
    norm_terms = jnp.stack([gain_one, gain_two, gain_three, bias_one, bias_two, bias_three], axis=1)
    qkv_part, out_part, cq_part, ckv_part, co_part, norm_part = (
        lax.psum_scatter(
            split_rows(grad_qkv, seq_count, ctx_count).astype(jnp.bfloat16),
            "ctx",
            scatter_dimension=1,
            tiled=True,
        ).astype(jnp.float32),
        lax.psum_scatter(
            split_rows(grad_so, seq_count, ctx_count).astype(jnp.bfloat16),
            "ctx",
            scatter_dimension=1,
            tiled=True,
        ).astype(jnp.float32),
        lax.psum_scatter(
            split_rows(grad_cq, seq_count, ctx_count).astype(jnp.bfloat16),
            "ctx",
            scatter_dimension=1,
            tiled=True,
        ).astype(jnp.float32),
        lax.psum_scatter(
            split_rows(grad_ckv, seq_count, ctx_count).astype(jnp.bfloat16),
            "ctx",
            scatter_dimension=1,
            tiled=True,
        ).astype(jnp.float32),
        lax.psum_scatter(
            split_rows(grad_co, seq_count, ctx_count).astype(jnp.bfloat16),
            "ctx",
            scatter_dimension=1,
            tiled=True,
        ).astype(jnp.float32),
        lax.psum_scatter(
            split_rows(norm_terms, seq_count, ctx_count).astype(jnp.bfloat16),
            "ctx",
            scatter_dimension=1,
            tiled=True,
        ).astype(jnp.float32),
    )
    qkv_shard, out_shard, cq_shard, ckv_shard, co_shard, norm_shard = (
        lax.psum_scatter(
            qkv_part.astype(jnp.bfloat16), "seq", scatter_dimension=0, tiled=True
        ).astype(jnp.float32),
        lax.psum_scatter(
            out_part.astype(jnp.bfloat16), "seq", scatter_dimension=0, tiled=True
        ).astype(jnp.float32),
        lax.psum_scatter(
            cq_part.astype(jnp.bfloat16), "seq", scatter_dimension=0, tiled=True
        ).astype(jnp.float32),
        lax.psum_scatter(
            ckv_part.astype(jnp.bfloat16), "seq", scatter_dimension=0, tiled=True
        ).astype(jnp.float32),
        lax.psum_scatter(
            co_part.astype(jnp.bfloat16), "seq", scatter_dimension=0, tiled=True
        ).astype(jnp.float32),
        lax.psum_scatter(
            norm_part.astype(jnp.bfloat16), "seq", scatter_dimension=0, tiled=True
        ).astype(jnp.float32),
    )
    norm_shard = join_rows(norm_shard)
    factors = jnp.sqrt(clip_limit / jnp.maximum(peaks, clip_limit))
    columns = jnp.repeat(factors, HD, axis=1)
    qkv_wide = self_qkv.astype(jnp.float32)
    clipped_self = jnp.concatenate(
        [qkv_wide[:, :width] * columns[0], qkv_wide[:, width : 2 * width] * columns[0]], axis=1
    ).astype(jnp.bfloat16)
    clipped_cross = jnp.concatenate(
        [
            cross_q.astype(jnp.float32) * columns[1],
            cross_kv[:, :width].astype(jnp.float32) * columns[1],
        ],
        axis=1,
    ).astype(jnp.bfloat16)
    return (
        output_rows[None],
        grad_inputs[None],
        grad_source[None],
        join_rows(qkv_shard),
        join_rows(out_shard),
        join_rows(cq_shard),
        join_rows(ckv_shard),
        join_rows(co_shard),
        join_rows(up_shard),
        join_rows(down_shard),
        norm_shard[:, :3].T,
        norm_shard[:, 3:].T,
        clipped_self,
        clipped_cross,
        peaks,
    )


F32 = jnp.float32
BF16 = jnp.bfloat16
SCALE = HD**-0.5


def fast_fits(mesh):
    seq_count, ctx_count = mesh.shape["seq"], mesh.shape["ctx"]
    if H % seq_count or H % ctx_count:
        return False
    held, pair = H // seq_count, H // ctx_count
    return held % pair == 0 and seq_count * (held // pair) == ctx_count and pair * HD == 128


def dot(left, right, contract=((1,), (0,))):
    return lax.dot_general(left, right, (contract, ((), ())), preferred_element_type=F32)


NT = ((1,), (1,))
TN = ((0,), (0,))


def norm_forward(values, gain, bias):
    centered = values - jnp.mean(values, axis=-1, keepdims=True)
    spread = jnp.mean(centered * centered, axis=-1, keepdims=True)
    inverse = lax.rsqrt(spread + norm_eps)
    hat = centered * inverse
    return hat, inverse, (hat * gain + bias).astype(BF16)


def norm_backward(grad, hat, inverse, gain):
    scaled = grad * gain
    inner = jnp.mean(scaled, axis=-1, keepdims=True)
    outer = jnp.mean(scaled * hat, axis=-1, keepdims=True)
    return (
        (scaled - inner - hat * outer) * inverse,
        jnp.sum(grad * hat, axis=0),
        jnp.sum(grad, axis=0),
    )


def self_forward_kernel(length_ref, row_ref, col_ref, q_ref, kv_ref, mix_ref, peak_ref):
    length = length_ref[0]
    row_pos = row_ref[...]
    col_pos = col_ref[...]
    allowed = (col_pos <= row_pos) & (col_pos < length)
    valid = row_pos < length

    @pl.when(pl.program_id(0) == 0)
    def _():
        peak_ref[...] = jnp.full_like(peak_ref, masked_score)

    for head in range(q_ref.shape[-1] // HD):
        cut = slice(head * HD, (head + 1) * HD)
        scores = dot(q_ref[0, :, cut], kv_ref[0, :, cut], NT) * SCALE
        scores = jnp.where(allowed, scores, masked_score)
        top = jnp.max(scores, axis=-1, keepdims=True)
        expos = jnp.exp(scores - top)
        probs = expos * (1.0 / jnp.sum(expos, axis=-1, keepdims=True))
        mix_ref[:, cut] = dot(probs.astype(BF16), kv_ref[1, :, cut]).astype(BF16)
        peak = jnp.max(jnp.where(valid, top, masked_score), axis=0, keepdims=True)
        peak_ref[head : head + 1, :] = jnp.maximum(
            peak_ref[head : head + 1, :], jnp.broadcast_to(peak, (1, 128))
        )


def self_forward(qkv, positions, length):
    count, width = qkv.shape[1:]
    step = min(256, count)
    return pl.pallas_call(
        self_forward_kernel,
        grid=(count // step,),
        in_specs=[
            pl.BlockSpec(memory_space=pltpu.SMEM),
            pl.BlockSpec((step, 1), lambda i: (i, 0)),
            pl.BlockSpec((1, count), lambda i: (0, 0)),
            pl.BlockSpec((1, step, width), lambda i: (0, i, 0)),
            pl.BlockSpec((2, count, width), lambda i: (0, 0, 0)),
        ],
        out_specs=[
            pl.BlockSpec((step, width), lambda i: (i, 0)),
            pl.BlockSpec((8, 128), lambda i: (0, 0)),
        ],
        out_shape=[
            jax.ShapeDtypeStruct((count, width), BF16),
            jax.ShapeDtypeStruct((8, 128), F32),
        ],
        compiler_params=pltpu.CompilerParams(vmem_limit_bytes=48 * 2**20),
        name="self_forward",
    )(length, positions[:, None], positions[None, :], qkv[0][None], qkv[1:])


def self_backward_kernel(length_ref, row_ref, col_ref, q_ref, kv_ref, g_ref, dq_ref, dkv_ref, acc):
    length = length_ref[0]
    row_pos = row_ref[...]
    col_pos = col_ref[...]
    allowed = (col_pos <= row_pos) & (col_pos < length)

    @pl.when(pl.program_id(0) == 0)
    def _():
        acc[...] = jnp.zeros_like(acc)

    for head in range(q_ref.shape[-1] // HD):
        cut = slice(head * HD, (head + 1) * HD)
        query, grad = q_ref[0, :, cut], g_ref[:, cut]
        scores = dot(query, kv_ref[0, :, cut], NT) * SCALE
        scores = jnp.where(allowed, scores, masked_score)
        top = jnp.max(scores, axis=-1, keepdims=True)
        expos = jnp.exp(scores - top)
        probs = expos * (1.0 / jnp.sum(expos, axis=-1, keepdims=True))
        dprobs = dot(grad, kv_ref[1, :, cut], NT)
        delta = jnp.sum(probs * dprobs, axis=-1, keepdims=True)
        dscores = (probs * (dprobs - delta)).astype(BF16)
        dq_ref[:, cut] = (dot(dscores, kv_ref[0, :, cut]) * SCALE).astype(BF16)
        acc[0, :, cut] += dot(dscores, query, TN)
        acc[1, :, cut] += dot(probs.astype(BF16), grad, TN)

    @pl.when(pl.program_id(0) == pl.num_programs(0) - 1)
    def _():
        dkv_ref[0] = (acc[0] * SCALE).astype(BF16)
        dkv_ref[1] = acc[1].astype(BF16)


def self_backward(qkv, positions, length, grad):
    count, width = qkv.shape[1:]
    step = min(256, count)
    dq, dkv = pl.pallas_call(
        self_backward_kernel,
        grid=(count // step,),
        in_specs=[
            pl.BlockSpec(memory_space=pltpu.SMEM),
            pl.BlockSpec((step, 1), lambda i: (i, 0)),
            pl.BlockSpec((1, count), lambda i: (0, 0)),
            pl.BlockSpec((1, step, width), lambda i: (0, i, 0)),
            pl.BlockSpec((2, count, width), lambda i: (0, 0, 0)),
            pl.BlockSpec((step, width), lambda i: (i, 0)),
        ],
        out_specs=[
            pl.BlockSpec((step, width), lambda i: (i, 0)),
            pl.BlockSpec((2, count, width), lambda i: (0, 0, 0)),
        ],
        out_shape=[
            jax.ShapeDtypeStruct((count, width), BF16),
            jax.ShapeDtypeStruct((2, count, width), BF16),
        ],
        scratch_shapes=[pltpu.VMEM((2, count, width), F32)],
        compiler_params=pltpu.CompilerParams(vmem_limit_bytes=48 * 2**20),
        name="self_backward",
    )(length, positions[:, None], positions[None, :], qkv[0][None], qkv[1:], grad)
    return jnp.concatenate([dq[None], dkv], axis=0)


def cross_forward_kernel(limit_ref, target_ref, row_ref, q_ref, kv_ref, mix_ref, peak_ref):
    slot = pl.program_id(0)
    width = q_ref.shape[-1]
    keys = kv_ref.shape[1]
    live = lax.broadcasted_iota(jnp.int32, (1, keys), 1) < limit_ref[slot]
    valid = row_ref[...] < target_ref[slot]

    @pl.when(slot == 0)
    def _():
        peak_ref[...] = jnp.full_like(peak_ref, masked_score)

    for head in range(width // HD):
        cut = slice(head * HD, (head + 1) * HD)
        vcut = slice(width + head * HD, width + (head + 1) * HD)
        scores = dot(q_ref[0, :, cut], kv_ref[0, :, cut], NT) * SCALE
        scores = jnp.where(live, scores, masked_score)
        top = jnp.max(scores, axis=-1, keepdims=True)
        expos = jnp.exp(scores - top)
        probs = expos * (1.0 / jnp.sum(expos, axis=-1, keepdims=True))
        mix_ref[0, :, cut] = dot(probs.astype(BF16), kv_ref[0, :, vcut]).astype(BF16)
        peak = jnp.max(jnp.where(valid, top, masked_score), axis=0, keepdims=True)
        peak_ref[head : head + 1, :] = jnp.maximum(
            peak_ref[head : head + 1, :], jnp.broadcast_to(peak, (1, 128))
        )


def cross_forward(query, kv, own_positions, target_lengths, source_lengths):
    slots, rows, width = query.shape
    keys = kv.shape[1]
    return pl.pallas_call(
        cross_forward_kernel,
        grid=(slots,),
        in_specs=[
            pl.BlockSpec(memory_space=pltpu.SMEM),
            pl.BlockSpec(memory_space=pltpu.SMEM),
            pl.BlockSpec((rows, 1), lambda i: (0, 0)),
            pl.BlockSpec((1, rows, width), lambda i: (i, 0, 0)),
            pl.BlockSpec((1, keys, 2 * width), lambda i: (i, 0, 0)),
        ],
        out_specs=[
            pl.BlockSpec((1, rows, width), lambda i: (i, 0, 0)),
            pl.BlockSpec((8, 128), lambda i: (0, 0)),
        ],
        out_shape=[
            jax.ShapeDtypeStruct((slots, rows, width), BF16),
            jax.ShapeDtypeStruct((8, 128), F32),
        ],
        compiler_params=pltpu.CompilerParams(vmem_limit_bytes=48 * 2**20),
        name="cross_forward",
    )(source_lengths, target_lengths, own_positions[:, None], query, kv)


def cross_backward_kernel(limit_ref, q_ref, kv_ref, g_ref, dq_ref, dkv_ref):
    slot = pl.program_id(0)
    width = q_ref.shape[-1]
    keys = kv_ref.shape[1]
    live = lax.broadcasted_iota(jnp.int32, (1, keys), 1) < limit_ref[slot]
    for head in range(width // HD):
        cut = slice(head * HD, (head + 1) * HD)
        vcut = slice(width + head * HD, width + (head + 1) * HD)
        query, grad = q_ref[0, :, cut], g_ref[0, :, cut]
        scores = dot(query, kv_ref[0, :, cut], NT) * SCALE
        scores = jnp.where(live, scores, masked_score)
        top = jnp.max(scores, axis=-1, keepdims=True)
        expos = jnp.exp(scores - top)
        probs = expos * (1.0 / jnp.sum(expos, axis=-1, keepdims=True))
        dprobs = dot(grad, kv_ref[0, :, vcut], NT)
        delta = jnp.sum(probs * dprobs, axis=-1, keepdims=True)
        dscores = (probs * (dprobs - delta)).astype(BF16)
        dq_ref[0, :, cut] = (dot(dscores, kv_ref[0, :, cut]) * SCALE).astype(BF16)
        dkv_ref[0, :, cut] = (dot(dscores, query, TN) * SCALE).astype(BF16)
        dkv_ref[0, :, vcut] = dot(probs.astype(BF16), grad, TN).astype(BF16)


def cross_backward(query, kv, source_lengths, grad):
    slots, rows, width = query.shape
    keys = kv.shape[1]
    return pl.pallas_call(
        cross_backward_kernel,
        grid=(slots,),
        in_specs=[
            pl.BlockSpec(memory_space=pltpu.SMEM),
            pl.BlockSpec((1, rows, width), lambda i: (i, 0, 0)),
            pl.BlockSpec((1, keys, 2 * width), lambda i: (i, 0, 0)),
            pl.BlockSpec((1, rows, width), lambda i: (i, 0, 0)),
        ],
        out_specs=[
            pl.BlockSpec((1, rows, width), lambda i: (i, 0, 0)),
            pl.BlockSpec((1, keys, 2 * width), lambda i: (i, 0, 0)),
        ],
        out_shape=[
            jax.ShapeDtypeStruct((slots, rows, width), BF16),
            jax.ShapeDtypeStruct((slots, keys, 2 * width), BF16),
        ],
        compiler_params=pltpu.CompilerParams(vmem_limit_bytes=48 * 2**20),
        name="cross_backward",
    )(source_lengths, query, kv, grad)


def gather_seq(rows):
    return lax.all_gather(rows, "seq", axis=0, tiled=True)


def scatter_seq(partial):
    return lax.psum_scatter(
        partial.astype(BF16), "seq", scatter_dimension=0, tiled=True
    ).astype(F32)


def swap(blocks, axis):
    return lax.all_to_all(blocks, axis, split_axis=0, concat_axis=0, tiled=True)


def columns_of(weight, parts):
    seq_count = lax.axis_size("seq")
    rows, columns = weight.shape
    width = columns // (parts * seq_count)
    blocks = weight.reshape(rows, parts, seq_count, width).transpose(2, 0, 1, 3)
    return swap(blocks.reshape(seq_count, rows, parts * width), "seq").reshape(
        seq_count * rows, parts * width
    )


def finish_rows(grad):
    return lax.psum_scatter(grad.astype(BF16), "ctx", scatter_dimension=0, tiled=True).astype(F32)


def finish_columns(grad, parts):
    seq_count, ctx_count = lax.axis_size("seq"), lax.axis_size("ctx")
    rows, columns = grad.shape
    share = rows // (seq_count * ctx_count)
    blocks = grad.astype(BF16).reshape(seq_count, ctx_count, share, columns).transpose(1, 0, 2, 3)
    own = lax.psum_scatter(
        blocks.reshape(ctx_count * seq_count * share, columns),
        "ctx",
        scatter_dimension=0,
        tiled=True,
    ).reshape(seq_count, share, columns)
    taken = swap(own, "seq").reshape(seq_count, share, parts, columns // parts)
    return taken.transpose(1, 2, 0, 3).reshape(share, seq_count * columns).astype(F32)


def fast_device(
    tokens,
    encoder_states,
    cotangent,
    target_lengths,
    source_lengths,
    block_table,
    self_qkv,
    self_out,
    cross_q,
    cross_kv,
    cross_out,
    mlp_up,
    mlp_down,
    norm_gain,
    norm_bias,
    clip_limit,
):
    rows = tokens.shape[1]
    source_rows = encoder_states.shape[1]
    seq_count, ctx_count = lax.axis_size("seq"), lax.axis_size("ctx")
    seq_index, ctx_index = lax.axis_index("seq"), lax.axis_index("ctx")
    held, pair = H // seq_count, H // ctx_count
    groups = held // pair
    own_width, pair_width = held * HD, pair * HD
    width = H * HD
    half = rows // 2
    all_positions = (
        block_table[:, :, None] * half + jnp.arange(half, dtype=jnp.int32)[None, None, :]
    ).reshape(-1)
    own_positions = lax.dynamic_slice_in_dim(all_positions, ctx_index * rows, rows, 0)
    valid_rows = (own_positions < target_lengths[0])[:, None]
    targets, sources = gather_seq(target_lengths), gather_seq(source_lengths)
    my_slot = ctx_index // groups
    my_length = lax.dynamic_slice_in_dim(targets, my_slot, 1, 0)

    w_qkv, w_cq, w_ckv = columns_of(self_qkv, 3), columns_of(cross_q, 1), columns_of(cross_kv, 2)
    w_up = columns_of(mlp_up, 1)

    inputs = tokens[0].astype(F32)
    hat_one, inverse_one, first_own = norm_forward(inputs, norm_gain[0], norm_bias[0])
    first_low = gather_seq(first_own)
    source_low = gather_seq(encoder_states[0])
    grad_rows = jnp.where(valid_rows, cotangent[0].astype(F32), 0.0)
    mlp_branch = gather_seq(grad_rows.astype(BF16))

    def to_heads(blocks, parts):
        blocks = blocks.reshape(seq_count, rows, parts, groups, pair_width)
        blocks = blocks.transpose(0, 3, 2, 1, 4).reshape(ctx_count, parts * rows, pair_width)
        taken = swap(blocks, "ctx").reshape(ctx_count, parts, rows, pair_width)
        return taken.transpose(1, 0, 2, 3).reshape(parts, ctx_count * rows, pair_width)

    def to_rows(heads):
        parts = heads.shape[0]
        blocks = heads.reshape(parts, ctx_count, rows, pair_width).transpose(1, 0, 2, 3)
        taken = swap(blocks.reshape(ctx_count, parts * rows, pair_width), "ctx")
        taken = taken.reshape(seq_count, groups, parts, rows, pair_width).transpose(0, 3, 2, 1, 4)
        return taken.reshape(seq_count * rows, parts * own_width)

    projected = dot(first_low, w_qkv).astype(BF16)
    qkv = to_heads(projected, 3)
    self_mix, self_peak = self_forward(qkv, all_positions, my_length)
    self_low = to_rows(self_mix[None])

    source_kv = dot(source_low, w_ckv).astype(BF16)
    cross_kvs = lax.all_gather(source_kv, "ctx", axis=0, tiled=True)
    cross_kvs = (
        cross_kvs.reshape(ctx_count, seq_count, source_rows, 2 * own_width)
        .transpose(1, 0, 2, 3)
        .reshape(seq_count, ctx_count * source_rows, 2 * own_width)
    )

    first_sum = inputs + scatter_seq(dot(self_low, self_out))
    hat_two, inverse_two, second_own = norm_forward(first_sum, norm_gain[1], norm_bias[1])
    second_low = gather_seq(second_own)
    cross_query = dot(second_low, w_cq).astype(BF16).reshape(seq_count, rows, own_width)
    cross_mix, cross_peak = cross_forward(cross_query, cross_kvs, own_positions, targets, sources)
    cross_low = cross_mix.reshape(seq_count * rows, own_width)
    second_sum = first_sum + scatter_seq(dot(cross_low, cross_out))
    hat_three, inverse_three, third_own = norm_forward(second_sum, norm_gain[2], norm_bias[2])
    third_low = gather_seq(third_own)

    hidden_pre = dot(third_low, w_up)
    hidden_act, gelu_back = jax.vjp(jax.nn.gelu, hidden_pre)
    hidden_low = hidden_act.astype(BF16)
    third_sum = second_sum + scatter_seq(dot(hidden_low, mlp_down))
    output_rows = jnp.where(valid_rows, third_sum, 0.0).astype(BF16)

    peak_self = lax.dynamic_update_slice_in_dim(
        jnp.full((H,), masked_score, F32),
        self_peak[:pair, 0],
        seq_index * held + (ctx_index % groups) * pair,
        0,
    )
    peak_cross = lax.dynamic_update_slice_in_dim(
        jnp.full((H,), masked_score, F32), cross_peak[:held, 0], seq_index * held, 0
    )
    peaks = lax.pmax(jnp.stack([peak_self, peak_cross]), ("seq", "ctx"))

    grad_down = dot(hidden_low, mlp_branch, TN)
    grad_pre = gelu_back(dot(mlp_branch, mlp_down, NT))[0].astype(BF16)
    grad_up = dot(third_low, grad_pre, TN)
    back_three, gain_three, bias_three = norm_backward(
        scatter_seq(dot(grad_pre, w_up, NT)), hat_three, inverse_three, norm_gain[2]
    )
    up_shard, down_shard = finish_columns(grad_up, 1), finish_rows(grad_down)

    grad_second = grad_rows + back_three
    cross_branch = gather_seq(grad_second.astype(BF16))
    grad_co = dot(cross_low, cross_branch, TN)
    cross_grad = dot(cross_branch, cross_out, NT).astype(BF16)
    dquery, dkv = cross_backward(
        cross_query, cross_kvs, sources, cross_grad.reshape(seq_count, rows, own_width)
    )
    dquery = dquery.reshape(seq_count * rows, own_width)
    dkv = (
        dkv.reshape(seq_count, ctx_count, source_rows, 2 * own_width)
        .transpose(1, 0, 2, 3)
        .reshape(ctx_count * seq_count * source_rows, 2 * own_width)
    )
    grad_source_kv = lax.psum_scatter(dkv, "ctx", scatter_dimension=0, tiled=True)
    grad_cq = dot(second_low, dquery, TN)
    grad_ckv = dot(source_low, grad_source_kv, TN)
    grad_source = scatter_seq(dot(grad_source_kv, w_ckv, NT))
    back_two, gain_two, bias_two = norm_backward(
        scatter_seq(dot(dquery, w_cq, NT)), hat_two, inverse_two, norm_gain[1]
    )
    grad_first = grad_second + back_two
    self_branch = gather_seq(grad_first.astype(BF16))
    grad_so = dot(self_low, self_branch, TN)
    self_grad = to_heads(dot(self_branch, self_out, NT).astype(BF16), 1)[0]
    grad_projected = to_rows(self_backward(qkv, all_positions, my_length, self_grad))
    grad_qkv = dot(first_low, grad_projected, TN)
    back_one, gain_one, bias_one = norm_backward(
        scatter_seq(dot(grad_projected, w_qkv, NT)), hat_one, inverse_one, norm_gain[0]
    )
    grad_inputs = grad_first + back_one

    norm_terms = jnp.stack([gain_one, gain_two, gain_three, bias_one, bias_two, bias_three])
    norm_sum = lax.psum(norm_terms, ("seq", "ctx"))
    norm_share = width // (seq_count * ctx_count)
    norm_shard = lax.dynamic_slice_in_dim(
        norm_sum, (seq_index * ctx_count + ctx_index) * norm_share, norm_share, 1
    )

    factors = jnp.sqrt(clip_limit / jnp.maximum(peaks, clip_limit))
    columns = jnp.repeat(factors, HD, axis=1)
    qkv_wide = self_qkv.astype(F32)
    clipped_self = jnp.concatenate(
        [qkv_wide[:, :width] * columns[0], qkv_wide[:, width : 2 * width] * columns[0]], axis=1
    ).astype(BF16)
    clipped_cross = jnp.concatenate(
        [cross_q.astype(F32) * columns[1], cross_kv[:, :width].astype(F32) * columns[1]], axis=1
    ).astype(BF16)
    return (
        output_rows[None],
        grad_inputs[None],
        grad_source[None],
        finish_columns(grad_qkv, 3),
        finish_rows(grad_so),
        finish_columns(grad_cq, 1),
        finish_columns(grad_ckv, 2),
        finish_rows(grad_co),
        up_shard,
        down_shard,
        norm_shard[:3],
        norm_shard[3:],
        clipped_self,
        clipped_cross,
        peaks,
    )


def solution(mesh):
    body = fast_device if fast_fits(mesh) else general_device
    return jax.shard_map(
        body,
        mesh=mesh,
        in_specs=(
            P("seq", "ctx", None),
            P("seq", "ctx", None),
            P("seq", "ctx", None),
            P("seq"),
            P("seq"),
            P(),
            P("seq", None),
            P("seq", None),
            P("seq", None),
            P("seq", None),
            P("seq", None),
            P("seq", None),
            P("seq", None),
            P(),
            P(),
            P(),
        ),
        out_specs=(
            P("seq", "ctx", None),
            P("seq", "ctx", None),
            P("seq", "ctx", None),
            P(("seq", "ctx"), None),
            P(("seq", "ctx"), None),
            P(("seq", "ctx"), None),
            P(("seq", "ctx"), None),
            P(("seq", "ctx"), None),
            P(("seq", "ctx"), None),
            P(("seq", "ctx"), None),
            P(None, ("seq", "ctx")),
            P(None, ("seq", "ctx")),
            P("seq", None),
            P("seq", None),
            P(),
        ),
        check_vma=False,
    )
```

```python
import functools

import jax
import jax.numpy as jnp
from jax import lax
from jax.experimental import pallas as pl
from jax.experimental.pallas import tpu as pltpu
from jax.sharding import PartitionSpec as P

H = 16
HD = 64


masked_score = -1000000000.0
norm_eps = 1e-05


def block_size(count):
    return max((step for step in range(1, min(count, 512) + 1) if count % step == 0))


def layer_norm(values, gain, bias):
    centered = values - jnp.mean(values, axis=-1, keepdims=True)
    spread = jnp.mean(centered * centered, axis=-1, keepdims=True)
    return centered * lax.rsqrt(spread + norm_eps) * gain + bias


def allowed_pairs(query_pos, key_pos, key_limit, causal):
    allowed = jnp.broadcast_to(
        (key_pos < key_limit)[None, :], (query_pos.shape[0], key_pos.shape[0])
    )
    if causal:
        allowed = allowed & (key_pos[None, :] <= query_pos[:, None])
    return allowed


def head_scores(query_heads, key_rows):
    key_heads = key_rows.reshape(key_rows.shape[0], H, HD)
    return jnp.einsum(
        "qhd,khd->hqk", query_heads, key_heads, preferred_element_type=jnp.float32
    ) * HD ** (-0.5)


def softmax_stats(query_heads, kv_rows, key_pos, query_pos, query_ok, key_limit, causal):
    count = kv_rows.shape[0]
    step = block_size(count)
    width = H * HD
    rows = query_heads.shape[0]

    def softmax_visit(carry, block):
        top, total, peak = carry
        block_rows, block_pos = block
        allowed = allowed_pairs(query_pos, block_pos, key_limit, causal)
        scores = jnp.where(
            allowed[None], head_scores(query_heads, block_rows[:, :width]), masked_score
        )
        new_top = jnp.maximum(top, jnp.max(scores, axis=-1))
        total = total * jnp.exp(top - new_top) + jnp.sum(
            jnp.exp(scores - new_top[..., None]), axis=-1
        )
        counted = jnp.where((allowed & query_ok[:, None])[None], scores, masked_score)
        peak = jnp.maximum(peak, jnp.max(counted, axis=(1, 2)))
        return ((new_top, total, peak), None)

    start = (
        jnp.full((H, rows), -jnp.inf, jnp.float32),
        jnp.zeros((H, rows), jnp.float32),
        jnp.full((H,), masked_score, jnp.float32),
    )
    blocks = (kv_rows.reshape(count // step, step, 2 * width), key_pos.reshape(count // step, step))
    return lax.scan(softmax_visit, start, blocks)[0]


def attend_values(query_heads, kv_rows, key_pos, query_pos, key_limit, causal, top, total):
    count = kv_rows.shape[0]
    step = block_size(count)
    width = H * HD
    rows = query_heads.shape[0]

    def attend_visit(acc, block):
        block_rows, block_pos = block
        allowed = allowed_pairs(query_pos, block_pos, key_limit, causal)
        scores = jnp.where(
            allowed[None], head_scores(query_heads, block_rows[:, :width]), masked_score
        )
        weights = (jnp.exp(scores - top[..., None]) / total[..., None]).astype(jnp.bfloat16)
        value_heads = block_rows[:, width:].reshape(step, H, HD)
        return (
            acc
            + jnp.einsum("hqk,khd->qhd", weights, value_heads, preferred_element_type=jnp.float32),
            None,
        )

    blocks = (kv_rows.reshape(count // step, step, 2 * width), key_pos.reshape(count // step, step))
    acc = lax.scan(attend_visit, jnp.zeros((rows, H, HD), jnp.float32), blocks)[0]
    return acc.reshape(rows, width)


def query_grads(
    query_heads, kv_rows, key_pos, query_pos, key_limit, causal, top, total, grad_heads, delta
):
    count = kv_rows.shape[0]
    step = block_size(count)
    width = H * HD
    rows = query_heads.shape[0]

    def query_visit(acc, block):
        block_rows, block_pos = block
        allowed = allowed_pairs(query_pos, block_pos, key_limit, causal)
        scores = jnp.where(
            allowed[None], head_scores(query_heads, block_rows[:, :width]), masked_score
        )
        probs = jnp.exp(scores - top[..., None]) / total[..., None]
        value_heads = block_rows[:, width:].reshape(step, H, HD)
        dprobs = jnp.einsum(
            "qhd,khd->hqk", grad_heads, value_heads, preferred_element_type=jnp.float32
        )
        dscores = (probs * (dprobs - delta[..., None])).astype(jnp.bfloat16)
        key_heads = block_rows[:, :width].reshape(step, H, HD)
        return (
            acc
            + jnp.einsum("hqk,khd->qhd", dscores, key_heads, preferred_element_type=jnp.float32),
            None,
        )

    blocks = (kv_rows.reshape(count // step, step, 2 * width), key_pos.reshape(count // step, step))
    acc = lax.scan(query_visit, jnp.zeros((rows, H, HD), jnp.float32), blocks)[0]
    return acc.reshape(rows, width) * HD ** (-0.5)


def key_grads(
    query_heads,
    kv_rows,
    key_pos,
    query_pos,
    key_limit,
    causal,
    top,
    total,
    grad_heads,
    delta,
    start,
    count,
):
    step = block_size(count)
    width = H * HD

    def piece(index):
        offset = start + index * step
        block_rows = lax.dynamic_slice_in_dim(kv_rows, offset, step, 0)
        block_pos = lax.dynamic_slice_in_dim(key_pos, offset, step, 0)
        allowed = allowed_pairs(query_pos, block_pos, key_limit, causal)
        scores = jnp.where(
            allowed[None], head_scores(query_heads, block_rows[:, :width]), masked_score
        )
        probs = jnp.exp(scores - top[..., None]) / total[..., None]
        value_heads = block_rows[:, width:].reshape(step, H, HD)
        dprobs = jnp.einsum(
            "qhd,khd->hqk", grad_heads, value_heads, preferred_element_type=jnp.float32
        )
        dscores = (probs * (dprobs - delta[..., None])).astype(jnp.bfloat16)
        dkeys = jnp.einsum(
            "hqk,qhd->khd", dscores, query_heads, preferred_element_type=jnp.float32
        ).reshape(step, width) * HD ** (-0.5)
        dvalues = jnp.einsum(
            "hqk,qhd->khd",
            probs.astype(jnp.bfloat16),
            grad_heads,
            preferred_element_type=jnp.float32,
        ).reshape(step, width)
        return jnp.concatenate([dkeys, dvalues], axis=1)

    return lax.map(piece, jnp.arange(count // step, dtype=jnp.int32)).reshape(count, 2 * width)


def split_rows(grad, seq_count, ctx_count):
    return grad.reshape(
        (seq_count, ctx_count, grad.shape[0] // (seq_count * ctx_count)) + grad.shape[1:]
    )


def join_rows(grad):
    return grad.reshape((grad.shape[2],) + grad.shape[3:])


def general_device(
    tokens,
    encoder_states,
    cotangent,
    target_lengths,
    source_lengths,
    block_table,
    self_qkv,
    self_out,
    cross_q,
    cross_kv,
    cross_out,
    mlp_up,
    mlp_down,
    norm_gain,
    norm_bias,
    clip_limit,
):
    rows = tokens.shape[1]
    width = H * HD
    half = rows // 2
    source_rows = encoder_states.shape[1]
    seq_count = lax.axis_size("seq")
    ctx_count = lax.axis_size("ctx")
    all_positions = (
        block_table[:, :, None] * half + jnp.arange(half, dtype=jnp.int32)[None, None, :]
    ).reshape(-1)
    own_positions = lax.dynamic_slice_in_dim(all_positions, lax.axis_index("ctx") * rows, rows, 0)
    length = target_lengths[0]
    source_length = source_lengths[0]
    query_ok = own_positions < length
    valid_rows = query_ok[:, None]
    source_positions = jnp.arange(source_rows * ctx_count, dtype=jnp.int32)
    w_qkv, w_out, w_cq, w_ckv, w_co = (
        lax.all_gather(self_qkv, "seq", axis=0, tiled=True),
        lax.all_gather(self_out, "seq", axis=0, tiled=True),
        lax.all_gather(cross_q, "seq", axis=0, tiled=True),
        lax.all_gather(cross_kv, "seq", axis=0, tiled=True),
        lax.all_gather(cross_out, "seq", axis=0, tiled=True),
    )
    inputs = tokens[0].astype(jnp.float32)
    first_norm, first_back = jax.vjp(layer_norm, inputs, norm_gain[0], norm_bias[0])
    first_low = first_norm.astype(jnp.bfloat16)
    projected = jnp.dot(first_low, w_qkv, preferred_element_type=jnp.float32).astype(jnp.bfloat16)
    self_query = projected[:, :width].reshape(rows, H, HD)
    source_kv = jnp.dot(encoder_states[0], w_ckv, preferred_element_type=jnp.float32).astype(
        jnp.bfloat16
    )
    self_kv, cross_kvs = (
        lax.all_gather(projected[:, width:], "ctx", axis=0, tiled=True),
        lax.all_gather(source_kv, "ctx", axis=0, tiled=True),
    )
    self_top, self_total, self_peak = softmax_stats(
        self_query, self_kv, all_positions, own_positions, query_ok, length, True
    )
    self_mix = attend_values(
        self_query, self_kv, all_positions, own_positions, length, True, self_top, self_total
    )
    self_low = self_mix.astype(jnp.bfloat16)
    first_sum = inputs + jnp.dot(self_low, w_out, preferred_element_type=jnp.float32)
    second_norm, second_back = jax.vjp(layer_norm, first_sum, norm_gain[1], norm_bias[1])
    second_low = second_norm.astype(jnp.bfloat16)
    cross_rows = jnp.dot(second_low, w_cq, preferred_element_type=jnp.float32).astype(jnp.bfloat16)
    cross_query = cross_rows.reshape(rows, H, HD)
    cross_top, cross_total, cross_peak = softmax_stats(
        cross_query, cross_kvs, source_positions, own_positions, query_ok, source_length, False
    )
    cross_mix = attend_values(
        cross_query,
        cross_kvs,
        source_positions,
        own_positions,
        source_length,
        False,
        cross_top,
        cross_total,
    )
    cross_low = cross_mix.astype(jnp.bfloat16)
    second_sum = first_sum + jnp.dot(cross_low, w_co, preferred_element_type=jnp.float32)
    third_norm, third_back = jax.vjp(layer_norm, second_sum, norm_gain[2], norm_bias[2])
    third_low = third_norm.astype(jnp.bfloat16)
    w_up, w_down = (
        lax.all_gather(mlp_up, "seq", axis=0, tiled=True),
        lax.all_gather(mlp_down, "seq", axis=0, tiled=True),
    )
    hidden_pre = jnp.dot(third_low, w_up, preferred_element_type=jnp.float32)
    hidden_act, gelu_back = jax.vjp(jax.nn.gelu, hidden_pre)
    hidden_low = hidden_act.astype(jnp.bfloat16)
    third_sum = second_sum + jnp.dot(hidden_low, w_down, preferred_element_type=jnp.float32)
    output_rows = jnp.where(valid_rows, third_sum, 0.0).astype(jnp.bfloat16)
    peaks = lax.pmax(jnp.stack([self_peak, cross_peak]), ("seq", "ctx"))
    grad_rows = jnp.where(valid_rows, cotangent[0].astype(jnp.float32), 0.0)
    mlp_branch = grad_rows.astype(jnp.bfloat16)
    grad_down = jnp.einsum("rf,rd->fd", hidden_low, mlp_branch, preferred_element_type=jnp.float32)
    grad_act = jnp.einsum("rd,fd->rf", mlp_branch, w_down, preferred_element_type=jnp.float32)
    grad_pre = gelu_back(grad_act)[0].astype(jnp.bfloat16)
    grad_up = jnp.einsum("rd,rf->df", third_low, grad_pre, preferred_element_type=jnp.float32)
    back_third, gain_three, bias_three = third_back(
        jnp.einsum("rf,df->rd", grad_pre, w_up, preferred_element_type=jnp.float32)
    )
    up_part, down_part = (
        lax.psum_scatter(
            split_rows(grad_up, seq_count, ctx_count).astype(jnp.bfloat16),
            "ctx",
            scatter_dimension=1,
            tiled=True,
        ).astype(jnp.float32),
        lax.psum_scatter(
            split_rows(grad_down, seq_count, ctx_count).astype(jnp.bfloat16),
            "ctx",
            scatter_dimension=1,
            tiled=True,
        ).astype(jnp.float32),
    )
    up_shard, down_shard = (
        lax.psum_scatter(
            up_part.astype(jnp.bfloat16), "seq", scatter_dimension=0, tiled=True
        ).astype(jnp.float32),
        lax.psum_scatter(
            down_part.astype(jnp.bfloat16), "seq", scatter_dimension=0, tiled=True
        ).astype(jnp.float32),
    )
    grad_second = grad_rows + back_third
    cross_branch = grad_second.astype(jnp.bfloat16)
    grad_co = jnp.einsum("rd,re->de", cross_low, cross_branch, preferred_element_type=jnp.float32)
    cross_heads_grad = (
        jnp.einsum("re,de->rd", cross_branch, w_co, preferred_element_type=jnp.float32)
        .astype(jnp.bfloat16)
        .reshape(rows, H, HD)
    )
    cross_delta = jnp.einsum(
        "qhd,qhd->hq", cross_heads_grad.astype(jnp.float32), cross_mix.reshape(rows, H, HD)
    )
    grad_cross_rows = query_grads(
        cross_query,
        cross_kvs,
        source_positions,
        own_positions,
        source_length,
        False,
        cross_top,
        cross_total,
        cross_heads_grad,
        cross_delta,
    ).astype(jnp.bfloat16)
    grad_source_kv = lax.psum_scatter(
        key_grads(
            cross_query,
            cross_kvs,
            source_positions,
            own_positions,
            source_length,
            False,
            cross_top,
            cross_total,
            cross_heads_grad,
            cross_delta,
            jnp.int32(0),
            source_rows * lax.axis_size("ctx"),
        ).astype(jnp.bfloat16),
        "ctx",
        scatter_dimension=0,
        tiled=True,
    )
    grad_cq = jnp.einsum(
        "rd,re->de", second_low, grad_cross_rows, preferred_element_type=jnp.float32
    )
    grad_ckv = jnp.einsum(
        "sd,se->de", encoder_states[0], grad_source_kv, preferred_element_type=jnp.float32
    )
    grad_source = jnp.einsum("se,de->sd", grad_source_kv, w_ckv, preferred_element_type=jnp.float32)
    back_second, gain_two, bias_two = second_back(
        jnp.einsum("re,de->rd", grad_cross_rows, w_cq, preferred_element_type=jnp.float32)
    )
    grad_first = grad_second + back_second
    self_branch = grad_first.astype(jnp.bfloat16)
    grad_so = jnp.einsum("rd,re->de", self_low, self_branch, preferred_element_type=jnp.float32)
    self_heads_grad = (
        jnp.einsum("re,de->rd", self_branch, w_out, preferred_element_type=jnp.float32)
        .astype(jnp.bfloat16)
        .reshape(rows, H, HD)
    )
    self_delta = jnp.einsum(
        "qhd,qhd->hq", self_heads_grad.astype(jnp.float32), self_mix.reshape(rows, H, HD)
    )
    grad_query = query_grads(
        self_query,
        self_kv,
        all_positions,
        own_positions,
        length,
        True,
        self_top,
        self_total,
        self_heads_grad,
        self_delta,
    ).astype(jnp.bfloat16)
    grad_kv = lax.psum_scatter(
        key_grads(
            self_query,
            self_kv,
            all_positions,
            own_positions,
            length,
            True,
            self_top,
            self_total,
            self_heads_grad,
            self_delta,
            jnp.int32(0),
            rows * lax.axis_size("ctx"),
        ).astype(jnp.bfloat16),
        "ctx",
        scatter_dimension=0,
        tiled=True,
    )
    grad_projected = jnp.concatenate([grad_query, grad_kv], axis=1)
    grad_qkv = jnp.einsum(
        "rd,re->de", first_low, grad_projected, preferred_element_type=jnp.float32
    )
    back_first, gain_one, bias_one = first_back(
        jnp.einsum("re,de->rd", grad_projected, w_qkv, preferred_element_type=jnp.float32)
    )
    grad_inputs = grad_first + back_first
    norm_terms = jnp.stack([gain_one, gain_two, gain_three, bias_one, bias_two, bias_three], axis=1)
    qkv_part, out_part, cq_part, ckv_part, co_part, norm_part = (
        lax.psum_scatter(
            split_rows(grad_qkv, seq_count, ctx_count).astype(jnp.bfloat16),
            "ctx",
            scatter_dimension=1,
            tiled=True,
        ).astype(jnp.float32),
        lax.psum_scatter(
            split_rows(grad_so, seq_count, ctx_count).astype(jnp.bfloat16),
            "ctx",
            scatter_dimension=1,
            tiled=True,
        ).astype(jnp.float32),
        lax.psum_scatter(
            split_rows(grad_cq, seq_count, ctx_count).astype(jnp.bfloat16),
            "ctx",
            scatter_dimension=1,
            tiled=True,
        ).astype(jnp.float32),
        lax.psum_scatter(
            split_rows(grad_ckv, seq_count, ctx_count).astype(jnp.bfloat16),
            "ctx",
            scatter_dimension=1,
            tiled=True,
        ).astype(jnp.float32),
        lax.psum_scatter(
            split_rows(grad_co, seq_count, ctx_count).astype(jnp.bfloat16),
            "ctx",
            scatter_dimension=1,
            tiled=True,
        ).astype(jnp.float32),
        lax.psum_scatter(
            split_rows(norm_terms, seq_count, ctx_count).astype(jnp.bfloat16),
            "ctx",
            scatter_dimension=1,
            tiled=True,
        ).astype(jnp.float32),
    )
    qkv_shard, out_shard, cq_shard, ckv_shard, co_shard, norm_shard = (
        lax.psum_scatter(
            qkv_part.astype(jnp.bfloat16), "seq", scatter_dimension=0, tiled=True
        ).astype(jnp.float32),
        lax.psum_scatter(
            out_part.astype(jnp.bfloat16), "seq", scatter_dimension=0, tiled=True
        ).astype(jnp.float32),
        lax.psum_scatter(
            cq_part.astype(jnp.bfloat16), "seq", scatter_dimension=0, tiled=True
        ).astype(jnp.float32),
        lax.psum_scatter(
            ckv_part.astype(jnp.bfloat16), "seq", scatter_dimension=0, tiled=True
        ).astype(jnp.float32),
        lax.psum_scatter(
            co_part.astype(jnp.bfloat16), "seq", scatter_dimension=0, tiled=True
        ).astype(jnp.float32),
        lax.psum_scatter(
            norm_part.astype(jnp.bfloat16), "seq", scatter_dimension=0, tiled=True
        ).astype(jnp.float32),
    )
    norm_shard = join_rows(norm_shard)
    factors = jnp.sqrt(clip_limit / jnp.maximum(peaks, clip_limit))
    columns = jnp.repeat(factors, HD, axis=1)
    qkv_wide = self_qkv.astype(jnp.float32)
    clipped_self = jnp.concatenate(
        [qkv_wide[:, :width] * columns[0], qkv_wide[:, width : 2 * width] * columns[0]], axis=1
    ).astype(jnp.bfloat16)
    clipped_cross = jnp.concatenate(
        [
            cross_q.astype(jnp.float32) * columns[1],
            cross_kv[:, :width].astype(jnp.float32) * columns[1],
        ],
        axis=1,
    ).astype(jnp.bfloat16)
    return (
        output_rows[None],
        grad_inputs[None],
        grad_source[None],
        join_rows(qkv_shard),
        join_rows(out_shard),
        join_rows(cq_shard),
        join_rows(ckv_shard),
        join_rows(co_shard),
        join_rows(up_shard),
        join_rows(down_shard),
        norm_shard[:, :3].T,
        norm_shard[:, 3:].T,
        clipped_self,
        clipped_cross,
        peaks,
    )


F32 = jnp.float32
BF16 = jnp.bfloat16
SCALE = HD**-0.5


def fast_fits(mesh):
    seq_count, ctx_count = mesh.shape["seq"], mesh.shape["ctx"]
    if H % seq_count or H % ctx_count:
        return False
    held, pair = H // seq_count, H // ctx_count
    return held % pair == 0 and seq_count * (held // pair) == ctx_count and pair * HD == 128


def dot(left, right, contract=((1,), (0,))):
    return lax.dot_general(left, right, (contract, ((), ())), preferred_element_type=F32)


NT = ((1,), (1,))
TN = ((0,), (0,))


def norm_forward(values, gain, bias):
    centered = values - jnp.mean(values, axis=-1, keepdims=True)
    spread = jnp.mean(centered * centered, axis=-1, keepdims=True)
    inverse = lax.rsqrt(spread + norm_eps)
    hat = centered * inverse
    return hat, inverse, (hat * gain + bias).astype(BF16)


def norm_backward(grad, hat, inverse, gain):
    scaled = grad * gain
    inner = jnp.mean(scaled, axis=-1, keepdims=True)
    outer = jnp.mean(scaled * hat, axis=-1, keepdims=True)
    return (
        (scaled - inner - hat * outer) * inverse,
        jnp.sum(grad * hat, axis=0),
        jnp.sum(grad, axis=0),
    )


def self_forward_kernel(length_ref, row_ref, col_ref, q_ref, kv_ref, mix_ref, peak_ref):
    length = length_ref[0]
    row_pos = row_ref[...]
    col_pos = col_ref[...]
    allowed = (col_pos <= row_pos) & (col_pos < length)
    valid = row_pos < length

    @pl.when(pl.program_id(0) == 0)
    def _():
        peak_ref[...] = jnp.full_like(peak_ref, masked_score)

    for head in range(q_ref.shape[-1] // HD):
        cut = slice(head * HD, (head + 1) * HD)
        scores = dot(q_ref[0, :, cut], kv_ref[0, :, cut], NT) * SCALE
        scores = jnp.where(allowed, scores, masked_score)
        top = jnp.max(scores, axis=-1, keepdims=True)
        expos = jnp.exp(scores - top)
        probs = expos * (1.0 / jnp.sum(expos, axis=-1, keepdims=True))
        mix_ref[:, cut] = dot(probs.astype(BF16), kv_ref[1, :, cut]).astype(BF16)
        peak = jnp.max(jnp.where(valid, top, masked_score), axis=0, keepdims=True)
        peak_ref[head : head + 1, :] = jnp.maximum(
            peak_ref[head : head + 1, :], jnp.broadcast_to(peak, (1, 128))
        )


def self_forward(qkv, positions, length):
    count, width = qkv.shape[1:]
    step = min(256, count)
    return pl.pallas_call(
        self_forward_kernel,
        grid=(count // step,),
        in_specs=[
            pl.BlockSpec(memory_space=pltpu.SMEM),
            pl.BlockSpec((step, 1), lambda i: (i, 0)),
            pl.BlockSpec((1, count), lambda i: (0, 0)),
            pl.BlockSpec((1, step, width), lambda i: (0, i, 0)),
            pl.BlockSpec((2, count, width), lambda i: (0, 0, 0)),
        ],
        out_specs=[
            pl.BlockSpec((step, width), lambda i: (i, 0)),
            pl.BlockSpec((8, 128), lambda i: (0, 0)),
        ],
        out_shape=[
            jax.ShapeDtypeStruct((count, width), BF16),
            jax.ShapeDtypeStruct((8, 128), F32),
        ],
        compiler_params=pltpu.CompilerParams(vmem_limit_bytes=48 * 2**20),
        name="self_forward",
    )(length, positions[:, None], positions[None, :], qkv[0][None], qkv[1:])


def self_backward_kernel(length_ref, row_ref, col_ref, q_ref, kv_ref, g_ref, dq_ref, dkv_ref, acc):
    length = length_ref[0]
    row_pos = row_ref[...]
    col_pos = col_ref[...]
    allowed = (col_pos <= row_pos) & (col_pos < length)

    @pl.when(pl.program_id(0) == 0)
    def _():
        acc[...] = jnp.zeros_like(acc)

    for head in range(q_ref.shape[-1] // HD):
        cut = slice(head * HD, (head + 1) * HD)
        query, grad = q_ref[0, :, cut], g_ref[:, cut]
        scores = dot(query, kv_ref[0, :, cut], NT) * SCALE
        scores = jnp.where(allowed, scores, masked_score)
        top = jnp.max(scores, axis=-1, keepdims=True)
        expos = jnp.exp(scores - top)
        probs = expos * (1.0 / jnp.sum(expos, axis=-1, keepdims=True))
        dprobs = dot(grad, kv_ref[1, :, cut], NT)
        delta = jnp.sum(probs * dprobs, axis=-1, keepdims=True)
        dscores = (probs * (dprobs - delta)).astype(BF16)
        dq_ref[:, cut] = (dot(dscores, kv_ref[0, :, cut]) * SCALE).astype(BF16)
        acc[0, :, cut] += dot(dscores, query, TN)
        acc[1, :, cut] += dot(probs.astype(BF16), grad, TN)

    @pl.when(pl.program_id(0) == pl.num_programs(0) - 1)
    def _():
        dkv_ref[0] = (acc[0] * SCALE).astype(BF16)
        dkv_ref[1] = acc[1].astype(BF16)


def self_backward(qkv, positions, length, grad):
    count, width = qkv.shape[1:]
    step = min(256, count)
    dq, dkv = pl.pallas_call(
        self_backward_kernel,
        grid=(count // step,),
        in_specs=[
            pl.BlockSpec(memory_space=pltpu.SMEM),
            pl.BlockSpec((step, 1), lambda i: (i, 0)),
            pl.BlockSpec((1, count), lambda i: (0, 0)),
            pl.BlockSpec((1, step, width), lambda i: (0, i, 0)),
            pl.BlockSpec((2, count, width), lambda i: (0, 0, 0)),
            pl.BlockSpec((step, width), lambda i: (i, 0)),
        ],
        out_specs=[
            pl.BlockSpec((step, width), lambda i: (i, 0)),
            pl.BlockSpec((2, count, width), lambda i: (0, 0, 0)),
        ],
        out_shape=[
            jax.ShapeDtypeStruct((count, width), BF16),
            jax.ShapeDtypeStruct((2, count, width), BF16),
        ],
        scratch_shapes=[pltpu.VMEM((2, count, width), F32)],
        compiler_params=pltpu.CompilerParams(vmem_limit_bytes=48 * 2**20),
        name="self_backward",
    )(length, positions[:, None], positions[None, :], qkv[0][None], qkv[1:], grad)
    return jnp.concatenate([dq[None], dkv], axis=0)


def cross_forward_kernel(limit_ref, target_ref, row_ref, q_ref, kv_ref, mix_ref, peak_ref):
    slot = pl.program_id(0)
    width = q_ref.shape[-1]
    keys = kv_ref.shape[1]
    live = lax.broadcasted_iota(jnp.int32, (1, keys), 1) < limit_ref[slot]
    valid = row_ref[...] < target_ref[slot]

    @pl.when(slot == 0)
    def _():
        peak_ref[...] = jnp.full_like(peak_ref, masked_score)

    for head in range(width // HD):
        cut = slice(head * HD, (head + 1) * HD)
        vcut = slice(width + head * HD, width + (head + 1) * HD)
        scores = dot(q_ref[0, :, cut], kv_ref[0, :, cut], NT) * SCALE
        scores = jnp.where(live, scores, masked_score)
        top = jnp.max(scores, axis=-1, keepdims=True)
        expos = jnp.exp(scores - top)
        probs = expos * (1.0 / jnp.sum(expos, axis=-1, keepdims=True))
        mix_ref[0, :, cut] = dot(probs.astype(BF16), kv_ref[0, :, vcut]).astype(BF16)
        peak = jnp.max(jnp.where(valid, top, masked_score), axis=0, keepdims=True)
        peak_ref[head : head + 1, :] = jnp.maximum(
            peak_ref[head : head + 1, :], jnp.broadcast_to(peak, (1, 128))
        )


def cross_forward(query, kv, own_positions, target_lengths, source_lengths):
    slots, rows, width = query.shape
    keys = kv.shape[1]
    return pl.pallas_call(
        cross_forward_kernel,
        grid=(slots,),
        in_specs=[
            pl.BlockSpec(memory_space=pltpu.SMEM),
            pl.BlockSpec(memory_space=pltpu.SMEM),
            pl.BlockSpec((rows, 1), lambda i: (0, 0)),
            pl.BlockSpec((1, rows, width), lambda i: (i, 0, 0)),
            pl.BlockSpec((1, keys, 2 * width), lambda i: (i, 0, 0)),
        ],
        out_specs=[
            pl.BlockSpec((1, rows, width), lambda i: (i, 0, 0)),
            pl.BlockSpec((8, 128), lambda i: (0, 0)),
        ],
        out_shape=[
            jax.ShapeDtypeStruct((slots, rows, width), BF16),
            jax.ShapeDtypeStruct((8, 128), F32),
        ],
        compiler_params=pltpu.CompilerParams(vmem_limit_bytes=48 * 2**20),
        name="cross_forward",
    )(source_lengths, target_lengths, own_positions[:, None], query, kv)


def cross_backward_kernel(limit_ref, q_ref, kv_ref, g_ref, dq_ref, dkv_ref):
    slot = pl.program_id(0)
    width = q_ref.shape[-1]
    keys = kv_ref.shape[1]
    live = lax.broadcasted_iota(jnp.int32, (1, keys), 1) < limit_ref[slot]
    for head in range(width // HD):
        cut = slice(head * HD, (head + 1) * HD)
        vcut = slice(width + head * HD, width + (head + 1) * HD)
        query, grad = q_ref[0, :, cut], g_ref[0, :, cut]
        scores = dot(query, kv_ref[0, :, cut], NT) * SCALE
        scores = jnp.where(live, scores, masked_score)
        top = jnp.max(scores, axis=-1, keepdims=True)
        expos = jnp.exp(scores - top)
        probs = expos * (1.0 / jnp.sum(expos, axis=-1, keepdims=True))
        dprobs = dot(grad, kv_ref[0, :, vcut], NT)
        delta = jnp.sum(probs * dprobs, axis=-1, keepdims=True)
        dscores = (probs * (dprobs - delta)).astype(BF16)
        dq_ref[0, :, cut] = (dot(dscores, kv_ref[0, :, cut]) * SCALE).astype(BF16)
        dkv_ref[0, :, cut] = (dot(dscores, query, TN) * SCALE).astype(BF16)
        dkv_ref[0, :, vcut] = dot(probs.astype(BF16), grad, TN).astype(BF16)


def cross_backward(query, kv, source_lengths, grad):
    slots, rows, width = query.shape
    keys = kv.shape[1]
    return pl.pallas_call(
        cross_backward_kernel,
        grid=(slots,),
        in_specs=[
            pl.BlockSpec(memory_space=pltpu.SMEM),
            pl.BlockSpec((1, rows, width), lambda i: (i, 0, 0)),
            pl.BlockSpec((1, keys, 2 * width), lambda i: (i, 0, 0)),
            pl.BlockSpec((1, rows, width), lambda i: (i, 0, 0)),
        ],
        out_specs=[
            pl.BlockSpec((1, rows, width), lambda i: (i, 0, 0)),
            pl.BlockSpec((1, keys, 2 * width), lambda i: (i, 0, 0)),
        ],
        out_shape=[
            jax.ShapeDtypeStruct((slots, rows, width), BF16),
            jax.ShapeDtypeStruct((slots, keys, 2 * width), BF16),
        ],
        compiler_params=pltpu.CompilerParams(vmem_limit_bytes=48 * 2**20),
        name="cross_backward",
    )(source_lengths, query, kv, grad)


MESH = pl.DeviceIdType.MESH


class Links:
    def __init__(self, send, recv, local):
        self.send, self.recv, self.local = send, recv, local
        self.count, self.local_count = 0, 0
        self.sends, self.saves = [], []

    def slots(self, count):
        start = self.count
        self.count += count
        return start

    def copy(self, index, src, dst, device):
        return pltpu.make_async_remote_copy(
            src_ref=src,
            dst_ref=dst,
            send_sem=self.send.at[index],
            recv_sem=self.recv.at[index],
            device_id=device,
            device_id_type=MESH,
        )

    def push(self, index, src, dst, device, when=None):
        made = self.copy(index, src, dst, device)
        if when is None:
            made.start()
        else:
            pl.when(when)(made.start)
        self.sends.append((made, when))

    def take(self, index, dst, device, when=None):
        made = self.copy(index, dst, dst, device)
        if when is None:
            made.wait_recv()
        else:
            pl.when(when)(made.wait_recv)

    def save(self, src, dst):
        made = pltpu.make_async_copy(src, dst, self.local.at[self.local_count])
        self.local_count += 1
        made.start()
        self.saves.append(made)
        return made

    def finish(self):
        for made, when in self.sends:
            if when is None:
                made.wait_send()
            else:
                pl.when(when)(made.wait_send)
        for made in self.saves:
            made.wait()
        self.sends, self.saves = [], []


class Place:
    def __init__(self):
        self.s, self.c = lax.axis_index("seq"), lax.axis_index("ctx")
        self.k, self.x = lax.rem(self.s, 2), lax.div(self.s, 2)
        self.y, self.z = lax.rem(self.c, 2), lax.div(self.c, 2)
        self.sib = self.s + 1 - 2 * self.k
        self.far = lax.rem(self.s + 2, 4)
        self.opp = lax.rem(self.sib + 2, 4)
        self.pair = self.c + 1 - 2 * self.y

    def greet(self):
        barrier = pltpu.get_barrier_semaphore()
        for other in (self.sib, self.far, self.opp):
            pl.semaphore_signal(barrier, inc=1, device_id=(other, self.c), device_id_type=MESH)
        for step in range(1, 8):
            pl.semaphore_signal(
                barrier,
                inc=1,
                device_id=(self.s, lax.rem(self.c + step, 8)),
                device_id_type=MESH,
            )
        pl.semaphore_wait(barrier, 10)


def rows_at(start, count):
    return pl.ds(pl.multiple_of(start, 16), count)


def lanes_at(start, count):
    return pl.ds(pl.multiple_of(start, 128), count)


class Columns:
    def __init__(self, links, place, weight, dest, parts, pieces=1):
        self.links, self.place, self.weight, self.dest = links, place, weight, dest
        rows, columns = weight.shape
        self.rows, self.whole, self.width = rows, columns // parts, columns // (4 * parts)
        self.step = rows // pieces
        self.jobs = [(part, piece) for piece in range(pieces) for part in range(parts)]
        self.base = {job: links.slots(5) for job in self.jobs}
        self.mine = place.k == place.y

    def source(self, job, target):
        part, piece = job
        return self.weight.at[
            pl.ds(piece * self.step, self.step),
            lanes_at(part * self.whole + target * self.width, self.width),
        ]

    def land(self, job, owner):
        part, piece = job
        return self.dest.at[
            rows_at(owner * self.rows + piece * self.step, self.step),
            pl.ds(part * self.width, self.width),
        ]

    def start(self, jobs=None):
        p = self.place
        for job in self.jobs if jobs is None else jobs:
            base = self.base[job]
            land = self.land(job, p.s)
            self.links.push(base, self.source(job, p.far), land, (p.far, p.c), self.mine)
            self.links.push(base + 1, self.source(job, p.opp), land, (p.opp, p.c), self.mine)
            self.links.push(base + 2, self.source(job, p.sib), land, (p.sib, p.c))
            self.links.save(self.source(job, p.s), land)

    def relay(self, jobs=None):
        p = self.place
        came = lax.rem(p.x + 1, 2) * 2 + p.y
        for job in self.jobs if jobs is None else jobs:
            base = self.base[job]
            land = self.land(job, came)
            self.links.take(base, land, (p.far, p.c), p.k == p.y)
            self.links.take(base + 1, land, (p.opp, p.c), p.k != p.y)
            self.links.push(base + 3, land, land, (p.s, p.pair))

    def finish(self):
        p = self.place
        for job in self.jobs:
            base = self.base[job]
            self.links.take(base + 2, self.land(job, p.sib), (p.sib, p.c))
            self.links.take(
                base + 3,
                self.land(job, lax.rem(p.x + 1, 2) * 2 + 1 - p.y),
                (p.s, p.pair),
            )


class Gather:
    def __init__(self, links, place, dest, rows, pieces=1):
        self.links, self.place, self.dest, self.rows = links, place, dest, rows
        self.step = rows // pieces
        self.base = [links.slots(3) for _ in range(pieces)]

    def land(self, piece, owner):
        return self.dest.at[rows_at(owner * self.rows + piece * self.step, self.step)]

    def start(self, piece=0):
        p, base = self.place, self.base[piece]
        land = self.land(piece, p.s)
        self.links.push(base, land, land, (p.far, p.c))
        self.links.push(base + 1, land, land, (p.sib, p.c))

    def forward(self, piece=0):
        p, base = self.place, self.base[piece]
        land = self.land(piece, p.far)
        self.links.take(base, land, (p.far, p.c))
        self.links.push(base + 2, land, land, (p.sib, p.c))

    def finish(self, piece=0):
        p, base = self.place, self.base[piece]
        self.links.take(base + 1, self.land(piece, p.sib), (p.sib, p.c))
        self.links.take(base + 2, self.land(piece, p.opp), (p.sib, p.c))

    def all(self):
        for piece in range(len(self.base)):
            self.start(piece)
        for piece in range(len(self.base)):
            self.forward(piece)
        for piece in range(len(self.base)):
            self.finish(piece)


class Reduce:
    def __init__(self, links, place, out, into, rows, pieces=1):
        self.links, self.place, self.out, self.into = links, place, out, into
        self.step = rows // pieces
        self.base = [links.slots(3) for _ in range(pieces)]

    def run(self, partial, then):
        p, links, out, into = self.place, self.links, self.out, self.into
        count, step = len(self.base), self.step
        cut = [pl.ds(piece * step, step) for piece in range(count)]
        here = (p.sib, p.c)
        for piece, base in enumerate(self.base):
            out[0, cut[piece]] = partial(p.opp, piece).astype(BF16)
            links.push(base, out.at[0, cut[piece]], into.at[0, cut[piece]], here)
        for piece, base in enumerate(self.base):
            held = partial(p.far, piece)
            links.take(base, into.at[0, cut[piece]], here)
            out[2, cut[piece]] = (held + into[0, cut[piece]].astype(F32)).astype(BF16)
            links.push(base + 1, out.at[2, cut[piece]], into.at[2, cut[piece]], (p.far, p.c))
        for piece, base in enumerate(self.base):
            out[1, cut[piece]] = partial(p.sib, piece).astype(BF16)
            links.push(base + 2, out.at[1, cut[piece]], into.at[1, cut[piece]], here)
        for piece, base in enumerate(self.base):
            held = partial(p.s, piece)
            links.take(base + 2, into.at[1, cut[piece]], here)
            held = held + into[1, cut[piece]].astype(F32)
            links.take(base + 1, into.at[2, cut[piece]], (p.far, p.c))
            then(piece, held + into[2, cut[piece]].astype(F32))


def row_positions(table_ref, owner, half):
    place = lax.broadcasted_iota(jnp.int32, (2 * half, 1), 0)
    first, second = table_ref[owner, 0] * half, table_ref[owner, 1] * half - half
    return place + jnp.where(place < half, first, second)


def column_positions(table_ref, owner, half):
    place = lax.broadcasted_iota(jnp.int32, (1, 2 * half), 1)
    first, second = table_ref[owner, 0] * half, table_ref[owner, 1] * half - half
    return place + jnp.where(place < half, first, second)


def softmax_rows(scores):
    top = jnp.max(scores, axis=-1, keepdims=True)
    expos = jnp.exp(scores - top)
    return expos * (1.0 / jnp.sum(expos, axis=-1, keepdims=True)), top


PIECES = 2
STEPS = 8


def forward_kernel(
    table_ref,
    target_ref,
    source_ref,
    tokens_ref,
    encoder_ref,
    cotangent_ref,
    qkv_ref,
    out_ref,
    cq_ref,
    ckv_ref,
    co_ref,
    up_ref,
    gain_ref,
    bias_ref,
    first_out,
    second_out,
    third_out,
    branch_out,
    source_out,
    w_qkv_out,
    w_cq_out,
    w_ckv_out,
    w_up_out,
    heads_out,
    mix_out,
    query_out,
    kvs_out,
    cross_out_ref,
    sums_out,
    peak_out,
    lens_out,
    first,
    second,
    third,
    branch,
    source,
    w_qkv,
    w_cq,
    w_ckv,
    sent,
    heads,
    mix_own,
    mix,
    query,
    kv_own,
    kvs,
    cross,
    sums,
    columns,
    lens,
    rs_out,
    rs_in,
    send_sem,
    recv_sem,
    local_sem,
):
    place, links = Place(), Links(send_sem, recv_sem, local_sem)
    p = place
    rows = tokens_ref.shape[1]
    source_rows = encoder_ref.shape[1]
    half = rows // 2
    width = w_cq.shape[1]
    pair_width = heads.shape[2]
    held = width // HD
    groups = width // pair_width
    place.greet()

    get_qkv = Columns(links, place, qkv_ref, w_qkv, 3)
    get_qkv.start()

    own = rows_at(p.s * rows, rows)
    inputs = tokens_ref[0].astype(F32)
    first[own] = norm_forward(inputs, gain_ref[0:1], bias_ref[0:1])[2]
    get_first = Gather(links, place, first, rows)
    get_first.start()
    source[rows_at(p.s * source_rows, source_rows)] = encoder_ref[0]
    get_source = Gather(links, place, source, source_rows)
    get_source.start()
    place_lens = links.slots(3)
    line = lax.broadcasted_iota(jnp.int32, (8, 128), 0)
    lens[pl.ds(p.s, 1)] = jnp.where(line < 4, target_ref[0], source_ref[0])[None]
    own_lens = lens.at[pl.ds(p.s, 1)]
    for step, other in enumerate((p.far, p.opp, p.sib)):
        links.push(place_lens + step, own_lens, own_lens, (other, p.c))
    for owner in range(STEPS):
        columns[:, owner * rows : (owner + 1) * rows] = column_positions(table_ref, owner, half)
    own_rows = row_positions(table_ref, p.c, half)
    valid = own_rows < target_ref[0]
    branch[own] = jnp.where(valid, cotangent_ref[0].astype(F32), 0.0).astype(BF16)
    get_cq = Columns(links, place, cq_ref, w_cq, 1)
    get_ckv = Columns(links, place, ckv_ref, w_ckv, 2)
    get_up = Columns(links, place, up_ref, w_up_out, 1, 4)

    get_qkv.relay()
    get_first.forward()
    get_source.forward()
    get_first.finish()
    get_source.finish()
    for made in links.saves:
        made.wait()
    links.saves = []
    get_qkv.finish()
    links.save(first, first_out)
    links.save(w_qkv, w_qkv_out)
    links.save(source, source_out)
    for step, other in enumerate((p.far, p.opp, p.sib)):
        links.take(place_lens + step, lens.at[pl.ds(other, 1)], (other, p.c))
    links.save(lens, lens_out)

    def project(block, carry):
        value = dot(first[rows_at(block * rows, rows)], w_qkv[...]).astype(BF16)
        for group in range(groups):
            for part in range(3):
                at = part * width + group * pair_width
                sent[block * groups + group, part] = value[:, at : at + pair_width]
        return carry

    lax.fori_loop(0, 4, project, 0)
    a2a = links.slots(STEPS)
    mine = rows_at(p.c * rows, rows)
    for step in range(1, STEPS):
        other = lax.rem(p.c + step, STEPS)
        links.push(a2a + step, sent.at[other], heads.at[:, mine], (p.s, other))
    keep = pltpu.make_async_copy(sent.at[p.c], heads.at[:, mine], local_sem.at[STEPS * 8 - 1])
    keep.start()
    get_cq.start()
    get_ckv.start()
    get_up.start(get_up.jobs[:2])
    get_branch = Gather(links, place, branch, rows)
    get_branch.start()
    keep.wait()
    get_cq.relay()
    get_ckv.relay()
    for step in range(1, STEPS):
        other = lax.rem(p.c + STEPS - step, STEPS)
        links.take(a2a + step, heads.at[:, rows_at(other * rows, rows)], (p.s, other))
    links.save(heads, heads_out)

    my_slot = lax.div(p.c, groups)
    my_group = lax.rem(p.c, groups)
    length = lens[pl.ds(my_slot, 1)][0, 0:1, 0:1]
    back = links.slots(STEPS)
    slot_rows = rows_at(my_slot * rows, rows)
    group_lanes = lanes_at(my_group * pair_width, pair_width)

    def back_copy(owner):
        return links.copy(
            back + p.c, mix_own.at[rows_at(owner * rows, rows)], mix.at[slot_rows, group_lanes], (p.s, owner)
        )

    def attend(block, peaks):
        at = rows_at(block * 2 * rows, 2 * rows)
        row_pos = jnp.concatenate(
            [row_positions(table_ref, 2 * block, half), row_positions(table_ref, 2 * block + 1, half)], axis=0
        )
        col_pos = columns[...]
        allowed = (col_pos <= row_pos) & (col_pos < length)
        ok = row_pos < length
        tops = []
        for head in range(pair_width // HD):
            cut = slice(head * HD, (head + 1) * HD)
            scores = dot(heads[0, at, cut], heads[1, :, cut], NT) * SCALE
            probs, top = softmax_rows(jnp.where(allowed, scores, masked_score))
            mix_own[at, cut] = dot(probs.astype(BF16), heads[2, :, cut]).astype(BF16)
            peak = jnp.max(jnp.where(ok, top, masked_score), axis=0, keepdims=True)
            tops.append(jnp.maximum(peaks[head], peak))
        return tuple(tops)

    low = jnp.full((1, 1), masked_score, F32)
    peaks = (low, low)
    for block in range(STEPS // 2):
        peaks = attend(block, peaks)
        for owner in (2 * block, 2 * block + 1):
            pl.when(p.c != owner)(back_copy(owner).start)
    for head in range(2):
        peak_out[head : head + 1] = jnp.broadcast_to(peaks[head], (1, 128))
    mix[slot_rows, group_lanes] = mix_own[mine]

    get_cq.finish()
    get_ckv.finish()
    for made in links.saves:
        made.wait()
    links.saves = []
    links.save(w_cq, w_cq_out)
    links.save(w_ckv, w_ckv_out)
    value = dot(source[...], w_ckv[...]).astype(BF16)
    for slot in range(4):
        kv_own[slot] = value[slot * source_rows : (slot + 1) * source_rows]
    own_keys = rows_at(p.c * source_rows, source_rows)
    kvs[:, own_keys] = kv_own[...]
    along, across = links.slots(4), links.slots(4)
    links.push(across, kv_own, kvs.at[:, own_keys], (p.s, p.pair))
    for step in range(1, 4):
        other = lax.rem(p.z + step, 4) * 2 + p.y
        links.push(along + step, kv_own, kvs.at[:, own_keys], (p.s, other))
    get_up.relay(get_up.jobs[:2])
    get_branch.forward()

    for owner in range(STEPS):

        @pl.when(p.c != owner)
        def _():
            lane = lanes_at((owner % groups) * pair_width, pair_width)
            links.take(
                back + owner, mix.at[pl.ds((owner // groups) * rows, rows), lane], (p.s, owner)
            )

    links.save(mix, mix_out)

    def boundary(index, left, weight, base, gather, store):
        def partial(block, piece):
            step = rows // PIECES
            return dot(left[rows_at(block * rows + piece * step, step)], weight[...])

        def then(piece, total):
            step = rows // PIECES
            cut = pl.ds(piece * step, step)
            value = base(piece) + total
            sums[index, cut] = value
            store[rows_at(p.s * rows + piece * step, step)] = norm_forward(
                value, gain_ref[index + 1 : index + 2], bias_ref[index + 1 : index + 2]
            )[2]
            gather.start(piece)

        Reduce(links, place, rs_out.at[index], rs_in.at[index], rows, PIECES).run(partial, then)

    step = rows // PIECES
    get_second = Gather(links, place, second, rows, PIECES)
    boundary(
        0,
        mix,
        out_ref,
        lambda piece: tokens_ref[0, piece * step : (piece + 1) * step].astype(F32),
        get_second,
        second,
    )
    for hop in range(1, 4):
        other = lax.rem(p.z + 4 - hop, 4) * 2 + p.y
        land = kvs.at[:, rows_at(other * source_rows, source_rows)]
        links.take(along + hop, land, (p.s, other))
        links.push(across + hop, land, land, (p.s, p.pair))
    get_up.start(get_up.jobs[2:])
    for piece in range(PIECES):
        get_second.forward(piece)
    for piece in range(PIECES):
        get_second.finish(piece)
    links.save(second, second_out)
    for hop in range(4):
        other = lax.rem(p.z + 4 - hop, 4) * 2 + 1 - p.y
        land = kvs.at[:, rows_at(other * source_rows, source_rows)]
        links.take(across + hop, land, (p.s, p.pair))
    links.save(kvs, kvs_out)

    keys = kvs.shape[1]

    def cross_attend(slot, peaks):
        at = rows_at(slot * rows, rows)
        asked = dot(second[at], w_cq[...]).astype(BF16)
        query[at] = asked
        limits = lens[pl.ds(slot, 1)]
        live = lax.broadcasted_iota(jnp.int32, (1, keys), 1) < limits[0, 4:5, 0:1]
        ok = own_rows < limits[0, 0:1, 0:1]
        tops = []
        for head in range(held):
            cut = slice(head * HD, (head + 1) * HD)
            vcut = slice(width + head * HD, width + (head + 1) * HD)
            scores = dot(asked[:, cut], kvs[slot, :, cut], NT) * SCALE
            probs, top = softmax_rows(jnp.where(live, scores, masked_score))
            cross[at, cut] = dot(probs.astype(BF16), kvs[slot, :, vcut]).astype(BF16)
            peak = jnp.max(jnp.where(ok, top, masked_score), axis=0, keepdims=True)
            tops.append(jnp.maximum(peaks[head], peak))
        return tuple(tops)

    peaks = lax.fori_loop(0, 4, cross_attend, (low,) * held)
    for head in range(held):
        peak_out[2 + head : 3 + head] = jnp.broadcast_to(peaks[head], (1, 128))
    links.save(query, query_out)
    links.save(cross, cross_out_ref)
    get_up.relay(get_up.jobs[2:])
    get_branch.finish()
    links.save(branch, branch_out)
    get_third = Gather(links, place, third, rows, PIECES)
    boundary(
        1, cross, co_ref, lambda piece: sums[0, piece * step : (piece + 1) * step], get_third, third
    )
    links.save(sums, sums_out)
    for piece in range(PIECES):
        get_third.forward(piece)
    for piece in range(PIECES):
        get_third.finish(piece)
    links.save(third, third_out)
    get_up.finish()
    for owner in range(STEPS):
        pl.when(p.c != owner)(back_copy(owner).wait_send)
    links.finish()


def forward_call(
    table, targets, sources, tokens, encoder, cotangent, qkv, out, cq, ckv, co, up, gain, bias
):
    rows, width = tokens.shape[1], out.shape[0]
    source_rows = encoder.shape[1]
    depth = tokens.shape[2]
    keys = 8 * source_rows
    any_space = pl.BlockSpec(memory_space=pl.ANY)
    vmem = pl.BlockSpec(memory_space=pltpu.VMEM)
    smem = pl.BlockSpec(memory_space=pltpu.SMEM)
    shapes = dict(
        first=((4 * rows, depth), BF16),
        second=((4 * rows, depth), BF16),
        third=((4 * rows, depth), BF16),
        branch=((4 * rows, depth), BF16),
        source=((4 * source_rows, depth), BF16),
        w_qkv=((depth, 3 * width), BF16),
        w_cq=((depth, width), BF16),
        w_ckv=((depth, 2 * width), BF16),
        w_up=((depth, up.shape[1] // 4), BF16),
        heads=((3, 8 * rows, 128), BF16),
        mix=((4 * rows, width), BF16),
        query=((4 * rows, width), BF16),
        kvs=((4, keys, 2 * width), BF16),
        cross=((4 * rows, width), BF16),
        sums=((2, rows, depth), F32),
        peak=((8, 128), F32),
        lens=((4, 8, 128), jnp.int32),
    )
    scratch = [
        shapes[name]
        for name in ("first", "second", "third", "branch", "source", "w_qkv", "w_cq", "w_ckv")
    ] + [
        ((8, 3, rows, 128), BF16),
        shapes["heads"],
        ((8 * rows, 128), BF16),
        shapes["mix"],
        shapes["query"],
        ((4, source_rows, 2 * width), BF16),
        shapes["kvs"],
        shapes["cross"],
        shapes["sums"],
        ((1, 8 * rows), jnp.int32),
        shapes["lens"],
        ((2, 3, rows, depth), BF16),
        ((2, 3, rows, depth), BF16),
    ]
    made = pl.pallas_call(
        forward_kernel,
        in_specs=[smem] * 3
        + [vmem] * 3
        + [any_space, vmem, any_space, any_space, vmem, any_space]
        + [vmem] * 2,
        out_specs=[vmem if name == "peak" else any_space for name in shapes],
        out_shape=[jax.ShapeDtypeStruct(*shape) for shape in shapes.values()],
        scratch_shapes=[pltpu.VMEM(*shape) for shape in scratch]
        + [
            pltpu.SemaphoreType.DMA((128,)),
            pltpu.SemaphoreType.DMA((128,)),
            pltpu.SemaphoreType.DMA((64,)),
        ],
        compiler_params=pltpu.CompilerParams(
            collective_id=0, has_side_effects=True, vmem_limit_bytes=48 * 2**20
        ),
        name="forward",
    )(table, targets, sources, tokens, encoder, cotangent, qkv, out, cq, ckv, co, up, gain, bias)
    return dict(zip(shapes, made))


def gather_seq(rows):
    return lax.all_gather(rows, "seq", axis=0, tiled=True)


def scatter_seq(partial):
    return lax.psum_scatter(
        partial.astype(BF16), "seq", scatter_dimension=0, tiled=True
    ).astype(F32)


def swap(blocks, axis):
    return lax.all_to_all(blocks, axis, split_axis=0, concat_axis=0, tiled=True)


def columns_of(weight, parts):
    seq_count = lax.axis_size("seq")
    rows, columns = weight.shape
    width = columns // (parts * seq_count)
    blocks = weight.reshape(rows, parts, seq_count, width).transpose(2, 0, 1, 3)
    return swap(blocks.reshape(seq_count, rows, parts * width), "seq").reshape(
        seq_count * rows, parts * width
    )


def finish_rows(grad):
    return lax.psum_scatter(grad.astype(BF16), "ctx", scatter_dimension=0, tiled=True).astype(F32)


def finish_columns(grad, parts):
    seq_count, ctx_count = lax.axis_size("seq"), lax.axis_size("ctx")
    rows, columns = grad.shape
    share = rows // (seq_count * ctx_count)
    blocks = grad.astype(BF16).reshape(seq_count, ctx_count, share, columns).transpose(1, 0, 2, 3)
    own = lax.psum_scatter(
        blocks.reshape(ctx_count * seq_count * share, columns),
        "ctx",
        scatter_dimension=0,
        tiled=True,
    ).reshape(seq_count, share, columns)
    taken = swap(own, "seq").reshape(seq_count, share, parts, columns // parts)
    return taken.transpose(1, 2, 0, 3).reshape(share, seq_count * columns).astype(F32)


def fast_device(
    tokens,
    encoder_states,
    cotangent,
    target_lengths,
    source_lengths,
    block_table,
    self_qkv,
    self_out,
    cross_q,
    cross_kv,
    cross_out,
    mlp_up,
    mlp_down,
    norm_gain,
    norm_bias,
    clip_limit,
):
    rows = tokens.shape[1]
    source_rows = encoder_states.shape[1]
    seq_count, ctx_count = lax.axis_size("seq"), lax.axis_size("ctx")
    seq_index, ctx_index = lax.axis_index("seq"), lax.axis_index("ctx")
    held, pair = H // seq_count, H // ctx_count
    groups = held // pair
    own_width, pair_width = held * HD, pair * HD
    width = H * HD
    half = rows // 2
    all_positions = (
        block_table[:, :, None] * half + jnp.arange(half, dtype=jnp.int32)[None, None, :]
    ).reshape(-1)
    own_positions = lax.dynamic_slice_in_dim(all_positions, ctx_index * rows, rows, 0)
    valid_rows = (own_positions < target_lengths[0])[:, None]
    my_slot = ctx_index // groups

    inputs = tokens[0].astype(F32)
    hat_one, inverse_one, _ = norm_forward(inputs, norm_gain[0], norm_bias[0])
    grad_rows = jnp.where(valid_rows, cotangent[0].astype(F32), 0.0)

    def to_heads(blocks, parts):
        blocks = blocks.reshape(seq_count, rows, parts, groups, pair_width)
        blocks = blocks.transpose(0, 3, 2, 1, 4).reshape(ctx_count, parts * rows, pair_width)
        taken = swap(blocks, "ctx").reshape(ctx_count, parts, rows, pair_width)
        return taken.transpose(1, 0, 2, 3).reshape(parts, ctx_count * rows, pair_width)

    def to_rows(heads):
        parts = heads.shape[0]
        blocks = heads.reshape(parts, ctx_count, rows, pair_width).transpose(1, 0, 2, 3)
        taken = swap(blocks.reshape(ctx_count, parts * rows, pair_width), "ctx")
        taken = taken.reshape(seq_count, groups, parts, rows, pair_width).transpose(0, 3, 2, 1, 4)
        return taken.reshape(seq_count * rows, parts * own_width)

    kept = forward_call(
        block_table,
        target_lengths,
        source_lengths,
        tokens,
        encoder_states,
        cotangent,
        self_qkv,
        self_out,
        cross_q,
        cross_kv,
        cross_out,
        mlp_up,
        norm_gain,
        norm_bias,
    )
    first_low, second_low, third_low = kept["first"], kept["second"], kept["third"]
    mlp_branch, source_low = kept["branch"], kept["source"]
    w_qkv, w_cq, w_ckv, w_up = kept["w_qkv"], kept["w_cq"], kept["w_ckv"], kept["w_up"]
    qkv, self_low, cross_kvs, cross_low = kept["heads"], kept["mix"], kept["kvs"], kept["cross"]
    cross_query = kept["query"].reshape(seq_count, rows, own_width)
    first_sum, second_sum = kept["sums"][0], kept["sums"][1]
    self_peak, cross_peak = kept["peak"], kept["peak"][2:]
    targets, sources = kept["lens"][:, 0, 0], kept["lens"][:, 4, 0]
    my_length = lax.dynamic_slice_in_dim(targets, my_slot, 1, 0)
    hat_two, inverse_two, _ = norm_forward(first_sum, norm_gain[1], norm_bias[1])
    hat_three, inverse_three, _ = norm_forward(second_sum, norm_gain[2], norm_bias[2])

    hidden_pre = dot(third_low, w_up)
    hidden_act, gelu_back = jax.vjp(jax.nn.gelu, hidden_pre)
    hidden_low = hidden_act.astype(BF16)
    third_sum = second_sum + scatter_seq(dot(hidden_low, mlp_down))
    output_rows = jnp.where(valid_rows, third_sum, 0.0).astype(BF16)

    peak_self = lax.dynamic_update_slice_in_dim(
        jnp.full((H,), masked_score, F32),
        self_peak[:pair, 0],
        seq_index * held + (ctx_index % groups) * pair,
        0,
    )
    peak_cross = lax.dynamic_update_slice_in_dim(
        jnp.full((H,), masked_score, F32), cross_peak[:held, 0], seq_index * held, 0
    )
    peaks = lax.pmax(jnp.stack([peak_self, peak_cross]), ("seq", "ctx"))

    grad_down = dot(hidden_low, mlp_branch, TN)
    grad_pre = gelu_back(dot(mlp_branch, mlp_down, NT))[0].astype(BF16)
    grad_up = dot(third_low, grad_pre, TN)
    back_three, gain_three, bias_three = norm_backward(
        scatter_seq(dot(grad_pre, w_up, NT)), hat_three, inverse_three, norm_gain[2]
    )
    up_shard, down_shard = finish_columns(grad_up, 1), finish_rows(grad_down)

    grad_second = grad_rows + back_three
    cross_branch = gather_seq(grad_second.astype(BF16))
    grad_co = dot(cross_low, cross_branch, TN)
    cross_grad = dot(cross_branch, cross_out, NT).astype(BF16)
    dquery, dkv = cross_backward(
        cross_query, cross_kvs, sources, cross_grad.reshape(seq_count, rows, own_width)
    )
    dquery = dquery.reshape(seq_count * rows, own_width)
    dkv = (
        dkv.reshape(seq_count, ctx_count, source_rows, 2 * own_width)
        .transpose(1, 0, 2, 3)
        .reshape(ctx_count * seq_count * source_rows, 2 * own_width)
    )
    grad_source_kv = lax.psum_scatter(dkv, "ctx", scatter_dimension=0, tiled=True)
    grad_cq = dot(second_low, dquery, TN)
    grad_ckv = dot(source_low, grad_source_kv, TN)
    grad_source = scatter_seq(dot(grad_source_kv, w_ckv, NT))
    back_two, gain_two, bias_two = norm_backward(
        scatter_seq(dot(dquery, w_cq, NT)), hat_two, inverse_two, norm_gain[1]
    )
    grad_first = grad_second + back_two
    self_branch = gather_seq(grad_first.astype(BF16))
    grad_so = dot(self_low, self_branch, TN)
    self_grad = to_heads(dot(self_branch, self_out, NT).astype(BF16), 1)[0]
    grad_projected = to_rows(self_backward(qkv, all_positions, my_length, self_grad))
    grad_qkv = dot(first_low, grad_projected, TN)
    back_one, gain_one, bias_one = norm_backward(
        scatter_seq(dot(grad_projected, w_qkv, NT)), hat_one, inverse_one, norm_gain[0]
    )
    grad_inputs = grad_first + back_one

    norm_terms = jnp.stack([gain_one, gain_two, gain_three, bias_one, bias_two, bias_three])
    norm_sum = lax.psum(norm_terms, ("seq", "ctx"))
    norm_share = width // (seq_count * ctx_count)
    norm_shard = lax.dynamic_slice_in_dim(
        norm_sum, (seq_index * ctx_count + ctx_index) * norm_share, norm_share, 1
    )

    factors = jnp.sqrt(clip_limit / jnp.maximum(peaks, clip_limit))
    columns = jnp.repeat(factors, HD, axis=1)
    qkv_wide = self_qkv.astype(F32)
    clipped_self = jnp.concatenate(
        [qkv_wide[:, :width] * columns[0], qkv_wide[:, width : 2 * width] * columns[0]], axis=1
    ).astype(BF16)
    clipped_cross = jnp.concatenate(
        [cross_q.astype(F32) * columns[1], cross_kv[:, :width].astype(F32) * columns[1]], axis=1
    ).astype(BF16)
    return (
        output_rows[None],
        grad_inputs[None],
        grad_source[None],
        finish_columns(grad_qkv, 3),
        finish_rows(grad_so),
        finish_columns(grad_cq, 1),
        finish_columns(grad_ckv, 2),
        finish_rows(grad_co),
        up_shard,
        down_shard,
        norm_shard[:3],
        norm_shard[3:],
        clipped_self,
        clipped_cross,
        peaks,
    )


def solution(mesh):
    body = fast_device if fast_fits(mesh) else general_device
    return jax.shard_map(
        body,
        mesh=mesh,
        in_specs=(
            P("seq", "ctx", None),
            P("seq", "ctx", None),
            P("seq", "ctx", None),
            P("seq"),
            P("seq"),
            P(),
            P("seq", None),
            P("seq", None),
            P("seq", None),
            P("seq", None),
            P("seq", None),
            P("seq", None),
            P("seq", None),
            P(),
            P(),
            P(),
        ),
        out_specs=(
            P("seq", "ctx", None),
            P("seq", "ctx", None),
            P("seq", "ctx", None),
            P(("seq", "ctx"), None),
            P(("seq", "ctx"), None),
            P(("seq", "ctx"), None),
            P(("seq", "ctx"), None),
            P(("seq", "ctx"), None),
            P(("seq", "ctx"), None),
            P(("seq", "ctx"), None),
            P(None, ("seq", "ctx")),
            P(None, ("seq", "ctx")),
            P("seq", None),
            P("seq", None),
            P(),
        ),
        check_vma=False,
    )
```

```python
import functools

import jax
import jax.numpy as jnp
from jax import lax
from jax.experimental import pallas as pl
from jax.experimental.pallas import tpu as pltpu
from jax.sharding import PartitionSpec as P

H = 16
HD = 64


masked_score = -1000000000.0
norm_eps = 1e-05


def block_size(count):
    return max((step for step in range(1, min(count, 512) + 1) if count % step == 0))


def layer_norm(values, gain, bias):
    centered = values - jnp.mean(values, axis=-1, keepdims=True)
    spread = jnp.mean(centered * centered, axis=-1, keepdims=True)
    return centered * lax.rsqrt(spread + norm_eps) * gain + bias


def allowed_pairs(query_pos, key_pos, key_limit, causal):
    allowed = jnp.broadcast_to(
        (key_pos < key_limit)[None, :], (query_pos.shape[0], key_pos.shape[0])
    )
    if causal:
        allowed = allowed & (key_pos[None, :] <= query_pos[:, None])
    return allowed


def head_scores(query_heads, key_rows):
    key_heads = key_rows.reshape(key_rows.shape[0], H, HD)
    return jnp.einsum(
        "qhd,khd->hqk", query_heads, key_heads, preferred_element_type=jnp.float32
    ) * HD ** (-0.5)


def softmax_stats(query_heads, kv_rows, key_pos, query_pos, query_ok, key_limit, causal):
    count = kv_rows.shape[0]
    step = block_size(count)
    width = H * HD
    rows = query_heads.shape[0]

    def softmax_visit(carry, block):
        top, total, peak = carry
        block_rows, block_pos = block
        allowed = allowed_pairs(query_pos, block_pos, key_limit, causal)
        scores = jnp.where(
            allowed[None], head_scores(query_heads, block_rows[:, :width]), masked_score
        )
        new_top = jnp.maximum(top, jnp.max(scores, axis=-1))
        total = total * jnp.exp(top - new_top) + jnp.sum(
            jnp.exp(scores - new_top[..., None]), axis=-1
        )
        counted = jnp.where((allowed & query_ok[:, None])[None], scores, masked_score)
        peak = jnp.maximum(peak, jnp.max(counted, axis=(1, 2)))
        return ((new_top, total, peak), None)

    start = (
        jnp.full((H, rows), -jnp.inf, jnp.float32),
        jnp.zeros((H, rows), jnp.float32),
        jnp.full((H,), masked_score, jnp.float32),
    )
    blocks = (kv_rows.reshape(count // step, step, 2 * width), key_pos.reshape(count // step, step))
    return lax.scan(softmax_visit, start, blocks)[0]


def attend_values(query_heads, kv_rows, key_pos, query_pos, key_limit, causal, top, total):
    count = kv_rows.shape[0]
    step = block_size(count)
    width = H * HD
    rows = query_heads.shape[0]

    def attend_visit(acc, block):
        block_rows, block_pos = block
        allowed = allowed_pairs(query_pos, block_pos, key_limit, causal)
        scores = jnp.where(
            allowed[None], head_scores(query_heads, block_rows[:, :width]), masked_score
        )
        weights = (jnp.exp(scores - top[..., None]) / total[..., None]).astype(jnp.bfloat16)
        value_heads = block_rows[:, width:].reshape(step, H, HD)
        return (
            acc
            + jnp.einsum("hqk,khd->qhd", weights, value_heads, preferred_element_type=jnp.float32),
            None,
        )

    blocks = (kv_rows.reshape(count // step, step, 2 * width), key_pos.reshape(count // step, step))
    acc = lax.scan(attend_visit, jnp.zeros((rows, H, HD), jnp.float32), blocks)[0]
    return acc.reshape(rows, width)


def query_grads(
    query_heads, kv_rows, key_pos, query_pos, key_limit, causal, top, total, grad_heads, delta
):
    count = kv_rows.shape[0]
    step = block_size(count)
    width = H * HD
    rows = query_heads.shape[0]

    def query_visit(acc, block):
        block_rows, block_pos = block
        allowed = allowed_pairs(query_pos, block_pos, key_limit, causal)
        scores = jnp.where(
            allowed[None], head_scores(query_heads, block_rows[:, :width]), masked_score
        )
        probs = jnp.exp(scores - top[..., None]) / total[..., None]
        value_heads = block_rows[:, width:].reshape(step, H, HD)
        dprobs = jnp.einsum(
            "qhd,khd->hqk", grad_heads, value_heads, preferred_element_type=jnp.float32
        )
        dscores = (probs * (dprobs - delta[..., None])).astype(jnp.bfloat16)
        key_heads = block_rows[:, :width].reshape(step, H, HD)
        return (
            acc
            + jnp.einsum("hqk,khd->qhd", dscores, key_heads, preferred_element_type=jnp.float32),
            None,
        )

    blocks = (kv_rows.reshape(count // step, step, 2 * width), key_pos.reshape(count // step, step))
    acc = lax.scan(query_visit, jnp.zeros((rows, H, HD), jnp.float32), blocks)[0]
    return acc.reshape(rows, width) * HD ** (-0.5)


def key_grads(
    query_heads,
    kv_rows,
    key_pos,
    query_pos,
    key_limit,
    causal,
    top,
    total,
    grad_heads,
    delta,
    start,
    count,
):
    step = block_size(count)
    width = H * HD

    def piece(index):
        offset = start + index * step
        block_rows = lax.dynamic_slice_in_dim(kv_rows, offset, step, 0)
        block_pos = lax.dynamic_slice_in_dim(key_pos, offset, step, 0)
        allowed = allowed_pairs(query_pos, block_pos, key_limit, causal)
        scores = jnp.where(
            allowed[None], head_scores(query_heads, block_rows[:, :width]), masked_score
        )
        probs = jnp.exp(scores - top[..., None]) / total[..., None]
        value_heads = block_rows[:, width:].reshape(step, H, HD)
        dprobs = jnp.einsum(
            "qhd,khd->hqk", grad_heads, value_heads, preferred_element_type=jnp.float32
        )
        dscores = (probs * (dprobs - delta[..., None])).astype(jnp.bfloat16)
        dkeys = jnp.einsum(
            "hqk,qhd->khd", dscores, query_heads, preferred_element_type=jnp.float32
        ).reshape(step, width) * HD ** (-0.5)
        dvalues = jnp.einsum(
            "hqk,qhd->khd",
            probs.astype(jnp.bfloat16),
            grad_heads,
            preferred_element_type=jnp.float32,
        ).reshape(step, width)
        return jnp.concatenate([dkeys, dvalues], axis=1)

    return lax.map(piece, jnp.arange(count // step, dtype=jnp.int32)).reshape(count, 2 * width)


def split_rows(grad, seq_count, ctx_count):
    return grad.reshape(
        (seq_count, ctx_count, grad.shape[0] // (seq_count * ctx_count)) + grad.shape[1:]
    )


def join_rows(grad):
    return grad.reshape((grad.shape[2],) + grad.shape[3:])


def general_device(
    tokens,
    encoder_states,
    cotangent,
    target_lengths,
    source_lengths,
    block_table,
    self_qkv,
    self_out,
    cross_q,
    cross_kv,
    cross_out,
    mlp_up,
    mlp_down,
    norm_gain,
    norm_bias,
    clip_limit,
):
    rows = tokens.shape[1]
    width = H * HD
    half = rows // 2
    source_rows = encoder_states.shape[1]
    seq_count = lax.axis_size("seq")
    ctx_count = lax.axis_size("ctx")
    all_positions = (
        block_table[:, :, None] * half + jnp.arange(half, dtype=jnp.int32)[None, None, :]
    ).reshape(-1)
    own_positions = lax.dynamic_slice_in_dim(all_positions, lax.axis_index("ctx") * rows, rows, 0)
    length = target_lengths[0]
    source_length = source_lengths[0]
    query_ok = own_positions < length
    valid_rows = query_ok[:, None]
    source_positions = jnp.arange(source_rows * ctx_count, dtype=jnp.int32)
    w_qkv, w_out, w_cq, w_ckv, w_co = (
        lax.all_gather(self_qkv, "seq", axis=0, tiled=True),
        lax.all_gather(self_out, "seq", axis=0, tiled=True),
        lax.all_gather(cross_q, "seq", axis=0, tiled=True),
        lax.all_gather(cross_kv, "seq", axis=0, tiled=True),
        lax.all_gather(cross_out, "seq", axis=0, tiled=True),
    )
    inputs = tokens[0].astype(jnp.float32)
    first_norm, first_back = jax.vjp(layer_norm, inputs, norm_gain[0], norm_bias[0])
    first_low = first_norm.astype(jnp.bfloat16)
    projected = jnp.dot(first_low, w_qkv, preferred_element_type=jnp.float32).astype(jnp.bfloat16)
    self_query = projected[:, :width].reshape(rows, H, HD)
    source_kv = jnp.dot(encoder_states[0], w_ckv, preferred_element_type=jnp.float32).astype(
        jnp.bfloat16
    )
    self_kv, cross_kvs = (
        lax.all_gather(projected[:, width:], "ctx", axis=0, tiled=True),
        lax.all_gather(source_kv, "ctx", axis=0, tiled=True),
    )
    self_top, self_total, self_peak = softmax_stats(
        self_query, self_kv, all_positions, own_positions, query_ok, length, True
    )
    self_mix = attend_values(
        self_query, self_kv, all_positions, own_positions, length, True, self_top, self_total
    )
    self_low = self_mix.astype(jnp.bfloat16)
    first_sum = inputs + jnp.dot(self_low, w_out, preferred_element_type=jnp.float32)
    second_norm, second_back = jax.vjp(layer_norm, first_sum, norm_gain[1], norm_bias[1])
    second_low = second_norm.astype(jnp.bfloat16)
    cross_rows = jnp.dot(second_low, w_cq, preferred_element_type=jnp.float32).astype(jnp.bfloat16)
    cross_query = cross_rows.reshape(rows, H, HD)
    cross_top, cross_total, cross_peak = softmax_stats(
        cross_query, cross_kvs, source_positions, own_positions, query_ok, source_length, False
    )
    cross_mix = attend_values(
        cross_query,
        cross_kvs,
        source_positions,
        own_positions,
        source_length,
        False,
        cross_top,
        cross_total,
    )
    cross_low = cross_mix.astype(jnp.bfloat16)
    second_sum = first_sum + jnp.dot(cross_low, w_co, preferred_element_type=jnp.float32)
    third_norm, third_back = jax.vjp(layer_norm, second_sum, norm_gain[2], norm_bias[2])
    third_low = third_norm.astype(jnp.bfloat16)
    w_up, w_down = (
        lax.all_gather(mlp_up, "seq", axis=0, tiled=True),
        lax.all_gather(mlp_down, "seq", axis=0, tiled=True),
    )
    hidden_pre = jnp.dot(third_low, w_up, preferred_element_type=jnp.float32)
    hidden_act, gelu_back = jax.vjp(jax.nn.gelu, hidden_pre)
    hidden_low = hidden_act.astype(jnp.bfloat16)
    third_sum = second_sum + jnp.dot(hidden_low, w_down, preferred_element_type=jnp.float32)
    output_rows = jnp.where(valid_rows, third_sum, 0.0).astype(jnp.bfloat16)
    peaks = lax.pmax(jnp.stack([self_peak, cross_peak]), ("seq", "ctx"))
    grad_rows = jnp.where(valid_rows, cotangent[0].astype(jnp.float32), 0.0)
    mlp_branch = grad_rows.astype(jnp.bfloat16)
    grad_down = jnp.einsum("rf,rd->fd", hidden_low, mlp_branch, preferred_element_type=jnp.float32)
    grad_act = jnp.einsum("rd,fd->rf", mlp_branch, w_down, preferred_element_type=jnp.float32)
    grad_pre = gelu_back(grad_act)[0].astype(jnp.bfloat16)
    grad_up = jnp.einsum("rd,rf->df", third_low, grad_pre, preferred_element_type=jnp.float32)
    back_third, gain_three, bias_three = third_back(
        jnp.einsum("rf,df->rd", grad_pre, w_up, preferred_element_type=jnp.float32)
    )
    up_part, down_part = (
        lax.psum_scatter(
            split_rows(grad_up, seq_count, ctx_count).astype(jnp.bfloat16),
            "ctx",
            scatter_dimension=1,
            tiled=True,
        ).astype(jnp.float32),
        lax.psum_scatter(
            split_rows(grad_down, seq_count, ctx_count).astype(jnp.bfloat16),
            "ctx",
            scatter_dimension=1,
            tiled=True,
        ).astype(jnp.float32),
    )
    up_shard, down_shard = (
        lax.psum_scatter(
            up_part.astype(jnp.bfloat16), "seq", scatter_dimension=0, tiled=True
        ).astype(jnp.float32),
        lax.psum_scatter(
            down_part.astype(jnp.bfloat16), "seq", scatter_dimension=0, tiled=True
        ).astype(jnp.float32),
    )
    grad_second = grad_rows + back_third
    cross_branch = grad_second.astype(jnp.bfloat16)
    grad_co = jnp.einsum("rd,re->de", cross_low, cross_branch, preferred_element_type=jnp.float32)
    cross_heads_grad = (
        jnp.einsum("re,de->rd", cross_branch, w_co, preferred_element_type=jnp.float32)
        .astype(jnp.bfloat16)
        .reshape(rows, H, HD)
    )
    cross_delta = jnp.einsum(
        "qhd,qhd->hq", cross_heads_grad.astype(jnp.float32), cross_mix.reshape(rows, H, HD)
    )
    grad_cross_rows = query_grads(
        cross_query,
        cross_kvs,
        source_positions,
        own_positions,
        source_length,
        False,
        cross_top,
        cross_total,
        cross_heads_grad,
        cross_delta,
    ).astype(jnp.bfloat16)
    grad_source_kv = lax.psum_scatter(
        key_grads(
            cross_query,
            cross_kvs,
            source_positions,
            own_positions,
            source_length,
            False,
            cross_top,
            cross_total,
            cross_heads_grad,
            cross_delta,
            jnp.int32(0),
            source_rows * lax.axis_size("ctx"),
        ).astype(jnp.bfloat16),
        "ctx",
        scatter_dimension=0,
        tiled=True,
    )
    grad_cq = jnp.einsum(
        "rd,re->de", second_low, grad_cross_rows, preferred_element_type=jnp.float32
    )
    grad_ckv = jnp.einsum(
        "sd,se->de", encoder_states[0], grad_source_kv, preferred_element_type=jnp.float32
    )
    grad_source = jnp.einsum("se,de->sd", grad_source_kv, w_ckv, preferred_element_type=jnp.float32)
    back_second, gain_two, bias_two = second_back(
        jnp.einsum("re,de->rd", grad_cross_rows, w_cq, preferred_element_type=jnp.float32)
    )
    grad_first = grad_second + back_second
    self_branch = grad_first.astype(jnp.bfloat16)
    grad_so = jnp.einsum("rd,re->de", self_low, self_branch, preferred_element_type=jnp.float32)
    self_heads_grad = (
        jnp.einsum("re,de->rd", self_branch, w_out, preferred_element_type=jnp.float32)
        .astype(jnp.bfloat16)
        .reshape(rows, H, HD)
    )
    self_delta = jnp.einsum(
        "qhd,qhd->hq", self_heads_grad.astype(jnp.float32), self_mix.reshape(rows, H, HD)
    )
    grad_query = query_grads(
        self_query,
        self_kv,
        all_positions,
        own_positions,
        length,
        True,
        self_top,
        self_total,
        self_heads_grad,
        self_delta,
    ).astype(jnp.bfloat16)
    grad_kv = lax.psum_scatter(
        key_grads(
            self_query,
            self_kv,
            all_positions,
            own_positions,
            length,
            True,
            self_top,
            self_total,
            self_heads_grad,
            self_delta,
            jnp.int32(0),
            rows * lax.axis_size("ctx"),
        ).astype(jnp.bfloat16),
        "ctx",
        scatter_dimension=0,
        tiled=True,
    )
    grad_projected = jnp.concatenate([grad_query, grad_kv], axis=1)
    grad_qkv = jnp.einsum(
        "rd,re->de", first_low, grad_projected, preferred_element_type=jnp.float32
    )
    back_first, gain_one, bias_one = first_back(
        jnp.einsum("re,de->rd", grad_projected, w_qkv, preferred_element_type=jnp.float32)
    )
    grad_inputs = grad_first + back_first
    norm_terms = jnp.stack([gain_one, gain_two, gain_three, bias_one, bias_two, bias_three], axis=1)
    qkv_part, out_part, cq_part, ckv_part, co_part, norm_part = (
        lax.psum_scatter(
            split_rows(grad_qkv, seq_count, ctx_count).astype(jnp.bfloat16),
            "ctx",
            scatter_dimension=1,
            tiled=True,
        ).astype(jnp.float32),
        lax.psum_scatter(
            split_rows(grad_so, seq_count, ctx_count).astype(jnp.bfloat16),
            "ctx",
            scatter_dimension=1,
            tiled=True,
        ).astype(jnp.float32),
        lax.psum_scatter(
            split_rows(grad_cq, seq_count, ctx_count).astype(jnp.bfloat16),
            "ctx",
            scatter_dimension=1,
            tiled=True,
        ).astype(jnp.float32),
        lax.psum_scatter(
            split_rows(grad_ckv, seq_count, ctx_count).astype(jnp.bfloat16),
            "ctx",
            scatter_dimension=1,
            tiled=True,
        ).astype(jnp.float32),
        lax.psum_scatter(
            split_rows(grad_co, seq_count, ctx_count).astype(jnp.bfloat16),
            "ctx",
            scatter_dimension=1,
            tiled=True,
        ).astype(jnp.float32),
        lax.psum_scatter(
            split_rows(norm_terms, seq_count, ctx_count).astype(jnp.bfloat16),
            "ctx",
            scatter_dimension=1,
            tiled=True,
        ).astype(jnp.float32),
    )
    qkv_shard, out_shard, cq_shard, ckv_shard, co_shard, norm_shard = (
        lax.psum_scatter(
            qkv_part.astype(jnp.bfloat16), "seq", scatter_dimension=0, tiled=True
        ).astype(jnp.float32),
        lax.psum_scatter(
            out_part.astype(jnp.bfloat16), "seq", scatter_dimension=0, tiled=True
        ).astype(jnp.float32),
        lax.psum_scatter(
            cq_part.astype(jnp.bfloat16), "seq", scatter_dimension=0, tiled=True
        ).astype(jnp.float32),
        lax.psum_scatter(
            ckv_part.astype(jnp.bfloat16), "seq", scatter_dimension=0, tiled=True
        ).astype(jnp.float32),
        lax.psum_scatter(
            co_part.astype(jnp.bfloat16), "seq", scatter_dimension=0, tiled=True
        ).astype(jnp.float32),
        lax.psum_scatter(
            norm_part.astype(jnp.bfloat16), "seq", scatter_dimension=0, tiled=True
        ).astype(jnp.float32),
    )
    norm_shard = join_rows(norm_shard)
    factors = jnp.sqrt(clip_limit / jnp.maximum(peaks, clip_limit))
    columns = jnp.repeat(factors, HD, axis=1)
    qkv_wide = self_qkv.astype(jnp.float32)
    clipped_self = jnp.concatenate(
        [qkv_wide[:, :width] * columns[0], qkv_wide[:, width : 2 * width] * columns[0]], axis=1
    ).astype(jnp.bfloat16)
    clipped_cross = jnp.concatenate(
        [
            cross_q.astype(jnp.float32) * columns[1],
            cross_kv[:, :width].astype(jnp.float32) * columns[1],
        ],
        axis=1,
    ).astype(jnp.bfloat16)
    return (
        output_rows[None],
        grad_inputs[None],
        grad_source[None],
        join_rows(qkv_shard),
        join_rows(out_shard),
        join_rows(cq_shard),
        join_rows(ckv_shard),
        join_rows(co_shard),
        join_rows(up_shard),
        join_rows(down_shard),
        norm_shard[:, :3].T,
        norm_shard[:, 3:].T,
        clipped_self,
        clipped_cross,
        peaks,
    )


F32 = jnp.float32
BF16 = jnp.bfloat16
SCALE = HD**-0.5


def fast_fits(mesh):
    seq_count, ctx_count = mesh.shape["seq"], mesh.shape["ctx"]
    if H % seq_count or H % ctx_count:
        return False
    held, pair = H // seq_count, H // ctx_count
    return held % pair == 0 and seq_count * (held // pair) == ctx_count and pair * HD == 128


def dot(left, right, contract=((1,), (0,))):
    return lax.dot_general(left, right, (contract, ((), ())), preferred_element_type=F32)


NT = ((1,), (1,))
TN = ((0,), (0,))


def norm_forward(values, gain, bias):
    centered = values - jnp.mean(values, axis=-1, keepdims=True)
    spread = jnp.mean(centered * centered, axis=-1, keepdims=True)
    inverse = lax.rsqrt(spread + norm_eps)
    hat = centered * inverse
    return hat, inverse, (hat * gain + bias).astype(BF16)


def norm_backward(grad, hat, inverse, gain):
    scaled = grad * gain
    inner = jnp.mean(scaled, axis=-1, keepdims=True)
    outer = jnp.mean(scaled * hat, axis=-1, keepdims=True)
    return (
        (scaled - inner - hat * outer) * inverse,
        jnp.sum(grad * hat, axis=0),
        jnp.sum(grad, axis=0),
    )


MESH = pl.DeviceIdType.MESH


class Links:
    def __init__(self, send, recv, local):
        self.send, self.recv, self.local = send, recv, local
        self.count, self.local_count = 0, 0
        self.sends, self.saves = [], []

    def slots(self, count):
        start = self.count
        self.count += count
        return start

    def copy(self, index, src, dst, device):
        return pltpu.make_async_remote_copy(
            src_ref=src,
            dst_ref=dst,
            send_sem=self.send.at[index],
            recv_sem=self.recv.at[index],
            device_id=device,
            device_id_type=MESH,
        )

    def push(self, index, src, dst, device, when=None):
        made = self.copy(index, src, dst, device)
        if when is None:
            made.start()
        else:
            pl.when(when)(made.start)
        self.sends.append((made, when))

    def take(self, index, dst, device, when=None):
        made = self.copy(index, dst, dst, device)
        if when is None:
            made.wait_recv()
        else:
            pl.when(when)(made.wait_recv)

    def save(self, src, dst):
        made = pltpu.make_async_copy(src, dst, self.local.at[self.local_count])
        self.local_count += 1
        made.start()
        self.saves.append(made)
        return made

    def finish(self):
        for made, when in self.sends:
            if when is None:
                made.wait_send()
            else:
                pl.when(when)(made.wait_send)
        for made in self.saves:
            made.wait()
        self.sends, self.saves = [], []


class Place:
    def __init__(self):
        self.s, self.c = lax.axis_index("seq"), lax.axis_index("ctx")
        self.k, self.x = lax.rem(self.s, 2), lax.div(self.s, 2)
        self.y, self.z = lax.rem(self.c, 2), lax.div(self.c, 2)
        self.sib = self.s + 1 - 2 * self.k
        self.far = lax.rem(self.s + 2, 4)
        self.opp = lax.rem(self.sib + 2, 4)
        self.pair = self.c + 1 - 2 * self.y

    def greet(self):
        barrier = pltpu.get_barrier_semaphore()
        for other in (self.sib, self.far, self.opp):
            pl.semaphore_signal(barrier, inc=1, device_id=(other, self.c), device_id_type=MESH)
        for step in range(1, 8):
            pl.semaphore_signal(
                barrier,
                inc=1,
                device_id=(self.s, lax.rem(self.c + step, 8)),
                device_id_type=MESH,
            )
        pl.semaphore_wait(barrier, 10)


def rows_at(start, count):
    return pl.ds(pl.multiple_of(start, 16), count)


def lanes_at(start, count):
    return pl.ds(pl.multiple_of(start, 128), count)


class Columns:
    def __init__(self, links, place, weight, dest, parts, pieces=1):
        self.links, self.place, self.weight, self.dest = links, place, weight, dest
        rows, columns = weight.shape
        self.rows, self.whole, self.width = rows, columns // parts, columns // (4 * parts)
        self.step = rows // pieces
        self.jobs = [(part, piece) for piece in range(pieces) for part in range(parts)]
        self.base = {job: links.slots(5) for job in self.jobs}
        self.mine = place.k == place.y

    def source(self, job, target):
        part, piece = job
        return self.weight.at[
            pl.ds(piece * self.step, self.step),
            lanes_at(part * self.whole + target * self.width, self.width),
        ]

    def land(self, job, owner):
        part, piece = job
        return self.dest.at[
            rows_at(owner * self.rows + piece * self.step, self.step),
            pl.ds(part * self.width, self.width),
        ]

    def start(self, jobs=None):
        p = self.place
        for job in self.jobs if jobs is None else jobs:
            base = self.base[job]
            land = self.land(job, p.s)
            self.links.push(base, self.source(job, p.far), land, (p.far, p.c), self.mine)
            self.links.push(base + 1, self.source(job, p.opp), land, (p.opp, p.c), self.mine)
            self.links.push(base + 2, self.source(job, p.sib), land, (p.sib, p.c))
            self.links.save(self.source(job, p.s), land)

    def relay(self, jobs=None):
        p = self.place
        came = lax.rem(p.x + 1, 2) * 2 + p.y
        for job in self.jobs if jobs is None else jobs:
            base = self.base[job]
            land = self.land(job, came)
            self.links.take(base, land, (p.far, p.c), p.k == p.y)
            self.links.take(base + 1, land, (p.opp, p.c), p.k != p.y)
            self.links.push(base + 3, land, land, (p.s, p.pair))

    def finish(self):
        p = self.place
        for job in self.jobs:
            base = self.base[job]
            self.links.take(base + 2, self.land(job, p.sib), (p.sib, p.c))
            self.links.take(
                base + 3,
                self.land(job, lax.rem(p.x + 1, 2) * 2 + 1 - p.y),
                (p.s, p.pair),
            )


class Gather:
    def __init__(self, links, place, dest, rows, pieces=1):
        self.links, self.place, self.dest, self.rows = links, place, dest, rows
        self.step = rows // pieces
        self.base = [links.slots(3) for _ in range(pieces)]

    def land(self, piece, owner):
        return self.dest.at[rows_at(owner * self.rows + piece * self.step, self.step)]

    def start(self, piece=0):
        p, base = self.place, self.base[piece]
        land = self.land(piece, p.s)
        self.links.push(base, land, land, (p.far, p.c))
        self.links.push(base + 1, land, land, (p.sib, p.c))

    def forward(self, piece=0):
        p, base = self.place, self.base[piece]
        land = self.land(piece, p.far)
        self.links.take(base, land, (p.far, p.c))
        self.links.push(base + 2, land, land, (p.sib, p.c))

    def finish(self, piece=0):
        p, base = self.place, self.base[piece]
        self.links.take(base + 1, self.land(piece, p.sib), (p.sib, p.c))
        self.links.take(base + 2, self.land(piece, p.opp), (p.sib, p.c))

    def all(self):
        for piece in range(len(self.base)):
            self.start(piece)
        for piece in range(len(self.base)):
            self.forward(piece)
        for piece in range(len(self.base)):
            self.finish(piece)


class Reduce:
    def __init__(self, links, place, out, into, rows, pieces=1):
        self.links, self.place, self.out, self.into = links, place, out, into
        self.step = rows // pieces
        self.base = [links.slots(3) for _ in range(pieces)]

    def run(self, partial, then):
        p, links, out, into = self.place, self.links, self.out, self.into
        count, step = len(self.base), self.step
        cut = [pl.ds(piece * step, step) for piece in range(count)]
        here = (p.sib, p.c)
        for piece, base in enumerate(self.base):
            out[0, cut[piece]] = partial(p.opp, piece).astype(BF16)
            links.push(base, out.at[0, cut[piece]], into.at[0, cut[piece]], here)
        for piece, base in enumerate(self.base):
            held = partial(p.far, piece)
            links.take(base, into.at[0, cut[piece]], here)
            out[2, cut[piece]] = (held + into[0, cut[piece]].astype(F32)).astype(BF16)
            links.push(base + 1, out.at[2, cut[piece]], into.at[2, cut[piece]], (p.far, p.c))
        for piece, base in enumerate(self.base):
            out[1, cut[piece]] = partial(p.sib, piece).astype(BF16)
            links.push(base + 2, out.at[1, cut[piece]], into.at[1, cut[piece]], here)
        for piece, base in enumerate(self.base):
            held = partial(p.s, piece)
            links.take(base + 2, into.at[1, cut[piece]], here)
            held = held + into[1, cut[piece]].astype(F32)
            links.take(base + 1, into.at[2, cut[piece]], (p.far, p.c))
            then(piece, held + into[2, cut[piece]].astype(F32))


def row_positions(table_ref, owner, half):
    place = lax.broadcasted_iota(jnp.int32, (2 * half, 1), 0)
    first, second = table_ref[owner, 0] * half, table_ref[owner, 1] * half - half
    return place + jnp.where(place < half, first, second)


def column_positions(table_ref, owner, half):
    place = lax.broadcasted_iota(jnp.int32, (1, 2 * half), 1)
    first, second = table_ref[owner, 0] * half, table_ref[owner, 1] * half - half
    return place + jnp.where(place < half, first, second)


def softmax_rows(scores):
    top = jnp.max(scores, axis=-1, keepdims=True)
    expos = jnp.exp(scores - top)
    return expos * (1.0 / jnp.sum(expos, axis=-1, keepdims=True)), top


PIECES = 2
STEPS = 8


def forward_kernel(
    table_ref,
    target_ref,
    source_ref,
    tokens_ref,
    encoder_ref,
    cotangent_ref,
    qkv_ref,
    out_ref,
    cq_ref,
    ckv_ref,
    co_ref,
    up_ref,
    gain_ref,
    bias_ref,
    first_out,
    second_out,
    third_out,
    branch_out,
    source_out,
    w_qkv_out,
    w_cq_out,
    w_ckv_out,
    w_up_out,
    heads_out,
    mix_out,
    query_out,
    kvs_out,
    cross_out_ref,
    sums_out,
    peak_out,
    lens_out,
    first,
    second,
    third,
    branch,
    source,
    w_qkv,
    w_cq,
    w_ckv,
    sent,
    heads,
    mix_own,
    mix,
    query,
    kv_own,
    kvs,
    cross,
    sums,
    columns,
    lens,
    rs_out,
    rs_in,
    send_sem,
    recv_sem,
    local_sem,
):
    place, links = Place(), Links(send_sem, recv_sem, local_sem)
    p = place
    rows = tokens_ref.shape[1]
    source_rows = encoder_ref.shape[1]
    half = rows // 2
    width = w_cq.shape[1]
    pair_width = heads.shape[2]
    held = width // HD
    groups = width // pair_width
    place.greet()

    get_qkv = Columns(links, place, qkv_ref, w_qkv, 3)
    get_qkv.start()

    own = rows_at(p.s * rows, rows)
    inputs = tokens_ref[0].astype(F32)
    first[own] = norm_forward(inputs, gain_ref[0:1], bias_ref[0:1])[2]
    get_first = Gather(links, place, first, rows)
    get_first.start()
    source[rows_at(p.s * source_rows, source_rows)] = encoder_ref[0]
    get_source = Gather(links, place, source, source_rows)
    get_source.start()
    place_lens = links.slots(3)
    line = lax.broadcasted_iota(jnp.int32, (8, 128), 0)
    lens[pl.ds(p.s, 1)] = jnp.where(line < 4, target_ref[0], source_ref[0])[None]
    own_lens = lens.at[pl.ds(p.s, 1)]
    for step, other in enumerate((p.far, p.opp, p.sib)):
        links.push(place_lens + step, own_lens, own_lens, (other, p.c))
    for owner in range(STEPS):
        columns[:, owner * rows : (owner + 1) * rows] = column_positions(table_ref, owner, half)
    own_rows = row_positions(table_ref, p.c, half)
    valid = own_rows < target_ref[0]
    branch[own] = jnp.where(valid, cotangent_ref[0].astype(F32), 0.0).astype(BF16)
    get_cq = Columns(links, place, cq_ref, w_cq, 1)
    get_ckv = Columns(links, place, ckv_ref, w_ckv, 2)
    get_up = Columns(links, place, up_ref, w_up_out, 1, 4)

    get_qkv.relay()
    get_first.forward()
    get_source.forward()
    get_first.finish()
    get_source.finish()
    for made in links.saves:
        made.wait()
    links.saves = []
    get_qkv.finish()
    links.save(first, first_out)
    links.save(w_qkv, w_qkv_out)
    links.save(source, source_out)
    for step, other in enumerate((p.far, p.opp, p.sib)):
        links.take(place_lens + step, lens.at[pl.ds(other, 1)], (other, p.c))
    links.save(lens, lens_out)

    def project(block, carry):
        value = dot(first[rows_at(block * rows, rows)], w_qkv[...]).astype(BF16)
        for group in range(groups):
            for part in range(3):
                at = part * width + group * pair_width
                sent[block * groups + group, part] = value[:, at : at + pair_width]
        return carry

    lax.fori_loop(0, 4, project, 0)
    a2a = links.slots(STEPS)
    mine = rows_at(p.c * rows, rows)
    for step in range(1, STEPS):
        other = lax.rem(p.c + step, STEPS)
        links.push(a2a + step, sent.at[other], heads.at[:, mine], (p.s, other))
    keep = pltpu.make_async_copy(sent.at[p.c], heads.at[:, mine], local_sem.at[STEPS * 8 - 1])
    keep.start()
    get_cq.start()
    get_ckv.start()
    get_up.start(get_up.jobs[:2])
    get_branch = Gather(links, place, branch, rows)
    get_branch.start()
    keep.wait()
    get_cq.relay()
    get_ckv.relay()
    for step in range(1, STEPS):
        other = lax.rem(p.c + STEPS - step, STEPS)
        links.take(a2a + step, heads.at[:, rows_at(other * rows, rows)], (p.s, other))
    links.save(heads, heads_out)

    my_slot = lax.div(p.c, groups)
    my_group = lax.rem(p.c, groups)
    length = lens[pl.ds(my_slot, 1)][0, 0:1, 0:1]
    back = links.slots(STEPS)
    slot_rows = rows_at(my_slot * rows, rows)
    group_lanes = lanes_at(my_group * pair_width, pair_width)

    def back_copy(owner):
        return links.copy(
            back + p.c, mix_own.at[rows_at(owner * rows, rows)], mix.at[slot_rows, group_lanes], (p.s, owner)
        )

    def attend(block, peaks):
        at = rows_at(block * 2 * rows, 2 * rows)
        row_pos = jnp.concatenate(
            [row_positions(table_ref, 2 * block, half), row_positions(table_ref, 2 * block + 1, half)], axis=0
        )
        col_pos = columns[...]
        allowed = (col_pos <= row_pos) & (col_pos < length)
        ok = row_pos < length
        tops = []
        for head in range(pair_width // HD):
            cut = slice(head * HD, (head + 1) * HD)
            scores = dot(heads[0, at, cut], heads[1, :, cut], NT) * SCALE
            probs, top = softmax_rows(jnp.where(allowed, scores, masked_score))
            mix_own[at, cut] = dot(probs.astype(BF16), heads[2, :, cut]).astype(BF16)
            peak = jnp.max(jnp.where(ok, top, masked_score), axis=0, keepdims=True)
            tops.append(jnp.maximum(peaks[head], peak))
        return tuple(tops)

    low = jnp.full((1, 1), masked_score, F32)
    peaks = (low, low)
    for block in range(STEPS // 2):
        peaks = attend(block, peaks)
        for owner in (2 * block, 2 * block + 1):
            pl.when(p.c != owner)(back_copy(owner).start)
    for head in range(2):
        peak_out[head : head + 1] = jnp.broadcast_to(peaks[head], (1, 128))
    mix[slot_rows, group_lanes] = mix_own[mine]

    get_cq.finish()
    get_ckv.finish()
    for made in links.saves:
        made.wait()
    links.saves = []
    links.save(w_cq, w_cq_out)
    links.save(w_ckv, w_ckv_out)
    value = dot(source[...], w_ckv[...]).astype(BF16)
    for slot in range(4):
        kv_own[slot] = value[slot * source_rows : (slot + 1) * source_rows]
    own_keys = rows_at(p.c * source_rows, source_rows)
    kvs[:, own_keys] = kv_own[...]
    along, across = links.slots(4), links.slots(4)
    links.push(across, kv_own, kvs.at[:, own_keys], (p.s, p.pair))
    for step in range(1, 4):
        other = lax.rem(p.z + step, 4) * 2 + p.y
        links.push(along + step, kv_own, kvs.at[:, own_keys], (p.s, other))
    get_up.relay(get_up.jobs[:2])
    get_branch.forward()

    for owner in range(STEPS):

        @pl.when(p.c != owner)
        def _():
            lane = lanes_at((owner % groups) * pair_width, pair_width)
            links.take(
                back + owner, mix.at[pl.ds((owner // groups) * rows, rows), lane], (p.s, owner)
            )

    links.save(mix, mix_out)

    def boundary(index, left, weight, base, gather, store):
        def partial(block, piece):
            step = rows // PIECES
            return dot(left[rows_at(block * rows + piece * step, step)], weight[...])

        def then(piece, total):
            step = rows // PIECES
            cut = pl.ds(piece * step, step)
            value = base(piece) + total
            sums[index, cut] = value
            store[rows_at(p.s * rows + piece * step, step)] = norm_forward(
                value, gain_ref[index + 1 : index + 2], bias_ref[index + 1 : index + 2]
            )[2]
            gather.start(piece)

        Reduce(links, place, rs_out.at[index], rs_in.at[index], rows, PIECES).run(partial, then)

    step = rows // PIECES
    get_second = Gather(links, place, second, rows, PIECES)
    boundary(
        0,
        mix,
        out_ref,
        lambda piece: tokens_ref[0, piece * step : (piece + 1) * step].astype(F32),
        get_second,
        second,
    )
    for hop in range(1, 4):
        other = lax.rem(p.z + 4 - hop, 4) * 2 + p.y
        land = kvs.at[:, rows_at(other * source_rows, source_rows)]
        links.take(along + hop, land, (p.s, other))
        links.push(across + hop, land, land, (p.s, p.pair))
    get_up.start(get_up.jobs[2:])
    for piece in range(PIECES):
        get_second.forward(piece)
    for piece in range(PIECES):
        get_second.finish(piece)
    links.save(second, second_out)
    for hop in range(4):
        other = lax.rem(p.z + 4 - hop, 4) * 2 + 1 - p.y
        land = kvs.at[:, rows_at(other * source_rows, source_rows)]
        links.take(across + hop, land, (p.s, p.pair))
    links.save(kvs, kvs_out)

    keys = kvs.shape[1]

    def cross_attend(slot, peaks):
        at = rows_at(slot * rows, rows)
        asked = dot(second[at], w_cq[...]).astype(BF16)
        query[at] = asked
        limits = lens[pl.ds(slot, 1)]
        live = lax.broadcasted_iota(jnp.int32, (1, keys), 1) < limits[0, 4:5, 0:1]
        ok = own_rows < limits[0, 0:1, 0:1]
        tops = []
        for head in range(held):
            cut = slice(head * HD, (head + 1) * HD)
            vcut = slice(width + head * HD, width + (head + 1) * HD)
            scores = dot(asked[:, cut], kvs[slot, :, cut], NT) * SCALE
            probs, top = softmax_rows(jnp.where(live, scores, masked_score))
            cross[at, cut] = dot(probs.astype(BF16), kvs[slot, :, vcut]).astype(BF16)
            peak = jnp.max(jnp.where(ok, top, masked_score), axis=0, keepdims=True)
            tops.append(jnp.maximum(peaks[head], peak))
        return tuple(tops)

    peaks = lax.fori_loop(0, 4, cross_attend, (low,) * held)
    for head in range(held):
        peak_out[2 + head : 3 + head] = jnp.broadcast_to(peaks[head], (1, 128))
    links.save(query, query_out)
    links.save(cross, cross_out_ref)
    get_up.relay(get_up.jobs[2:])
    get_branch.finish()
    links.save(branch, branch_out)
    get_third = Gather(links, place, third, rows, PIECES)
    boundary(
        1, cross, co_ref, lambda piece: sums[0, piece * step : (piece + 1) * step], get_third, third
    )
    links.save(sums, sums_out)
    for piece in range(PIECES):
        get_third.forward(piece)
    for piece in range(PIECES):
        get_third.finish(piece)
    links.save(third, third_out)
    get_up.finish()
    for owner in range(STEPS):
        pl.when(p.c != owner)(back_copy(owner).wait_send)
    links.finish()


def forward_call(
    table, targets, sources, tokens, encoder, cotangent, qkv, out, cq, ckv, co, up, gain, bias
):
    rows, width = tokens.shape[1], out.shape[0]
    source_rows = encoder.shape[1]
    depth = tokens.shape[2]
    keys = 8 * source_rows
    any_space = pl.BlockSpec(memory_space=pl.ANY)
    vmem = pl.BlockSpec(memory_space=pltpu.VMEM)
    smem = pl.BlockSpec(memory_space=pltpu.SMEM)
    shapes = dict(
        first=((4 * rows, depth), BF16),
        second=((4 * rows, depth), BF16),
        third=((4 * rows, depth), BF16),
        branch=((4 * rows, depth), BF16),
        source=((4 * source_rows, depth), BF16),
        w_qkv=((depth, 3 * width), BF16),
        w_cq=((depth, width), BF16),
        w_ckv=((depth, 2 * width), BF16),
        w_up=((depth, up.shape[1] // 4), BF16),
        heads=((3, 8 * rows, 128), BF16),
        mix=((4 * rows, width), BF16),
        query=((4 * rows, width), BF16),
        kvs=((4, keys, 2 * width), BF16),
        cross=((4 * rows, width), BF16),
        sums=((2, rows, depth), F32),
        peak=((8, 128), F32),
        lens=((4, 8, 128), jnp.int32),
    )
    scratch = [
        shapes[name]
        for name in ("first", "second", "third", "branch", "source", "w_qkv", "w_cq", "w_ckv")
    ] + [
        ((8, 3, rows, 128), BF16),
        shapes["heads"],
        ((8 * rows, 128), BF16),
        shapes["mix"],
        shapes["query"],
        ((4, source_rows, 2 * width), BF16),
        shapes["kvs"],
        shapes["cross"],
        shapes["sums"],
        ((1, 8 * rows), jnp.int32),
        shapes["lens"],
        ((2, 3, rows, depth), BF16),
        ((2, 3, rows, depth), BF16),
    ]
    made = pl.pallas_call(
        forward_kernel,
        in_specs=[smem] * 3
        + [vmem] * 3
        + [any_space, vmem, any_space, any_space, vmem, any_space]
        + [vmem] * 2,
        out_specs=[vmem if name == "peak" else any_space for name in shapes],
        out_shape=[jax.ShapeDtypeStruct(*shape) for shape in shapes.values()],
        scratch_shapes=[pltpu.VMEM(*shape) for shape in scratch]
        + [
            pltpu.SemaphoreType.DMA((128,)),
            pltpu.SemaphoreType.DMA((128,)),
            pltpu.SemaphoreType.DMA((64,)),
        ],
        compiler_params=pltpu.CompilerParams(
            collective_id=0, has_side_effects=True, vmem_limit_bytes=48 * 2**20
        ),
        name="forward",
    )(table, targets, sources, tokens, encoder, cotangent, qkv, out, cq, ckv, co, up, gain, bias)
    return dict(zip(shapes, made))


class Sum:
    def __init__(self, links, place, full, into, away, result, lead=False, own=None):
        self.links, self.place, self.full, self.own = links, place, full, own
        self.into, self.away, self.result, self.lead = into, away, result, lead
        self.base = links.slots(7)

    def target(self, turn):
        return lax.rem(self.place.z + 1 + turn, 4)

    def start(self, turns=(0, 1, 2, 3)):
        p = self.place
        for turn in turns:
            to = self.target(turn)
            src = self.full.at[to, 1 - p.y] if self.lead else self.full.at[:, to, 1 - p.y]
            self.links.push(self.base + turn, src, self.into.at[to], (p.s, p.pair))

    def turn(self, turns=(0, 1, 2, 3)):
        p, links, into = self.place, self.links, self.into
        for turn in turns:
            to = self.target(turn)
            links.take(self.base + turn, into.at[to], (p.s, p.pair))

            def add(a, carry):
                if self.own is not None:
                    mine = self.own[to, a] if self.lead else self.own[a, to]
                else:
                    mine = self.full[to, p.y, a] if self.lead else self.full[a, to, p.y]
                into[to, a] = (mine.astype(F32) + into[to, a].astype(F32)).astype(BF16)
                return carry

            lax.fori_loop(0, into.shape[1], add, 0)
            if turn < 3:
                links.push(
                    self.base + 4 + turn, into.at[to], self.away.at[turn], (p.s, to * 2 + p.y)
                )

    def finish(self):
        p, links, into, away = self.place, self.links, self.into, self.away
        for turn in range(3):
            came = lax.rem(p.z + 3 - turn, 4) * 2 + p.y
            links.take(self.base + 4 + turn, away.at[turn], (p.s, came))

        def add(a, carry):
            total = into[p.z, a].astype(F32) + away[0, a].astype(F32)
            total = total + (away[1, a].astype(F32) + away[2, a].astype(F32))
            self.result[a] = total.astype(BF16)
            return carry

        lax.fori_loop(0, into.shape[1], add, 0)


class Exchange:
    def __init__(self, links, place, result, taken):
        self.links, self.place, self.result, self.taken = links, place, result, taken
        self.base = links.slots(3)
        self.others = (place.far, place.opp, place.sib)

    def start(self):
        p = self.place
        for step, other in enumerate(self.others):
            self.links.push(
                self.base + step,
                self.result.at[pl.ds(other, 1)],
                self.taken.at[pl.ds(p.s, 1)],
                (other, p.c),
            )
        self.taken[pl.ds(p.s, 1)] = self.result[pl.ds(p.s, 1)]

    def finish(self):
        for step, other in enumerate(self.others):
            self.links.take(
                self.base + step, self.taken.at[pl.ds(other, 1)], (other, self.place.c)
            )


def norm_terms_of(values):
    centered = values - jnp.mean(values, axis=-1, keepdims=True)
    spread = jnp.mean(centered * centered, axis=-1, keepdims=True)
    inverse = lax.rsqrt(spread + norm_eps)
    return centered * inverse, inverse


def backward_body(r):
    place, links = Place(), Links(r.send_sem, r.recv_sem, r.local_sem)
    p = place
    rows = r.tokens.shape[1]
    half = rows // 2
    width = r.w_cq.shape[1]
    source_rows = r.source.shape[0] // 4
    keys = r.kvs.shape[1]
    pair_width = r.heads.shape[2]
    held, groups = width // HD, width // pair_width
    depth = r.first.shape[1]
    step = rows // PIECES
    share = depth // 4

    loads = {}
    for name in r.loaded:
        loads[name] = pltpu.make_async_copy(
            getattr(r, name + "_hbm"), getattr(r, name), r.load_sem.at[len(loads)]
        )
        loads[name].start()

    def need(*wanted):
        for name in wanted:
            loads.pop(name).wait()

    place.greet()
    down = Sum(links, place, r.down_full, r.down_into, r.down_away, r.down_result, True, r.down_own)
    up = Sum(links, place, r.up_full, r.up_into, r.up_away, r.up_result, False, r.up_own)
    own_down = links.save(r.down_full.at[:, p.y], r.down_own)
    own_up = links.save(r.up_full.at[:, :, p.y], r.up_own)
    links.saves = []
    for turn in (0, 1):
        up.start((turn,))
        down.start((turn,))

    r.peaks_ctx[pl.ds(p.c, 1)] = r.peak[...][None]
    peak_base = links.slots(STEPS)
    own_peak = r.peaks_ctx.at[pl.ds(p.c, 1)]
    for hop in range(1, STEPS):
        links.push(peak_base + hop, own_peak, own_peak, (p.s, lax.rem(p.c + hop, STEPS)))

    own_rows = row_positions(r.table, p.c, half)
    r.norms[...] = jnp.zeros_like(r.norms)

    def add_norms(index, gain, bias):
        r.norms[index : index + 1] += gain[None]
        r.norms[index + 3 : index + 4] += bias[None]

    get_cross = Gather(links, place, r.cross_branch, rows, PIECES)

    def after_third(piece, total):
        cut = slice(piece * step, (piece + 1) * step)
        hat, inverse = norm_terms_of(r.sums[1, cut])
        back, gain, bias = norm_backward(total, hat, inverse, r.gain[2:3])
        add_norms(2, gain, bias)
        valid = own_rows[cut] < r.target[0]
        value = jnp.where(valid, r.cotangent[0, cut].astype(F32), 0.0) + back
        r.grad_sum[cut] = value
        r.cross_branch[rows_at(p.s * rows + piece * step, step)] = value.astype(BF16)
        get_cross.start(piece)

    def stored(ref):
        return lambda block, piece: ref[rows_at(block * rows + piece * step, step)].astype(F32)

    need("sums")
    Reduce(links, place, r.rs_out.at[0], r.rs_in.at[0], rows, PIECES).run(
        stored(r.grad_third), after_third
    )
    for hop in range(1, STEPS):
        other = lax.rem(p.c + STEPS - hop, STEPS)
        links.take(peak_base + hop, r.peaks_ctx.at[pl.ds(other, 1)], (p.s, other))
    best = []
    for group in range(groups):
        tile = r.peaks_ctx[group]
        for owner in range(group + groups, STEPS, groups):
            tile = jnp.maximum(tile, r.peaks_ctx[owner])
        best.append(tile)
    everyone = best[0]
    for tile in best[1:]:
        everyone = jnp.maximum(everyone, tile)
    mine = jnp.concatenate([tile[0:2] for tile in best] + [everyone[2 : 2 + held]], axis=0)
    r.peaks_seq[pl.ds(p.s, 1)] = mine[None]
    peak_seq = links.slots(3)
    own_peak = r.peaks_seq.at[pl.ds(p.s, 1)]
    for hop, other in enumerate((p.far, p.opp, p.sib)):
        links.push(peak_seq + hop, own_peak, own_peak, (other, p.c))

    for piece in range(PIECES):
        get_cross.forward(piece)
    need("w_co", "cross", "query", "kvs", "w_cq", "second")
    for piece in range(PIECES):
        get_cross.finish(piece)

    def cross_back(slot, carry):
        at = rows_at(slot * rows, rows)
        grad_rows = dot(r.cross_branch[at], r.w_co[...], NT).astype(BF16)
        live = lax.broadcasted_iota(jnp.int32, (1, keys), 1) < r.lens[pl.ds(slot, 1)][0, 4:5, 0:1]
        for head in range(held):
            cut = slice(head * HD, (head + 1) * HD)
            vcut = slice(width + head * HD, width + (head + 1) * HD)
            asked, grad = r.query[at, cut], grad_rows[:, cut]
            scores = dot(asked, r.kvs[slot, :, cut], NT) * SCALE
            probs, _ = softmax_rows(jnp.where(live, scores, masked_score))
            dprobs = dot(grad, r.kvs[slot, :, vcut], NT)
            delta = jnp.sum(probs * dprobs, axis=-1, keepdims=True)
            dscores = (probs * (dprobs - delta)).astype(BF16)
            r.dquery[at, cut] = (dot(dscores, r.kvs[slot, :, cut]) * SCALE).astype(BF16)
            shape = (4, 2, source_rows, HD)
            r.dkv_full[slot, :, :, :, cut] = (
                (dot(dscores, asked, TN) * SCALE).astype(BF16).reshape(shape)
            )
            r.dkv_full[slot, :, :, :, vcut] = (
                dot(probs.astype(BF16), grad, TN).astype(BF16).reshape(shape)
            )
        return carry

    lax.fori_loop(0, 4, cross_back, 0)
    dkv = Sum(links, place, r.dkv_full, r.dkv_into, r.dkv_away, r.dkv_result)
    dkv.start()

    own_down.wait()
    own_up.wait()
    up.turn((0,))
    down.turn((0,))
    up.start((2,))
    down.start((2,))

    get_self = Gather(links, place, r.self_branch, rows, PIECES)

    def after_second(piece, total):
        cut = slice(piece * step, (piece + 1) * step)
        hat, inverse = norm_terms_of(r.sums[0, cut])
        back, gain, bias = norm_backward(total, hat, inverse, r.gain[1:2])
        add_norms(1, gain, bias)
        value = r.grad_sum[cut] + back
        r.grad_sum[cut] = value
        r.self_branch[rows_at(p.s * rows + piece * step, step)] = value.astype(BF16)
        get_self.start(piece)

    Reduce(links, place, r.rs_out.at[1], r.rs_in.at[1], rows, PIECES).run(
        lambda block, piece: dot(
            r.dquery[rows_at(block * rows + piece * step, step)], r.w_cq[...], NT
        ),
        after_second,
    )

    def row_grad(left, right, full):
        def one(part, carry):
            lanes = lanes_at(part * 128, 128)
            value = dot(left[:, lanes], right[...], TN).astype(BF16)
            full[pl.ds(part * 2, 2)] = value.reshape((2, 2) + full.shape[2:])
            return carry

        lax.fori_loop(0, left.shape[1] // 128, one, 0)

    def column_grad(left, right, full):
        def one(block, carry):
            lanes = lanes_at(block * share, share)
            value = dot(left[:, lanes], right(), TN).astype(BF16)
            full[pl.ds(block, 1)] = value.reshape((1,) + full.shape[1:])
            return carry

        lax.fori_loop(0, 4, one, 0)

    row_grad(r.cross, r.cross_branch, r.co_full)
    for piece in range(PIECES):
        get_self.forward(piece)
    column_grad(r.second, lambda: r.dquery[...], r.cq_full)
    for piece in range(PIECES):
        get_self.finish(piece)

    need("w_out", "heads", "mix")

    def mix_back(slot, carry):
        value = dot(r.self_branch[rows_at(slot * rows, rows)], r.w_out[...], NT).astype(BF16)
        for group in range(groups):
            r.gsent[slot * groups + group] = value[:, group * pair_width : (group + 1) * pair_width]
        return carry

    lax.fori_loop(0, 4, mix_back, 0)
    a2a = links.slots(STEPS)
    mine_rows = rows_at(p.c * rows, rows)
    for hop in range(1, STEPS):
        other = lax.rem(p.c + hop, STEPS)
        links.push(a2a + hop, r.gsent.at[other], r.gheads.at[mine_rows], (p.s, other))
    r.gheads[mine_rows] = r.gsent[p.c]
    for owner in range(STEPS):
        r.columns[:, owner * rows : (owner + 1) * rows] = column_positions(r.table, owner, half)
    row_grad(r.mix, r.self_branch, r.so_full)
    dkv.turn()
    up.turn((1,))
    down.turn((1,))
    up.start((3,))
    down.start((3,))
    co = Sum(links, place, r.co_full, r.co_into, r.co_away, r.co_result, True)
    cq = Sum(links, place, r.cq_full, r.cq_into, r.cq_away, r.cq_result)
    so = Sum(links, place, r.so_full, r.so_into, r.so_away, r.so_result, True)
    for hop in range(1, STEPS):
        other = lax.rem(p.c + STEPS - hop, STEPS)
        links.take(a2a + hop, r.gheads.at[rows_at(other * rows, rows)], (p.s, other))

    my_slot, my_group = lax.div(p.c, groups), lax.rem(p.c, groups)
    length = r.lens[pl.ds(my_slot, 1)][0, 0:1, 0:1]
    slot_rows = rows_at(my_slot * rows, rows)
    group_lanes = lanes_at(my_group * pair_width, pair_width)
    back_q, back_kv = links.slots(STEPS), links.slots(STEPS)
    r.acc[...] = jnp.zeros_like(r.acc)

    def q_copy(owner):
        at = rows_at(owner * rows, rows)
        return links.copy(
            back_q + p.c, r.dq_own.at[at], r.dproj.at[0, slot_rows, group_lanes], (p.s, owner)
        )

    def kv_copy(owner):
        at = rows_at(owner * rows, rows)
        return links.copy(
            back_kv + p.c,
            r.dkv_own.at[:, at],
            r.dproj.at[pl.ds(1, 2), slot_rows, group_lanes],
            (p.s, owner),
        )

    def attend_back(block, carry):
        at = rows_at(block * 2 * rows, 2 * rows)
        row_pos = jnp.concatenate(
            [
                row_positions(r.table, 2 * block, half),
                row_positions(r.table, 2 * block + 1, half),
            ],
            axis=0,
        )
        col_pos = r.columns[...]
        allowed = (col_pos <= row_pos) & (col_pos < length)
        for head in range(pair_width // HD):
            cut = slice(head * HD, (head + 1) * HD)
            asked, grad = r.heads[0, at, cut], r.gheads[at, cut]
            scores = dot(asked, r.heads[1, :, cut], NT) * SCALE
            probs, _ = softmax_rows(jnp.where(allowed, scores, masked_score))
            dprobs = dot(grad, r.heads[2, :, cut], NT)
            delta = jnp.sum(probs * dprobs, axis=-1, keepdims=True)
            dscores = (probs * (dprobs - delta)).astype(BF16)
            r.dq_own[at, cut] = (dot(dscores, r.heads[1, :, cut]) * SCALE).astype(BF16)
            r.acc[0, :, cut] += dot(dscores, asked, TN)
            r.acc[1, :, cut] += dot(probs.astype(BF16), grad, TN)
        return carry

    for block in range(STEPS // 2):
        attend_back(block, 0)
        for owner in (2 * block, 2 * block + 1):
            pl.when(p.c != owner)(q_copy(owner).start)
    for owner in range(STEPS):
        at = rows_at(owner * rows, rows)
        r.dkv_own[0, at] = (r.acc[0, at] * SCALE).astype(BF16)
        r.dkv_own[1, at] = r.acc[1, at].astype(BF16)
        pl.when(p.c != owner)(kv_copy(owner).start)
    r.dproj[0, slot_rows, group_lanes] = r.dq_own[mine_rows]
    r.dproj[pl.ds(1, 2), slot_rows, group_lanes] = r.dkv_own[:, mine_rows]

    co.start()
    cq.start()
    so.start()
    need("w_ckv", "source")
    dkv.finish()
    r.dsource[...] = r.dkv_result[...].reshape(4 * source_rows, 2 * width)
    column_grad(r.source, lambda: r.dsource[...], r.ckv_full)
    ckv = Sum(links, place, r.ckv_full, r.ckv_into, r.ckv_away, r.ckv_result)
    ckv.start()

    def after_output(piece, total):
        cut = slice(piece * step, (piece + 1) * step)
        valid = own_rows[cut] < r.target[0]
        r.output[cut] = jnp.where(valid, r.sums[1, cut] + total, 0.0).astype(BF16)

    Reduce(links, place, r.rs_out.at[2], r.rs_in.at[2], rows, PIECES).run(
        stored(r.third_part), after_output
    )

    def after_encoder(piece, total):
        r.grad_source[...] = total

    Reduce(links, place, r.enc_out, r.enc_in, source_rows).run(
        lambda block, piece: dot(
            r.dsource[rows_at(block * source_rows, source_rows)], r.w_ckv[...], NT
        ),
        after_encoder,
    )

    need("w_qkv", "first")
    for owner in range(STEPS):

        @pl.when(p.c != owner)
        def _():
            at = pl.ds((owner // groups) * rows, rows)
            lane = lanes_at((owner % groups) * pair_width, pair_width)
            links.take(back_q + owner, r.dproj.at[0, at, lane], (p.s, owner))
            links.take(back_kv + owner, r.dproj.at[pl.ds(1, 2), at, lane], (p.s, owner))

    def first_partial(block, piece):
        at = rows_at(block * rows + piece * step, step)
        total = dot(r.dproj[0, at], r.w_qkv[:, :width], NT)
        total += dot(r.dproj[1, at], r.w_qkv[:, width : 2 * width], NT)
        return total + dot(r.dproj[2, at], r.w_qkv[:, 2 * width :], NT)

    def after_first(piece, total):
        cut = slice(piece * step, (piece + 1) * step)
        hat, inverse = norm_terms_of(r.tokens[0, cut].astype(F32))
        back, gain, bias = norm_backward(total, hat, inverse, r.gain[0:1])
        add_norms(0, gain, bias)
        r.grad_inputs[cut] = r.grad_sum[cut] + back

    def qkv_grad(block, carry):
        lanes = lanes_at(block * share, share)
        left = r.first[:, lanes]
        for part in range(3):
            value = dot(left, r.dproj[part], TN).astype(BF16)
            r.qkv_full[pl.ds(block, 1), :, :, :, part * width : (part + 1) * width] = value.reshape(
                (1,) + r.qkv_full.shape[1:4] + (width,)
            )
        return carry

    lax.fori_loop(0, 4, qkv_grad, 0)
    qkv = Sum(links, place, r.qkv_full, r.qkv_into, r.qkv_away, r.qkv_result)
    qkv.start()
    Reduce(links, place, r.rs_out.at[3], r.rs_in.at[3], rows, PIECES).run(first_partial, after_first)

    norm_seq, norm_ctx = links.slots(3), links.slots(STEPS)
    others = (p.far, p.opp, p.sib)
    for hop, other in enumerate(others):
        links.push(
            norm_seq + hop,
            r.norms.at[:, lanes_at(other * share, share)],
            r.norms_seq.at[pl.ds(p.s, 1)].at[0],
            (other, p.c),
        )
    up.turn((2,))
    down.turn((2,))
    total = r.norms[:, lanes_at(p.s * share, share)]
    for hop, other in enumerate(others):
        links.take(norm_seq + hop, r.norms_seq.at[pl.ds(other, 1)].at[0], (other, p.c))
        total = total + r.norms_seq[pl.ds(other, 1)][0]
    r.norms_ctx[pl.ds(p.c, 1)] = total[None]
    own_norms = r.norms_ctx.at[pl.ds(p.c, 1)]
    for hop in range(1, STEPS):
        links.push(norm_ctx + hop, own_norms, own_norms, (p.s, lax.rem(p.c + hop, STEPS)))
    up.turn((3,))
    down.turn((3,))
    for job in (co, cq, so, ckv, qkv):
        job.turn()
    sums = {}
    up.finish()
    sums["up"] = Exchange(links, place, r.up_result, r.up_taken)
    sums["up"].start()
    down.finish()
    links.save(r.down_result, r.down_hbm)
    for job in (co, so):
        job.finish()
    for name, job in (("cq", cq), ("ckv", ckv), ("qkv", qkv)):
        job.finish()
        sums[name] = Exchange(links, place, getattr(r, name + "_result"), getattr(r, name + "_taken"))
        sums[name].start()
    for hop in range(1, STEPS):
        other = lax.rem(p.c + STEPS - hop, STEPS)
        links.take(norm_ctx + hop, r.norms_ctx.at[pl.ds(other, 1)], (p.s, other))
    total = r.norms_ctx[0]
    for owner in range(1, STEPS):
        total = total + r.norms_ctx[owner]
    r.norm_sum[...] = total
    for hop, other in enumerate(others):
        links.take(peak_seq + hop, r.peaks_seq.at[pl.ds(other, 1)], (other, p.c))
    for job in sums.values():
        job.finish()
    for owner in range(STEPS):
        pl.when(p.c != owner)(q_copy(owner).wait_send)
        pl.when(p.c != owner)(kv_copy(owner).wait_send)
    links.finish()


def backward_call(kept, given):
    rows, depth = given["tokens"].shape[1:]
    width = kept["w_cq"].shape[1]
    source_rows = kept["source"].shape[0] // 4
    keys = kept["kvs"].shape[1]
    share = depth // 32
    hidden = kept["w_up"].shape[1]
    any_space = pl.BlockSpec(memory_space=pl.ANY)
    vmem = pl.BlockSpec(memory_space=pltpu.VMEM)
    smem = pl.BlockSpec(memory_space=pltpu.SMEM)
    inputs = dict(
        table=(smem, given["table"]),
        target=(smem, given["target"]),
        tokens=(vmem, given["tokens"]),
        cotangent=(vmem, given["cotangent"]),
        gain=(vmem, given["gain"]),
        peak=(vmem, kept["peak"]),
        lens=(vmem, kept["lens"]),
        grad_third=(vmem, given["grad_third"]),
        third_part=(vmem, given["third_part"]),
        up_full=(any_space, given["grad_up"].reshape(4, 4, 2, share, hidden)),
        down_full=(any_space, given["grad_down"].reshape(4, 2, hidden // (8 * share), share, depth)),
    )
    loaded = dict(
        sums=kept["sums"],
        w_co=given["cross_out"],
        cross=kept["cross"],
        query=kept["query"],
        kvs=kept["kvs"],
        w_cq=kept["w_cq"],
        second=kept["second"],
        w_out=given["self_out"],
        heads=kept["heads"],
        mix=kept["mix"],
        w_ckv=kept["w_ckv"],
        source=kept["source"],
        w_qkv=kept["w_qkv"],
        first=kept["first"],
    )
    for name, value in loaded.items():
        inputs[name + "_hbm"] = (any_space, value)
    outs = dict(
        output=((rows, depth), BF16),
        grad_inputs=((rows, depth), F32),
        grad_source=((source_rows, depth), F32),
        down_hbm=((hidden // (8 * share), share, depth), BF16),
        co_result=((1, share, depth), BF16),
        so_result=((1, share, depth), BF16),
        up_taken=((4, share, hidden), BF16),
        cq_taken=((4, share, width), BF16),
        ckv_taken=((4, share, 2 * width), BF16),
        qkv_taken=((4, share, 3 * width), BF16),
        norm_sum=((8, depth // 4), F32),
        peaks_seq=((4, 8, 128), F32),
    )
    down_blocks = hidden // (8 * share)
    scratch = {name: (value.shape, value.dtype) for name, value in loaded.items()}
    scratch |= dict(
        down_own=((4, down_blocks, share, depth), BF16),
        down_into=((4, down_blocks, share, depth), BF16),
        down_away=((3, down_blocks, share, depth), BF16),
        down_result=((down_blocks, share, depth), BF16),
        up_own=((4, 4, share, hidden), BF16),
        up_into=((4, 4, share, hidden), BF16),
        up_away=((3, 4, share, hidden), BF16),
        up_result=((4, share, hidden), BF16),
        peaks_ctx=((8, 8, 128), F32),
        norms=((8, depth), F32),
        norms_seq=((4, 8, depth // 4), F32),
        norms_ctx=((8, 8, depth // 4), F32),
        cross_branch=((4 * rows, depth), BF16),
        self_branch=((4 * rows, depth), BF16),
        grad_sum=((rows, depth), F32),
        rs_out=((4, 3, rows, depth), BF16),
        rs_in=((4, 3, rows, depth), BF16),
        enc_out=((3, source_rows, depth), BF16),
        enc_in=((3, source_rows, depth), BF16),
        dquery=((4 * rows, width), BF16),
        dsource=((4 * source_rows, 2 * width), BF16),
        gsent=((8, rows, 128), BF16),
        gheads=((8 * rows, 128), BF16),
        columns=((1, 8 * rows), jnp.int32),
        acc=((2, 8 * rows, 128), F32),
        dq_own=((8 * rows, 128), BF16),
        dkv_own=((2, 8 * rows, 128), BF16),
        dproj=((3, 4 * rows, width), BF16),
    )
    for name in ("co", "so"):
        scratch[name + "_full"] = ((4, 2, 1, share, depth), BF16)
        scratch[name + "_into"] = ((4, 1, share, depth), BF16)
        scratch[name + "_away"] = ((3, 1, share, depth), BF16)
    for name, columns, r in (
        ("cq", width, share),
        ("ckv", 2 * width, share),
        ("qkv", 3 * width, share),
        ("dkv", 2 * width, source_rows),
    ):
        scratch[name + "_full"] = ((4, 4, 2, r, columns), BF16)
        scratch[name + "_into"] = ((4, 4, r, columns), BF16)
        scratch[name + "_away"] = ((3, 4, r, columns), BF16)
        scratch[name + "_result"] = ((4, r, columns), BF16)
    sems = dict(send_sem=224, recv_sem=224, local_sem=4, load_sem=len(loaded))
    names = list(inputs) + list(outs) + list(scratch) + list(sems)

    def kernel(*refs):
        held = dict(zip(names, refs), loaded=tuple(loaded))
        backward_body(type("Refs", (), held))

    made = pl.pallas_call(
        kernel,
        in_specs=[spec for spec, _ in inputs.values()],
        out_specs=[any_space if name == "down_hbm" else vmem for name in outs],
        out_shape=[jax.ShapeDtypeStruct(*shape) for shape in outs.values()],
        scratch_shapes=[pltpu.VMEM(*shape) for shape in scratch.values()]
        + [pltpu.SemaphoreType.DMA((count,)) for count in sems.values()],
        compiler_params=pltpu.CompilerParams(
            collective_id=1, has_side_effects=True, vmem_limit_bytes=60 * 2**20
        ),
        name="backward",
    )(*[value for _, value in inputs.values()])
    return dict(zip(outs, made))


def finish_kernel(
    clip_ref,
    peaks_ref,
    norm_ref,
    qkv_w,
    cq_w,
    ckv_w,
    output_ref,
    inputs_ref,
    source_ref,
    down_ref,
    co_ref,
    so_ref,
    up_ref,
    cq_ref,
    ckv_ref,
    qkv_ref,
    output_out,
    inputs_out,
    source_out,
    qkv_out,
    so_out,
    cq_out,
    ckv_out,
    co_out,
    up_out,
    down_out,
    gain_out,
    bias_out,
    self_out,
    cross_out,
):
    output_out[0] = output_ref[...]
    inputs_out[0] = inputs_ref[...]
    source_out[0] = source_ref[...]
    share = so_out.shape[0]
    so_out[...] = so_ref[0].astype(F32)
    co_out[...] = co_ref[0].astype(F32)
    for block in range(down_ref.shape[0]):
        down_out[block * share : (block + 1) * share] = down_ref[block].astype(F32)

    def columns(out, taken, parts):
        whole, width = out.shape[1] // parts, out.shape[1] // (4 * parts)
        for owner in range(4):
            for part in range(parts):
                at = part * whole + owner * width
                out[:, at : at + width] = taken[owner, :, part * width : (part + 1) * width].astype(
                    F32
                )

    columns(up_out, up_ref, 1)
    columns(cq_out, cq_ref, 1)
    columns(ckv_out, ckv_ref, 2)
    columns(qkv_out, qkv_ref, 3)
    spread = gain_out.shape[1]
    turned = pltpu.roll(norm_ref[...], norm_ref.shape[1] - lax.axis_index("ctx") * spread, 1)
    gain_out[...] = turned[0:3, :spread]
    bias_out[...] = turned[3:6, :spread]
    lane = lax.broadcasted_iota(jnp.int32, (1, 128), 1)
    held = peaks_ref.shape[1] // 2
    for owner in range(4):
        for two in range(held // 2):
            head = owner * held + two * 2
            at = slice(head * HD, head * HD + 128)
            for kind, jobs in (
                (0, ((self_out, qkv_w, 0, 0), (self_out, qkv_w, H * HD, H * HD))),
                (1, ((cross_out, cq_w, 0, 0), (cross_out, ckv_w, 0, H * HD))),
            ):
                top = [peaks_ref[owner, kind * held + two * 2 + i : kind * held + two * 2 + i + 1] for i in (0, 1)]
                limit = [clip_ref[kind, head + i] for i in (0, 1)]
                limits = jnp.where(lane < HD, limit[0], limit[1])
                tops = jnp.where(lane < HD, top[0], top[1])
                factor = jnp.sqrt(limits / jnp.maximum(tops, limits))
                for out, weight, start, goal in jobs:
                    out[:, goal + head * HD : goal + head * HD + 128] = (
                        weight[:, start + head * HD : start + head * HD + 128].astype(F32) * factor
                    ).astype(BF16)


def finish_call(made, given):
    rows, depth = given["tokens"].shape[1:]
    hidden = given["mlp_up"].shape[1]
    source_rows, share = made["grad_source"].shape[0], made["so_result"].shape[1]
    columns = H * HD
    weight_rows = given["self_qkv"].shape[0]
    shapes = [
        ((1, rows, depth), BF16),
        ((1, rows, depth), F32),
        ((1, source_rows, depth), F32),
        ((share, 3 * columns), F32),
        ((share, depth), F32),
        ((share, columns), F32),
        ((share, 2 * columns), F32),
        ((share, depth), F32),
        ((share, hidden), F32),
        ((hidden // 32, depth), F32),
        ((3, share), F32),
        ((3, share), F32),
        ((weight_rows, 2 * columns), BF16),
        ((weight_rows, 2 * columns), BF16),
    ]
    vmem = pl.BlockSpec(memory_space=pltpu.VMEM)
    return pl.pallas_call(
        finish_kernel,
        in_specs=[pl.BlockSpec(memory_space=pltpu.SMEM)] + [vmem] * 15,
        out_specs=[vmem] * len(shapes),
        out_shape=[jax.ShapeDtypeStruct(*shape) for shape in shapes],
        compiler_params=pltpu.CompilerParams(vmem_limit_bytes=48 * 2**20),
        name="finish",
    )(
        given["clip"],
        made["peaks_seq"],
        made["norm_sum"],
        given["self_qkv"],
        given["cross_q"],
        given["cross_kv"],
        made["output"],
        made["grad_inputs"],
        made["grad_source"],
        made["down_hbm"],
        made["co_result"],
        made["so_result"],
        made["up_taken"],
        made["cq_taken"],
        made["ckv_taken"],
        made["qkv_taken"],
    )


def fast_device(
    tokens,
    encoder_states,
    cotangent,
    target_lengths,
    source_lengths,
    block_table,
    self_qkv,
    self_out,
    cross_q,
    cross_kv,
    cross_out,
    mlp_up,
    mlp_down,
    norm_gain,
    norm_bias,
    clip_limit,
):
    kept = forward_call(
        block_table,
        target_lengths,
        source_lengths,
        tokens,
        encoder_states,
        cotangent,
        self_qkv,
        self_out,
        cross_q,
        cross_kv,
        cross_out,
        mlp_up,
        norm_gain,
        norm_bias,
    )
    third_low, mlp_branch, w_up = kept["third"], kept["branch"], kept["w_up"]
    hidden_pre = dot(third_low, w_up)
    hidden_act, gelu_back = jax.vjp(jax.nn.gelu, hidden_pre)
    hidden_low = hidden_act.astype(BF16)
    grad_pre = gelu_back(dot(mlp_branch, mlp_down, NT))[0].astype(BF16)
    given = dict(
        table=block_table,
        target=target_lengths,
        tokens=tokens,
        cotangent=cotangent,
        gain=norm_gain,
        grad_third=dot(grad_pre, w_up, NT).astype(BF16),
        third_part=dot(hidden_low, mlp_down).astype(BF16),
        grad_up=dot(third_low, grad_pre, TN).astype(BF16),
        grad_down=dot(hidden_low, mlp_branch, TN).astype(BF16),
        cross_out=cross_out,
        self_out=self_out,
        self_qkv=self_qkv,
        cross_q=cross_q,
        cross_kv=cross_kv,
        mlp_up=mlp_up,
        clip=clip_limit,
    )
    made = backward_call(kept, given)
    held = H // 4
    tops = made["peaks_seq"][:, :, 0].reshape(4, 2, held).transpose(1, 0, 2).reshape(2, H)
    return (*finish_call(made, given), tops)


def solution(mesh):
    body = fast_device if fast_fits(mesh) else general_device
    return jax.shard_map(
        body,
        mesh=mesh,
        in_specs=(
            P("seq", "ctx", None),
            P("seq", "ctx", None),
            P("seq", "ctx", None),
            P("seq"),
            P("seq"),
            P(),
            P("seq", None),
            P("seq", None),
            P("seq", None),
            P("seq", None),
            P("seq", None),
            P("seq", None),
            P("seq", None),
            P(),
            P(),
            P(),
        ),
        out_specs=(
            P("seq", "ctx", None),
            P("seq", "ctx", None),
            P("seq", "ctx", None),
            P(("seq", "ctx"), None),
            P(("seq", "ctx"), None),
            P(("seq", "ctx"), None),
            P(("seq", "ctx"), None),
            P(("seq", "ctx"), None),
            P(("seq", "ctx"), None),
            P(("seq", "ctx"), None),
            P(None, ("seq", "ctx")),
            P(None, ("seq", "ctx")),
            P("seq", None),
            P("seq", None),
            P(),
        ),
        check_vma=False,
    )
```

```python
import functools

import jax
import jax.numpy as jnp
from jax import lax
from jax.experimental import pallas as pl
from jax.experimental.pallas import tpu as pltpu
from jax.sharding import PartitionSpec as P

H = 16
HD = 64


masked_score = -1000000000.0
norm_eps = 1e-05


def block_size(count):
    return max((step for step in range(1, min(count, 512) + 1) if count % step == 0))


def layer_norm(values, gain, bias):
    centered = values - jnp.mean(values, axis=-1, keepdims=True)
    spread = jnp.mean(centered * centered, axis=-1, keepdims=True)
    return centered * lax.rsqrt(spread + norm_eps) * gain + bias


def allowed_pairs(query_pos, key_pos, key_limit, causal):
    allowed = jnp.broadcast_to(
        (key_pos < key_limit)[None, :], (query_pos.shape[0], key_pos.shape[0])
    )
    if causal:
        allowed = allowed & (key_pos[None, :] <= query_pos[:, None])
    return allowed


def head_scores(query_heads, key_rows):
    key_heads = key_rows.reshape(key_rows.shape[0], H, HD)
    return jnp.einsum(
        "qhd,khd->hqk", query_heads, key_heads, preferred_element_type=jnp.float32
    ) * HD ** (-0.5)


def softmax_stats(query_heads, kv_rows, key_pos, query_pos, query_ok, key_limit, causal):
    count = kv_rows.shape[0]
    step = block_size(count)
    width = H * HD
    rows = query_heads.shape[0]

    def softmax_visit(carry, block):
        top, total, peak = carry
        block_rows, block_pos = block
        allowed = allowed_pairs(query_pos, block_pos, key_limit, causal)
        scores = jnp.where(
            allowed[None], head_scores(query_heads, block_rows[:, :width]), masked_score
        )
        new_top = jnp.maximum(top, jnp.max(scores, axis=-1))
        total = total * jnp.exp(top - new_top) + jnp.sum(
            jnp.exp(scores - new_top[..., None]), axis=-1
        )
        counted = jnp.where((allowed & query_ok[:, None])[None], scores, masked_score)
        peak = jnp.maximum(peak, jnp.max(counted, axis=(1, 2)))
        return ((new_top, total, peak), None)

    start = (
        jnp.full((H, rows), -jnp.inf, jnp.float32),
        jnp.zeros((H, rows), jnp.float32),
        jnp.full((H,), masked_score, jnp.float32),
    )
    blocks = (kv_rows.reshape(count // step, step, 2 * width), key_pos.reshape(count // step, step))
    return lax.scan(softmax_visit, start, blocks)[0]


def attend_values(query_heads, kv_rows, key_pos, query_pos, key_limit, causal, top, total):
    count = kv_rows.shape[0]
    step = block_size(count)
    width = H * HD
    rows = query_heads.shape[0]

    def attend_visit(acc, block):
        block_rows, block_pos = block
        allowed = allowed_pairs(query_pos, block_pos, key_limit, causal)
        scores = jnp.where(
            allowed[None], head_scores(query_heads, block_rows[:, :width]), masked_score
        )
        weights = (jnp.exp(scores - top[..., None]) / total[..., None]).astype(jnp.bfloat16)
        value_heads = block_rows[:, width:].reshape(step, H, HD)
        return (
            acc
            + jnp.einsum("hqk,khd->qhd", weights, value_heads, preferred_element_type=jnp.float32),
            None,
        )

    blocks = (kv_rows.reshape(count // step, step, 2 * width), key_pos.reshape(count // step, step))
    acc = lax.scan(attend_visit, jnp.zeros((rows, H, HD), jnp.float32), blocks)[0]
    return acc.reshape(rows, width)


def query_grads(
    query_heads, kv_rows, key_pos, query_pos, key_limit, causal, top, total, grad_heads, delta
):
    count = kv_rows.shape[0]
    step = block_size(count)
    width = H * HD
    rows = query_heads.shape[0]

    def query_visit(acc, block):
        block_rows, block_pos = block
        allowed = allowed_pairs(query_pos, block_pos, key_limit, causal)
        scores = jnp.where(
            allowed[None], head_scores(query_heads, block_rows[:, :width]), masked_score
        )
        probs = jnp.exp(scores - top[..., None]) / total[..., None]
        value_heads = block_rows[:, width:].reshape(step, H, HD)
        dprobs = jnp.einsum(
            "qhd,khd->hqk", grad_heads, value_heads, preferred_element_type=jnp.float32
        )
        dscores = (probs * (dprobs - delta[..., None])).astype(jnp.bfloat16)
        key_heads = block_rows[:, :width].reshape(step, H, HD)
        return (
            acc
            + jnp.einsum("hqk,khd->qhd", dscores, key_heads, preferred_element_type=jnp.float32),
            None,
        )

    blocks = (kv_rows.reshape(count // step, step, 2 * width), key_pos.reshape(count // step, step))
    acc = lax.scan(query_visit, jnp.zeros((rows, H, HD), jnp.float32), blocks)[0]
    return acc.reshape(rows, width) * HD ** (-0.5)


def key_grads(
    query_heads,
    kv_rows,
    key_pos,
    query_pos,
    key_limit,
    causal,
    top,
    total,
    grad_heads,
    delta,
    start,
    count,
):
    step = block_size(count)
    width = H * HD

    def piece(index):
        offset = start + index * step
        block_rows = lax.dynamic_slice_in_dim(kv_rows, offset, step, 0)
        block_pos = lax.dynamic_slice_in_dim(key_pos, offset, step, 0)
        allowed = allowed_pairs(query_pos, block_pos, key_limit, causal)
        scores = jnp.where(
            allowed[None], head_scores(query_heads, block_rows[:, :width]), masked_score
        )
        probs = jnp.exp(scores - top[..., None]) / total[..., None]
        value_heads = block_rows[:, width:].reshape(step, H, HD)
        dprobs = jnp.einsum(
            "qhd,khd->hqk", grad_heads, value_heads, preferred_element_type=jnp.float32
        )
        dscores = (probs * (dprobs - delta[..., None])).astype(jnp.bfloat16)
        dkeys = jnp.einsum(
            "hqk,qhd->khd", dscores, query_heads, preferred_element_type=jnp.float32
        ).reshape(step, width) * HD ** (-0.5)
        dvalues = jnp.einsum(
            "hqk,qhd->khd",
            probs.astype(jnp.bfloat16),
            grad_heads,
            preferred_element_type=jnp.float32,
        ).reshape(step, width)
        return jnp.concatenate([dkeys, dvalues], axis=1)

    return lax.map(piece, jnp.arange(count // step, dtype=jnp.int32)).reshape(count, 2 * width)


def split_rows(grad, seq_count, ctx_count):
    return grad.reshape(
        (seq_count, ctx_count, grad.shape[0] // (seq_count * ctx_count)) + grad.shape[1:]
    )


def join_rows(grad):
    return grad.reshape((grad.shape[2],) + grad.shape[3:])


def general_device(
    tokens,
    encoder_states,
    cotangent,
    target_lengths,
    source_lengths,
    block_table,
    self_qkv,
    self_out,
    cross_q,
    cross_kv,
    cross_out,
    mlp_up,
    mlp_down,
    norm_gain,
    norm_bias,
    clip_limit,
):
    rows = tokens.shape[1]
    width = H * HD
    half = rows // 2
    source_rows = encoder_states.shape[1]
    seq_count = lax.axis_size("seq")
    ctx_count = lax.axis_size("ctx")
    all_positions = (
        block_table[:, :, None] * half + jnp.arange(half, dtype=jnp.int32)[None, None, :]
    ).reshape(-1)
    own_positions = lax.dynamic_slice_in_dim(all_positions, lax.axis_index("ctx") * rows, rows, 0)
    length = target_lengths[0]
    source_length = source_lengths[0]
    query_ok = own_positions < length
    valid_rows = query_ok[:, None]
    source_positions = jnp.arange(source_rows * ctx_count, dtype=jnp.int32)
    w_qkv, w_out, w_cq, w_ckv, w_co = (
        lax.all_gather(self_qkv, "seq", axis=0, tiled=True),
        lax.all_gather(self_out, "seq", axis=0, tiled=True),
        lax.all_gather(cross_q, "seq", axis=0, tiled=True),
        lax.all_gather(cross_kv, "seq", axis=0, tiled=True),
        lax.all_gather(cross_out, "seq", axis=0, tiled=True),
    )
    inputs = tokens[0].astype(jnp.float32)
    first_norm, first_back = jax.vjp(layer_norm, inputs, norm_gain[0], norm_bias[0])
    first_low = first_norm.astype(jnp.bfloat16)
    projected = jnp.dot(first_low, w_qkv, preferred_element_type=jnp.float32).astype(jnp.bfloat16)
    self_query = projected[:, :width].reshape(rows, H, HD)
    source_kv = jnp.dot(encoder_states[0], w_ckv, preferred_element_type=jnp.float32).astype(
        jnp.bfloat16
    )
    self_kv, cross_kvs = (
        lax.all_gather(projected[:, width:], "ctx", axis=0, tiled=True),
        lax.all_gather(source_kv, "ctx", axis=0, tiled=True),
    )
    self_top, self_total, self_peak = softmax_stats(
        self_query, self_kv, all_positions, own_positions, query_ok, length, True
    )
    self_mix = attend_values(
        self_query, self_kv, all_positions, own_positions, length, True, self_top, self_total
    )
    self_low = self_mix.astype(jnp.bfloat16)
    first_sum = inputs + jnp.dot(self_low, w_out, preferred_element_type=jnp.float32)
    second_norm, second_back = jax.vjp(layer_norm, first_sum, norm_gain[1], norm_bias[1])
    second_low = second_norm.astype(jnp.bfloat16)
    cross_rows = jnp.dot(second_low, w_cq, preferred_element_type=jnp.float32).astype(jnp.bfloat16)
    cross_query = cross_rows.reshape(rows, H, HD)
    cross_top, cross_total, cross_peak = softmax_stats(
        cross_query, cross_kvs, source_positions, own_positions, query_ok, source_length, False
    )
    cross_mix = attend_values(
        cross_query,
        cross_kvs,
        source_positions,
        own_positions,
        source_length,
        False,
        cross_top,
        cross_total,
    )
    cross_low = cross_mix.astype(jnp.bfloat16)
    second_sum = first_sum + jnp.dot(cross_low, w_co, preferred_element_type=jnp.float32)
    third_norm, third_back = jax.vjp(layer_norm, second_sum, norm_gain[2], norm_bias[2])
    third_low = third_norm.astype(jnp.bfloat16)
    w_up, w_down = (
        lax.all_gather(mlp_up, "seq", axis=0, tiled=True),
        lax.all_gather(mlp_down, "seq", axis=0, tiled=True),
    )
    hidden_pre = jnp.dot(third_low, w_up, preferred_element_type=jnp.float32)
    hidden_act, gelu_back = jax.vjp(jax.nn.gelu, hidden_pre)
    hidden_low = hidden_act.astype(jnp.bfloat16)
    third_sum = second_sum + jnp.dot(hidden_low, w_down, preferred_element_type=jnp.float32)
    output_rows = jnp.where(valid_rows, third_sum, 0.0).astype(jnp.bfloat16)
    peaks = lax.pmax(jnp.stack([self_peak, cross_peak]), ("seq", "ctx"))
    grad_rows = jnp.where(valid_rows, cotangent[0].astype(jnp.float32), 0.0)
    mlp_branch = grad_rows.astype(jnp.bfloat16)
    grad_down = jnp.einsum("rf,rd->fd", hidden_low, mlp_branch, preferred_element_type=jnp.float32)
    grad_act = jnp.einsum("rd,fd->rf", mlp_branch, w_down, preferred_element_type=jnp.float32)
    grad_pre = gelu_back(grad_act)[0].astype(jnp.bfloat16)
    grad_up = jnp.einsum("rd,rf->df", third_low, grad_pre, preferred_element_type=jnp.float32)
    back_third, gain_three, bias_three = third_back(
        jnp.einsum("rf,df->rd", grad_pre, w_up, preferred_element_type=jnp.float32)
    )
    up_part, down_part = (
        lax.psum_scatter(
            split_rows(grad_up, seq_count, ctx_count).astype(jnp.bfloat16),
            "ctx",
            scatter_dimension=1,
            tiled=True,
        ).astype(jnp.float32),
        lax.psum_scatter(
            split_rows(grad_down, seq_count, ctx_count).astype(jnp.bfloat16),
            "ctx",
            scatter_dimension=1,
            tiled=True,
        ).astype(jnp.float32),
    )
    up_shard, down_shard = (
        lax.psum_scatter(
            up_part.astype(jnp.bfloat16), "seq", scatter_dimension=0, tiled=True
        ).astype(jnp.float32),
        lax.psum_scatter(
            down_part.astype(jnp.bfloat16), "seq", scatter_dimension=0, tiled=True
        ).astype(jnp.float32),
    )
    grad_second = grad_rows + back_third
    cross_branch = grad_second.astype(jnp.bfloat16)
    grad_co = jnp.einsum("rd,re->de", cross_low, cross_branch, preferred_element_type=jnp.float32)
    cross_heads_grad = (
        jnp.einsum("re,de->rd", cross_branch, w_co, preferred_element_type=jnp.float32)
        .astype(jnp.bfloat16)
        .reshape(rows, H, HD)
    )
    cross_delta = jnp.einsum(
        "qhd,qhd->hq", cross_heads_grad.astype(jnp.float32), cross_mix.reshape(rows, H, HD)
    )
    grad_cross_rows = query_grads(
        cross_query,
        cross_kvs,
        source_positions,
        own_positions,
        source_length,
        False,
        cross_top,
        cross_total,
        cross_heads_grad,
        cross_delta,
    ).astype(jnp.bfloat16)
    grad_source_kv = lax.psum_scatter(
        key_grads(
            cross_query,
            cross_kvs,
            source_positions,
            own_positions,
            source_length,
            False,
            cross_top,
            cross_total,
            cross_heads_grad,
            cross_delta,
            jnp.int32(0),
            source_rows * lax.axis_size("ctx"),
        ).astype(jnp.bfloat16),
        "ctx",
        scatter_dimension=0,
        tiled=True,
    )
    grad_cq = jnp.einsum(
        "rd,re->de", second_low, grad_cross_rows, preferred_element_type=jnp.float32
    )
    grad_ckv = jnp.einsum(
        "sd,se->de", encoder_states[0], grad_source_kv, preferred_element_type=jnp.float32
    )
    grad_source = jnp.einsum("se,de->sd", grad_source_kv, w_ckv, preferred_element_type=jnp.float32)
    back_second, gain_two, bias_two = second_back(
        jnp.einsum("re,de->rd", grad_cross_rows, w_cq, preferred_element_type=jnp.float32)
    )
    grad_first = grad_second + back_second
    self_branch = grad_first.astype(jnp.bfloat16)
    grad_so = jnp.einsum("rd,re->de", self_low, self_branch, preferred_element_type=jnp.float32)
    self_heads_grad = (
        jnp.einsum("re,de->rd", self_branch, w_out, preferred_element_type=jnp.float32)
        .astype(jnp.bfloat16)
        .reshape(rows, H, HD)
    )
    self_delta = jnp.einsum(
        "qhd,qhd->hq", self_heads_grad.astype(jnp.float32), self_mix.reshape(rows, H, HD)
    )
    grad_query = query_grads(
        self_query,
        self_kv,
        all_positions,
        own_positions,
        length,
        True,
        self_top,
        self_total,
        self_heads_grad,
        self_delta,
    ).astype(jnp.bfloat16)
    grad_kv = lax.psum_scatter(
        key_grads(
            self_query,
            self_kv,
            all_positions,
            own_positions,
            length,
            True,
            self_top,
            self_total,
            self_heads_grad,
            self_delta,
            jnp.int32(0),
            rows * lax.axis_size("ctx"),
        ).astype(jnp.bfloat16),
        "ctx",
        scatter_dimension=0,
        tiled=True,
    )
    grad_projected = jnp.concatenate([grad_query, grad_kv], axis=1)
    grad_qkv = jnp.einsum(
        "rd,re->de", first_low, grad_projected, preferred_element_type=jnp.float32
    )
    back_first, gain_one, bias_one = first_back(
        jnp.einsum("re,de->rd", grad_projected, w_qkv, preferred_element_type=jnp.float32)
    )
    grad_inputs = grad_first + back_first
    norm_terms = jnp.stack([gain_one, gain_two, gain_three, bias_one, bias_two, bias_three], axis=1)
    qkv_part, out_part, cq_part, ckv_part, co_part, norm_part = (
        lax.psum_scatter(
            split_rows(grad_qkv, seq_count, ctx_count).astype(jnp.bfloat16),
            "ctx",
            scatter_dimension=1,
            tiled=True,
        ).astype(jnp.float32),
        lax.psum_scatter(
            split_rows(grad_so, seq_count, ctx_count).astype(jnp.bfloat16),
            "ctx",
            scatter_dimension=1,
            tiled=True,
        ).astype(jnp.float32),
        lax.psum_scatter(
            split_rows(grad_cq, seq_count, ctx_count).astype(jnp.bfloat16),
            "ctx",
            scatter_dimension=1,
            tiled=True,
        ).astype(jnp.float32),
        lax.psum_scatter(
            split_rows(grad_ckv, seq_count, ctx_count).astype(jnp.bfloat16),
            "ctx",
            scatter_dimension=1,
            tiled=True,
        ).astype(jnp.float32),
        lax.psum_scatter(
            split_rows(grad_co, seq_count, ctx_count).astype(jnp.bfloat16),
            "ctx",
            scatter_dimension=1,
            tiled=True,
        ).astype(jnp.float32),
        lax.psum_scatter(
            split_rows(norm_terms, seq_count, ctx_count).astype(jnp.bfloat16),
            "ctx",
            scatter_dimension=1,
            tiled=True,
        ).astype(jnp.float32),
    )
    qkv_shard, out_shard, cq_shard, ckv_shard, co_shard, norm_shard = (
        lax.psum_scatter(
            qkv_part.astype(jnp.bfloat16), "seq", scatter_dimension=0, tiled=True
        ).astype(jnp.float32),
        lax.psum_scatter(
            out_part.astype(jnp.bfloat16), "seq", scatter_dimension=0, tiled=True
        ).astype(jnp.float32),
        lax.psum_scatter(
            cq_part.astype(jnp.bfloat16), "seq", scatter_dimension=0, tiled=True
        ).astype(jnp.float32),
        lax.psum_scatter(
            ckv_part.astype(jnp.bfloat16), "seq", scatter_dimension=0, tiled=True
        ).astype(jnp.float32),
        lax.psum_scatter(
            co_part.astype(jnp.bfloat16), "seq", scatter_dimension=0, tiled=True
        ).astype(jnp.float32),
        lax.psum_scatter(
            norm_part.astype(jnp.bfloat16), "seq", scatter_dimension=0, tiled=True
        ).astype(jnp.float32),
    )
    norm_shard = join_rows(norm_shard)
    factors = jnp.sqrt(clip_limit / jnp.maximum(peaks, clip_limit))
    columns = jnp.repeat(factors, HD, axis=1)
    qkv_wide = self_qkv.astype(jnp.float32)
    clipped_self = jnp.concatenate(
        [qkv_wide[:, :width] * columns[0], qkv_wide[:, width : 2 * width] * columns[0]], axis=1
    ).astype(jnp.bfloat16)
    clipped_cross = jnp.concatenate(
        [
            cross_q.astype(jnp.float32) * columns[1],
            cross_kv[:, :width].astype(jnp.float32) * columns[1],
        ],
        axis=1,
    ).astype(jnp.bfloat16)
    return (
        output_rows[None],
        grad_inputs[None],
        grad_source[None],
        join_rows(qkv_shard),
        join_rows(out_shard),
        join_rows(cq_shard),
        join_rows(ckv_shard),
        join_rows(co_shard),
        join_rows(up_shard),
        join_rows(down_shard),
        norm_shard[:, :3].T,
        norm_shard[:, 3:].T,
        clipped_self,
        clipped_cross,
        peaks,
    )


F32 = jnp.float32
BF16 = jnp.bfloat16
SCALE = HD**-0.5


def fast_fits(mesh):
    seq_count, ctx_count = mesh.shape["seq"], mesh.shape["ctx"]
    if H % seq_count or H % ctx_count:
        return False
    held, pair = H // seq_count, H // ctx_count
    return held % pair == 0 and seq_count * (held // pair) == ctx_count and pair * HD == 128


def dot(left, right, contract=((1,), (0,))):
    return lax.dot_general(left, right, (contract, ((), ())), preferred_element_type=F32)


NT = ((1,), (1,))
TN = ((0,), (0,))


def norm_forward(values, gain, bias):
    centered = values - jnp.mean(values, axis=-1, keepdims=True)
    spread = jnp.mean(centered * centered, axis=-1, keepdims=True)
    inverse = lax.rsqrt(spread + norm_eps)
    hat = centered * inverse
    return hat, inverse, (hat * gain + bias).astype(BF16)


def norm_backward(grad, hat, inverse, gain):
    scaled = grad * gain
    inner = jnp.mean(scaled, axis=-1, keepdims=True)
    outer = jnp.mean(scaled * hat, axis=-1, keepdims=True)
    return (
        (scaled - inner - hat * outer) * inverse,
        jnp.sum(grad * hat, axis=0),
        jnp.sum(grad, axis=0),
    )


MESH = pl.DeviceIdType.MESH


class Links:
    def __init__(self, send, recv, local):
        self.send, self.recv, self.local = send, recv, local
        self.count, self.local_count = 0, 0
        self.sends, self.saves = [], []

    def slots(self, count):
        start = self.count
        self.count += count
        return start

    def copy(self, index, src, dst, device):
        return pltpu.make_async_remote_copy(
            src_ref=src,
            dst_ref=dst,
            send_sem=self.send.at[index],
            recv_sem=self.recv.at[index],
            device_id=device,
            device_id_type=MESH,
        )

    def push(self, index, src, dst, device, when=None):
        made = self.copy(index, src, dst, device)
        if when is None:
            made.start()
        else:
            pl.when(when)(made.start)
        self.sends.append((made, when))

    def take(self, index, dst, device, when=None):
        made = self.copy(index, dst, dst, device)
        if when is None:
            made.wait_recv()
        else:
            pl.when(when)(made.wait_recv)

    def save(self, src, dst):
        made = pltpu.make_async_copy(src, dst, self.local.at[self.local_count])
        self.local_count += 1
        made.start()
        self.saves.append(made)
        return made

    def finish(self):
        for made, when in self.sends:
            if when is None:
                made.wait_send()
            else:
                pl.when(when)(made.wait_send)
        for made in self.saves:
            made.wait()
        self.sends, self.saves = [], []


class Place:
    def __init__(self):
        self.s, self.c = lax.axis_index("seq"), lax.axis_index("ctx")
        self.k, self.x = lax.rem(self.s, 2), lax.div(self.s, 2)
        self.y, self.z = lax.rem(self.c, 2), lax.div(self.c, 2)
        self.sib = self.s + 1 - 2 * self.k
        self.far = lax.rem(self.s + 2, 4)
        self.opp = lax.rem(self.sib + 2, 4)
        self.pair = self.c + 1 - 2 * self.y

    def greet(self):
        barrier = pltpu.get_barrier_semaphore()
        for other in (self.sib, self.far, self.opp):
            pl.semaphore_signal(barrier, inc=1, device_id=(other, self.c), device_id_type=MESH)
        for step in range(1, 8):
            pl.semaphore_signal(
                barrier,
                inc=1,
                device_id=(self.s, lax.rem(self.c + step, 8)),
                device_id_type=MESH,
            )
        pl.semaphore_wait(barrier, 10)


def rows_at(start, count):
    return pl.ds(pl.multiple_of(start, 16), count)


def lanes_at(start, count):
    return pl.ds(pl.multiple_of(start, 128), count)


class Columns:
    def __init__(self, links, place, weight, dest, parts, pieces=1):
        self.links, self.place, self.weight, self.dest = links, place, weight, dest
        rows, columns = weight.shape
        self.rows, self.whole, self.width = rows, columns // parts, columns // (4 * parts)
        self.step = rows // pieces
        self.jobs = [(part, piece) for piece in range(pieces) for part in range(parts)]
        self.base = {job: links.slots(5) for job in self.jobs}
        self.mine = place.k == place.y

    def source(self, job, target):
        part, piece = job
        return self.weight.at[
            pl.ds(piece * self.step, self.step),
            lanes_at(part * self.whole + target * self.width, self.width),
        ]

    def land(self, job, owner):
        part, piece = job
        return self.dest.at[
            rows_at(owner * self.rows + piece * self.step, self.step),
            pl.ds(part * self.width, self.width),
        ]

    def start(self, jobs=None):
        p = self.place
        for job in self.jobs if jobs is None else jobs:
            base = self.base[job]
            land = self.land(job, p.s)
            self.links.push(base, self.source(job, p.far), land, (p.far, p.c), self.mine)
            self.links.push(base + 1, self.source(job, p.opp), land, (p.opp, p.c), self.mine)
            self.links.push(base + 2, self.source(job, p.sib), land, (p.sib, p.c))
            self.links.save(self.source(job, p.s), land)

    def relay(self, jobs=None):
        p = self.place
        came = lax.rem(p.x + 1, 2) * 2 + p.y
        for job in self.jobs if jobs is None else jobs:
            base = self.base[job]
            land = self.land(job, came)
            self.links.take(base, land, (p.far, p.c), p.k == p.y)
            self.links.take(base + 1, land, (p.opp, p.c), p.k != p.y)
            self.links.push(base + 3, land, land, (p.s, p.pair))

    def finish(self):
        p = self.place
        for job in self.jobs:
            base = self.base[job]
            self.links.take(base + 2, self.land(job, p.sib), (p.sib, p.c))
            self.links.take(
                base + 3,
                self.land(job, lax.rem(p.x + 1, 2) * 2 + 1 - p.y),
                (p.s, p.pair),
            )


class Gather:
    def __init__(self, links, place, dest, rows, pieces=1):
        self.links, self.place, self.dest, self.rows = links, place, dest, rows
        self.step = rows // pieces
        self.base = [links.slots(3) for _ in range(pieces)]

    def land(self, piece, owner):
        return self.dest.at[rows_at(owner * self.rows + piece * self.step, self.step)]

    def start(self, piece=0):
        p, base = self.place, self.base[piece]
        land = self.land(piece, p.s)
        self.links.push(base, land, land, (p.far, p.c))
        self.links.push(base + 1, land, land, (p.sib, p.c))

    def forward(self, piece=0):
        p, base = self.place, self.base[piece]
        land = self.land(piece, p.far)
        self.links.take(base, land, (p.far, p.c))
        self.links.push(base + 2, land, land, (p.sib, p.c))

    def finish(self, piece=0):
        p, base = self.place, self.base[piece]
        self.links.take(base + 1, self.land(piece, p.sib), (p.sib, p.c))
        self.links.take(base + 2, self.land(piece, p.opp), (p.sib, p.c))

    def all(self):
        for piece in range(len(self.base)):
            self.start(piece)
        for piece in range(len(self.base)):
            self.forward(piece)
        for piece in range(len(self.base)):
            self.finish(piece)


class Reduce:
    def __init__(self, links, place, out, into, rows, pieces=1):
        self.links, self.place, self.out, self.into = links, place, out, into
        self.step = rows // pieces
        self.base = [links.slots(3) for _ in range(pieces)]

    def run(self, partial, then):
        p, links, out, into = self.place, self.links, self.out, self.into
        count, step = len(self.base), self.step
        cut = [pl.ds(piece * step, step) for piece in range(count)]
        here = (p.sib, p.c)
        for piece, base in enumerate(self.base):
            out[0, cut[piece]] = partial(p.opp, piece).astype(BF16)
            links.push(base, out.at[0, cut[piece]], into.at[0, cut[piece]], here)
        for piece, base in enumerate(self.base):
            held = partial(p.far, piece)
            links.take(base, into.at[0, cut[piece]], here)
            out[2, cut[piece]] = (held + into[0, cut[piece]].astype(F32)).astype(BF16)
            links.push(base + 1, out.at[2, cut[piece]], into.at[2, cut[piece]], (p.far, p.c))
        for piece, base in enumerate(self.base):
            out[1, cut[piece]] = partial(p.sib, piece).astype(BF16)
            links.push(base + 2, out.at[1, cut[piece]], into.at[1, cut[piece]], here)
        for piece, base in enumerate(self.base):
            held = partial(p.s, piece)
            links.take(base + 2, into.at[1, cut[piece]], here)
            held = held + into[1, cut[piece]].astype(F32)
            links.take(base + 1, into.at[2, cut[piece]], (p.far, p.c))
            then(piece, held + into[2, cut[piece]].astype(F32))


def row_positions(table_ref, owner, half):
    place = lax.broadcasted_iota(jnp.int32, (2 * half, 1), 0)
    first, second = table_ref[owner, 0] * half, table_ref[owner, 1] * half - half
    return place + jnp.where(place < half, first, second)


def column_positions(table_ref, owner, half):
    place = lax.broadcasted_iota(jnp.int32, (1, 2 * half), 1)
    first, second = table_ref[owner, 0] * half, table_ref[owner, 1] * half - half
    return place + jnp.where(place < half, first, second)


def softmax_rows(scores):
    top = jnp.max(scores, axis=-1, keepdims=True)
    expos = jnp.exp(scores - top)
    return expos * (1.0 / jnp.sum(expos, axis=-1, keepdims=True)), top


PIECES = 2
STEPS = 8


def forward_kernel(
    table_ref,
    target_ref,
    source_ref,
    tokens_ref,
    encoder_ref,
    cotangent_ref,
    qkv_ref,
    out_ref,
    cq_ref,
    ckv_ref,
    co_ref,
    up_ref,
    gain_ref,
    bias_ref,
    first_out,
    second_out,
    third_out,
    branch_out,
    source_out,
    w_qkv_out,
    w_cq_out,
    w_ckv_out,
    w_up_out,
    heads_out,
    mix_out,
    query_out,
    kvs_out,
    cross_out_ref,
    sums_out,
    peak_out,
    lens_out,
    first,
    second,
    third,
    branch,
    source,
    w_qkv,
    w_cq,
    w_ckv,
    sent,
    heads,
    mix_own,
    mix,
    query,
    kv_own,
    kvs,
    cross,
    sums,
    columns,
    lens,
    rs_out,
    rs_in,
    send_sem,
    recv_sem,
    local_sem,
):
    place, links = Place(), Links(send_sem, recv_sem, local_sem)
    p = place
    rows = tokens_ref.shape[1]
    source_rows = encoder_ref.shape[1]
    half = rows // 2
    width = w_cq.shape[1]
    pair_width = heads.shape[2]
    held = width // HD
    groups = width // pair_width
    place.greet()

    get_qkv = Columns(links, place, qkv_ref, w_qkv, 3)
    get_qkv.start()

    own = rows_at(p.s * rows, rows)
    inputs = tokens_ref[0].astype(F32)
    first[own] = norm_forward(inputs, gain_ref[0:1], bias_ref[0:1])[2]
    get_first = Gather(links, place, first, rows)
    get_first.start()
    source[rows_at(p.s * source_rows, source_rows)] = encoder_ref[0]
    get_source = Gather(links, place, source, source_rows)
    get_source.start()
    place_lens = links.slots(3)
    line = lax.broadcasted_iota(jnp.int32, (8, 128), 0)
    lens[pl.ds(p.s, 1)] = jnp.where(line < 4, target_ref[0], source_ref[0])[None]
    own_lens = lens.at[pl.ds(p.s, 1)]
    for step, other in enumerate((p.far, p.opp, p.sib)):
        links.push(place_lens + step, own_lens, own_lens, (other, p.c))
    for owner in range(STEPS):
        columns[:, owner * rows : (owner + 1) * rows] = column_positions(table_ref, owner, half)
    own_rows = row_positions(table_ref, p.c, half)
    valid = own_rows < target_ref[0]
    branch[own] = jnp.where(valid, cotangent_ref[0].astype(F32), 0.0).astype(BF16)
    get_cq = Columns(links, place, cq_ref, w_cq, 1)
    get_ckv = Columns(links, place, ckv_ref, w_ckv, 2)
    get_up = Columns(links, place, up_ref, w_up_out, 1, 4)

    get_qkv.relay()
    get_first.forward()
    get_source.forward()
    get_first.finish()
    get_source.finish()
    for made in links.saves:
        made.wait()
    links.saves = []
    get_qkv.finish()
    links.save(first, first_out)
    links.save(w_qkv, w_qkv_out)
    links.save(source, source_out)
    for step, other in enumerate((p.far, p.opp, p.sib)):
        links.take(place_lens + step, lens.at[pl.ds(other, 1)], (other, p.c))
    links.save(lens, lens_out)

    def project(block, carry):
        value = dot(first[rows_at(block * rows, rows)], w_qkv[...]).astype(BF16)
        for group in range(groups):
            for part in range(3):
                at = part * width + group * pair_width
                sent[block * groups + group, part] = value[:, at : at + pair_width]
        return carry

    lax.fori_loop(0, 4, project, 0)
    a2a = links.slots(STEPS)
    mine = rows_at(p.c * rows, rows)
    for step in range(1, STEPS):
        other = lax.rem(p.c + step, STEPS)
        links.push(a2a + step, sent.at[other], heads.at[:, mine], (p.s, other))
    keep = pltpu.make_async_copy(sent.at[p.c], heads.at[:, mine], local_sem.at[STEPS * 8 - 1])
    keep.start()
    get_cq.start()
    get_ckv.start()
    get_up.start(get_up.jobs[:2])
    get_branch = Gather(links, place, branch, rows)
    get_branch.start()
    keep.wait()
    get_cq.relay()
    get_ckv.relay()
    for step in range(1, STEPS):
        other = lax.rem(p.c + STEPS - step, STEPS)
        links.take(a2a + step, heads.at[:, rows_at(other * rows, rows)], (p.s, other))
    links.save(heads, heads_out)

    my_slot = lax.div(p.c, groups)
    my_group = lax.rem(p.c, groups)
    length = lens[pl.ds(my_slot, 1)][0, 0:1, 0:1]
    back = links.slots(STEPS)
    slot_rows = rows_at(my_slot * rows, rows)
    group_lanes = lanes_at(my_group * pair_width, pair_width)

    def back_copy(owner):
        return links.copy(
            back + p.c, mix_own.at[rows_at(owner * rows, rows)], mix.at[slot_rows, group_lanes], (p.s, owner)
        )

    def attend(block, peaks):
        at = rows_at(block * 2 * rows, 2 * rows)
        row_pos = jnp.concatenate(
            [row_positions(table_ref, 2 * block, half), row_positions(table_ref, 2 * block + 1, half)], axis=0
        )
        col_pos = columns[...]
        allowed = (col_pos <= row_pos) & (col_pos < length)
        ok = row_pos < length
        tops = []
        for head in range(pair_width // HD):
            cut = slice(head * HD, (head + 1) * HD)
            scores = dot(heads[0, at, cut], heads[1, :, cut], NT) * SCALE
            probs, top = softmax_rows(jnp.where(allowed, scores, masked_score))
            mix_own[at, cut] = dot(probs.astype(BF16), heads[2, :, cut]).astype(BF16)
            peak = jnp.max(jnp.where(ok, top, masked_score), axis=0, keepdims=True)
            tops.append(jnp.maximum(peaks[head], peak))
        return tuple(tops)

    low = jnp.full((1, 1), masked_score, F32)
    peaks = (low, low)
    for block in range(STEPS // 2):
        peaks = attend(block, peaks)
        for owner in (2 * block, 2 * block + 1):
            pl.when(p.c != owner)(back_copy(owner).start)
    for head in range(2):
        peak_out[head : head + 1] = jnp.broadcast_to(peaks[head], (1, 128))
    mix[slot_rows, group_lanes] = mix_own[mine]

    get_cq.finish()
    get_ckv.finish()
    for made in links.saves:
        made.wait()
    links.saves = []
    links.save(w_cq, w_cq_out)
    links.save(w_ckv, w_ckv_out)
    value = dot(source[...], w_ckv[...]).astype(BF16)
    for slot in range(4):
        kv_own[slot] = value[slot * source_rows : (slot + 1) * source_rows]
    own_keys = rows_at(p.c * source_rows, source_rows)
    kvs[:, own_keys] = kv_own[...]
    along, across = links.slots(4), links.slots(4)
    links.push(across, kv_own, kvs.at[:, own_keys], (p.s, p.pair))
    for step in range(1, 4):
        other = lax.rem(p.z + step, 4) * 2 + p.y
        links.push(along + step, kv_own, kvs.at[:, own_keys], (p.s, other))
    get_up.relay(get_up.jobs[:2])
    get_branch.forward()

    for owner in range(STEPS):

        @pl.when(p.c != owner)
        def _():
            lane = lanes_at((owner % groups) * pair_width, pair_width)
            links.take(
                back + owner, mix.at[pl.ds((owner // groups) * rows, rows), lane], (p.s, owner)
            )

    links.save(mix, mix_out)

    def boundary(index, left, weight, base, gather, store):
        def partial(block, piece):
            step = rows // PIECES
            return dot(left[rows_at(block * rows + piece * step, step)], weight[...])

        def then(piece, total):
            step = rows // PIECES
            cut = pl.ds(piece * step, step)
            value = base(piece) + total
            sums[index, cut] = value
            store[rows_at(p.s * rows + piece * step, step)] = norm_forward(
                value, gain_ref[index + 1 : index + 2], bias_ref[index + 1 : index + 2]
            )[2]
            gather.start(piece)

        Reduce(links, place, rs_out.at[index], rs_in.at[index], rows, PIECES).run(partial, then)

    step = rows // PIECES
    get_second = Gather(links, place, second, rows, PIECES)
    boundary(
        0,
        mix,
        out_ref,
        lambda piece: tokens_ref[0, piece * step : (piece + 1) * step].astype(F32),
        get_second,
        second,
    )
    for hop in range(1, 4):
        other = lax.rem(p.z + 4 - hop, 4) * 2 + p.y
        land = kvs.at[:, rows_at(other * source_rows, source_rows)]
        links.take(along + hop, land, (p.s, other))
        links.push(across + hop, land, land, (p.s, p.pair))
    get_up.start(get_up.jobs[2:])
    for piece in range(PIECES):
        get_second.forward(piece)
    for piece in range(PIECES):
        get_second.finish(piece)
    links.save(second, second_out)
    for hop in range(4):
        other = lax.rem(p.z + 4 - hop, 4) * 2 + 1 - p.y
        land = kvs.at[:, rows_at(other * source_rows, source_rows)]
        links.take(across + hop, land, (p.s, p.pair))
    links.save(kvs, kvs_out)

    keys = kvs.shape[1]

    def cross_attend(slot, peaks):
        at = rows_at(slot * rows, rows)
        asked = dot(second[at], w_cq[...]).astype(BF16)
        query[at] = asked
        limits = lens[pl.ds(slot, 1)]
        live = lax.broadcasted_iota(jnp.int32, (1, keys), 1) < limits[0, 4:5, 0:1]
        ok = own_rows < limits[0, 0:1, 0:1]
        tops = []
        for head in range(held):
            cut = slice(head * HD, (head + 1) * HD)
            vcut = slice(width + head * HD, width + (head + 1) * HD)
            scores = dot(asked[:, cut], kvs[slot, :, cut], NT) * SCALE
            probs, top = softmax_rows(jnp.where(live, scores, masked_score))
            cross[at, cut] = dot(probs.astype(BF16), kvs[slot, :, vcut]).astype(BF16)
            peak = jnp.max(jnp.where(ok, top, masked_score), axis=0, keepdims=True)
            tops.append(jnp.maximum(peaks[head], peak))
        return tuple(tops)

    peaks = lax.fori_loop(0, 4, cross_attend, (low,) * held)
    for head in range(held):
        peak_out[2 + head : 3 + head] = jnp.broadcast_to(peaks[head], (1, 128))
    links.save(query, query_out)
    links.save(cross, cross_out_ref)
    get_up.relay(get_up.jobs[2:])
    get_branch.finish()
    links.save(branch, branch_out)
    get_third = Gather(links, place, third, rows, PIECES)
    boundary(
        1, cross, co_ref, lambda piece: sums[0, piece * step : (piece + 1) * step], get_third, third
    )
    links.save(sums, sums_out)
    for piece in range(PIECES):
        get_third.forward(piece)
    for piece in range(PIECES):
        get_third.finish(piece)
    links.save(third, third_out)
    get_up.finish()
    for owner in range(STEPS):
        pl.when(p.c != owner)(back_copy(owner).wait_send)
    links.finish()


def forward_call(
    table, targets, sources, tokens, encoder, cotangent, qkv, out, cq, ckv, co, up, gain, bias
):
    rows, width = tokens.shape[1], out.shape[0]
    source_rows = encoder.shape[1]
    depth = tokens.shape[2]
    keys = 8 * source_rows
    any_space = pl.BlockSpec(memory_space=pl.ANY)
    vmem = pl.BlockSpec(memory_space=pltpu.VMEM)
    smem = pl.BlockSpec(memory_space=pltpu.SMEM)
    shapes = dict(
        first=((4 * rows, depth), BF16),
        second=((4 * rows, depth), BF16),
        third=((4 * rows, depth), BF16),
        branch=((4 * rows, depth), BF16),
        source=((4 * source_rows, depth), BF16),
        w_qkv=((depth, 3 * width), BF16),
        w_cq=((depth, width), BF16),
        w_ckv=((depth, 2 * width), BF16),
        w_up=((depth, up.shape[1] // 4), BF16),
        heads=((3, 8 * rows, 128), BF16),
        mix=((4 * rows, width), BF16),
        query=((4 * rows, width), BF16),
        kvs=((4, keys, 2 * width), BF16),
        cross=((4 * rows, width), BF16),
        sums=((2, rows, depth), F32),
        peak=((8, 128), F32),
        lens=((4, 8, 128), jnp.int32),
    )
    scratch = [
        shapes[name]
        for name in ("first", "second", "third", "branch", "source", "w_qkv", "w_cq", "w_ckv")
    ] + [
        ((8, 3, rows, 128), BF16),
        shapes["heads"],
        ((8 * rows, 128), BF16),
        shapes["mix"],
        shapes["query"],
        ((4, source_rows, 2 * width), BF16),
        shapes["kvs"],
        shapes["cross"],
        shapes["sums"],
        ((1, 8 * rows), jnp.int32),
        shapes["lens"],
        ((2, 3, rows, depth), BF16),
        ((2, 3, rows, depth), BF16),
    ]
    made = pl.pallas_call(
        forward_kernel,
        in_specs=[smem] * 3
        + [vmem] * 3
        + [any_space, vmem, any_space, any_space, vmem, any_space]
        + [vmem] * 2,
        out_specs=[vmem if name == "peak" else any_space for name in shapes],
        out_shape=[jax.ShapeDtypeStruct(*shape) for shape in shapes.values()],
        scratch_shapes=[pltpu.VMEM(*shape) for shape in scratch]
        + [
            pltpu.SemaphoreType.DMA((128,)),
            pltpu.SemaphoreType.DMA((128,)),
            pltpu.SemaphoreType.DMA((64,)),
        ],
        compiler_params=pltpu.CompilerParams(
            collective_id=0, has_side_effects=True, vmem_limit_bytes=60 * 2**20
        ),
        name="forward",
    )(table, targets, sources, tokens, encoder, cotangent, qkv, out, cq, ckv, co, up, gain, bias)
    return dict(zip(shapes, made))


class Sum:
    def __init__(self, links, place, full, into, away, result, lead=False, own=None):
        self.links, self.place, self.full, self.own = links, place, full, own
        self.into, self.away, self.result, self.lead = into, away, result, lead
        self.base = links.slots(7)
        self.near = place.z + 1 - 2 * lax.rem(place.z, 2)
        self.across = lax.rem(place.z + 2, 4)
        self.order = (lax.rem(self.near + 2, 4), self.across, self.near, place.z)

    def start(self, turns=(0, 1, 2, 3)):
        p = self.place
        for turn in turns:
            to = self.order[turn]
            src = self.full.at[to, 1 - p.y] if self.lead else self.full.at[:, to, 1 - p.y]
            self.links.push(self.base + turn, src, self.into.at[to], (p.s, p.pair))

    def turn(self, turns=(0, 1, 2, 3)):
        p, links, into, away = self.place, self.links, self.into, self.away
        for turn in turns:
            to = self.order[turn]
            links.take(self.base + turn, into.at[to], (p.s, p.pair))
            if turn == 1:
                links.take(self.base + 4, away.at[0], (p.s, self.near * 2 + p.y))

            def add(a, carry):
                if self.own is not None:
                    mine = self.own[to, a] if self.lead else self.own[a, to]
                else:
                    mine = self.full[to, p.y, a] if self.lead else self.full[a, to, p.y]
                total = mine.astype(F32) + into[to, a].astype(F32)
                if turn == 1:
                    total = total + away[0, a].astype(F32)
                into[to, a] = total.astype(BF16)
                return carry

            if turn < 3:
                lax.fori_loop(0, into.shape[1], add, 0)
                goal = self.across if turn == 1 else self.near
                links.push(
                    self.base + 4 + turn, into.at[to], away.at[turn], (p.s, goal * 2 + p.y)
                )

    def finish(self):
        p, links, into, away = self.place, self.links, self.into, self.away
        links.take(self.base + 5, away.at[1], (p.s, self.across * 2 + p.y))
        links.take(self.base + 6, away.at[2], (p.s, self.near * 2 + p.y))

        def add(a, carry):
            if self.own is not None:
                mine = self.own[p.z, a] if self.lead else self.own[a, p.z]
            else:
                mine = self.full[p.z, p.y, a] if self.lead else self.full[a, p.z, p.y]
            total = mine.astype(F32) + into[p.z, a].astype(F32)
            total = total + (away[1, a].astype(F32) + away[2, a].astype(F32))
            self.result[a] = total.astype(BF16)
            return carry

        lax.fori_loop(0, into.shape[1], add, 0)


class Exchange:
    def __init__(self, links, place, result, taken):
        self.links, self.place, self.result, self.taken = links, place, result, taken
        self.base = links.slots(3)
        self.others = (place.far, place.opp, place.sib)

    def start(self):
        p = self.place
        for step, other in enumerate(self.others):
            self.links.push(
                self.base + step,
                self.result.at[pl.ds(other, 1)],
                self.taken.at[pl.ds(p.s, 1)],
                (other, p.c),
            )
        self.taken[pl.ds(p.s, 1)] = self.result[pl.ds(p.s, 1)]

    def finish(self):
        for step, other in enumerate(self.others):
            self.links.take(
                self.base + step, self.taken.at[pl.ds(other, 1)], (other, self.place.c)
            )


def norm_terms_of(values):
    centered = values - jnp.mean(values, axis=-1, keepdims=True)
    spread = jnp.mean(centered * centered, axis=-1, keepdims=True)
    inverse = lax.rsqrt(spread + norm_eps)
    return centered * inverse, inverse


def backward_body(r):
    place, links = Place(), Links(r.send_sem, r.recv_sem, r.local_sem)
    p = place
    rows = r.tokens.shape[1]
    half = rows // 2
    width = r.w_cq.shape[1]
    source_rows = r.source.shape[0] // 4
    keys = r.kvs.shape[1]
    pair_width = r.heads.shape[2]
    held, groups = width // HD, width // pair_width
    depth = r.first.shape[1]
    step = rows // PIECES
    share = depth // 4

    loads = {}
    for name in r.loaded:
        loads[name] = pltpu.make_async_copy(
            getattr(r, name + "_hbm"), getattr(r, name), r.load_sem.at[len(loads)]
        )
        loads[name].start()

    def need(*wanted):
        for name in wanted:
            loads.pop(name).wait()

    place.greet()
    r.peaks_ctx[pl.ds(p.c, 1)] = r.peak[...][None]
    peak_base = links.slots(STEPS)
    own_peak = r.peaks_ctx.at[pl.ds(p.c, 1)]
    for hop in range(1, STEPS):
        links.push(peak_base + hop, own_peak, own_peak, (p.s, lax.rem(p.c + hop, STEPS)))

    down = Sum(links, place, r.down_full, r.down_into, r.down_away, r.down_result, True, r.down_own)
    up = Sum(links, place, r.up_full, r.up_into, r.up_away, r.up_result, False, r.up_own)
    own_down = links.save(r.down_full.at[:, p.y], r.down_own)
    own_up = links.save(r.up_full.at[:, :, p.y], r.up_own)
    links.saves = []
    up.start((0,))
    down.start((0,))
    up.start((1,))
    down.start((1,))

    own_rows = row_positions(r.table, p.c, half)
    r.norms[...] = jnp.zeros_like(r.norms)

    def add_norms(index, gain, bias):
        r.norms[index : index + 1] += gain[None]
        r.norms[index + 3 : index + 4] += bias[None]

    get_cross = Gather(links, place, r.cross_branch, rows, PIECES)

    def after_third(piece, total):
        cut = slice(piece * step, (piece + 1) * step)
        hat, inverse = norm_terms_of(r.sums[1, cut])
        back, gain, bias = norm_backward(total, hat, inverse, r.gain[2:3])
        add_norms(2, gain, bias)
        valid = own_rows[cut] < r.target[0]
        value = jnp.where(valid, r.cotangent[0, cut].astype(F32), 0.0) + back
        r.grad_sum[cut] = value
        r.cross_branch[rows_at(p.s * rows + piece * step, step)] = value.astype(BF16)
        get_cross.start(piece)

    def stored(ref):
        return lambda block, piece: ref[rows_at(block * rows + piece * step, step)].astype(F32)

    need("sums")
    Reduce(links, place, r.rs_out.at[0], r.rs_in.at[0], rows, PIECES).run(
        stored(r.grad_third), after_third
    )
    for hop in range(1, STEPS):
        other = lax.rem(p.c + STEPS - hop, STEPS)
        links.take(peak_base + hop, r.peaks_ctx.at[pl.ds(other, 1)], (p.s, other))
    best = []
    for group in range(groups):
        tile = r.peaks_ctx[group]
        for owner in range(group + groups, STEPS, groups):
            tile = jnp.maximum(tile, r.peaks_ctx[owner])
        best.append(tile)
    everyone = best[0]
    for tile in best[1:]:
        everyone = jnp.maximum(everyone, tile)
    mine = jnp.concatenate([tile[0:2] for tile in best] + [everyone[2 : 2 + held]], axis=0)
    r.peaks_seq[pl.ds(p.s, 1)] = mine[None]
    peak_seq = links.slots(3)
    own_peak = r.peaks_seq.at[pl.ds(p.s, 1)]
    for hop, other in enumerate((p.far, p.opp, p.sib)):
        links.push(peak_seq + hop, own_peak, own_peak, (other, p.c))

    for piece in range(PIECES):
        get_cross.forward(piece)
    need("w_co", "cross", "query", "kvs", "w_cq", "second")
    for piece in range(PIECES):
        get_cross.finish(piece)

    def cross_back(slot, carry):
        at = rows_at(slot * rows, rows)
        grad_rows = dot(r.cross_branch[at], r.w_co[...], NT).astype(BF16)
        live = lax.broadcasted_iota(jnp.int32, (1, keys), 1) < r.lens[pl.ds(slot, 1)][0, 4:5, 0:1]
        for head in range(held):
            cut = slice(head * HD, (head + 1) * HD)
            vcut = slice(width + head * HD, width + (head + 1) * HD)
            asked, grad = r.query[at, cut], grad_rows[:, cut]
            scores = dot(asked, r.kvs[slot, :, cut], NT) * SCALE
            probs, _ = softmax_rows(jnp.where(live, scores, masked_score))
            dprobs = dot(grad, r.kvs[slot, :, vcut], NT)
            delta = jnp.sum(probs * dprobs, axis=-1, keepdims=True)
            dscores = (probs * (dprobs - delta)).astype(BF16)
            r.dquery[at, cut] = (dot(dscores, r.kvs[slot, :, cut]) * SCALE).astype(BF16)
            shape = (4, 2, source_rows, HD)
            r.dkv_full[slot, :, :, :, cut] = (
                (dot(dscores, asked, TN) * SCALE).astype(BF16).reshape(shape)
            )
            r.dkv_full[slot, :, :, :, vcut] = (
                dot(probs.astype(BF16), grad, TN).astype(BF16).reshape(shape)
            )
        return carry

    lax.fori_loop(0, 4, cross_back, 0)
    dkv = Sum(links, place, r.dkv_full, r.dkv_into, r.dkv_away, r.dkv_result)
    own_up.wait()
    own_down.wait()
    up.turn((0,))
    up.start((2,))

    get_self = Gather(links, place, r.self_branch, rows, PIECES)

    def after_second(piece, total):
        cut = slice(piece * step, (piece + 1) * step)
        hat, inverse = norm_terms_of(r.sums[0, cut])
        back, gain, bias = norm_backward(total, hat, inverse, r.gain[1:2])
        add_norms(1, gain, bias)
        value = r.grad_sum[cut] + back
        r.grad_sum[cut] = value
        r.self_branch[rows_at(p.s * rows + piece * step, step)] = value.astype(BF16)
        get_self.start(piece)

    Reduce(links, place, r.rs_out.at[1], r.rs_in.at[1], rows, PIECES).run(
        lambda block, piece: dot(
            r.dquery[rows_at(block * rows + piece * step, step)], r.w_cq[...], NT
        ),
        after_second,
    )

    def row_grad(left, right, full):
        def one(part, carry):
            lanes = lanes_at(part * 128, 128)
            value = dot(left[:, lanes], right[...], TN).astype(BF16)
            full[pl.ds(part * 2, 2)] = value.reshape((2, 2) + full.shape[2:])
            return carry

        lax.fori_loop(0, left.shape[1] // 128, one, 0)

    def column_grad(left, right, full):
        def one(block, carry):
            lanes = lanes_at(block * share, share)
            value = dot(left[:, lanes], right(), TN).astype(BF16)
            full[pl.ds(block, 1)] = value.reshape((1,) + full.shape[1:])
            return carry

        lax.fori_loop(0, 4, one, 0)

    row_grad(r.cross, r.cross_branch, r.co_full)
    for piece in range(PIECES):
        get_self.forward(piece)
    column_grad(r.second, lambda: r.dquery[...], r.cq_full)
    for piece in range(PIECES):
        get_self.finish(piece)
    down.turn((0,))

    need("w_out", "heads", "mix")

    def mix_back(slot, carry):
        value = dot(r.self_branch[rows_at(slot * rows, rows)], r.w_out[...], NT).astype(BF16)
        for group in range(groups):
            r.gsent[slot * groups + group] = value[:, group * pair_width : (group + 1) * pair_width]
        return carry

    lax.fori_loop(0, 4, mix_back, 0)
    a2a = links.slots(STEPS)
    mine_rows = rows_at(p.c * rows, rows)
    for hop in range(1, STEPS):
        other = lax.rem(p.c + hop, STEPS)
        links.push(a2a + hop, r.gsent.at[other], r.gheads.at[mine_rows], (p.s, other))
    r.gheads[mine_rows] = r.gsent[p.c]
    down.start((2,))
    for owner in range(STEPS):
        r.columns[:, owner * rows : (owner + 1) * rows] = column_positions(r.table, owner, half)
    row_grad(r.mix, r.self_branch, r.so_full)
    up.turn((1,))
    co = Sum(links, place, r.co_full, r.co_into, r.co_away, r.co_result, True)
    cq = Sum(links, place, r.cq_full, r.cq_into, r.cq_away, r.cq_result)
    so = Sum(links, place, r.so_full, r.so_into, r.so_away, r.so_result, True)
    for hop in range(1, STEPS):
        other = lax.rem(p.c + STEPS - hop, STEPS)
        links.take(a2a + hop, r.gheads.at[rows_at(other * rows, rows)], (p.s, other))

    my_slot, my_group = lax.div(p.c, groups), lax.rem(p.c, groups)
    length = r.lens[pl.ds(my_slot, 1)][0, 0:1, 0:1]
    slot_rows = rows_at(my_slot * rows, rows)
    group_lanes = lanes_at(my_group * pair_width, pair_width)
    back_q, back_kv = links.slots(STEPS), links.slots(STEPS)
    r.acc[...] = jnp.zeros_like(r.acc)

    def q_copy(owner):
        at = rows_at(owner * rows, rows)
        return links.copy(
            back_q + p.c, r.dq_own.at[at], r.dproj.at[0, slot_rows, group_lanes], (p.s, owner)
        )

    def kv_copy(owner):
        at = rows_at(owner * rows, rows)
        return links.copy(
            back_kv + p.c,
            r.dkv_own.at[:, at],
            r.dproj.at[pl.ds(1, 2), slot_rows, group_lanes],
            (p.s, owner),
        )

    def attend_back(block, carry):
        at = rows_at(block * 2 * rows, 2 * rows)
        row_pos = jnp.concatenate(
            [
                row_positions(r.table, 2 * block, half),
                row_positions(r.table, 2 * block + 1, half),
            ],
            axis=0,
        )
        col_pos = r.columns[...]
        allowed = (col_pos <= row_pos) & (col_pos < length)
        for head in range(pair_width // HD):
            cut = slice(head * HD, (head + 1) * HD)
            asked, grad = r.heads[0, at, cut], r.gheads[at, cut]
            scores = dot(asked, r.heads[1, :, cut], NT) * SCALE
            probs, _ = softmax_rows(jnp.where(allowed, scores, masked_score))
            dprobs = dot(grad, r.heads[2, :, cut], NT)
            delta = jnp.sum(probs * dprobs, axis=-1, keepdims=True)
            dscores = (probs * (dprobs - delta)).astype(BF16)
            r.dq_own[at, cut] = (dot(dscores, r.heads[1, :, cut]) * SCALE).astype(BF16)
            r.acc[0, :, cut] += dot(dscores, asked, TN)
            r.acc[1, :, cut] += dot(probs.astype(BF16), grad, TN)
        return carry

    for block in range(STEPS // 2):
        attend_back(block, 0)
        for owner in (2 * block, 2 * block + 1):
            pl.when(p.c != owner)(q_copy(owner).start)
    for owner in range(STEPS):
        at = rows_at(owner * rows, rows)
        r.dkv_own[0, at] = (r.acc[0, at] * SCALE).astype(BF16)
        r.dkv_own[1, at] = r.acc[1, at].astype(BF16)
        pl.when(p.c != owner)(kv_copy(owner).start)
    r.dproj[0, slot_rows, group_lanes] = r.dq_own[mine_rows]
    r.dproj[pl.ds(1, 2), slot_rows, group_lanes] = r.dkv_own[:, mine_rows]

    dkv.start()
    up.start((3,))
    down.start((3,))
    co.start()
    cq.start()
    so.start()
    down.turn((1,))
    up.turn((2,))
    down.turn((2,))

    def after_output(piece, total):
        cut = slice(piece * step, (piece + 1) * step)
        valid = own_rows[cut] < r.target[0]
        r.output[cut] = jnp.where(valid, r.sums[1, cut] + total, 0.0).astype(BF16)

    Reduce(links, place, r.rs_out.at[2], r.rs_in.at[2], rows, PIECES).run(
        stored(r.third_part), after_output
    )

    dkv.turn()
    need("w_qkv", "first")
    for owner in range(STEPS):

        @pl.when(p.c != owner)
        def _():
            at = pl.ds((owner // groups) * rows, rows)
            lane = lanes_at((owner % groups) * pair_width, pair_width)
            links.take(back_q + owner, r.dproj.at[0, at, lane], (p.s, owner))
            links.take(back_kv + owner, r.dproj.at[pl.ds(1, 2), at, lane], (p.s, owner))

    def first_partial(block, piece):
        at = rows_at(block * rows + piece * step, step)
        total = dot(r.dproj[0, at], r.w_qkv[:, :width], NT)
        total += dot(r.dproj[1, at], r.w_qkv[:, width : 2 * width], NT)
        return total + dot(r.dproj[2, at], r.w_qkv[:, 2 * width :], NT)

    def after_first(piece, total):
        cut = slice(piece * step, (piece + 1) * step)
        hat, inverse = norm_terms_of(r.tokens[0, cut].astype(F32))
        back, gain, bias = norm_backward(total, hat, inverse, r.gain[0:1])
        add_norms(0, gain, bias)
        r.grad_inputs[cut] = r.grad_sum[cut] + back

    def qkv_grad(block, carry):
        lanes = lanes_at(block * share, share)
        left = r.first[:, lanes]
        for part in range(3):
            value = dot(left, r.dproj[part], TN).astype(BF16)
            r.qkv_full[pl.ds(block, 1), :, :, :, part * width : (part + 1) * width] = value.reshape(
                (1,) + r.qkv_full.shape[1:4] + (width,)
            )
        return carry

    lax.fori_loop(0, 4, qkv_grad, 0)
    qkv = Sum(links, place, r.qkv_full, r.qkv_into, r.qkv_away, r.qkv_result)
    qkv.start()
    Reduce(links, place, r.rs_out.at[3], r.rs_in.at[3], rows, PIECES).run(first_partial, after_first)

    norm_seq, norm_ctx = links.slots(3), links.slots(STEPS)
    others = (p.far, p.opp, p.sib)
    for hop, other in enumerate(others):
        links.push(
            norm_seq + hop,
            r.norms.at[:, lanes_at(other * share, share)],
            r.norms_seq.at[pl.ds(p.s, 1)].at[0],
            (other, p.c),
        )
    up.turn((3,))
    down.turn((3,))

    def after_encoder(piece, total):
        r.grad_source[...] = total

    need("w_ckv", "source")
    dkv.finish()
    r.dsource[...] = r.dkv_result[...].reshape(4 * source_rows, 2 * width)
    column_grad(r.source, lambda: r.dsource[...], r.ckv_full)
    ckv = Sum(links, place, r.ckv_full, r.ckv_into, r.ckv_away, r.ckv_result)
    ckv.start()
    Reduce(links, place, r.enc_out, r.enc_in, source_rows).run(
        lambda block, piece: dot(
            r.dsource[rows_at(block * source_rows, source_rows)], r.w_ckv[...], NT
        ),
        after_encoder,
    )
    for job in (co, cq, so):
        job.turn()
    total = r.norms[:, lanes_at(p.s * share, share)]
    for hop, other in enumerate(others):
        links.take(norm_seq + hop, r.norms_seq.at[pl.ds(other, 1)].at[0], (other, p.c))
        total = total + r.norms_seq[pl.ds(other, 1)][0]
    r.norms_ctx[pl.ds(p.c, 1)] = total[None]
    own_norms = r.norms_ctx.at[pl.ds(p.c, 1)]
    for hop in range(1, STEPS):
        links.push(norm_ctx + hop, own_norms, own_norms, (p.s, lax.rem(p.c + hop, STEPS)))
    for job in (qkv, ckv):
        job.turn()
    sums = {}
    up.finish()
    sums["up"] = Exchange(links, place, r.up_result, r.up_taken)
    sums["up"].start()
    down.finish()
    links.save(r.down_result, r.down_hbm)
    for job in (co, so):
        job.finish()
    for name, job in (("cq", cq), ("ckv", ckv), ("qkv", qkv)):
        job.finish()
        sums[name] = Exchange(links, place, getattr(r, name + "_result"), getattr(r, name + "_taken"))
        sums[name].start()
    for hop in range(1, STEPS):
        other = lax.rem(p.c + STEPS - hop, STEPS)
        links.take(norm_ctx + hop, r.norms_ctx.at[pl.ds(other, 1)], (p.s, other))
    total = r.norms_ctx[0]
    for owner in range(1, STEPS):
        total = total + r.norms_ctx[owner]
    r.norm_sum[...] = total
    for hop, other in enumerate(others):
        links.take(peak_seq + hop, r.peaks_seq.at[pl.ds(other, 1)], (other, p.c))
    for job in sums.values():
        job.finish()
    for owner in range(STEPS):
        pl.when(p.c != owner)(q_copy(owner).wait_send)
        pl.when(p.c != owner)(kv_copy(owner).wait_send)
    links.finish()


def backward_call(kept, given):
    rows, depth = given["tokens"].shape[1:]
    width = kept["w_cq"].shape[1]
    source_rows = kept["source"].shape[0] // 4
    keys = kept["kvs"].shape[1]
    share = depth // 32
    hidden = kept["w_up"].shape[1]
    any_space = pl.BlockSpec(memory_space=pl.ANY)
    vmem = pl.BlockSpec(memory_space=pltpu.VMEM)
    smem = pl.BlockSpec(memory_space=pltpu.SMEM)
    inputs = dict(
        table=(smem, given["table"]),
        target=(smem, given["target"]),
        tokens=(vmem, given["tokens"]),
        cotangent=(vmem, given["cotangent"]),
        gain=(vmem, given["gain"]),
        peak=(vmem, kept["peak"]),
        lens=(vmem, kept["lens"]),
        grad_third=(vmem, given["grad_third"]),
        third_part=(vmem, given["third_part"]),
        up_full=(any_space, given["grad_up"].reshape(4, 4, 2, share, hidden)),
        down_full=(any_space, given["grad_down"].reshape(4, 2, hidden // (8 * share), share, depth)),
    )
    loaded = dict(
        sums=kept["sums"],
        w_co=given["cross_out"],
        cross=kept["cross"],
        query=kept["query"],
        kvs=kept["kvs"],
        w_cq=kept["w_cq"],
        second=kept["second"],
        w_out=given["self_out"],
        heads=kept["heads"],
        mix=kept["mix"],
        w_ckv=kept["w_ckv"],
        source=kept["source"],
        w_qkv=kept["w_qkv"],
        first=kept["first"],
    )
    for name, value in loaded.items():
        inputs[name + "_hbm"] = (any_space, value)
    outs = dict(
        output=((rows, depth), BF16),
        grad_inputs=((rows, depth), F32),
        grad_source=((source_rows, depth), F32),
        down_hbm=((hidden // (8 * share), share, depth), BF16),
        co_result=((1, share, depth), BF16),
        so_result=((1, share, depth), BF16),
        up_taken=((4, share, hidden), BF16),
        cq_taken=((4, share, width), BF16),
        ckv_taken=((4, share, 2 * width), BF16),
        qkv_taken=((4, share, 3 * width), BF16),
        norm_sum=((8, depth // 4), F32),
        peaks_seq=((4, 8, 128), F32),
    )
    down_blocks = hidden // (8 * share)
    scratch = {name: (value.shape, value.dtype) for name, value in loaded.items()}
    scratch |= dict(
        down_own=((4, down_blocks, share, depth), BF16),
        down_into=((4, down_blocks, share, depth), BF16),
        down_away=((3, down_blocks, share, depth), BF16),
        down_result=((down_blocks, share, depth), BF16),
        up_own=((4, 4, share, hidden), BF16),
        up_into=((4, 4, share, hidden), BF16),
        up_away=((3, 4, share, hidden), BF16),
        up_result=((4, share, hidden), BF16),
        peaks_ctx=((8, 8, 128), F32),
        norms=((8, depth), F32),
        norms_seq=((4, 8, depth // 4), F32),
        norms_ctx=((8, 8, depth // 4), F32),
        cross_branch=((4 * rows, depth), BF16),
        self_branch=((4 * rows, depth), BF16),
        grad_sum=((rows, depth), F32),
        rs_out=((4, 3, rows, depth), BF16),
        rs_in=((4, 3, rows, depth), BF16),
        enc_out=((3, source_rows, depth), BF16),
        enc_in=((3, source_rows, depth), BF16),
        dquery=((4 * rows, width), BF16),
        dsource=((4 * source_rows, 2 * width), BF16),
        gsent=((8, rows, 128), BF16),
        gheads=((8 * rows, 128), BF16),
        columns=((1, 8 * rows), jnp.int32),
        acc=((2, 8 * rows, 128), F32),
        dq_own=((8 * rows, 128), BF16),
        dkv_own=((2, 8 * rows, 128), BF16),
        dproj=((3, 4 * rows, width), BF16),
    )
    for name in ("co", "so"):
        scratch[name + "_full"] = ((4, 2, 1, share, depth), BF16)
        scratch[name + "_into"] = ((4, 1, share, depth), BF16)
        scratch[name + "_away"] = ((3, 1, share, depth), BF16)
    for name, columns, r in (
        ("cq", width, share),
        ("ckv", 2 * width, share),
        ("qkv", 3 * width, share),
        ("dkv", 2 * width, source_rows),
    ):
        scratch[name + "_full"] = ((4, 4, 2, r, columns), BF16)
        scratch[name + "_into"] = ((4, 4, r, columns), BF16)
        scratch[name + "_away"] = ((3, 4, r, columns), BF16)
        scratch[name + "_result"] = ((4, r, columns), BF16)
    sems = dict(send_sem=224, recv_sem=224, local_sem=4, load_sem=len(loaded))
    names = list(inputs) + list(outs) + list(scratch) + list(sems)

    def kernel(*refs):
        held = dict(zip(names, refs), loaded=tuple(loaded))
        backward_body(type("Refs", (), held))

    made = pl.pallas_call(
        kernel,
        in_specs=[spec for spec, _ in inputs.values()],
        out_specs=[any_space if name == "down_hbm" else vmem for name in outs],
        out_shape=[jax.ShapeDtypeStruct(*shape) for shape in outs.values()],
        scratch_shapes=[pltpu.VMEM(*shape) for shape in scratch.values()]
        + [pltpu.SemaphoreType.DMA((count,)) for count in sems.values()],
        compiler_params=pltpu.CompilerParams(
            collective_id=1, has_side_effects=True, vmem_limit_bytes=60 * 2**20
        ),
        name="backward",
    )(*[value for _, value in inputs.values()])
    return dict(zip(outs, made))


def finish_kernel(
    clip_ref,
    peaks_ref,
    norm_ref,
    qkv_w,
    cq_w,
    ckv_w,
    output_ref,
    inputs_ref,
    source_ref,
    down_ref,
    co_ref,
    so_ref,
    up_ref,
    cq_ref,
    ckv_ref,
    qkv_ref,
    output_out,
    inputs_out,
    source_out,
    qkv_out,
    so_out,
    cq_out,
    ckv_out,
    co_out,
    up_out,
    down_out,
    gain_out,
    bias_out,
    self_out,
    cross_out,
):
    output_out[0] = output_ref[...]
    inputs_out[0] = inputs_ref[...]
    source_out[0] = source_ref[...]
    share = so_out.shape[0]
    so_out[...] = so_ref[0].astype(F32)
    co_out[...] = co_ref[0].astype(F32)
    for block in range(down_ref.shape[0]):
        down_out[block * share : (block + 1) * share] = down_ref[block].astype(F32)

    def columns(out, taken, parts):
        whole, width = out.shape[1] // parts, out.shape[1] // (4 * parts)
        for owner in range(4):
            for part in range(parts):
                at = part * whole + owner * width
                out[:, at : at + width] = taken[owner, :, part * width : (part + 1) * width].astype(
                    F32
                )

    columns(up_out, up_ref, 1)
    columns(cq_out, cq_ref, 1)
    columns(ckv_out, ckv_ref, 2)
    columns(qkv_out, qkv_ref, 3)
    spread = gain_out.shape[1]
    turned = pltpu.roll(norm_ref[...], norm_ref.shape[1] - lax.axis_index("ctx") * spread, 1)
    gain_out[...] = turned[0:3, :spread]
    bias_out[...] = turned[3:6, :spread]
    lane = lax.broadcasted_iota(jnp.int32, (1, 128), 1)
    held = peaks_ref.shape[1] // 2
    for owner in range(4):
        for two in range(held // 2):
            head = owner * held + two * 2
            at = slice(head * HD, head * HD + 128)
            for kind, jobs in (
                (0, ((self_out, qkv_w, 0, 0), (self_out, qkv_w, H * HD, H * HD))),
                (1, ((cross_out, cq_w, 0, 0), (cross_out, ckv_w, 0, H * HD))),
            ):
                top = [peaks_ref[owner, kind * held + two * 2 + i : kind * held + two * 2 + i + 1] for i in (0, 1)]
                limit = [clip_ref[kind, head + i] for i in (0, 1)]
                limits = jnp.where(lane < HD, limit[0], limit[1])
                tops = jnp.where(lane < HD, top[0], top[1])
                factor = jnp.sqrt(limits / jnp.maximum(tops, limits))
                for out, weight, start, goal in jobs:
                    out[:, goal + head * HD : goal + head * HD + 128] = (
                        weight[:, start + head * HD : start + head * HD + 128].astype(F32) * factor
                    ).astype(BF16)


def finish_call(made, given):
    rows, depth = given["tokens"].shape[1:]
    hidden = given["mlp_up"].shape[1]
    source_rows, share = made["grad_source"].shape[0], made["so_result"].shape[1]
    columns = H * HD
    weight_rows = given["self_qkv"].shape[0]
    shapes = [
        ((1, rows, depth), BF16),
        ((1, rows, depth), F32),
        ((1, source_rows, depth), F32),
        ((share, 3 * columns), F32),
        ((share, depth), F32),
        ((share, columns), F32),
        ((share, 2 * columns), F32),
        ((share, depth), F32),
        ((share, hidden), F32),
        ((hidden // 32, depth), F32),
        ((3, share), F32),
        ((3, share), F32),
        ((weight_rows, 2 * columns), BF16),
        ((weight_rows, 2 * columns), BF16),
    ]
    vmem = pl.BlockSpec(memory_space=pltpu.VMEM)
    return pl.pallas_call(
        finish_kernel,
        in_specs=[pl.BlockSpec(memory_space=pltpu.SMEM)] + [vmem] * 15,
        out_specs=[vmem] * len(shapes),
        out_shape=[jax.ShapeDtypeStruct(*shape) for shape in shapes],
        compiler_params=pltpu.CompilerParams(vmem_limit_bytes=60 * 2**20),
        name="finish",
    )(
        given["clip"],
        made["peaks_seq"],
        made["norm_sum"],
        given["self_qkv"],
        given["cross_q"],
        given["cross_kv"],
        made["output"],
        made["grad_inputs"],
        made["grad_source"],
        made["down_hbm"],
        made["co_result"],
        made["so_result"],
        made["up_taken"],
        made["cq_taken"],
        made["ckv_taken"],
        made["qkv_taken"],
    )


def fast_device(
    tokens,
    encoder_states,
    cotangent,
    target_lengths,
    source_lengths,
    block_table,
    self_qkv,
    self_out,
    cross_q,
    cross_kv,
    cross_out,
    mlp_up,
    mlp_down,
    norm_gain,
    norm_bias,
    clip_limit,
):
    kept = forward_call(
        block_table,
        target_lengths,
        source_lengths,
        tokens,
        encoder_states,
        cotangent,
        self_qkv,
        self_out,
        cross_q,
        cross_kv,
        cross_out,
        mlp_up,
        norm_gain,
        norm_bias,
    )
    third_low, mlp_branch, w_up = kept["third"], kept["branch"], kept["w_up"]
    hidden_pre = dot(third_low, w_up)
    hidden_act, gelu_back = jax.vjp(jax.nn.gelu, hidden_pre)
    hidden_low = hidden_act.astype(BF16)
    grad_pre = gelu_back(dot(mlp_branch, mlp_down, NT))[0].astype(BF16)
    given = dict(
        table=block_table,
        target=target_lengths,
        tokens=tokens,
        cotangent=cotangent,
        gain=norm_gain,
        grad_third=dot(grad_pre, w_up, NT).astype(BF16),
        third_part=dot(hidden_low, mlp_down).astype(BF16),
        grad_up=dot(third_low, grad_pre, TN).astype(BF16),
        grad_down=dot(hidden_low, mlp_branch, TN).astype(BF16),
        cross_out=cross_out,
        self_out=self_out,
        self_qkv=self_qkv,
        cross_q=cross_q,
        cross_kv=cross_kv,
        mlp_up=mlp_up,
        clip=clip_limit,
    )
    made = backward_call(kept, given)
    held = H // 4
    tops = made["peaks_seq"][:, :, 0].reshape(4, 2, held).transpose(1, 0, 2).reshape(2, H)
    return (*finish_call(made, given), tops)


def solution(mesh):
    body = fast_device if fast_fits(mesh) else general_device
    return jax.shard_map(
        body,
        mesh=mesh,
        in_specs=(
            P("seq", "ctx", None),
            P("seq", "ctx", None),
            P("seq", "ctx", None),
            P("seq"),
            P("seq"),
            P(),
            P("seq", None),
            P("seq", None),
            P("seq", None),
            P("seq", None),
            P("seq", None),
            P("seq", None),
            P("seq", None),
            P(),
            P(),
            P(),
        ),
        out_specs=(
            P("seq", "ctx", None),
            P("seq", "ctx", None),
            P("seq", "ctx", None),
            P(("seq", "ctx"), None),
            P(("seq", "ctx"), None),
            P(("seq", "ctx"), None),
            P(("seq", "ctx"), None),
            P(("seq", "ctx"), None),
            P(("seq", "ctx"), None),
            P(("seq", "ctx"), None),
            P(None, ("seq", "ctx")),
            P(None, ("seq", "ctx")),
            P("seq", None),
            P("seq", None),
            P(),
        ),
        check_vma=False,
    )
```

```python
import functools

import jax
import jax.numpy as jnp
from jax import lax
from jax.experimental import pallas as pl
from jax.experimental.pallas import tpu as pltpu
from jax.sharding import PartitionSpec as P

H = 16
HD = 64


masked_score = -1000000000.0
norm_eps = 1e-05


def block_size(count):
    return max((step for step in range(1, min(count, 512) + 1) if count % step == 0))


def layer_norm(values, gain, bias):
    centered = values - jnp.mean(values, axis=-1, keepdims=True)
    spread = jnp.mean(centered * centered, axis=-1, keepdims=True)
    return centered * lax.rsqrt(spread + norm_eps) * gain + bias


def allowed_pairs(query_pos, key_pos, key_limit, causal):
    allowed = jnp.broadcast_to(
        (key_pos < key_limit)[None, :], (query_pos.shape[0], key_pos.shape[0])
    )
    if causal:
        allowed = allowed & (key_pos[None, :] <= query_pos[:, None])
    return allowed


def head_scores(query_heads, key_rows):
    key_heads = key_rows.reshape(key_rows.shape[0], H, HD)
    return jnp.einsum(
        "qhd,khd->hqk", query_heads, key_heads, preferred_element_type=jnp.float32
    ) * HD ** (-0.5)


def softmax_stats(query_heads, kv_rows, key_pos, query_pos, query_ok, key_limit, causal):
    count = kv_rows.shape[0]
    step = block_size(count)
    width = H * HD
    rows = query_heads.shape[0]

    def softmax_visit(carry, block):
        top, total, peak = carry
        block_rows, block_pos = block
        allowed = allowed_pairs(query_pos, block_pos, key_limit, causal)
        scores = jnp.where(
            allowed[None], head_scores(query_heads, block_rows[:, :width]), masked_score
        )
        new_top = jnp.maximum(top, jnp.max(scores, axis=-1))
        total = total * jnp.exp(top - new_top) + jnp.sum(
            jnp.exp(scores - new_top[..., None]), axis=-1
        )
        counted = jnp.where((allowed & query_ok[:, None])[None], scores, masked_score)
        peak = jnp.maximum(peak, jnp.max(counted, axis=(1, 2)))
        return ((new_top, total, peak), None)

    start = (
        jnp.full((H, rows), -jnp.inf, jnp.float32),
        jnp.zeros((H, rows), jnp.float32),
        jnp.full((H,), masked_score, jnp.float32),
    )
    blocks = (kv_rows.reshape(count // step, step, 2 * width), key_pos.reshape(count // step, step))
    return lax.scan(softmax_visit, start, blocks)[0]


def attend_values(query_heads, kv_rows, key_pos, query_pos, key_limit, causal, top, total):
    count = kv_rows.shape[0]
    step = block_size(count)
    width = H * HD
    rows = query_heads.shape[0]

    def attend_visit(acc, block):
        block_rows, block_pos = block
        allowed = allowed_pairs(query_pos, block_pos, key_limit, causal)
        scores = jnp.where(
            allowed[None], head_scores(query_heads, block_rows[:, :width]), masked_score
        )
        weights = (jnp.exp(scores - top[..., None]) / total[..., None]).astype(jnp.bfloat16)
        value_heads = block_rows[:, width:].reshape(step, H, HD)
        return (
            acc
            + jnp.einsum("hqk,khd->qhd", weights, value_heads, preferred_element_type=jnp.float32),
            None,
        )

    blocks = (kv_rows.reshape(count // step, step, 2 * width), key_pos.reshape(count // step, step))
    acc = lax.scan(attend_visit, jnp.zeros((rows, H, HD), jnp.float32), blocks)[0]
    return acc.reshape(rows, width)


def query_grads(
    query_heads, kv_rows, key_pos, query_pos, key_limit, causal, top, total, grad_heads, delta
):
    count = kv_rows.shape[0]
    step = block_size(count)
    width = H * HD
    rows = query_heads.shape[0]

    def query_visit(acc, block):
        block_rows, block_pos = block
        allowed = allowed_pairs(query_pos, block_pos, key_limit, causal)
        scores = jnp.where(
            allowed[None], head_scores(query_heads, block_rows[:, :width]), masked_score
        )
        probs = jnp.exp(scores - top[..., None]) / total[..., None]
        value_heads = block_rows[:, width:].reshape(step, H, HD)
        dprobs = jnp.einsum(
            "qhd,khd->hqk", grad_heads, value_heads, preferred_element_type=jnp.float32
        )
        dscores = (probs * (dprobs - delta[..., None])).astype(jnp.bfloat16)
        key_heads = block_rows[:, :width].reshape(step, H, HD)
        return (
            acc
            + jnp.einsum("hqk,khd->qhd", dscores, key_heads, preferred_element_type=jnp.float32),
            None,
        )

    blocks = (kv_rows.reshape(count // step, step, 2 * width), key_pos.reshape(count // step, step))
    acc = lax.scan(query_visit, jnp.zeros((rows, H, HD), jnp.float32), blocks)[0]
    return acc.reshape(rows, width) * HD ** (-0.5)


def key_grads(
    query_heads,
    kv_rows,
    key_pos,
    query_pos,
    key_limit,
    causal,
    top,
    total,
    grad_heads,
    delta,
    start,
    count,
):
    step = block_size(count)
    width = H * HD

    def piece(index):
        offset = start + index * step
        block_rows = lax.dynamic_slice_in_dim(kv_rows, offset, step, 0)
        block_pos = lax.dynamic_slice_in_dim(key_pos, offset, step, 0)
        allowed = allowed_pairs(query_pos, block_pos, key_limit, causal)
        scores = jnp.where(
            allowed[None], head_scores(query_heads, block_rows[:, :width]), masked_score
        )
        probs = jnp.exp(scores - top[..., None]) / total[..., None]
        value_heads = block_rows[:, width:].reshape(step, H, HD)
        dprobs = jnp.einsum(
            "qhd,khd->hqk", grad_heads, value_heads, preferred_element_type=jnp.float32
        )
        dscores = (probs * (dprobs - delta[..., None])).astype(jnp.bfloat16)
        dkeys = jnp.einsum(
            "hqk,qhd->khd", dscores, query_heads, preferred_element_type=jnp.float32
        ).reshape(step, width) * HD ** (-0.5)
        dvalues = jnp.einsum(
            "hqk,qhd->khd",
            probs.astype(jnp.bfloat16),
            grad_heads,
            preferred_element_type=jnp.float32,
        ).reshape(step, width)
        return jnp.concatenate([dkeys, dvalues], axis=1)

    return lax.map(piece, jnp.arange(count // step, dtype=jnp.int32)).reshape(count, 2 * width)


def split_rows(grad, seq_count, ctx_count):
    return grad.reshape(
        (seq_count, ctx_count, grad.shape[0] // (seq_count * ctx_count)) + grad.shape[1:]
    )


def join_rows(grad):
    return grad.reshape((grad.shape[2],) + grad.shape[3:])


def general_device(
    tokens,
    encoder_states,
    cotangent,
    target_lengths,
    source_lengths,
    block_table,
    self_qkv,
    self_out,
    cross_q,
    cross_kv,
    cross_out,
    mlp_up,
    mlp_down,
    norm_gain,
    norm_bias,
    clip_limit,
):
    rows = tokens.shape[1]
    width = H * HD
    half = rows // 2
    source_rows = encoder_states.shape[1]
    seq_count = lax.axis_size("seq")
    ctx_count = lax.axis_size("ctx")
    all_positions = (
        block_table[:, :, None] * half + jnp.arange(half, dtype=jnp.int32)[None, None, :]
    ).reshape(-1)
    own_positions = lax.dynamic_slice_in_dim(all_positions, lax.axis_index("ctx") * rows, rows, 0)
    length = target_lengths[0]
    source_length = source_lengths[0]
    query_ok = own_positions < length
    valid_rows = query_ok[:, None]
    source_positions = jnp.arange(source_rows * ctx_count, dtype=jnp.int32)
    w_qkv, w_out, w_cq, w_ckv, w_co = (
        lax.all_gather(self_qkv, "seq", axis=0, tiled=True),
        lax.all_gather(self_out, "seq", axis=0, tiled=True),
        lax.all_gather(cross_q, "seq", axis=0, tiled=True),
        lax.all_gather(cross_kv, "seq", axis=0, tiled=True),
        lax.all_gather(cross_out, "seq", axis=0, tiled=True),
    )
    inputs = tokens[0].astype(jnp.float32)
    first_norm, first_back = jax.vjp(layer_norm, inputs, norm_gain[0], norm_bias[0])
    first_low = first_norm.astype(jnp.bfloat16)
    projected = jnp.dot(first_low, w_qkv, preferred_element_type=jnp.float32).astype(jnp.bfloat16)
    self_query = projected[:, :width].reshape(rows, H, HD)
    source_kv = jnp.dot(encoder_states[0], w_ckv, preferred_element_type=jnp.float32).astype(
        jnp.bfloat16
    )
    self_kv, cross_kvs = (
        lax.all_gather(projected[:, width:], "ctx", axis=0, tiled=True),
        lax.all_gather(source_kv, "ctx", axis=0, tiled=True),
    )
    self_top, self_total, self_peak = softmax_stats(
        self_query, self_kv, all_positions, own_positions, query_ok, length, True
    )
    self_mix = attend_values(
        self_query, self_kv, all_positions, own_positions, length, True, self_top, self_total
    )
    self_low = self_mix.astype(jnp.bfloat16)
    first_sum = inputs + jnp.dot(self_low, w_out, preferred_element_type=jnp.float32)
    second_norm, second_back = jax.vjp(layer_norm, first_sum, norm_gain[1], norm_bias[1])
    second_low = second_norm.astype(jnp.bfloat16)
    cross_rows = jnp.dot(second_low, w_cq, preferred_element_type=jnp.float32).astype(jnp.bfloat16)
    cross_query = cross_rows.reshape(rows, H, HD)
    cross_top, cross_total, cross_peak = softmax_stats(
        cross_query, cross_kvs, source_positions, own_positions, query_ok, source_length, False
    )
    cross_mix = attend_values(
        cross_query,
        cross_kvs,
        source_positions,
        own_positions,
        source_length,
        False,
        cross_top,
        cross_total,
    )
    cross_low = cross_mix.astype(jnp.bfloat16)
    second_sum = first_sum + jnp.dot(cross_low, w_co, preferred_element_type=jnp.float32)
    third_norm, third_back = jax.vjp(layer_norm, second_sum, norm_gain[2], norm_bias[2])
    third_low = third_norm.astype(jnp.bfloat16)
    w_up, w_down = (
        lax.all_gather(mlp_up, "seq", axis=0, tiled=True),
        lax.all_gather(mlp_down, "seq", axis=0, tiled=True),
    )
    hidden_pre = jnp.dot(third_low, w_up, preferred_element_type=jnp.float32)
    hidden_act, gelu_back = jax.vjp(jax.nn.gelu, hidden_pre)
    hidden_low = hidden_act.astype(jnp.bfloat16)
    third_sum = second_sum + jnp.dot(hidden_low, w_down, preferred_element_type=jnp.float32)
    output_rows = jnp.where(valid_rows, third_sum, 0.0).astype(jnp.bfloat16)
    peaks = lax.pmax(jnp.stack([self_peak, cross_peak]), ("seq", "ctx"))
    grad_rows = jnp.where(valid_rows, cotangent[0].astype(jnp.float32), 0.0)
    mlp_branch = grad_rows.astype(jnp.bfloat16)
    grad_down = jnp.einsum("rf,rd->fd", hidden_low, mlp_branch, preferred_element_type=jnp.float32)
    grad_act = jnp.einsum("rd,fd->rf", mlp_branch, w_down, preferred_element_type=jnp.float32)
    grad_pre = gelu_back(grad_act)[0].astype(jnp.bfloat16)
    grad_up = jnp.einsum("rd,rf->df", third_low, grad_pre, preferred_element_type=jnp.float32)
    back_third, gain_three, bias_three = third_back(
        jnp.einsum("rf,df->rd", grad_pre, w_up, preferred_element_type=jnp.float32)
    )
    up_part, down_part = (
        lax.psum_scatter(
            split_rows(grad_up, seq_count, ctx_count).astype(jnp.bfloat16),
            "ctx",
            scatter_dimension=1,
            tiled=True,
        ).astype(jnp.float32),
        lax.psum_scatter(
            split_rows(grad_down, seq_count, ctx_count).astype(jnp.bfloat16),
            "ctx",
            scatter_dimension=1,
            tiled=True,
        ).astype(jnp.float32),
    )
    up_shard, down_shard = (
        lax.psum_scatter(
            up_part.astype(jnp.bfloat16), "seq", scatter_dimension=0, tiled=True
        ).astype(jnp.float32),
        lax.psum_scatter(
            down_part.astype(jnp.bfloat16), "seq", scatter_dimension=0, tiled=True
        ).astype(jnp.float32),
    )
    grad_second = grad_rows + back_third
    cross_branch = grad_second.astype(jnp.bfloat16)
    grad_co = jnp.einsum("rd,re->de", cross_low, cross_branch, preferred_element_type=jnp.float32)
    cross_heads_grad = (
        jnp.einsum("re,de->rd", cross_branch, w_co, preferred_element_type=jnp.float32)
        .astype(jnp.bfloat16)
        .reshape(rows, H, HD)
    )
    cross_delta = jnp.einsum(
        "qhd,qhd->hq", cross_heads_grad.astype(jnp.float32), cross_mix.reshape(rows, H, HD)
    )
    grad_cross_rows = query_grads(
        cross_query,
        cross_kvs,
        source_positions,
        own_positions,
        source_length,
        False,
        cross_top,
        cross_total,
        cross_heads_grad,
        cross_delta,
    ).astype(jnp.bfloat16)
    grad_source_kv = lax.psum_scatter(
        key_grads(
            cross_query,
            cross_kvs,
            source_positions,
            own_positions,
            source_length,
            False,
            cross_top,
            cross_total,
            cross_heads_grad,
            cross_delta,
            jnp.int32(0),
            source_rows * lax.axis_size("ctx"),
        ).astype(jnp.bfloat16),
        "ctx",
        scatter_dimension=0,
        tiled=True,
    )
    grad_cq = jnp.einsum(
        "rd,re->de", second_low, grad_cross_rows, preferred_element_type=jnp.float32
    )
    grad_ckv = jnp.einsum(
        "sd,se->de", encoder_states[0], grad_source_kv, preferred_element_type=jnp.float32
    )
    grad_source = jnp.einsum("se,de->sd", grad_source_kv, w_ckv, preferred_element_type=jnp.float32)
    back_second, gain_two, bias_two = second_back(
        jnp.einsum("re,de->rd", grad_cross_rows, w_cq, preferred_element_type=jnp.float32)
    )
    grad_first = grad_second + back_second
    self_branch = grad_first.astype(jnp.bfloat16)
    grad_so = jnp.einsum("rd,re->de", self_low, self_branch, preferred_element_type=jnp.float32)
    self_heads_grad = (
        jnp.einsum("re,de->rd", self_branch, w_out, preferred_element_type=jnp.float32)
        .astype(jnp.bfloat16)
        .reshape(rows, H, HD)
    )
    self_delta = jnp.einsum(
        "qhd,qhd->hq", self_heads_grad.astype(jnp.float32), self_mix.reshape(rows, H, HD)
    )
    grad_query = query_grads(
        self_query,
        self_kv,
        all_positions,
        own_positions,
        length,
        True,
        self_top,
        self_total,
        self_heads_grad,
        self_delta,
    ).astype(jnp.bfloat16)
    grad_kv = lax.psum_scatter(
        key_grads(
            self_query,
            self_kv,
            all_positions,
            own_positions,
            length,
            True,
            self_top,
            self_total,
            self_heads_grad,
            self_delta,
            jnp.int32(0),
            rows * lax.axis_size("ctx"),
        ).astype(jnp.bfloat16),
        "ctx",
        scatter_dimension=0,
        tiled=True,
    )
    grad_projected = jnp.concatenate([grad_query, grad_kv], axis=1)
    grad_qkv = jnp.einsum(
        "rd,re->de", first_low, grad_projected, preferred_element_type=jnp.float32
    )
    back_first, gain_one, bias_one = first_back(
        jnp.einsum("re,de->rd", grad_projected, w_qkv, preferred_element_type=jnp.float32)
    )
    grad_inputs = grad_first + back_first
    norm_terms = jnp.stack([gain_one, gain_two, gain_three, bias_one, bias_two, bias_three], axis=1)
    qkv_part, out_part, cq_part, ckv_part, co_part, norm_part = (
        lax.psum_scatter(
            split_rows(grad_qkv, seq_count, ctx_count).astype(jnp.bfloat16),
            "ctx",
            scatter_dimension=1,
            tiled=True,
        ).astype(jnp.float32),
        lax.psum_scatter(
            split_rows(grad_so, seq_count, ctx_count).astype(jnp.bfloat16),
            "ctx",
            scatter_dimension=1,
            tiled=True,
        ).astype(jnp.float32),
        lax.psum_scatter(
            split_rows(grad_cq, seq_count, ctx_count).astype(jnp.bfloat16),
            "ctx",
            scatter_dimension=1,
            tiled=True,
        ).astype(jnp.float32),
        lax.psum_scatter(
            split_rows(grad_ckv, seq_count, ctx_count).astype(jnp.bfloat16),
            "ctx",
            scatter_dimension=1,
            tiled=True,
        ).astype(jnp.float32),
        lax.psum_scatter(
            split_rows(grad_co, seq_count, ctx_count).astype(jnp.bfloat16),
            "ctx",
            scatter_dimension=1,
            tiled=True,
        ).astype(jnp.float32),
        lax.psum_scatter(
            split_rows(norm_terms, seq_count, ctx_count).astype(jnp.bfloat16),
            "ctx",
            scatter_dimension=1,
            tiled=True,
        ).astype(jnp.float32),
    )
    qkv_shard, out_shard, cq_shard, ckv_shard, co_shard, norm_shard = (
        lax.psum_scatter(
            qkv_part.astype(jnp.bfloat16), "seq", scatter_dimension=0, tiled=True
        ).astype(jnp.float32),
        lax.psum_scatter(
            out_part.astype(jnp.bfloat16), "seq", scatter_dimension=0, tiled=True
        ).astype(jnp.float32),
        lax.psum_scatter(
            cq_part.astype(jnp.bfloat16), "seq", scatter_dimension=0, tiled=True
        ).astype(jnp.float32),
        lax.psum_scatter(
            ckv_part.astype(jnp.bfloat16), "seq", scatter_dimension=0, tiled=True
        ).astype(jnp.float32),
        lax.psum_scatter(
            co_part.astype(jnp.bfloat16), "seq", scatter_dimension=0, tiled=True
        ).astype(jnp.float32),
        lax.psum_scatter(
            norm_part.astype(jnp.bfloat16), "seq", scatter_dimension=0, tiled=True
        ).astype(jnp.float32),
    )
    norm_shard = join_rows(norm_shard)
    factors = jnp.sqrt(clip_limit / jnp.maximum(peaks, clip_limit))
    columns = jnp.repeat(factors, HD, axis=1)
    qkv_wide = self_qkv.astype(jnp.float32)
    clipped_self = jnp.concatenate(
        [qkv_wide[:, :width] * columns[0], qkv_wide[:, width : 2 * width] * columns[0]], axis=1
    ).astype(jnp.bfloat16)
    clipped_cross = jnp.concatenate(
        [
            cross_q.astype(jnp.float32) * columns[1],
            cross_kv[:, :width].astype(jnp.float32) * columns[1],
        ],
        axis=1,
    ).astype(jnp.bfloat16)
    return (
        output_rows[None],
        grad_inputs[None],
        grad_source[None],
        join_rows(qkv_shard),
        join_rows(out_shard),
        join_rows(cq_shard),
        join_rows(ckv_shard),
        join_rows(co_shard),
        join_rows(up_shard),
        join_rows(down_shard),
        norm_shard[:, :3].T,
        norm_shard[:, 3:].T,
        clipped_self,
        clipped_cross,
        peaks,
    )


F32 = jnp.float32
BF16 = jnp.bfloat16
SCALE = HD**-0.5


def fast_fits(mesh):
    seq_count, ctx_count = mesh.shape["seq"], mesh.shape["ctx"]
    if H % seq_count or H % ctx_count:
        return False
    held, pair = H // seq_count, H // ctx_count
    return held % pair == 0 and seq_count * (held // pair) == ctx_count and pair * HD == 128


def dot(left, right, contract=((1,), (0,))):
    return lax.dot_general(left, right, (contract, ((), ())), preferred_element_type=F32)


NT = ((1,), (1,))
TN = ((0,), (0,))


def norm_forward(values, gain, bias):
    centered = values - jnp.mean(values, axis=-1, keepdims=True)
    spread = jnp.mean(centered * centered, axis=-1, keepdims=True)
    inverse = lax.rsqrt(spread + norm_eps)
    hat = centered * inverse
    return hat, inverse, (hat * gain + bias).astype(BF16)


def norm_backward(grad, hat, inverse, gain):
    scaled = grad * gain
    inner = jnp.mean(scaled, axis=-1, keepdims=True)
    outer = jnp.mean(scaled * hat, axis=-1, keepdims=True)
    return (
        (scaled - inner - hat * outer) * inverse,
        jnp.sum(grad * hat, axis=0),
        jnp.sum(grad, axis=0),
    )


MESH = pl.DeviceIdType.MESH


class Links:
    def __init__(self, send, recv, local):
        self.send, self.recv, self.local = send, recv, local
        self.count, self.local_count = 0, 0
        self.sends, self.saves = [], []

    def slots(self, count):
        start = self.count
        self.count += count
        return start

    def copy(self, index, src, dst, device):
        return pltpu.make_async_remote_copy(
            src_ref=src,
            dst_ref=dst,
            send_sem=self.send.at[index],
            recv_sem=self.recv.at[index],
            device_id=device,
            device_id_type=MESH,
        )

    def push(self, index, src, dst, device, when=None):
        made = self.copy(index, src, dst, device)
        if when is None:
            made.start()
        else:
            pl.when(when)(made.start)
        self.sends.append((made, when))

    def take(self, index, dst, device, when=None):
        made = self.copy(index, dst, dst, device)
        if when is None:
            made.wait_recv()
        else:
            pl.when(when)(made.wait_recv)

    def save(self, src, dst):
        made = pltpu.make_async_copy(src, dst, self.local.at[self.local_count])
        self.local_count += 1
        made.start()
        self.saves.append(made)
        return made

    def finish(self):
        for made, when in self.sends:
            if when is None:
                made.wait_send()
            else:
                pl.when(when)(made.wait_send)
        for made in self.saves:
            made.wait()
        self.sends, self.saves = [], []


class Team:
    def __init__(self, own, near, far, opp):
        self.own, self.near, self.far, self.opp = own, near, far, opp

    def turned(self):
        return Team(self.own, self.far, self.near, self.opp)


class Place:
    def __init__(self):
        self.s, self.c = lax.axis_index("seq"), lax.axis_index("ctx")
        self.k, self.x = lax.rem(self.s, 2), lax.div(self.s, 2)
        self.y, self.z = lax.rem(self.c, 2), lax.div(self.c, 2)
        self.sib = self.s + 1 - 2 * self.k
        self.far = lax.rem(self.s + 2, 4)
        self.opp = lax.rem(self.sib + 2, 4)
        self.pair = self.c + 1 - 2 * self.y
        other = 1 - self.x
        self.seq = Team(self.s, ((self.sib, self.c), self.sib), ((self.far, self.c), self.far), ((self.opp, self.c), self.opp))
        self.flat = Team(
            self.x * 2 + self.y,
            ((self.s, self.pair), self.x * 2 + 1 - self.y),
            ((self.far, self.c), other * 2 + self.y),
            ((self.far, self.pair), other * 2 + 1 - self.y),
        )

    def greet(self):
        barrier = pltpu.get_barrier_semaphore()
        for other in (self.sib, self.far, self.opp):
            pl.semaphore_signal(barrier, inc=1, device_id=(other, self.c), device_id_type=MESH)
        for step in range(1, 8):
            pl.semaphore_signal(
                barrier,
                inc=1,
                device_id=(self.s, lax.rem(self.c + step, 8)),
                device_id_type=MESH,
            )
        for other in ((self.far, self.pair), (self.sib, self.pair)):
            pl.semaphore_signal(barrier, inc=1, device_id=other, device_id_type=MESH)
        pl.semaphore_wait(barrier, 12)


def rows_at(start, count):
    return pl.ds(pl.multiple_of(start, 16), count)


def lanes_at(start, count):
    return pl.ds(pl.multiple_of(start, 128), count)


class Columns:
    def __init__(self, links, place, weight, dest, parts, pieces=1):
        self.links, self.place, self.weight, self.dest = links, place, weight, dest
        rows, columns = weight.shape
        self.rows, self.whole, self.width = rows, columns // parts, columns // (4 * parts)
        self.step = rows // pieces
        self.jobs = [(part, piece) for piece in range(pieces) for part in range(parts)]
        self.base = {job: links.slots(5) for job in self.jobs}
        self.mine = place.k == place.y

    def source(self, job, target):
        part, piece = job
        return self.weight.at[
            pl.ds(piece * self.step, self.step),
            lanes_at(part * self.whole + target * self.width, self.width),
        ]

    def land(self, job, owner):
        part, piece = job
        return self.dest.at[
            rows_at(owner * self.rows + piece * self.step, self.step),
            pl.ds(part * self.width, self.width),
        ]

    def start(self, jobs=None):
        p = self.place
        for job in self.jobs if jobs is None else jobs:
            base = self.base[job]
            land = self.land(job, p.s)
            self.links.push(base, self.source(job, p.far), land, (p.far, p.c), self.mine)
            self.links.push(base + 1, self.source(job, p.opp), land, (p.opp, p.c), self.mine)
            self.links.push(base + 2, self.source(job, p.sib), land, (p.sib, p.c))
            self.links.save(self.source(job, p.s), land)

    def relay(self, jobs=None):
        p = self.place
        came = lax.rem(p.x + 1, 2) * 2 + p.y
        for job in self.jobs if jobs is None else jobs:
            base = self.base[job]
            land = self.land(job, came)
            self.links.take(base, land, (p.far, p.c), p.k == p.y)
            self.links.take(base + 1, land, (p.opp, p.c), p.k != p.y)
            self.links.push(base + 3, land, land, (p.s, p.pair))

    def finish(self):
        p = self.place
        for job in self.jobs:
            base = self.base[job]
            self.links.take(base + 2, self.land(job, p.sib), (p.sib, p.c))
            self.links.take(
                base + 3,
                self.land(job, lax.rem(p.x + 1, 2) * 2 + 1 - p.y),
                (p.s, p.pair),
            )


class Gather:
    def __init__(self, links, teams, dest, rows):
        self.links, self.teams, self.dest, self.rows = links, teams, dest, rows
        self.step = rows // len(teams)
        self.base = [links.slots(3) for _ in teams]

    def land(self, piece, owner):
        return self.dest.at[rows_at(owner * self.rows + piece * self.step, self.step)]

    def start(self, piece=0):
        t, base = self.teams[piece], self.base[piece]
        land = self.land(piece, t.own)
        self.links.push(base, land, land, t.far[0])
        self.links.push(base + 1, land, land, t.near[0])

    def forward(self, piece=0):
        t, base = self.teams[piece], self.base[piece]
        land = self.land(piece, t.far[1])
        self.links.take(base, land, t.far[0])
        self.links.push(base + 2, land, land, t.near[0])

    def finish(self, piece=0):
        t, base = self.teams[piece], self.base[piece]
        self.links.take(base + 1, self.land(piece, t.near[1]), t.near[0])
        self.links.take(base + 2, self.land(piece, t.opp[1]), t.near[0])

    def start_all(self):
        for piece in range(len(self.teams)):
            self.start(piece)

    def forward_all(self):
        for piece in range(len(self.teams)):
            self.forward(piece)

    def finish_all(self):
        for piece in range(len(self.teams)):
            self.finish(piece)


class Reduce:
    def __init__(self, links, teams, out, into, rows, partial):
        self.links, self.teams, self.out, self.into, self.partial = links, teams, out, into, partial
        self.step = rows // len(teams)
        self.base = [links.slots(3) for _ in teams]
        self.cut = [pl.ds(piece * self.step, self.step) for piece in range(len(teams))]

    def pieces(self):
        return [(piece, t, self.base[piece], self.cut[piece]) for piece, t in enumerate(self.teams)]

    def first(self):
        for piece, t, base, cut in self.pieces():
            self.out[0, cut] = self.partial(t.opp[1], piece).astype(BF16)
            self.links.push(base, self.out.at[0, cut], self.into.at[0, cut], t.near[0])
        for piece, t, base, cut in self.pieces():
            self.out[1, cut] = self.partial(t.near[1], piece).astype(BF16)
            self.links.push(base + 2, self.out.at[1, cut], self.into.at[1, cut], t.near[0])

    def second(self):
        for piece, t, base, cut in self.pieces():
            held = self.partial(t.far[1], piece).astype(F32)
            self.links.take(base, self.into.at[0, cut], t.near[0])
            self.out[2, cut] = (held + self.into[0, cut].astype(F32)).astype(BF16)
            self.links.push(base + 1, self.out.at[2, cut], self.into.at[2, cut], t.far[0])

    def last(self, then):
        for piece, t, base, cut in self.pieces():
            held = self.partial(t.own, piece).astype(F32)
            self.links.take(base + 2, self.into.at[1, cut], t.near[0])
            held = held + self.into[1, cut].astype(F32)
            self.links.take(base + 1, self.into.at[2, cut], t.far[0])
            then(piece, held + self.into[2, cut].astype(F32))

    def run(self, then):
        self.first()
        self.second()
        self.last(then)


class Shared:
    def __init__(self, links, place, weight, dest, pieces):
        self.links, self.place, self.weight, self.dest = links, place, weight, dest
        self.rows, self.width = weight.shape[0], weight.shape[1] // 4
        self.step = self.rows // pieces
        self.jobs = range(pieces)
        self.base = [links.slots(3) for _ in self.jobs]

    def source(self, job, slice_index):
        return self.weight.at[
            pl.ds(job * self.step, self.step), lanes_at(slice_index * self.width, self.width)
        ]

    def land(self, job, owner):
        return self.dest.at[rows_at(owner * self.rows + job * self.step, self.step)]

    def start(self, jobs):
        p = self.place
        for job in jobs:
            land = self.land(job, p.s)
            self.links.push(self.base[job], self.source(job, p.flat.far[1]), land, (p.far, p.c))
            self.links.push(self.base[job] + 1, self.source(job, p.flat.own), land, (p.sib, p.c))
            self.links.save(self.source(job, p.flat.own), land)

    def forward(self, jobs):
        p = self.place
        for job in jobs:
            land = self.land(job, p.far)
            self.links.take(self.base[job], land, (p.far, p.c))
            self.links.push(self.base[job] + 2, land, land, (p.sib, p.c))

    def finish(self):
        p = self.place
        for job in self.jobs:
            self.links.take(self.base[job] + 1, self.land(job, p.sib), (p.sib, p.c))
            self.links.take(self.base[job] + 2, self.land(job, p.opp), (p.sib, p.c))


def gelu_pair(value):
    rate = 0.7978845608028654
    square = value * value
    bent = jnp.tanh(rate * value * (1.0 + 0.044715 * square))
    half = 0.5 * (1.0 + bent)
    slope = half + 0.5 * value * (1.0 - bent * bent) * (rate * (1.0 + 0.134145 * square))
    return value * half, slope


def row_positions(table_ref, owner, half):
    place = lax.broadcasted_iota(jnp.int32, (2 * half, 1), 0)
    first, second = table_ref[owner, 0] * half, table_ref[owner, 1] * half - half
    return place + jnp.where(place < half, first, second)


def column_positions(table_ref, owner, half):
    place = lax.broadcasted_iota(jnp.int32, (1, 2 * half), 1)
    first, second = table_ref[owner, 0] * half, table_ref[owner, 1] * half - half
    return place + jnp.where(place < half, first, second)


def softmax_rows(scores):
    top = jnp.max(scores, axis=-1, keepdims=True)
    expos = jnp.exp(scores - top)
    return expos * (1.0 / jnp.sum(expos, axis=-1, keepdims=True)), top


PIECES = 2
STEPS = 8


def forward_kernel(
    table_ref,
    target_ref,
    source_ref,
    tokens_ref,
    encoder_ref,
    cotangent_ref,
    qkv_ref,
    out_ref,
    cq_ref,
    ckv_ref,
    co_ref,
    up_ref,
    down_ref,
    gain_ref,
    bias_ref,
    first_out,
    second_out,
    third_out,
    branch_out,
    source_out,
    w_qkv_out,
    w_cq_out,
    w_ckv_out,
    hidden_out,
    slopes_out,
    grad_third_out,
    third_part_out,
    heads_out,
    mix_out,
    query_out,
    kvs_out,
    cross_out_ref,
    sums_out,
    peak_out,
    lens_out,
    first,
    second,
    third,
    branch,
    source,
    w_qkv,
    w_cq,
    w_ckv,
    sent,
    heads,
    mix_own,
    mix,
    query,
    kv_own,
    kvs,
    cross,
    sums,
    columns,
    lens,
    rs_out,
    rs_in,
    part,
    w_up,
    w_down,
    hidden,
    slopes,
    grad_third,
    third_part,
    send_sem,
    recv_sem,
    local_sem,
):
    place, links = Place(), Links(send_sem, recv_sem, local_sem)
    p = place
    rows = tokens_ref.shape[1]
    source_rows = encoder_ref.shape[1]
    half = rows // 2
    width = w_cq.shape[1]
    pair_width = heads.shape[2]
    held = width // HD
    groups = width // pair_width
    place.greet()

    get_qkv = Columns(links, place, qkv_ref, w_qkv, 3)
    get_qkv.start()

    own = rows_at(p.s * rows, rows)
    inputs = tokens_ref[0].astype(F32)
    first[own] = norm_forward(inputs, gain_ref[0:1], bias_ref[0:1])[2]
    get_first = Gather(links, (p.seq,), first, rows)
    get_first.start()
    source[rows_at(p.s * source_rows, source_rows)] = encoder_ref[0]
    get_source = Gather(links, (p.seq,), source, source_rows)
    get_source.start()
    place_lens = links.slots(3)
    line = lax.broadcasted_iota(jnp.int32, (8, 128), 0)
    lens[pl.ds(p.s, 1)] = jnp.where(line < 4, target_ref[0], source_ref[0])[None]
    own_lens = lens.at[pl.ds(p.s, 1)]
    for step, other in enumerate((p.far, p.opp, p.sib)):
        links.push(place_lens + step, own_lens, own_lens, (other, p.c))
    for owner in range(STEPS):
        columns[:, owner * rows : (owner + 1) * rows] = column_positions(table_ref, owner, half)
    own_rows = row_positions(table_ref, p.c, half)
    valid = own_rows < target_ref[0]
    own_flat = p.flat.own * rows
    branch[rows_at(own_flat, rows)] = jnp.where(valid, cotangent_ref[0].astype(F32), 0.0).astype(BF16)
    get_cq = Columns(links, place, cq_ref, w_cq, 1)
    get_ckv = Columns(links, place, ckv_ref, w_ckv, 2)
    get_up = Shared(links, place, up_ref, w_up, 4)
    flat = (p.flat, p.flat.turned())

    get_qkv.relay()
    get_first.forward()
    get_source.forward()
    get_first.finish()
    get_source.finish()
    for made in links.saves:
        made.wait()
    links.saves = []
    get_qkv.finish()
    links.save(first, first_out)
    links.save(w_qkv, w_qkv_out)
    links.save(source, source_out)
    for step, other in enumerate((p.far, p.opp, p.sib)):
        links.take(place_lens + step, lens.at[pl.ds(other, 1)], (other, p.c))
    links.save(lens, lens_out)

    def project(block, carry):
        value = dot(first[rows_at(block * rows, rows)], w_qkv[...]).astype(BF16)
        for group in range(groups):
            for part in range(3):
                at = part * width + group * pair_width
                sent[block * groups + group, part] = value[:, at : at + pair_width]
        return carry

    lax.fori_loop(0, 4, project, 0)
    a2a = links.slots(STEPS)
    mine = rows_at(p.c * rows, rows)
    for step in range(1, STEPS):
        other = lax.rem(p.c + step, STEPS)
        links.push(a2a + step, sent.at[other], heads.at[:, mine], (p.s, other))
    keep = pltpu.make_async_copy(sent.at[p.c], heads.at[:, mine], local_sem.at[STEPS * 8 - 1])
    keep.start()
    get_cq.start()
    get_ckv.start()
    get_up.start((0, 1))
    keeps = p.k == p.y
    get_down = links.slots(1)
    links.push(get_down, down_ref, w_down, (p.sib, p.c), keeps)
    own_down = pltpu.make_async_copy(down_ref, w_down, local_sem.at[STEPS * 8 - 2])
    pl.when(keeps)(own_down.start)
    get_branch = Gather(links, flat, branch, rows)
    get_branch.start_all()
    keep.wait()
    get_cq.relay()
    get_ckv.relay()
    for step in range(1, STEPS):
        other = lax.rem(p.c + STEPS - step, STEPS)
        links.take(a2a + step, heads.at[:, rows_at(other * rows, rows)], (p.s, other))
    links.save(heads, heads_out)

    my_slot = lax.div(p.c, groups)
    my_group = lax.rem(p.c, groups)
    length = lens[pl.ds(my_slot, 1)][0, 0:1, 0:1]
    back = links.slots(STEPS)
    slot_rows = rows_at(my_slot * rows, rows)
    group_lanes = lanes_at(my_group * pair_width, pair_width)

    def back_copy(owner):
        return links.copy(
            back + p.c, mix_own.at[rows_at(owner * rows, rows)], mix.at[slot_rows, group_lanes], (p.s, owner)
        )

    def attend(block, peaks):
        at = rows_at(block * 2 * rows, 2 * rows)
        row_pos = jnp.concatenate(
            [row_positions(table_ref, 2 * block, half), row_positions(table_ref, 2 * block + 1, half)], axis=0
        )
        col_pos = columns[...]
        allowed = (col_pos <= row_pos) & (col_pos < length)
        ok = row_pos < length
        tops = []
        for head in range(pair_width // HD):
            cut = slice(head * HD, (head + 1) * HD)
            scores = dot(heads[0, at, cut], heads[1, :, cut], NT) * SCALE
            probs, top = softmax_rows(jnp.where(allowed, scores, masked_score))
            mix_own[at, cut] = dot(probs.astype(BF16), heads[2, :, cut]).astype(BF16)
            peak = jnp.max(jnp.where(ok, top, masked_score), axis=0, keepdims=True)
            tops.append(jnp.maximum(peaks[head], peak))
        return tuple(tops)

    low = jnp.full((1, 1), masked_score, F32)
    peaks = (low, low)
    for block in range(STEPS // 2):
        peaks = attend(block, peaks)
        for owner in (2 * block, 2 * block + 1):
            pl.when(p.c != owner)(back_copy(owner).start)
    for head in range(2):
        peak_out[head : head + 1] = jnp.broadcast_to(peaks[head], (1, 128))
    mix[slot_rows, group_lanes] = mix_own[mine]

    get_cq.finish()
    get_ckv.finish()
    for made in links.saves:
        made.wait()
    links.saves = []
    links.save(w_cq, w_cq_out)
    links.save(w_ckv, w_ckv_out)
    value = dot(source[...], w_ckv[...]).astype(BF16)
    for slot in range(4):
        kv_own[slot] = value[slot * source_rows : (slot + 1) * source_rows]
    own_keys = rows_at(p.c * source_rows, source_rows)
    kvs[:, own_keys] = kv_own[...]
    along, across = links.slots(4), links.slots(4)
    links.push(across, kv_own, kvs.at[:, own_keys], (p.s, p.pair))
    for step in range(1, 4):
        other = lax.rem(p.z + step, 4) * 2 + p.y
        links.push(along + step, kv_own, kvs.at[:, own_keys], (p.s, other))
    get_up.forward((0, 1))
    get_branch.forward_all()

    for owner in range(STEPS):

        @pl.when(p.c != owner)
        def _():
            lane = lanes_at((owner % groups) * pair_width, pair_width)
            links.take(
                back + owner, mix.at[pl.ds((owner // groups) * rows, rows), lane], (p.s, owner)
            )

    links.save(mix, mix_out)

    def boundary(index, left, weight, base, gather, start):
        step = rows // PIECES

        def tile(number, carry):
            lanes = lanes_at(number * 256, 256)
            part[:, lanes] = dot(left[...], weight[:, lanes]).astype(BF16)
            return carry

        lax.fori_loop(0, part.shape[1] // 256, tile, 0)

        def then(piece, total):
            cut = pl.ds(piece * step, step)
            value = base(piece) + total
            sums[index, cut] = value
            gather.dest[rows_at(start + piece * step, step)] = norm_forward(
                value, gain_ref[index + 1 : index + 2], bias_ref[index + 1 : index + 2]
            )[2]
            gather.start(piece)

        Reduce(
            links,
            (p.seq,) * PIECES,
            rs_out.at[index],
            rs_in.at[index],
            rows,
            lambda block, piece: part[rows_at(block * rows + piece * step, step)],
        ).run(then)

    step = rows // PIECES
    get_second = Gather(links, (p.seq,) * PIECES, second, rows)
    boundary(
        0,
        mix,
        out_ref,
        lambda piece: tokens_ref[0, piece * step : (piece + 1) * step].astype(F32),
        get_second,
        p.s * rows,
    )
    for hop in range(1, 4):
        other = lax.rem(p.z + 4 - hop, 4) * 2 + p.y
        land = kvs.at[:, rows_at(other * source_rows, source_rows)]
        links.take(along + hop, land, (p.s, other))
        links.push(across + hop, land, land, (p.s, p.pair))
    get_up.start((2, 3))
    get_second.forward_all()
    get_second.finish_all()
    links.save(second, second_out)
    for hop in range(4):
        other = lax.rem(p.z + 4 - hop, 4) * 2 + 1 - p.y
        land = kvs.at[:, rows_at(other * source_rows, source_rows)]
        links.take(across + hop, land, (p.s, p.pair))
    links.save(kvs, kvs_out)

    keys = kvs.shape[1]

    def cross_attend(slot, peaks):
        at = rows_at(slot * rows, rows)
        asked = dot(second[at], w_cq[...]).astype(BF16)
        query[at] = asked
        limits = lens[pl.ds(slot, 1)]
        live = lax.broadcasted_iota(jnp.int32, (1, keys), 1) < limits[0, 4:5, 0:1]
        ok = own_rows < limits[0, 0:1, 0:1]
        tops = []
        for head in range(held):
            cut = slice(head * HD, (head + 1) * HD)
            vcut = slice(width + head * HD, width + (head + 1) * HD)
            scores = dot(asked[:, cut], kvs[slot, :, cut], NT) * SCALE
            probs, top = softmax_rows(jnp.where(live, scores, masked_score))
            cross[at, cut] = dot(probs.astype(BF16), kvs[slot, :, vcut]).astype(BF16)
            peak = jnp.max(jnp.where(ok, top, masked_score), axis=0, keepdims=True)
            tops.append(jnp.maximum(peaks[head], peak))
        return tuple(tops)

    peaks = lax.fori_loop(0, 4, cross_attend, (low,) * held)
    for head in range(held):
        peak_out[2 + head : 3 + head] = jnp.broadcast_to(peaks[head], (1, 128))
    links.save(query, query_out)
    links.save(cross, cross_out_ref)
    get_up.forward((2, 3))
    get_branch.finish_all()
    links.save(branch, branch_out)
    get_third = Gather(links, flat, third, rows)
    boundary(
        1,
        cross,
        co_ref,
        lambda piece: sums[0, piece * step : (piece + 1) * step],
        get_third,
        own_flat,
    )
    links.save(sums, sums_out)
    get_third.forward_all()
    get_up.finish()
    for made in links.saves:
        made.wait()
    links.saves = []
    pl.when(keeps)(own_down.wait)
    links.take(get_down, w_down, (p.sib, p.c), p.k != p.y)
    get_third.finish_all()
    links.save(third, third_out)

    def units(number, carry):
        lanes = lanes_at(number * 256, 256)
        value, slope = gelu_pair(dot(third[...], w_up[:, lanes]))
        hidden[:, lanes] = value.astype(BF16)
        grad = dot(branch[...], w_down[rows_at(number * 256, 256)], NT)
        slopes[:, lanes] = (grad * slope).astype(BF16)
        return carry

    lax.fori_loop(0, w_up.shape[1] // 256, units, 0)
    links.save(hidden, hidden_out)
    links.save(slopes, slopes_out)

    def back_rows(number, carry):
        lanes = lanes_at(number * 256, 256)
        grad_third[:, lanes] = dot(slopes[...], w_up[rows_at(number * 256, 256)], NT).astype(BF16)
        third_part[:, lanes] = dot(hidden[...], w_down[:, lanes]).astype(BF16)
        return carry

    lax.fori_loop(0, third.shape[1] // 256, back_rows, 0)
    links.save(grad_third, grad_third_out)
    links.save(third_part, third_part_out)
    for owner in range(STEPS):
        pl.when(p.c != owner)(back_copy(owner).wait_send)
    links.finish()


def forward_call(
    table, targets, sources, tokens, encoder, cotangent, qkv, out, cq, ckv, co, up, down, gain, bias
):
    rows, width = tokens.shape[1], out.shape[0]
    source_rows = encoder.shape[1]
    depth = tokens.shape[2]
    keys = 8 * source_rows
    any_space = pl.BlockSpec(memory_space=pl.ANY)
    vmem = pl.BlockSpec(memory_space=pltpu.VMEM)
    smem = pl.BlockSpec(memory_space=pltpu.SMEM)
    shapes = dict(
        first=((4 * rows, depth), BF16),
        second=((4 * rows, depth), BF16),
        third=((4 * rows, depth), BF16),
        branch=((4 * rows, depth), BF16),
        source=((4 * source_rows, depth), BF16),
        w_qkv=((depth, 3 * width), BF16),
        w_cq=((depth, width), BF16),
        w_ckv=((depth, 2 * width), BF16),
        hidden=((4 * rows, up.shape[1] // 4), BF16),
        slopes=((4 * rows, up.shape[1] // 4), BF16),
        grad_third=((4 * rows, depth), BF16),
        third_part=((4 * rows, depth), BF16),
        heads=((3, 8 * rows, 128), BF16),
        mix=((4 * rows, width), BF16),
        query=((4 * rows, width), BF16),
        kvs=((4, keys, 2 * width), BF16),
        cross=((4 * rows, width), BF16),
        sums=((2, rows, depth), F32),
        peak=((8, 128), F32),
        lens=((4, 8, 128), jnp.int32),
    )
    scratch = [
        shapes[name]
        for name in ("first", "second", "third", "branch", "source", "w_qkv", "w_cq", "w_ckv")
    ] + [
        ((8, 3, rows, 128), BF16),
        shapes["heads"],
        ((8 * rows, 128), BF16),
        shapes["mix"],
        shapes["query"],
        ((4, source_rows, 2 * width), BF16),
        shapes["kvs"],
        shapes["cross"],
        shapes["sums"],
        ((1, 8 * rows), jnp.int32),
        shapes["lens"],
        ((2, 3, rows, depth), BF16),
        ((2, 3, rows, depth), BF16),
        ((4 * rows, depth), BF16),
        ((depth, up.shape[1] // 4), BF16),
        (down.shape, BF16),
        shapes["hidden"],
        shapes["slopes"],
        shapes["grad_third"],
        shapes["third_part"],
    ]
    made = pl.pallas_call(
        forward_kernel,
        in_specs=[smem] * 3
        + [vmem] * 3
        + [any_space, vmem, any_space, any_space, vmem, any_space, any_space]
        + [vmem] * 2,
        out_specs=[vmem if name == "peak" else any_space for name in shapes],
        out_shape=[jax.ShapeDtypeStruct(*shape) for shape in shapes.values()],
        scratch_shapes=[pltpu.VMEM(*shape) for shape in scratch]
        + [
            pltpu.SemaphoreType.DMA((128,)),
            pltpu.SemaphoreType.DMA((128,)),
            pltpu.SemaphoreType.DMA((64,)),
        ],
        compiler_params=pltpu.CompilerParams(
            collective_id=0, has_side_effects=True, vmem_limit_bytes=60 * 2**20
        ),
        name="forward",
    )(table, targets, sources, tokens, encoder, cotangent, qkv, out, cq, ckv, co, up, down, gain, bias)
    return dict(zip(shapes, made))


class Sum:
    def __init__(self, links, place, full, into, away, result, lead=False, cores=False):
        self.links, self.place, self.full = links, place, full
        self.half = place.k if cores else place.y
        self.other = (place.sib, place.c) if cores else (place.s, place.pair)
        self.into, self.away, self.result, self.lead = into, away, result, lead
        self.base = links.slots(7)
        self.near = place.z + 1 - 2 * lax.rem(place.z, 2)
        self.across = lax.rem(place.z + 2, 4)
        self.order = (lax.rem(self.near + 2, 4), self.across, self.near, place.z)

    def start(self, turns=(0, 1, 2, 3)):
        for turn in turns:
            to = self.order[turn]
            give = 1 - self.half
            src = self.full.at[to, give] if self.lead else self.full.at[:, to, give]
            self.links.push(self.base + turn, src, self.into.at[to], self.other)

    def turn(self, turns=(0, 1, 2, 3)):
        p, links, into, away = self.place, self.links, self.into, self.away
        for turn in turns:
            to = self.order[turn]
            links.take(self.base + turn, into.at[to], self.other)
            if turn == 1:
                links.take(self.base + 4, away.at[0], (p.s, self.near * 2 + p.y))

            def add(a, carry):
                mine = self.full[to, self.half, a] if self.lead else self.full[a, to, self.half]
                total = mine.astype(F32) + into[to, a].astype(F32)
                if turn == 1:
                    total = total + away[0, a].astype(F32)
                into[to, a] = total.astype(BF16)
                return carry

            if turn < 3:
                lax.fori_loop(0, into.shape[1], add, 0)
                goal = self.across if turn == 1 else self.near
                links.push(
                    self.base + 4 + turn, into.at[to], away.at[turn], (p.s, goal * 2 + p.y)
                )

    def finish(self):
        p, links, into, away = self.place, self.links, self.into, self.away
        links.take(self.base + 5, away.at[1], (p.s, self.across * 2 + p.y))
        links.take(self.base + 6, away.at[2], (p.s, self.near * 2 + p.y))

        def add(a, carry):
            mine = self.full[p.z, self.half, a] if self.lead else self.full[a, p.z, self.half]
            total = mine.astype(F32) + into[p.z, a].astype(F32)
            total = total + (away[1, a].astype(F32) + away[2, a].astype(F32))
            self.result[a] = total.astype(BF16)
            return carry

        lax.fori_loop(0, into.shape[1], add, 0)


class Exchange:
    def __init__(self, links, team, result, taken):
        self.links, self.team, self.result, self.taken = links, team, result, taken
        self.base = links.slots(3)
        self.others = (team.far, team.opp, team.near)

    def start(self):
        own = pl.ds(self.team.own, 1)
        for step, (device, index) in enumerate(self.others):
            src = self.result.at[pl.ds(index, 1)]
            self.links.push(self.base + step, src, self.taken.at[own], device)
        self.taken[own] = self.result[own]

    def finish(self):
        for step, (device, index) in enumerate(self.others):
            self.links.take(self.base + step, self.taken.at[pl.ds(index, 1)], device)


def norm_terms_of(values):
    centered = values - jnp.mean(values, axis=-1, keepdims=True)
    spread = jnp.mean(centered * centered, axis=-1, keepdims=True)
    inverse = lax.rsqrt(spread + norm_eps)
    return centered * inverse, inverse


def backward_body(r):
    place, links = Place(), Links(r.send_sem, r.recv_sem, r.local_sem)
    p = place
    rows = r.tokens.shape[1]
    half = rows // 2
    width = r.w_cq.shape[1]
    source_rows = r.source.shape[0] // 4
    keys = r.kvs.shape[1]
    pair_width = r.heads.shape[2]
    held, groups = width // HD, width // pair_width
    depth = r.tokens.shape[2]
    step = rows // PIECES
    share = depth // 4

    loads = {}

    def load(names):
        for name in names:
            at = r.load_sem.at[r.loaded.index(name)]
            loads[name] = pltpu.make_async_copy(getattr(r, name + "_hbm"), getattr(r, name), at)
            loads[name].start()

    r.part, r.third_part = r.hidden.at[:, :depth], r.hidden.at[:, depth : 2 * depth]
    r.second, r.first = r.slopes.at[:, :depth], r.slopes.at[:, depth : 2 * depth]
    soon = ("hidden", "branch", "third", "slopes", "sums")
    late = ("third_part", "second", "first")
    load(soon)

    def need(*wanted):
        for name in wanted:
            loads.pop(name).wait()

    place.greet()
    r.peaks_ctx[pl.ds(p.c, 1)] = r.peak[...][None]
    peak_base = links.slots(STEPS)
    own_peak = r.peaks_ctx.at[pl.ds(p.c, 1)]
    for hop in range(1, STEPS):
        links.push(peak_base + hop, own_peak, own_peak, (p.s, lax.rem(p.c + hop, STEPS)))

    own_rows = row_positions(r.table, p.c, half)
    r.norms[...] = jnp.zeros_like(r.norms)

    def add_norms(index, gain, bias):
        r.norms[index : index + 1] += gain[None]
        r.norms[index + 3 : index + 4] += bias[None]

    get_cross = Gather(links, (p.seq,) * PIECES, r.cross_branch, rows)

    def after_third(piece, total):
        cut = slice(piece * step, (piece + 1) * step)
        hat, inverse = norm_terms_of(r.sums[1, cut])
        back, gain, bias = norm_backward(total, hat, inverse, r.gain[2:3])
        add_norms(2, gain, bias)
        valid = own_rows[cut] < r.target[0]
        value = jnp.where(valid, r.cotangent[0, cut].astype(F32), 0.0) + back
        r.grad_sum[cut] = value
        r.cross_branch[rows_at(p.s * rows + piece * step, step)] = value.astype(BF16)
        get_cross.start(piece)

    def stored(ref):
        return lambda block, piece: ref[rows_at(block * rows + piece * step, step)].astype(F32)

    flat = (p.flat, p.flat.turned())
    sum_third = Reduce(
        links, flat, r.rs_out.at[0], r.rs_in.at[0], rows, stored(r.grad_third)
    )
    sum_third.first()

    def down_grad(block, carry):
        value = dot(r.hidden[:, lanes_at(block * 256, 256)], r.branch[...], TN).astype(BF16)
        r.down_full[lax.div(block, 2), lax.rem(block, 2)] = value.reshape(r.down_full.shape[2:])
        return carry

    need("hidden", "branch")
    lax.fori_loop(0, 3, down_grad, 0)
    sum_third.second()
    load([name for name in r.loaded if name not in soon + late])
    lax.fori_loop(3, 8, down_grad, 0)
    down = Sum(
        links, place, r.down_full, r.down_into, r.down_away, r.down_result, True, cores=True
    )
    down.start()
    need("third", "slopes")

    def up_grad(number, carry):
        block, side = lax.div(number, 2), lax.rem(number, 2)
        lanes = lanes_at(side * depth, depth)
        left = r.third[:, lanes_at(block * share, share)]
        value = dot(left, r.slopes[:, lanes], TN).astype(BF16)
        at = pl.ds(lax.div(block, 2) * 2, 2)
        r.up_full[:, lax.rem(block, 2), at, :, lanes] = value.reshape(4, 2, share // 8, depth)
        return carry

    lax.fori_loop(0, 8, up_grad, 0)
    load(late)
    down.turn((0,))
    up = Sum(links, place, r.up_full, r.up_into, r.up_away, r.up_result, True, cores=True)
    up.start()
    need("sums")
    sum_third.last(after_third)
    for hop in range(1, STEPS):
        other = lax.rem(p.c + STEPS - hop, STEPS)
        links.take(peak_base + hop, r.peaks_ctx.at[pl.ds(other, 1)], (p.s, other))
    best = []
    for group in range(groups):
        tile = r.peaks_ctx[group]
        for owner in range(group + groups, STEPS, groups):
            tile = jnp.maximum(tile, r.peaks_ctx[owner])
        best.append(tile)
    everyone = best[0]
    for tile in best[1:]:
        everyone = jnp.maximum(everyone, tile)
    mine = jnp.concatenate([tile[0:2] for tile in best] + [everyone[2 : 2 + held]], axis=0)
    r.peaks_seq[pl.ds(p.s, 1)] = mine[None]
    peak_seq = links.slots(3)
    own_peak = r.peaks_seq.at[pl.ds(p.s, 1)]
    for hop, other in enumerate((p.far, p.opp, p.sib)):
        links.push(peak_seq + hop, own_peak, own_peak, (other, p.c))

    up.turn((0,))
    get_cross.forward_all()
    down.turn((2,))
    need("w_co", "cross", "query", "kvs", "w_cq", "second")
    get_cross.finish_all()
    up.turn((2,))

    def cross_back(slot, carry):
        at = rows_at(slot * rows, rows)
        grad_rows = dot(r.cross_branch[at], r.w_co[...], NT).astype(BF16)
        live = lax.broadcasted_iota(jnp.int32, (1, keys), 1) < r.lens[pl.ds(slot, 1)][0, 4:5, 0:1]
        for head in range(held):
            cut = slice(head * HD, (head + 1) * HD)
            vcut = slice(width + head * HD, width + (head + 1) * HD)
            asked, grad = r.query[at, cut], grad_rows[:, cut]
            scores = dot(asked, r.kvs[slot, :, cut], NT) * SCALE
            probs, _ = softmax_rows(jnp.where(live, scores, masked_score))
            dprobs = dot(grad, r.kvs[slot, :, vcut], NT)
            delta = jnp.sum(probs * dprobs, axis=-1, keepdims=True)
            dscores = (probs * (dprobs - delta)).astype(BF16)
            r.dquery[at, cut] = (dot(dscores, r.kvs[slot, :, cut]) * SCALE).astype(BF16)
            shape = (4, 2, source_rows, HD)
            r.dkv_full[slot, :, :, :, cut] = (
                (dot(dscores, asked, TN) * SCALE).astype(BF16).reshape(shape)
            )
            r.dkv_full[slot, :, :, :, vcut] = (
                dot(probs.astype(BF16), grad, TN).astype(BF16).reshape(shape)
            )
        return carry

    lax.fori_loop(0, 4, cross_back, 0)
    dkv = Sum(links, place, r.dkv_full, r.dkv_into, r.dkv_away, r.dkv_result)
    need("third_part")
    sum_output = Reduce(
        links, flat, r.rs_out.at[2], r.rs_in.at[2], rows, stored(r.third_part)
    )
    sum_output.first()
    dkv.start()

    get_self = Gather(links, (p.seq,) * PIECES, r.self_branch, rows)

    def after_second(piece, total):
        cut = slice(piece * step, (piece + 1) * step)
        hat, inverse = norm_terms_of(r.sums[0, cut])
        back, gain, bias = norm_backward(total, hat, inverse, r.gain[1:2])
        add_norms(1, gain, bias)
        value = r.grad_sum[cut] + back
        r.grad_sum[cut] = value
        r.self_branch[rows_at(p.s * rows + piece * step, step)] = value.astype(BF16)
        get_self.start(piece)

    def cross_rows(number, carry):
        lanes = lanes_at(number * 256, 256)
        r.part[:, lanes] = dot(r.dquery[...], r.w_cq[rows_at(number * 256, 256)], NT).astype(BF16)
        return carry

    lax.fori_loop(0, depth // 256, cross_rows, 0)
    Reduce(
        links, (p.seq,) * PIECES, r.rs_out.at[1], r.rs_in.at[1], rows, stored(r.part)
    ).run(after_second)

    def row_grad(left, right, full):
        def one(part, carry):
            lanes = lanes_at(part * 128, 128)
            value = dot(left[:, lanes], right[...], TN).astype(BF16)
            full[pl.ds(part * 2, 2)] = value.reshape((2, 2) + full.shape[2:])
            return carry

        lax.fori_loop(0, left.shape[1] // 128, one, 0)

    def column_grad(left, right, full):
        def one(block, carry):
            lanes = lanes_at(block * share, share)
            value = dot(left[:, lanes], right(), TN).astype(BF16)
            full[pl.ds(block, 1)] = value.reshape((1,) + full.shape[1:])
            return carry

        lax.fori_loop(0, 4, one, 0)

    row_grad(r.cross, r.cross_branch, r.co_full)
    get_self.forward_all()
    column_grad(r.second, lambda: r.dquery[...], r.cq_full)
    get_self.finish_all()

    need("w_out", "heads", "mix")

    def mix_back(slot, carry):
        value = dot(r.self_branch[rows_at(slot * rows, rows)], r.w_out[...], NT).astype(BF16)
        for group in range(groups):
            r.gsent[slot * groups + group] = value[:, group * pair_width : (group + 1) * pair_width]
        return carry

    lax.fori_loop(0, 4, mix_back, 0)
    a2a = links.slots(STEPS)
    mine_rows = rows_at(p.c * rows, rows)
    for hop in range(1, STEPS):
        other = lax.rem(p.c + hop, STEPS)
        links.push(a2a + hop, r.gsent.at[other], r.gheads.at[mine_rows], (p.s, other))
    r.gheads[mine_rows] = r.gsent[p.c]
    for owner in range(STEPS):
        r.columns[:, owner * rows : (owner + 1) * rows] = column_positions(r.table, owner, half)
    sum_output.second()
    row_grad(r.mix, r.self_branch, r.so_full)
    dkv.turn()
    down.turn((1,))
    co = Sum(links, place, r.co_full, r.co_into, r.co_away, r.co_result, True)
    cq = Sum(links, place, r.cq_full, r.cq_into, r.cq_away, r.cq_result)
    so = Sum(links, place, r.so_full, r.so_into, r.so_away, r.so_result, True)
    for hop in range(1, STEPS):
        other = lax.rem(p.c + STEPS - hop, STEPS)
        links.take(a2a + hop, r.gheads.at[rows_at(other * rows, rows)], (p.s, other))

    my_slot, my_group = lax.div(p.c, groups), lax.rem(p.c, groups)
    length = r.lens[pl.ds(my_slot, 1)][0, 0:1, 0:1]
    slot_rows = rows_at(my_slot * rows, rows)
    group_lanes = lanes_at(my_group * pair_width, pair_width)
    back_q, back_kv = links.slots(STEPS), links.slots(STEPS)
    r.acc[...] = jnp.zeros_like(r.acc)

    def q_copy(owner):
        at = rows_at(owner * rows, rows)
        return links.copy(
            back_q + p.c, r.dq_own.at[at], r.dproj.at[0, slot_rows, group_lanes], (p.s, owner)
        )

    def kv_copy(owner):
        at = rows_at(owner * rows, rows)
        return links.copy(
            back_kv + p.c,
            r.dkv_own.at[:, at],
            r.dproj.at[pl.ds(1, 2), slot_rows, group_lanes],
            (p.s, owner),
        )

    def attend_back(block, carry):
        at = rows_at(block * 2 * rows, 2 * rows)
        row_pos = jnp.concatenate(
            [
                row_positions(r.table, 2 * block, half),
                row_positions(r.table, 2 * block + 1, half),
            ],
            axis=0,
        )
        col_pos = r.columns[...]
        allowed = (col_pos <= row_pos) & (col_pos < length)
        for head in range(pair_width // HD):
            cut = slice(head * HD, (head + 1) * HD)
            asked, grad = r.heads[0, at, cut], r.gheads[at, cut]
            scores = dot(asked, r.heads[1, :, cut], NT) * SCALE
            probs, _ = softmax_rows(jnp.where(allowed, scores, masked_score))
            dprobs = dot(grad, r.heads[2, :, cut], NT)
            delta = jnp.sum(probs * dprobs, axis=-1, keepdims=True)
            dscores = (probs * (dprobs - delta)).astype(BF16)
            r.dq_own[at, cut] = (dot(dscores, r.heads[1, :, cut]) * SCALE).astype(BF16)
            r.acc[0, :, cut] += dot(dscores, asked, TN)
            r.acc[1, :, cut] += dot(probs.astype(BF16), grad, TN)
        return carry

    for block in range(STEPS // 2):
        attend_back(block, 0)
        for owner in (2 * block, 2 * block + 1):
            pl.when(p.c != owner)(q_copy(owner).start)
    for owner in range(STEPS):
        at = rows_at(owner * rows, rows)
        r.dkv_own[0, at] = (r.acc[0, at] * SCALE).astype(BF16)
        r.dkv_own[1, at] = r.acc[1, at].astype(BF16)
        pl.when(p.c != owner)(kv_copy(owner).start)
    r.dproj[0, slot_rows, group_lanes] = r.dq_own[mine_rows]
    r.dproj[pl.ds(1, 2), slot_rows, group_lanes] = r.dkv_own[:, mine_rows]

    up.turn((1,))
    need("w_ckv", "source")
    dkv.finish()
    r.dsource[...] = r.dkv_result[...].reshape(4 * source_rows, 2 * width)
    column_grad(r.source, lambda: r.dsource[...], r.ckv_full)
    ckv = Sum(links, place, r.ckv_full, r.ckv_into, r.ckv_away, r.ckv_result)
    for job in (co, cq, so, ckv):
        job.start()

    def source_partial(block, piece):
        return dot(r.dsource[rows_at(block * source_rows, source_rows)], r.w_ckv[...], NT)

    def after_encoder(piece, total):
        r.grad_source[...] = total

    Reduce(links, (p.seq,), r.enc_out, r.enc_in, source_rows, source_partial).run(after_encoder)

    def after_output(piece, total):
        cut = slice(piece * step, (piece + 1) * step)
        valid = own_rows[cut] < r.target[0]
        r.output[cut] = jnp.where(valid, r.sums[1, cut] + total, 0.0).astype(BF16)

    sum_output.last(after_output)
    need("w_qkv", "first")
    for owner in range(STEPS):

        @pl.when(p.c != owner)
        def _():
            at = pl.ds((owner // groups) * rows, rows)
            lane = lanes_at((owner % groups) * pair_width, pair_width)
            links.take(back_q + owner, r.dproj.at[0, at, lane], (p.s, owner))
            links.take(back_kv + owner, r.dproj.at[pl.ds(1, 2), at, lane], (p.s, owner))

    def first_rows(number, carry):
        at = rows_at(number * 256, 256)
        total = dot(r.dproj[0], r.w_qkv[at, :width], NT)
        total += dot(r.dproj[1], r.w_qkv[at, width : 2 * width], NT)
        total += dot(r.dproj[2], r.w_qkv[at, 2 * width :], NT)
        r.part[:, lanes_at(number * 256, 256)] = total.astype(BF16)
        return carry

    lax.fori_loop(0, depth // 256, first_rows, 0)

    def after_first(piece, total):
        cut = slice(piece * step, (piece + 1) * step)
        hat, inverse = norm_terms_of(r.tokens[0, cut].astype(F32))
        back, gain, bias = norm_backward(total, hat, inverse, r.gain[0:1])
        add_norms(0, gain, bias)
        r.grad_inputs[cut] = r.grad_sum[cut] + back

    def qkv_grad(block, carry):
        lanes = lanes_at(block * share, share)
        left = r.first[:, lanes]
        for part in range(3):
            value = dot(left, r.dproj[part], TN).astype(BF16)
            r.qkv_full[pl.ds(block, 1), :, :, :, part * width : (part + 1) * width] = value.reshape(
                (1,) + r.qkv_full.shape[1:4] + (width,)
            )
        return carry

    lax.fori_loop(0, 4, qkv_grad, 0)
    qkv = Sum(links, place, r.qkv_full, r.qkv_into, r.qkv_away, r.qkv_result)
    qkv.start()
    Reduce(
        links, (p.seq,) * PIECES, r.rs_out.at[3], r.rs_in.at[3], rows, stored(r.part)
    ).run(after_first)

    norm_seq, norm_ctx = links.slots(3), links.slots(STEPS)
    others = (p.far, p.opp, p.sib)
    for hop, other in enumerate(others):
        links.push(
            norm_seq + hop,
            r.norms.at[:, lanes_at(other * share, share)],
            r.norms_seq.at[pl.ds(p.s, 1)].at[0],
            (other, p.c),
        )
    for job in (co, cq, so, ckv):
        job.turn()
    total = r.norms[:, lanes_at(p.s * share, share)]
    for hop, other in enumerate(others):
        links.take(norm_seq + hop, r.norms_seq.at[pl.ds(other, 1)].at[0], (other, p.c))
        total = total + r.norms_seq[pl.ds(other, 1)][0]
    r.norms_ctx[pl.ds(p.c, 1)] = total[None]
    own_norms = r.norms_ctx.at[pl.ds(p.c, 1)]
    for hop in range(1, STEPS):
        links.push(norm_ctx + hop, own_norms, own_norms, (p.s, lax.rem(p.c + hop, STEPS)))
    sums = {}
    for job in (up, down):
        job.turn((3,))
        job.finish()
    sums["up"] = Exchange(links, p.flat, r.up_result, r.up_taken)
    sums["up"].start()
    keeps, swapped = p.k == p.y, links.slots(1)
    links.push(swapped, r.down_result, r.down_taken, (p.sib, p.pair), p.k != p.y)

    @pl.when(keeps)
    def _():
        r.down_taken[...] = r.down_result[...]

    qkv.turn()
    for job in (co, so):
        job.finish()
    for name, job in (("cq", cq), ("ckv", ckv), ("qkv", qkv)):
        job.finish()
        sums[name] = Exchange(links, p.seq, getattr(r, name + "_result"), getattr(r, name + "_taken"))
        sums[name].start()
    for hop in range(1, STEPS):
        other = lax.rem(p.c + STEPS - hop, STEPS)
        links.take(norm_ctx + hop, r.norms_ctx.at[pl.ds(other, 1)], (p.s, other))
    total = r.norms_ctx[0]
    for owner in range(1, STEPS):
        total = total + r.norms_ctx[owner]
    r.norm_sum[...] = total
    for hop, other in enumerate(others):
        links.take(peak_seq + hop, r.peaks_seq.at[pl.ds(other, 1)], (other, p.c))
    for job in sums.values():
        job.finish()
    links.take(swapped, r.down_taken, (p.sib, p.pair), p.k != p.y)
    for owner in range(STEPS):
        pl.when(p.c != owner)(q_copy(owner).wait_send)
        pl.when(p.c != owner)(kv_copy(owner).wait_send)
    links.finish()


def backward_call(kept, given):
    rows, depth = given["tokens"].shape[1:]
    width = kept["w_cq"].shape[1]
    source_rows = kept["source"].shape[0] // 4
    keys = kept["kvs"].shape[1]
    share = depth // 32
    hidden = kept["hidden"].shape[1]
    any_space = pl.BlockSpec(memory_space=pl.ANY)
    vmem = pl.BlockSpec(memory_space=pltpu.VMEM)
    smem = pl.BlockSpec(memory_space=pltpu.SMEM)
    inputs = dict(
        table=(smem, given["table"]),
        target=(smem, given["target"]),
        tokens=(vmem, given["tokens"]),
        cotangent=(vmem, given["cotangent"]),
        gain=(vmem, given["gain"]),
        peak=(vmem, kept["peak"]),
        lens=(vmem, kept["lens"]),
        grad_third=(vmem, kept["grad_third"]),
    )
    loaded = dict(
        hidden=kept["hidden"],
        branch=kept["branch"],
        third=kept["third"],
        slopes=kept["slopes"],
        third_part=kept["third_part"],
        sums=kept["sums"],
        w_co=given["cross_out"],
        cross=kept["cross"],
        query=kept["query"],
        kvs=kept["kvs"],
        w_cq=kept["w_cq"],
        second=kept["second"],
        w_out=given["self_out"],
        heads=kept["heads"],
        mix=kept["mix"],
        w_ckv=kept["w_ckv"],
        source=kept["source"],
        w_qkv=kept["w_qkv"],
        first=kept["first"],
    )
    for name, value in loaded.items():
        inputs[name + "_hbm"] = (any_space, value)
    outs = dict(
        output=((rows, depth), BF16),
        grad_inputs=((rows, depth), F32),
        grad_source=((source_rows, depth), F32),
        down_taken=((hidden // (8 * share), share, depth), BF16),
        co_result=((1, share, depth), BF16),
        so_result=((1, share, depth), BF16),
        up_taken=((4, share, hidden), BF16),
        cq_taken=((4, share, width), BF16),
        ckv_taken=((4, share, 2 * width), BF16),
        qkv_taken=((4, share, 3 * width), BF16),
        norm_sum=((8, depth // 4), F32),
        peaks_seq=((4, 8, 128), F32),
    )
    down_blocks = hidden // (8 * share)
    scratch = {
        name: (value.shape, value.dtype)
        for name, value in loaded.items()
        if name not in ("third_part", "second", "first")
    }
    scratch |= dict(
        down_full=((4, 2, down_blocks, share, depth), BF16),
        up_full=((4, 2, 4, share, hidden), BF16),
        down_into=((4, down_blocks, share, depth), BF16),
        down_away=((3, down_blocks, share, depth), BF16),
        down_result=((down_blocks, share, depth), BF16),
        up_into=((4, 4, share, hidden), BF16),
        up_away=((3, 4, share, hidden), BF16),
        up_result=((4, share, hidden), BF16),
        peaks_ctx=((8, 8, 128), F32),
        norms=((8, depth), F32),
        norms_seq=((4, 8, depth // 4), F32),
        norms_ctx=((8, 8, depth // 4), F32),
        cross_branch=((4 * rows, depth), BF16),
        self_branch=((4 * rows, depth), BF16),
        grad_sum=((rows, depth), F32),
        rs_out=((4, 3, rows, depth), BF16),
        rs_in=((4, 3, rows, depth), BF16),
        enc_out=((3, source_rows, depth), BF16),
        enc_in=((3, source_rows, depth), BF16),
        dquery=((4 * rows, width), BF16),
        dsource=((4 * source_rows, 2 * width), BF16),
        gsent=((8, rows, 128), BF16),
        gheads=((8 * rows, 128), BF16),
        columns=((1, 8 * rows), jnp.int32),
        acc=((2, 8 * rows, 128), F32),
        dq_own=((8 * rows, 128), BF16),
        dkv_own=((2, 8 * rows, 128), BF16),
        dproj=((3, 4 * rows, width), BF16),
    )
    for name in ("co", "so"):
        scratch[name + "_full"] = ((4, 2, 1, share, depth), BF16)
        scratch[name + "_into"] = ((4, 1, share, depth), BF16)
        scratch[name + "_away"] = ((3, 1, share, depth), BF16)
    for name, columns, r in (
        ("cq", width, share),
        ("ckv", 2 * width, share),
        ("qkv", 3 * width, share),
        ("dkv", 2 * width, source_rows),
    ):
        scratch[name + "_full"] = ((4, 4, 2, r, columns), BF16)
        scratch[name + "_into"] = ((4, 4, r, columns), BF16)
        scratch[name + "_away"] = ((3, 4, r, columns), BF16)
        scratch[name + "_result"] = ((4, r, columns), BF16)
    sems = dict(send_sem=224, recv_sem=224, local_sem=4, load_sem=len(loaded))
    names = list(inputs) + list(outs) + list(scratch) + list(sems)

    def kernel(*refs):
        held = dict(zip(names, refs), loaded=tuple(loaded))
        backward_body(type("Refs", (), held))

    made = pl.pallas_call(
        kernel,
        in_specs=[spec for spec, _ in inputs.values()],
        out_specs=[vmem] * len(outs),
        out_shape=[jax.ShapeDtypeStruct(*shape) for shape in outs.values()],
        scratch_shapes=[pltpu.VMEM(*shape) for shape in scratch.values()]
        + [pltpu.SemaphoreType.DMA((count,)) for count in sems.values()],
        compiler_params=pltpu.CompilerParams(
            collective_id=1, has_side_effects=True, vmem_limit_bytes=60 * 2**20
        ),
        name="backward",
    )(*[value for _, value in inputs.values()])
    return dict(zip(outs, made))


def finish_kernel(
    clip_ref,
    peaks_ref,
    norm_ref,
    qkv_w,
    cq_w,
    ckv_w,
    output_ref,
    inputs_ref,
    source_ref,
    down_ref,
    co_ref,
    so_ref,
    up_ref,
    cq_ref,
    ckv_ref,
    qkv_ref,
    output_out,
    inputs_out,
    source_out,
    qkv_out,
    so_out,
    cq_out,
    ckv_out,
    co_out,
    up_out,
    down_out,
    gain_out,
    bias_out,
    self_out,
    cross_out,
):
    output_out[0] = output_ref[...]
    inputs_out[0] = inputs_ref[...]
    source_out[0] = source_ref[...]
    share = so_out.shape[0]
    so_out[...] = so_ref[0].astype(F32)
    co_out[...] = co_ref[0].astype(F32)
    for block in range(down_ref.shape[0]):
        down_out[block * share : (block + 1) * share] = down_ref[block].astype(F32)

    def columns(out, taken, parts):
        whole, width = out.shape[1] // parts, out.shape[1] // (4 * parts)
        for owner in range(4):
            for part in range(parts):
                at = part * whole + owner * width
                out[:, at : at + width] = taken[owner, :, part * width : (part + 1) * width].astype(
                    F32
                )

    columns(up_out, up_ref, 1)
    columns(cq_out, cq_ref, 1)
    columns(ckv_out, ckv_ref, 2)
    columns(qkv_out, qkv_ref, 3)
    spread = gain_out.shape[1]
    turned = pltpu.roll(norm_ref[...], norm_ref.shape[1] - lax.axis_index("ctx") * spread, 1)
    gain_out[...] = turned[0:3, :spread]
    bias_out[...] = turned[3:6, :spread]
    lane = lax.broadcasted_iota(jnp.int32, (1, 128), 1)
    held = peaks_ref.shape[1] // 2
    for owner in range(4):
        for two in range(held // 2):
            head = owner * held + two * 2
            at = slice(head * HD, head * HD + 128)
            for kind, jobs in (
                (0, ((self_out, qkv_w, 0, 0), (self_out, qkv_w, H * HD, H * HD))),
                (1, ((cross_out, cq_w, 0, 0), (cross_out, ckv_w, 0, H * HD))),
            ):
                top = [peaks_ref[owner, kind * held + two * 2 + i : kind * held + two * 2 + i + 1] for i in (0, 1)]
                limit = [clip_ref[kind, head + i] for i in (0, 1)]
                limits = jnp.where(lane < HD, limit[0], limit[1])
                tops = jnp.where(lane < HD, top[0], top[1])
                factor = jnp.sqrt(limits / jnp.maximum(tops, limits))
                for out, weight, start, goal in jobs:
                    out[:, goal + head * HD : goal + head * HD + 128] = (
                        weight[:, start + head * HD : start + head * HD + 128].astype(F32) * factor
                    ).astype(BF16)


def finish_call(made, given):
    rows, depth = given["tokens"].shape[1:]
    hidden = given["mlp_up"].shape[1]
    source_rows, share = made["grad_source"].shape[0], made["so_result"].shape[1]
    columns = H * HD
    weight_rows = given["self_qkv"].shape[0]
    shapes = [
        ((1, rows, depth), BF16),
        ((1, rows, depth), F32),
        ((1, source_rows, depth), F32),
        ((share, 3 * columns), F32),
        ((share, depth), F32),
        ((share, columns), F32),
        ((share, 2 * columns), F32),
        ((share, depth), F32),
        ((share, hidden), F32),
        ((hidden // 32, depth), F32),
        ((3, share), F32),
        ((3, share), F32),
        ((weight_rows, 2 * columns), BF16),
        ((weight_rows, 2 * columns), BF16),
    ]
    vmem = pl.BlockSpec(memory_space=pltpu.VMEM)
    return pl.pallas_call(
        finish_kernel,
        in_specs=[pl.BlockSpec(memory_space=pltpu.SMEM)] + [vmem] * 15,
        out_specs=[vmem] * len(shapes),
        out_shape=[jax.ShapeDtypeStruct(*shape) for shape in shapes],
        compiler_params=pltpu.CompilerParams(vmem_limit_bytes=60 * 2**20),
        name="finish",
    )(
        given["clip"],
        made["peaks_seq"],
        made["norm_sum"],
        given["self_qkv"],
        given["cross_q"],
        given["cross_kv"],
        made["output"],
        made["grad_inputs"],
        made["grad_source"],
        made["down_taken"],
        made["co_result"],
        made["so_result"],
        made["up_taken"],
        made["cq_taken"],
        made["ckv_taken"],
        made["qkv_taken"],
    )


def fast_device(
    tokens,
    encoder_states,
    cotangent,
    target_lengths,
    source_lengths,
    block_table,
    self_qkv,
    self_out,
    cross_q,
    cross_kv,
    cross_out,
    mlp_up,
    mlp_down,
    norm_gain,
    norm_bias,
    clip_limit,
):
    kept = forward_call(
        block_table,
        target_lengths,
        source_lengths,
        tokens,
        encoder_states,
        cotangent,
        self_qkv,
        self_out,
        cross_q,
        cross_kv,
        cross_out,
        mlp_up,
        mlp_down,
        norm_gain,
        norm_bias,
    )
    given = dict(
        table=block_table,
        target=target_lengths,
        tokens=tokens,
        cotangent=cotangent,
        gain=norm_gain,
        cross_out=cross_out,
        self_out=self_out,
        self_qkv=self_qkv,
        cross_q=cross_q,
        cross_kv=cross_kv,
        mlp_up=mlp_up,
        clip=clip_limit,
    )
    made = backward_call(kept, given)
    held = H // 4
    tops = made["peaks_seq"][:, :, 0].reshape(4, 2, held).transpose(1, 0, 2).reshape(2, H)
    return (*finish_call(made, given), tops)


def solution(mesh):
    body = fast_device if fast_fits(mesh) else general_device
    return jax.shard_map(
        body,
        mesh=mesh,
        in_specs=(
            P("seq", "ctx", None),
            P("seq", "ctx", None),
            P("seq", "ctx", None),
            P("seq"),
            P("seq"),
            P(),
            P("seq", None),
            P("seq", None),
            P("seq", None),
            P("seq", None),
            P("seq", None),
            P("seq", None),
            P("seq", None),
            P(),
            P(),
            P(),
        ),
        out_specs=(
            P("seq", "ctx", None),
            P("seq", "ctx", None),
            P("seq", "ctx", None),
            P(("seq", "ctx"), None),
            P(("seq", "ctx"), None),
            P(("seq", "ctx"), None),
            P(("seq", "ctx"), None),
            P(("seq", "ctx"), None),
            P(("seq", "ctx"), None),
            P(("seq", "ctx"), None),
            P(None, ("seq", "ctx")),
            P(None, ("seq", "ctx")),
            P("seq", None),
            P("seq", None),
            P(),
        ),
        check_vma=False,
    )
```

```python
import functools

import jax
import jax.numpy as jnp
from jax import lax
from jax.experimental import pallas as pl
from jax.experimental.pallas import tpu as pltpu
from jax.sharding import PartitionSpec as P

H = 16
HD = 64


masked_score = -1000000000.0
norm_eps = 1e-05


def block_size(count):
    return max((step for step in range(1, min(count, 512) + 1) if count % step == 0))


def layer_norm(values, gain, bias):
    centered = values - jnp.mean(values, axis=-1, keepdims=True)
    spread = jnp.mean(centered * centered, axis=-1, keepdims=True)
    return centered * lax.rsqrt(spread + norm_eps) * gain + bias


def allowed_pairs(query_pos, key_pos, key_limit, causal):
    allowed = jnp.broadcast_to(
        (key_pos < key_limit)[None, :], (query_pos.shape[0], key_pos.shape[0])
    )
    if causal:
        allowed = allowed & (key_pos[None, :] <= query_pos[:, None])
    return allowed


def head_scores(query_heads, key_rows):
    key_heads = key_rows.reshape(key_rows.shape[0], H, HD)
    return jnp.einsum(
        "qhd,khd->hqk", query_heads, key_heads, preferred_element_type=jnp.float32
    ) * HD ** (-0.5)


def softmax_stats(query_heads, kv_rows, key_pos, query_pos, query_ok, key_limit, causal):
    count = kv_rows.shape[0]
    step = block_size(count)
    width = H * HD
    rows = query_heads.shape[0]

    def softmax_visit(carry, block):
        top, total, peak = carry
        block_rows, block_pos = block
        allowed = allowed_pairs(query_pos, block_pos, key_limit, causal)
        scores = jnp.where(
            allowed[None], head_scores(query_heads, block_rows[:, :width]), masked_score
        )
        new_top = jnp.maximum(top, jnp.max(scores, axis=-1))
        total = total * jnp.exp(top - new_top) + jnp.sum(
            jnp.exp(scores - new_top[..., None]), axis=-1
        )
        counted = jnp.where((allowed & query_ok[:, None])[None], scores, masked_score)
        peak = jnp.maximum(peak, jnp.max(counted, axis=(1, 2)))
        return ((new_top, total, peak), None)

    start = (
        jnp.full((H, rows), -jnp.inf, jnp.float32),
        jnp.zeros((H, rows), jnp.float32),
        jnp.full((H,), masked_score, jnp.float32),
    )
    blocks = (kv_rows.reshape(count // step, step, 2 * width), key_pos.reshape(count // step, step))
    return lax.scan(softmax_visit, start, blocks)[0]


def attend_values(query_heads, kv_rows, key_pos, query_pos, key_limit, causal, top, total):
    count = kv_rows.shape[0]
    step = block_size(count)
    width = H * HD
    rows = query_heads.shape[0]

    def attend_visit(acc, block):
        block_rows, block_pos = block
        allowed = allowed_pairs(query_pos, block_pos, key_limit, causal)
        scores = jnp.where(
            allowed[None], head_scores(query_heads, block_rows[:, :width]), masked_score
        )
        weights = (jnp.exp(scores - top[..., None]) / total[..., None]).astype(jnp.bfloat16)
        value_heads = block_rows[:, width:].reshape(step, H, HD)
        return (
            acc
            + jnp.einsum("hqk,khd->qhd", weights, value_heads, preferred_element_type=jnp.float32),
            None,
        )

    blocks = (kv_rows.reshape(count // step, step, 2 * width), key_pos.reshape(count // step, step))
    acc = lax.scan(attend_visit, jnp.zeros((rows, H, HD), jnp.float32), blocks)[0]
    return acc.reshape(rows, width)


def query_grads(
    query_heads, kv_rows, key_pos, query_pos, key_limit, causal, top, total, grad_heads, delta
):
    count = kv_rows.shape[0]
    step = block_size(count)
    width = H * HD
    rows = query_heads.shape[0]

    def query_visit(acc, block):
        block_rows, block_pos = block
        allowed = allowed_pairs(query_pos, block_pos, key_limit, causal)
        scores = jnp.where(
            allowed[None], head_scores(query_heads, block_rows[:, :width]), masked_score
        )
        probs = jnp.exp(scores - top[..., None]) / total[..., None]
        value_heads = block_rows[:, width:].reshape(step, H, HD)
        dprobs = jnp.einsum(
            "qhd,khd->hqk", grad_heads, value_heads, preferred_element_type=jnp.float32
        )
        dscores = (probs * (dprobs - delta[..., None])).astype(jnp.bfloat16)
        key_heads = block_rows[:, :width].reshape(step, H, HD)
        return (
            acc
            + jnp.einsum("hqk,khd->qhd", dscores, key_heads, preferred_element_type=jnp.float32),
            None,
        )

    blocks = (kv_rows.reshape(count // step, step, 2 * width), key_pos.reshape(count // step, step))
    acc = lax.scan(query_visit, jnp.zeros((rows, H, HD), jnp.float32), blocks)[0]
    return acc.reshape(rows, width) * HD ** (-0.5)


def key_grads(
    query_heads,
    kv_rows,
    key_pos,
    query_pos,
    key_limit,
    causal,
    top,
    total,
    grad_heads,
    delta,
    start,
    count,
):
    step = block_size(count)
    width = H * HD

    def piece(index):
        offset = start + index * step
        block_rows = lax.dynamic_slice_in_dim(kv_rows, offset, step, 0)
        block_pos = lax.dynamic_slice_in_dim(key_pos, offset, step, 0)
        allowed = allowed_pairs(query_pos, block_pos, key_limit, causal)
        scores = jnp.where(
            allowed[None], head_scores(query_heads, block_rows[:, :width]), masked_score
        )
        probs = jnp.exp(scores - top[..., None]) / total[..., None]
        value_heads = block_rows[:, width:].reshape(step, H, HD)
        dprobs = jnp.einsum(
            "qhd,khd->hqk", grad_heads, value_heads, preferred_element_type=jnp.float32
        )
        dscores = (probs * (dprobs - delta[..., None])).astype(jnp.bfloat16)
        dkeys = jnp.einsum(
            "hqk,qhd->khd", dscores, query_heads, preferred_element_type=jnp.float32
        ).reshape(step, width) * HD ** (-0.5)
        dvalues = jnp.einsum(
            "hqk,qhd->khd",
            probs.astype(jnp.bfloat16),
            grad_heads,
            preferred_element_type=jnp.float32,
        ).reshape(step, width)
        return jnp.concatenate([dkeys, dvalues], axis=1)

    return lax.map(piece, jnp.arange(count // step, dtype=jnp.int32)).reshape(count, 2 * width)


def split_rows(grad, seq_count, ctx_count):
    return grad.reshape(
        (seq_count, ctx_count, grad.shape[0] // (seq_count * ctx_count)) + grad.shape[1:]
    )


def join_rows(grad):
    return grad.reshape((grad.shape[2],) + grad.shape[3:])


def general_device(
    tokens,
    encoder_states,
    cotangent,
    target_lengths,
    source_lengths,
    block_table,
    self_qkv,
    self_out,
    cross_q,
    cross_kv,
    cross_out,
    mlp_up,
    mlp_down,
    norm_gain,
    norm_bias,
    clip_limit,
):
    rows = tokens.shape[1]
    width = H * HD
    half = rows // 2
    source_rows = encoder_states.shape[1]
    seq_count = lax.axis_size("seq")
    ctx_count = lax.axis_size("ctx")
    all_positions = (
        block_table[:, :, None] * half + jnp.arange(half, dtype=jnp.int32)[None, None, :]
    ).reshape(-1)
    own_positions = lax.dynamic_slice_in_dim(all_positions, lax.axis_index("ctx") * rows, rows, 0)
    length = target_lengths[0]
    source_length = source_lengths[0]
    query_ok = own_positions < length
    valid_rows = query_ok[:, None]
    source_positions = jnp.arange(source_rows * ctx_count, dtype=jnp.int32)
    w_qkv, w_out, w_cq, w_ckv, w_co = (
        lax.all_gather(self_qkv, "seq", axis=0, tiled=True),
        lax.all_gather(self_out, "seq", axis=0, tiled=True),
        lax.all_gather(cross_q, "seq", axis=0, tiled=True),
        lax.all_gather(cross_kv, "seq", axis=0, tiled=True),
        lax.all_gather(cross_out, "seq", axis=0, tiled=True),
    )
    inputs = tokens[0].astype(jnp.float32)
    first_norm, first_back = jax.vjp(layer_norm, inputs, norm_gain[0], norm_bias[0])
    first_low = first_norm.astype(jnp.bfloat16)
    projected = jnp.dot(first_low, w_qkv, preferred_element_type=jnp.float32).astype(jnp.bfloat16)
    self_query = projected[:, :width].reshape(rows, H, HD)
    source_kv = jnp.dot(encoder_states[0], w_ckv, preferred_element_type=jnp.float32).astype(
        jnp.bfloat16
    )
    self_kv, cross_kvs = (
        lax.all_gather(projected[:, width:], "ctx", axis=0, tiled=True),
        lax.all_gather(source_kv, "ctx", axis=0, tiled=True),
    )
    self_top, self_total, self_peak = softmax_stats(
        self_query, self_kv, all_positions, own_positions, query_ok, length, True
    )
    self_mix = attend_values(
        self_query, self_kv, all_positions, own_positions, length, True, self_top, self_total
    )
    self_low = self_mix.astype(jnp.bfloat16)
    first_sum = inputs + jnp.dot(self_low, w_out, preferred_element_type=jnp.float32)
    second_norm, second_back = jax.vjp(layer_norm, first_sum, norm_gain[1], norm_bias[1])
    second_low = second_norm.astype(jnp.bfloat16)
    cross_rows = jnp.dot(second_low, w_cq, preferred_element_type=jnp.float32).astype(jnp.bfloat16)
    cross_query = cross_rows.reshape(rows, H, HD)
    cross_top, cross_total, cross_peak = softmax_stats(
        cross_query, cross_kvs, source_positions, own_positions, query_ok, source_length, False
    )
    cross_mix = attend_values(
        cross_query,
        cross_kvs,
        source_positions,
        own_positions,
        source_length,
        False,
        cross_top,
        cross_total,
    )
    cross_low = cross_mix.astype(jnp.bfloat16)
    second_sum = first_sum + jnp.dot(cross_low, w_co, preferred_element_type=jnp.float32)
    third_norm, third_back = jax.vjp(layer_norm, second_sum, norm_gain[2], norm_bias[2])
    third_low = third_norm.astype(jnp.bfloat16)
    w_up, w_down = (
        lax.all_gather(mlp_up, "seq", axis=0, tiled=True),
        lax.all_gather(mlp_down, "seq", axis=0, tiled=True),
    )
    hidden_pre = jnp.dot(third_low, w_up, preferred_element_type=jnp.float32)
    hidden_act, gelu_back = jax.vjp(jax.nn.gelu, hidden_pre)
    hidden_low = hidden_act.astype(jnp.bfloat16)
    third_sum = second_sum + jnp.dot(hidden_low, w_down, preferred_element_type=jnp.float32)
    output_rows = jnp.where(valid_rows, third_sum, 0.0).astype(jnp.bfloat16)
    peaks = lax.pmax(jnp.stack([self_peak, cross_peak]), ("seq", "ctx"))
    grad_rows = jnp.where(valid_rows, cotangent[0].astype(jnp.float32), 0.0)
    mlp_branch = grad_rows.astype(jnp.bfloat16)
    grad_down = jnp.einsum("rf,rd->fd", hidden_low, mlp_branch, preferred_element_type=jnp.float32)
    grad_act = jnp.einsum("rd,fd->rf", mlp_branch, w_down, preferred_element_type=jnp.float32)
    grad_pre = gelu_back(grad_act)[0].astype(jnp.bfloat16)
    grad_up = jnp.einsum("rd,rf->df", third_low, grad_pre, preferred_element_type=jnp.float32)
    back_third, gain_three, bias_three = third_back(
        jnp.einsum("rf,df->rd", grad_pre, w_up, preferred_element_type=jnp.float32)
    )
    up_part, down_part = (
        lax.psum_scatter(
            split_rows(grad_up, seq_count, ctx_count).astype(jnp.bfloat16),
            "ctx",
            scatter_dimension=1,
            tiled=True,
        ).astype(jnp.float32),
        lax.psum_scatter(
            split_rows(grad_down, seq_count, ctx_count).astype(jnp.bfloat16),
            "ctx",
            scatter_dimension=1,
            tiled=True,
        ).astype(jnp.float32),
    )
    up_shard, down_shard = (
        lax.psum_scatter(
            up_part.astype(jnp.bfloat16), "seq", scatter_dimension=0, tiled=True
        ).astype(jnp.float32),
        lax.psum_scatter(
            down_part.astype(jnp.bfloat16), "seq", scatter_dimension=0, tiled=True
        ).astype(jnp.float32),
    )
    grad_second = grad_rows + back_third
    cross_branch = grad_second.astype(jnp.bfloat16)
    grad_co = jnp.einsum("rd,re->de", cross_low, cross_branch, preferred_element_type=jnp.float32)
    cross_heads_grad = (
        jnp.einsum("re,de->rd", cross_branch, w_co, preferred_element_type=jnp.float32)
        .astype(jnp.bfloat16)
        .reshape(rows, H, HD)
    )
    cross_delta = jnp.einsum(
        "qhd,qhd->hq", cross_heads_grad.astype(jnp.float32), cross_mix.reshape(rows, H, HD)
    )
    grad_cross_rows = query_grads(
        cross_query,
        cross_kvs,
        source_positions,
        own_positions,
        source_length,
        False,
        cross_top,
        cross_total,
        cross_heads_grad,
        cross_delta,
    ).astype(jnp.bfloat16)
    grad_source_kv = lax.psum_scatter(
        key_grads(
            cross_query,
            cross_kvs,
            source_positions,
            own_positions,
            source_length,
            False,
            cross_top,
            cross_total,
            cross_heads_grad,
            cross_delta,
            jnp.int32(0),
            source_rows * lax.axis_size("ctx"),
        ).astype(jnp.bfloat16),
        "ctx",
        scatter_dimension=0,
        tiled=True,
    )
    grad_cq = jnp.einsum(
        "rd,re->de", second_low, grad_cross_rows, preferred_element_type=jnp.float32
    )
    grad_ckv = jnp.einsum(
        "sd,se->de", encoder_states[0], grad_source_kv, preferred_element_type=jnp.float32
    )
    grad_source = jnp.einsum("se,de->sd", grad_source_kv, w_ckv, preferred_element_type=jnp.float32)
    back_second, gain_two, bias_two = second_back(
        jnp.einsum("re,de->rd", grad_cross_rows, w_cq, preferred_element_type=jnp.float32)
    )
    grad_first = grad_second + back_second
    self_branch = grad_first.astype(jnp.bfloat16)
    grad_so = jnp.einsum("rd,re->de", self_low, self_branch, preferred_element_type=jnp.float32)
    self_heads_grad = (
        jnp.einsum("re,de->rd", self_branch, w_out, preferred_element_type=jnp.float32)
        .astype(jnp.bfloat16)
        .reshape(rows, H, HD)
    )
    self_delta = jnp.einsum(
        "qhd,qhd->hq", self_heads_grad.astype(jnp.float32), self_mix.reshape(rows, H, HD)
    )
    grad_query = query_grads(
        self_query,
        self_kv,
        all_positions,
        own_positions,
        length,
        True,
        self_top,
        self_total,
        self_heads_grad,
        self_delta,
    ).astype(jnp.bfloat16)
    grad_kv = lax.psum_scatter(
        key_grads(
            self_query,
            self_kv,
            all_positions,
            own_positions,
            length,
            True,
            self_top,
            self_total,
            self_heads_grad,
            self_delta,
            jnp.int32(0),
            rows * lax.axis_size("ctx"),
        ).astype(jnp.bfloat16),
        "ctx",
        scatter_dimension=0,
        tiled=True,
    )
    grad_projected = jnp.concatenate([grad_query, grad_kv], axis=1)
    grad_qkv = jnp.einsum(
        "rd,re->de", first_low, grad_projected, preferred_element_type=jnp.float32
    )
    back_first, gain_one, bias_one = first_back(
        jnp.einsum("re,de->rd", grad_projected, w_qkv, preferred_element_type=jnp.float32)
    )
    grad_inputs = grad_first + back_first
    norm_terms = jnp.stack([gain_one, gain_two, gain_three, bias_one, bias_two, bias_three], axis=1)
    qkv_part, out_part, cq_part, ckv_part, co_part, norm_part = (
        lax.psum_scatter(
            split_rows(grad_qkv, seq_count, ctx_count).astype(jnp.bfloat16),
            "ctx",
            scatter_dimension=1,
            tiled=True,
        ).astype(jnp.float32),
        lax.psum_scatter(
            split_rows(grad_so, seq_count, ctx_count).astype(jnp.bfloat16),
            "ctx",
            scatter_dimension=1,
            tiled=True,
        ).astype(jnp.float32),
        lax.psum_scatter(
            split_rows(grad_cq, seq_count, ctx_count).astype(jnp.bfloat16),
            "ctx",
            scatter_dimension=1,
            tiled=True,
        ).astype(jnp.float32),
        lax.psum_scatter(
            split_rows(grad_ckv, seq_count, ctx_count).astype(jnp.bfloat16),
            "ctx",
            scatter_dimension=1,
            tiled=True,
        ).astype(jnp.float32),
        lax.psum_scatter(
            split_rows(grad_co, seq_count, ctx_count).astype(jnp.bfloat16),
            "ctx",
            scatter_dimension=1,
            tiled=True,
        ).astype(jnp.float32),
        lax.psum_scatter(
            split_rows(norm_terms, seq_count, ctx_count).astype(jnp.bfloat16),
            "ctx",
            scatter_dimension=1,
            tiled=True,
        ).astype(jnp.float32),
    )
    qkv_shard, out_shard, cq_shard, ckv_shard, co_shard, norm_shard = (
        lax.psum_scatter(
            qkv_part.astype(jnp.bfloat16), "seq", scatter_dimension=0, tiled=True
        ).astype(jnp.float32),
        lax.psum_scatter(
            out_part.astype(jnp.bfloat16), "seq", scatter_dimension=0, tiled=True
        ).astype(jnp.float32),
        lax.psum_scatter(
            cq_part.astype(jnp.bfloat16), "seq", scatter_dimension=0, tiled=True
        ).astype(jnp.float32),
        lax.psum_scatter(
            ckv_part.astype(jnp.bfloat16), "seq", scatter_dimension=0, tiled=True
        ).astype(jnp.float32),
        lax.psum_scatter(
            co_part.astype(jnp.bfloat16), "seq", scatter_dimension=0, tiled=True
        ).astype(jnp.float32),
        lax.psum_scatter(
            norm_part.astype(jnp.bfloat16), "seq", scatter_dimension=0, tiled=True
        ).astype(jnp.float32),
    )
    norm_shard = join_rows(norm_shard)
    factors = jnp.sqrt(clip_limit / jnp.maximum(peaks, clip_limit))
    columns = jnp.repeat(factors, HD, axis=1)
    qkv_wide = self_qkv.astype(jnp.float32)
    clipped_self = jnp.concatenate(
        [qkv_wide[:, :width] * columns[0], qkv_wide[:, width : 2 * width] * columns[0]], axis=1
    ).astype(jnp.bfloat16)
    clipped_cross = jnp.concatenate(
        [
            cross_q.astype(jnp.float32) * columns[1],
            cross_kv[:, :width].astype(jnp.float32) * columns[1],
        ],
        axis=1,
    ).astype(jnp.bfloat16)
    return (
        output_rows[None],
        grad_inputs[None],
        grad_source[None],
        join_rows(qkv_shard),
        join_rows(out_shard),
        join_rows(cq_shard),
        join_rows(ckv_shard),
        join_rows(co_shard),
        join_rows(up_shard),
        join_rows(down_shard),
        norm_shard[:, :3].T,
        norm_shard[:, 3:].T,
        clipped_self,
        clipped_cross,
        peaks,
    )


F32 = jnp.float32
BF16 = jnp.bfloat16
SCALE = HD**-0.5


def fast_fits(mesh):
    seq_count, ctx_count = mesh.shape["seq"], mesh.shape["ctx"]
    if H % seq_count or H % ctx_count:
        return False
    held, pair = H // seq_count, H // ctx_count
    return held % pair == 0 and seq_count * (held // pair) == ctx_count and pair * HD == 128


def dot(left, right, contract=((1,), (0,))):
    return lax.dot_general(left, right, (contract, ((), ())), preferred_element_type=F32)


NT = ((1,), (1,))
TN = ((0,), (0,))


def norm_forward(values, gain, bias):
    centered = values - jnp.mean(values, axis=-1, keepdims=True)
    spread = jnp.mean(centered * centered, axis=-1, keepdims=True)
    inverse = lax.rsqrt(spread + norm_eps)
    hat = centered * inverse
    return hat, inverse, (hat * gain + bias).astype(BF16)


def norm_backward(grad, hat, inverse, gain):
    scaled = grad * gain
    inner = jnp.mean(scaled, axis=-1, keepdims=True)
    outer = jnp.mean(scaled * hat, axis=-1, keepdims=True)
    return (
        (scaled - inner - hat * outer) * inverse,
        jnp.sum(grad * hat, axis=0),
        jnp.sum(grad, axis=0),
    )


MESH = pl.DeviceIdType.MESH


class Links:
    def __init__(self, send, recv, local):
        self.send, self.recv, self.local = send, recv, local
        self.count, self.local_count = 0, 0
        self.sends, self.saves = [], []

    def slots(self, count):
        start = self.count
        self.count += count
        return start

    def copy(self, index, src, dst, device):
        return pltpu.make_async_remote_copy(
            src_ref=src,
            dst_ref=dst,
            send_sem=self.send.at[index],
            recv_sem=self.recv.at[index],
            device_id=device,
            device_id_type=MESH,
        )

    def push(self, index, src, dst, device, when=None):
        made = self.copy(index, src, dst, device)
        if when is None:
            made.start()
        else:
            pl.when(when)(made.start)
        self.sends.append((made, when))

    def take(self, index, dst, device, when=None):
        made = self.copy(index, dst, dst, device)
        if when is None:
            made.wait_recv()
        else:
            pl.when(when)(made.wait_recv)

    def save(self, src, dst):
        made = pltpu.make_async_copy(src, dst, self.local.at[self.local_count])
        self.local_count += 1
        made.start()
        self.saves.append(made)
        return made

    def finish(self):
        for made, when in self.sends:
            if when is None:
                made.wait_send()
            else:
                pl.when(when)(made.wait_send)
        for made in self.saves:
            made.wait()
        self.sends, self.saves = [], []


class Team:
    def __init__(self, own, near, far, opp):
        self.own, self.near, self.far, self.opp = own, near, far, opp

    def turned(self):
        return Team(self.own, self.far, self.near, self.opp)


class Place:
    def __init__(self):
        self.s, self.c = lax.axis_index("seq"), lax.axis_index("ctx")
        self.k, self.x = lax.rem(self.s, 2), lax.div(self.s, 2)
        self.y, self.z = lax.rem(self.c, 2), lax.div(self.c, 2)
        self.sib = self.s + 1 - 2 * self.k
        self.far = lax.rem(self.s + 2, 4)
        self.opp = lax.rem(self.sib + 2, 4)
        self.pair = self.c + 1 - 2 * self.y
        other = 1 - self.x
        self.seq = Team(self.s, ((self.sib, self.c), self.sib), ((self.far, self.c), self.far), ((self.opp, self.c), self.opp))
        self.flat = Team(
            self.x * 2 + self.y,
            ((self.s, self.pair), self.x * 2 + 1 - self.y),
            ((self.far, self.c), other * 2 + self.y),
            ((self.far, self.pair), other * 2 + 1 - self.y),
        )

    def greet(self):
        barrier = pltpu.get_barrier_semaphore()
        for other in (self.sib, self.far, self.opp):
            pl.semaphore_signal(barrier, inc=1, device_id=(other, self.c), device_id_type=MESH)
        for step in range(1, 8):
            pl.semaphore_signal(
                barrier,
                inc=1,
                device_id=(self.s, lax.rem(self.c + step, 8)),
                device_id_type=MESH,
            )
        for other in ((self.far, self.pair), (self.sib, self.pair)):
            pl.semaphore_signal(barrier, inc=1, device_id=other, device_id_type=MESH)
        pl.semaphore_wait(barrier, 12)


def rows_at(start, count):
    return pl.ds(pl.multiple_of(start, 16), count)


def lanes_at(start, count):
    return pl.ds(pl.multiple_of(start, 128), count)


class Columns:
    def __init__(self, links, place, weight, dest, parts, pieces=1):
        self.links, self.place, self.weight, self.dest = links, place, weight, dest
        rows, columns = weight.shape
        self.rows, self.whole, self.width = rows, columns // parts, columns // (4 * parts)
        self.step = rows // pieces
        self.jobs = [(part, piece) for piece in range(pieces) for part in range(parts)]
        self.base = {job: links.slots(5) for job in self.jobs}
        self.mine = place.k == place.y

    def source(self, job, target):
        part, piece = job
        return self.weight.at[
            pl.ds(piece * self.step, self.step),
            lanes_at(part * self.whole + target * self.width, self.width),
        ]

    def land(self, job, owner):
        part, piece = job
        return self.dest.at[
            rows_at(owner * self.rows + piece * self.step, self.step),
            pl.ds(part * self.width, self.width),
        ]

    def start(self, jobs=None):
        p = self.place
        for job in self.jobs if jobs is None else jobs:
            base = self.base[job]
            land = self.land(job, p.s)
            self.links.push(base, self.source(job, p.far), land, (p.far, p.c), self.mine)
            self.links.push(base + 1, self.source(job, p.opp), land, (p.opp, p.c), self.mine)
            self.links.push(base + 2, self.source(job, p.sib), land, (p.sib, p.c))
            self.links.save(self.source(job, p.s), land)

    def relay(self, jobs=None):
        p = self.place
        came = lax.rem(p.x + 1, 2) * 2 + p.y
        for job in self.jobs if jobs is None else jobs:
            base = self.base[job]
            land = self.land(job, came)
            self.links.take(base, land, (p.far, p.c), p.k == p.y)
            self.links.take(base + 1, land, (p.opp, p.c), p.k != p.y)
            self.links.push(base + 3, land, land, (p.s, p.pair))

    def finish(self):
        p = self.place
        for job in self.jobs:
            base = self.base[job]
            self.links.take(base + 2, self.land(job, p.sib), (p.sib, p.c))
            self.links.take(
                base + 3,
                self.land(job, lax.rem(p.x + 1, 2) * 2 + 1 - p.y),
                (p.s, p.pair),
            )


class Gather:
    def __init__(self, links, teams, dest, rows):
        self.links, self.teams, self.dest, self.rows = links, teams, dest, rows
        self.step = rows // len(teams)
        self.base = [links.slots(3) for _ in teams]

    def land(self, piece, owner):
        return self.dest.at[rows_at(owner * self.rows + piece * self.step, self.step)]

    def start(self, piece=0):
        t, base = self.teams[piece], self.base[piece]
        land = self.land(piece, t.own)
        self.links.push(base, land, land, t.far[0])
        self.links.push(base + 1, land, land, t.near[0])

    def forward(self, piece=0):
        t, base = self.teams[piece], self.base[piece]
        land = self.land(piece, t.far[1])
        self.links.take(base, land, t.far[0])
        self.links.push(base + 2, land, land, t.near[0])

    def finish(self, piece=0):
        t, base = self.teams[piece], self.base[piece]
        self.links.take(base + 1, self.land(piece, t.near[1]), t.near[0])
        self.links.take(base + 2, self.land(piece, t.opp[1]), t.near[0])

    def start_all(self):
        for piece in range(len(self.teams)):
            self.start(piece)

    def forward_all(self):
        for piece in range(len(self.teams)):
            self.forward(piece)

    def finish_all(self):
        for piece in range(len(self.teams)):
            self.finish(piece)


class Reduce:
    def __init__(self, links, teams, out, into, rows, partial):
        self.links, self.teams, self.out, self.into, self.partial = links, teams, out, into, partial
        self.step = rows // len(teams)
        self.base = [links.slots(3) for _ in teams]
        self.cut = [pl.ds(piece * self.step, self.step) for piece in range(len(teams))]

    def pieces(self):
        return [(piece, t, self.base[piece], self.cut[piece]) for piece, t in enumerate(self.teams)]

    def first(self):
        for piece, t, base, cut in self.pieces():
            self.out[0, cut] = self.partial(t.opp[1], piece).astype(BF16)
            self.links.push(base, self.out.at[0, cut], self.into.at[0, cut], t.near[0])
        for piece, t, base, cut in self.pieces():
            self.out[1, cut] = self.partial(t.near[1], piece).astype(BF16)
            self.links.push(base + 2, self.out.at[1, cut], self.into.at[1, cut], t.near[0])

    def second(self):
        for piece, t, base, cut in self.pieces():
            held = self.partial(t.far[1], piece).astype(F32)
            self.links.take(base, self.into.at[0, cut], t.near[0])
            self.out[2, cut] = (held + self.into[0, cut].astype(F32)).astype(BF16)
            self.links.push(base + 1, self.out.at[2, cut], self.into.at[2, cut], t.far[0])

    def last(self, then):
        for piece, t, base, cut in self.pieces():
            held = self.partial(t.own, piece).astype(F32)
            self.links.take(base + 2, self.into.at[1, cut], t.near[0])
            held = held + self.into[1, cut].astype(F32)
            self.links.take(base + 1, self.into.at[2, cut], t.far[0])
            then(piece, held + self.into[2, cut].astype(F32))

    def run(self, then):
        self.first()
        self.second()
        self.last(then)


class Shared:
    def __init__(self, links, place, weight, dest, pieces):
        self.links, self.place, self.weight, self.dest = links, place, weight, dest
        self.rows, self.width = weight.shape[0], weight.shape[1] // 4
        self.step = self.rows // pieces
        self.jobs = range(pieces)
        self.base = [links.slots(3) for _ in self.jobs]

    def source(self, job, slice_index):
        return self.weight.at[
            pl.ds(job * self.step, self.step), lanes_at(slice_index * self.width, self.width)
        ]

    def land(self, job, owner):
        return self.dest.at[rows_at(owner * self.rows + job * self.step, self.step)]

    def start(self, jobs):
        p = self.place
        for job in jobs:
            land = self.land(job, p.s)
            self.links.push(self.base[job], self.source(job, p.flat.far[1]), land, (p.far, p.c))
            self.links.push(self.base[job] + 1, self.source(job, p.flat.own), land, (p.sib, p.c))
            self.links.save(self.source(job, p.flat.own), land)

    def forward(self, jobs):
        p = self.place
        for job in jobs:
            land = self.land(job, p.far)
            self.links.take(self.base[job], land, (p.far, p.c))
            self.links.push(self.base[job] + 2, land, land, (p.sib, p.c))

    def finish(self):
        p = self.place
        for job in self.jobs:
            self.links.take(self.base[job] + 1, self.land(job, p.sib), (p.sib, p.c))
            self.links.take(self.base[job] + 2, self.land(job, p.opp), (p.sib, p.c))


def gelu_pair(value):
    rate = 0.7978845608028654
    square = value * value
    bent = jnp.tanh(rate * value * (1.0 + 0.044715 * square))
    half = 0.5 * (1.0 + bent)
    slope = half + 0.5 * value * (1.0 - bent * bent) * (rate * (1.0 + 0.134145 * square))
    return value * half, slope


def row_positions(table_ref, owner, half):
    place = lax.broadcasted_iota(jnp.int32, (2 * half, 1), 0)
    first, second = table_ref[owner, 0] * half, table_ref[owner, 1] * half - half
    return place + jnp.where(place < half, first, second)


def column_positions(table_ref, owner, half):
    place = lax.broadcasted_iota(jnp.int32, (1, 2 * half), 1)
    first, second = table_ref[owner, 0] * half, table_ref[owner, 1] * half - half
    return place + jnp.where(place < half, first, second)


def softmax_rows(scores):
    top = jnp.max(scores, axis=-1, keepdims=True)
    expos = jnp.exp(scores - top)
    return expos * (1.0 / jnp.sum(expos, axis=-1, keepdims=True)), top


def softmax_columns(scores):
    expos = jnp.exp(scores - jnp.max(scores, axis=0, keepdims=True))
    return expos * (1.0 / jnp.sum(expos, axis=0, keepdims=True))


PIECES = 2
STEPS = 8


def forward_kernel(
    table_ref,
    target_ref,
    source_ref,
    tokens_ref,
    encoder_ref,
    cotangent_ref,
    qkv_ref,
    out_ref,
    cq_ref,
    ckv_ref,
    co_ref,
    up_ref,
    down_ref,
    gain_ref,
    bias_ref,
    first_out,
    second_out,
    third_out,
    branch_out,
    source_out,
    w_qkv_out,
    w_cq_out,
    w_ckv_out,
    hidden_out,
    slopes_out,
    grad_third_out,
    third_part_out,
    heads_out,
    mix_out,
    query_out,
    kvs_out,
    cross_out_ref,
    sums_out,
    peak_out,
    lens_out,
    first,
    second,
    third,
    branch,
    source,
    w_qkv,
    w_cq,
    w_ckv,
    sent,
    heads,
    mix_own,
    mix,
    query,
    kv_own,
    kvs,
    cross,
    sums,
    columns,
    lens,
    rs_out,
    rs_in,
    part,
    w_up,
    w_down,
    hidden,
    slopes,
    grad_third,
    third_part,
    send_sem,
    recv_sem,
    local_sem,
):
    place, links = Place(), Links(send_sem, recv_sem, local_sem)
    p = place
    rows = tokens_ref.shape[1]
    source_rows = encoder_ref.shape[1]
    half = rows // 2
    width = w_cq.shape[1]
    pair_width = heads.shape[2]
    held = width // HD
    groups = width // pair_width
    place.greet()

    get_qkv = Columns(links, place, qkv_ref, w_qkv, 3)
    get_qkv.start()

    own = rows_at(p.s * rows, rows)
    inputs = tokens_ref[0].astype(F32)
    first[own] = norm_forward(inputs, gain_ref[0:1], bias_ref[0:1])[2]
    get_first = Gather(links, (p.seq,), first, rows)
    get_first.start()
    source[rows_at(p.s * source_rows, source_rows)] = encoder_ref[0]
    get_source = Gather(links, (p.seq,), source, source_rows)
    get_source.start()
    place_lens = links.slots(3)
    line = lax.broadcasted_iota(jnp.int32, (8, 128), 0)
    lens[pl.ds(p.s, 1)] = jnp.where(line < 4, target_ref[0], source_ref[0])[None]
    own_lens = lens.at[pl.ds(p.s, 1)]
    for step, other in enumerate((p.far, p.opp, p.sib)):
        links.push(place_lens + step, own_lens, own_lens, (other, p.c))
    for owner in range(STEPS):
        columns[:, owner * rows : (owner + 1) * rows] = column_positions(table_ref, owner, half)
    own_rows = row_positions(table_ref, p.c, half)
    valid = own_rows < target_ref[0]
    own_flat = p.flat.own * rows
    branch[rows_at(own_flat, rows)] = jnp.where(valid, cotangent_ref[0].astype(F32), 0.0).astype(BF16)
    get_cq = Columns(links, place, cq_ref, w_cq, 1)
    get_ckv = Columns(links, place, ckv_ref, w_ckv, 2)
    get_up = Shared(links, place, up_ref, w_up, 4)
    flat = (p.flat, p.flat.turned())

    get_qkv.relay()
    get_first.forward()
    get_source.forward()
    get_first.finish()
    get_source.finish()
    for made in links.saves:
        made.wait()
    links.saves = []
    get_qkv.finish()
    links.save(first, first_out)
    links.save(w_qkv, w_qkv_out)
    links.save(source, source_out)
    for step, other in enumerate((p.far, p.opp, p.sib)):
        links.take(place_lens + step, lens.at[pl.ds(other, 1)], (other, p.c))
    links.save(lens, lens_out)

    def project(block, carry):
        value = dot(first[rows_at(block * rows, rows)], w_qkv[...]).astype(BF16)
        for group in range(groups):
            for part in range(3):
                at = part * width + group * pair_width
                sent[block * groups + group, part] = value[:, at : at + pair_width]
        return carry

    lax.fori_loop(0, 4, project, 0)
    a2a = links.slots(STEPS)
    mine = rows_at(p.c * rows, rows)
    for step in range(1, STEPS):
        other = lax.rem(p.c + step, STEPS)
        links.push(a2a + step, sent.at[other], heads.at[:, mine], (p.s, other))
    keep = pltpu.make_async_copy(sent.at[p.c], heads.at[:, mine], local_sem.at[STEPS * 8 - 1])
    keep.start()
    get_cq.start()
    get_ckv.start()
    get_up.start((0, 1))
    keeps = p.k == p.y
    get_down = links.slots(1)
    links.push(get_down, down_ref, w_down, (p.sib, p.c), keeps)
    own_down = pltpu.make_async_copy(down_ref, w_down, local_sem.at[STEPS * 8 - 2])
    pl.when(keeps)(own_down.start)
    get_branch = Gather(links, flat, branch, rows)
    get_branch.start_all()
    keep.wait()
    get_cq.relay()
    get_ckv.relay()
    for step in range(1, STEPS):
        other = lax.rem(p.c + STEPS - step, STEPS)
        links.take(a2a + step, heads.at[:, rows_at(other * rows, rows)], (p.s, other))
    links.save(heads, heads_out)

    my_slot = lax.div(p.c, groups)
    my_group = lax.rem(p.c, groups)
    length = lens[pl.ds(my_slot, 1)][0, 0:1, 0:1]
    back = links.slots(STEPS)
    slot_rows = rows_at(my_slot * rows, rows)
    group_lanes = lanes_at(my_group * pair_width, pair_width)

    def back_copy(owner):
        return links.copy(
            back + p.c, mix_own.at[rows_at(owner * rows, rows)], mix.at[slot_rows, group_lanes], (p.s, owner)
        )

    columns[...] = jnp.where(columns[...] < length, columns[...], STEPS * rows)

    def attend(block, peaks):
        at = rows_at(block * 2 * rows, 2 * rows)
        row_pos = jnp.concatenate(
            [row_positions(table_ref, 2 * block, half), row_positions(table_ref, 2 * block + 1, half)], axis=0
        )
        allowed = columns[...] <= row_pos
        ok = row_pos < length
        tops = []
        for head in range(pair_width // HD):
            cut = slice(head * HD, (head + 1) * HD)
            scores = dot(heads[0, at, cut], heads[1, :, cut], NT) * SCALE
            probs, top = softmax_rows(jnp.where(allowed, scores, masked_score))
            mix_own[at, cut] = dot(probs.astype(BF16), heads[2, :, cut]).astype(BF16)
            peak = jnp.max(jnp.where(ok, top, masked_score), axis=0, keepdims=True)
            tops.append(jnp.maximum(peaks[head], peak))
        return tuple(tops)

    low = jnp.full((1, 1), masked_score, F32)
    peaks = (low, low)
    for block in range(STEPS // 2):
        peaks = attend(block, peaks)
        for owner in (2 * block, 2 * block + 1):
            pl.when(p.c != owner)(back_copy(owner).start)
    for head in range(2):
        peak_out[head : head + 1] = jnp.broadcast_to(peaks[head], (1, 128))
    mix[slot_rows, group_lanes] = mix_own[mine]

    get_cq.finish()
    get_ckv.finish()
    for made in links.saves:
        made.wait()
    links.saves = []
    links.save(w_cq, w_cq_out)
    links.save(w_ckv, w_ckv_out)
    value = dot(source[...], w_ckv[...]).astype(BF16)
    for slot in range(4):
        kv_own[slot] = value[slot * source_rows : (slot + 1) * source_rows]
    own_keys = rows_at(p.c * source_rows, source_rows)
    kvs[:, own_keys] = kv_own[...]
    along, across = links.slots(4), links.slots(4)
    links.push(across, kv_own, kvs.at[:, own_keys], (p.s, p.pair))
    for step in range(1, 4):
        other = lax.rem(p.z + step, 4) * 2 + p.y
        links.push(along + step, kv_own, kvs.at[:, own_keys], (p.s, other))
    get_up.forward((0, 1))
    get_branch.forward_all()

    for owner in range(STEPS):

        @pl.when(p.c != owner)
        def _():
            lane = lanes_at((owner % groups) * pair_width, pair_width)
            links.take(
                back + owner, mix.at[pl.ds((owner // groups) * rows, rows), lane], (p.s, owner)
            )

    links.save(mix, mix_out)

    def boundary(index, left, weight, base, gather, start):
        step = rows // PIECES

        def tile(number, carry):
            lanes = lanes_at(number * 256, 256)
            part[:, lanes] = dot(left[...], weight[:, lanes]).astype(BF16)
            return carry

        lax.fori_loop(0, part.shape[1] // 256, tile, 0)

        def then(piece, total):
            cut = pl.ds(piece * step, step)
            value = base(piece) + total
            sums[index, cut] = value
            gather.dest[rows_at(start + piece * step, step)] = norm_forward(
                value, gain_ref[index + 1 : index + 2], bias_ref[index + 1 : index + 2]
            )[2]
            gather.start(piece)

        Reduce(
            links,
            (p.seq,) * PIECES,
            rs_out.at[index],
            rs_in.at[index],
            rows,
            lambda block, piece: part[rows_at(block * rows + piece * step, step)],
        ).run(then)

    step = rows // PIECES
    get_second = Gather(links, (p.seq,) * PIECES, second, rows)
    boundary(
        0,
        mix,
        out_ref,
        lambda piece: tokens_ref[0, piece * step : (piece + 1) * step].astype(F32),
        get_second,
        p.s * rows,
    )
    for hop in range(1, 4):
        other = lax.rem(p.z + 4 - hop, 4) * 2 + p.y
        land = kvs.at[:, rows_at(other * source_rows, source_rows)]
        links.take(along + hop, land, (p.s, other))
        links.push(across + hop, land, land, (p.s, p.pair))
    get_up.start((2, 3))
    get_second.forward_all()
    get_second.finish_all()
    links.save(second, second_out)
    for hop in range(4):
        other = lax.rem(p.z + 4 - hop, 4) * 2 + 1 - p.y
        land = kvs.at[:, rows_at(other * source_rows, source_rows)]
        links.take(across + hop, land, (p.s, p.pair))
    links.save(kvs, kvs_out)

    keys = kvs.shape[1]

    def cross_attend(slot, peaks):
        at = rows_at(slot * rows, rows)
        asked = dot(second[at], w_cq[...]).astype(BF16)
        query[at] = asked
        limits = lens[pl.ds(slot, 1)]
        live = lax.broadcasted_iota(jnp.int32, (1, keys), 1) < limits[0, 4:5, 0:1]
        ok = own_rows < limits[0, 0:1, 0:1]
        tops = []
        for head in range(held):
            cut = slice(head * HD, (head + 1) * HD)
            vcut = slice(width + head * HD, width + (head + 1) * HD)
            scores = dot(asked[:, cut], kvs[slot, :, cut], NT) * SCALE
            probs, top = softmax_rows(jnp.where(live, scores, masked_score))
            cross[at, cut] = dot(probs.astype(BF16), kvs[slot, :, vcut]).astype(BF16)
            peak = jnp.max(jnp.where(ok, top, masked_score), axis=0, keepdims=True)
            tops.append(jnp.maximum(peaks[head], peak))
        return tuple(tops)

    peaks = lax.fori_loop(0, 4, cross_attend, (low,) * held)
    for head in range(held):
        peak_out[2 + head : 3 + head] = jnp.broadcast_to(peaks[head], (1, 128))
    links.save(query, query_out)
    links.save(cross, cross_out_ref)
    get_up.forward((2, 3))
    get_branch.finish_all()
    links.save(branch, branch_out)
    get_third = Gather(links, flat, third, rows)
    boundary(
        1,
        cross,
        co_ref,
        lambda piece: sums[0, piece * step : (piece + 1) * step],
        get_third,
        own_flat,
    )
    links.save(sums, sums_out)
    get_third.forward_all()
    get_up.finish()
    for made in links.saves:
        made.wait()
    links.saves = []
    pl.when(keeps)(own_down.wait)
    links.take(get_down, w_down, (p.sib, p.c), p.k != p.y)
    get_third.finish_all()
    links.save(third, third_out)

    def units(number, carry):
        lanes = lanes_at(number * 256, 256)
        value, slope = gelu_pair(dot(third[...], w_up[:, lanes]))
        hidden[:, lanes] = value.astype(BF16)
        grad = dot(branch[...], w_down[rows_at(number * 256, 256)], NT)
        slopes[:, lanes] = (grad * slope).astype(BF16)
        return carry

    lax.fori_loop(0, w_up.shape[1] // 256, units, 0, unroll=2)
    links.save(hidden, hidden_out)
    links.save(slopes, slopes_out)

    def back_rows(number, carry):
        lanes = lanes_at(number * 256, 256)
        grad_third[:, lanes] = dot(slopes[...], w_up[rows_at(number * 256, 256)], NT).astype(BF16)
        third_part[:, lanes] = dot(hidden[...], w_down[:, lanes]).astype(BF16)
        return carry

    lax.fori_loop(0, third.shape[1] // 256, back_rows, 0, unroll=2)
    links.save(grad_third, grad_third_out)
    links.save(third_part, third_part_out)
    for owner in range(STEPS):
        pl.when(p.c != owner)(back_copy(owner).wait_send)
    links.finish()


def forward_call(
    table, targets, sources, tokens, encoder, cotangent, qkv, out, cq, ckv, co, up, down, gain, bias
):
    rows, width = tokens.shape[1], out.shape[0]
    source_rows = encoder.shape[1]
    depth = tokens.shape[2]
    keys = 8 * source_rows
    any_space = pl.BlockSpec(memory_space=pl.ANY)
    vmem = pl.BlockSpec(memory_space=pltpu.VMEM)
    smem = pl.BlockSpec(memory_space=pltpu.SMEM)
    shapes = dict(
        first=((4 * rows, depth), BF16),
        second=((4 * rows, depth), BF16),
        third=((4 * rows, depth), BF16),
        branch=((4 * rows, depth), BF16),
        source=((4 * source_rows, depth), BF16),
        w_qkv=((depth, 3 * width), BF16),
        w_cq=((depth, width), BF16),
        w_ckv=((depth, 2 * width), BF16),
        hidden=((4 * rows, up.shape[1] // 4), BF16),
        slopes=((4 * rows, up.shape[1] // 4), BF16),
        grad_third=((4 * rows, depth), BF16),
        third_part=((4 * rows, depth), BF16),
        heads=((3, 8 * rows, 128), BF16),
        mix=((4 * rows, width), BF16),
        query=((4 * rows, width), BF16),
        kvs=((4, keys, 2 * width), BF16),
        cross=((4 * rows, width), BF16),
        sums=((2, rows, depth), F32),
        peak=((8, 128), F32),
        lens=((4, 8, 128), jnp.int32),
    )
    scratch = [
        shapes[name]
        for name in ("first", "second", "third", "branch", "source", "w_qkv", "w_cq", "w_ckv")
    ] + [
        ((8, 3, rows, 128), BF16),
        shapes["heads"],
        ((8 * rows, 128), BF16),
        shapes["mix"],
        shapes["query"],
        ((4, source_rows, 2 * width), BF16),
        shapes["kvs"],
        shapes["cross"],
        shapes["sums"],
        ((1, 8 * rows), jnp.int32),
        shapes["lens"],
        ((2, 3, rows, depth), BF16),
        ((2, 3, rows, depth), BF16),
        ((4 * rows, depth), BF16),
        ((depth, up.shape[1] // 4), BF16),
        (down.shape, BF16),
        shapes["hidden"],
        shapes["slopes"],
        shapes["grad_third"],
        shapes["third_part"],
    ]
    made = pl.pallas_call(
        forward_kernel,
        in_specs=[smem] * 3
        + [vmem] * 3
        + [any_space, vmem, any_space, any_space, vmem, any_space, any_space]
        + [vmem] * 2,
        out_specs=[vmem if name == "peak" else any_space for name in shapes],
        out_shape=[jax.ShapeDtypeStruct(*shape) for shape in shapes.values()],
        scratch_shapes=[pltpu.VMEM(*shape) for shape in scratch]
        + [
            pltpu.SemaphoreType.DMA((128,)),
            pltpu.SemaphoreType.DMA((128,)),
            pltpu.SemaphoreType.DMA((64,)),
        ],
        compiler_params=pltpu.CompilerParams(
            collective_id=0, has_side_effects=True, vmem_limit_bytes=61 * 2**20
        ),
        name="forward",
    )(table, targets, sources, tokens, encoder, cotangent, qkv, out, cq, ckv, co, up, down, gain, bias)
    return dict(zip(shapes, made))


class Sum:
    def __init__(self, links, place, full, into, away, result, lead=False, cores=False):
        self.links, self.place, self.full = links, place, full
        self.half = place.k if cores else place.y
        self.other = (place.sib, place.c) if cores else (place.s, place.pair)
        self.into, self.away, self.result, self.lead = into, away, result, lead
        self.base = links.slots(7)
        self.near = place.z + 1 - 2 * lax.rem(place.z, 2)
        self.across = lax.rem(place.z + 2, 4)
        self.order = (lax.rem(self.near + 2, 4), self.across, self.near, place.z)

    def start(self, turns=(0, 1, 2, 3)):
        for turn in turns:
            to = self.order[turn]
            give = 1 - self.half
            src = self.full.at[to, give] if self.lead else self.full.at[:, to, give]
            self.links.push(self.base + turn, src, self.into.at[to], self.other)

    def turn(self, turns=(0, 1, 2, 3)):
        p, links, into, away = self.place, self.links, self.into, self.away
        for turn in turns:
            to = self.order[turn]
            links.take(self.base + turn, into.at[to], self.other)
            if turn == 1:
                links.take(self.base + 4, away.at[0], (p.s, self.near * 2 + p.y))

            def add(a, carry):
                mine = self.full[to, self.half, a] if self.lead else self.full[a, to, self.half]
                total = mine.astype(F32) + into[to, a].astype(F32)
                if turn == 1:
                    total = total + away[0, a].astype(F32)
                into[to, a] = total.astype(BF16)
                return carry

            if turn < 3:
                lax.fori_loop(0, into.shape[1], add, 0)
                goal = self.across if turn == 1 else self.near
                links.push(
                    self.base + 4 + turn, into.at[to], away.at[turn], (p.s, goal * 2 + p.y)
                )

    def finish(self):
        p, links, into, away = self.place, self.links, self.into, self.away
        links.take(self.base + 5, away.at[1], (p.s, self.across * 2 + p.y))
        links.take(self.base + 6, away.at[2], (p.s, self.near * 2 + p.y))

        def add(a, carry):
            mine = self.full[p.z, self.half, a] if self.lead else self.full[a, p.z, self.half]
            total = mine.astype(F32) + into[p.z, a].astype(F32)
            total = total + (away[1, a].astype(F32) + away[2, a].astype(F32))
            self.result[a] = total.astype(BF16)
            return carry

        lax.fori_loop(0, into.shape[1], add, 0)


class Exchange:
    def __init__(self, links, team, result, taken):
        self.links, self.team, self.result, self.taken = links, team, result, taken
        self.base = links.slots(3)
        self.others = (team.far, team.opp, team.near)

    def start(self):
        own = pl.ds(self.team.own, 1)
        for step, (device, index) in enumerate(self.others):
            src = self.result.at[pl.ds(index, 1)]
            self.links.push(self.base + step, src, self.taken.at[own], device)
        self.taken[own] = self.result[own]

    def finish(self):
        for step, (device, index) in enumerate(self.others):
            self.links.take(self.base + step, self.taken.at[pl.ds(index, 1)], device)


def norm_terms_of(values):
    centered = values - jnp.mean(values, axis=-1, keepdims=True)
    spread = jnp.mean(centered * centered, axis=-1, keepdims=True)
    inverse = lax.rsqrt(spread + norm_eps)
    return centered * inverse, inverse


def backward_body(r):
    place, links = Place(), Links(r.send_sem, r.recv_sem, r.local_sem)
    p = place
    rows = r.tokens.shape[1]
    half = rows // 2
    width = r.w_cq.shape[1]
    source_rows = r.source.shape[0] // 4
    keys = r.kvs.shape[1]
    pair_width = r.heads.shape[2]
    held, groups = width // HD, width // pair_width
    depth = r.tokens.shape[2]
    step = rows // PIECES
    share = depth // 4

    loads = {}

    def load(names):
        for name in names:
            at = r.load_sem.at[r.loaded.index(name)]
            loads[name] = pltpu.make_async_copy(getattr(r, name + "_hbm"), getattr(r, name), at)
            loads[name].start()

    r.part, r.third_part = r.hidden.at[:, :depth], r.hidden.at[:, depth : 2 * depth]
    r.second, r.first = r.slopes.at[:, :depth], r.slopes.at[:, depth : 2 * depth]
    soon = ("hidden", "branch", "third", "slopes", "sums")
    late = ("third_part", "second", "first")
    load(soon)

    def need(*wanted):
        for name in wanted:
            loads.pop(name).wait()

    place.greet()
    r.peaks_ctx[pl.ds(p.c, 1)] = r.peak[...][None]
    peak_base = links.slots(STEPS)
    own_peak = r.peaks_ctx.at[pl.ds(p.c, 1)]
    for hop in range(1, STEPS):
        links.push(peak_base + hop, own_peak, own_peak, (p.s, lax.rem(p.c + hop, STEPS)))

    own_rows = row_positions(r.table, p.c, half)
    r.norms[...] = jnp.zeros_like(r.norms)

    def add_norms(index, gain, bias):
        r.norms[index : index + 1] += gain[None]
        r.norms[index + 3 : index + 4] += bias[None]

    get_cross = Gather(links, (p.seq,) * PIECES, r.cross_branch, rows)

    def after_third(piece, total):
        cut = slice(piece * step, (piece + 1) * step)
        hat, inverse = norm_terms_of(r.sums[1, cut])
        back, gain, bias = norm_backward(total, hat, inverse, r.gain[2:3])
        add_norms(2, gain, bias)
        valid = own_rows[cut] < r.target[0]
        value = jnp.where(valid, r.cotangent[0, cut].astype(F32), 0.0) + back
        r.grad_sum[cut] = value
        r.cross_branch[rows_at(p.s * rows + piece * step, step)] = value.astype(BF16)
        get_cross.start(piece)

    def stored(ref):
        return lambda block, piece: ref[rows_at(block * rows + piece * step, step)].astype(F32)

    flat = (p.flat, p.flat.turned())
    sum_third = Reduce(
        links, flat, r.rs_out.at[0], r.rs_in.at[0], rows, stored(r.grad_third)
    )
    sum_third.first()

    def down_grad(block, carry):
        value = dot(r.hidden[:, lanes_at(block * 256, 256)], r.branch[...], TN).astype(BF16)
        r.down_full[lax.div(block, 2), lax.rem(block, 2)] = value.reshape(r.down_full.shape[2:])
        return carry

    need("hidden", "branch")
    lax.fori_loop(0, 3, down_grad, 0)
    sum_third.second()
    load([name for name in r.loaded if name not in soon + late])
    lax.fori_loop(3, 8, down_grad, 0)
    down = Sum(
        links, place, r.down_full, r.down_into, r.down_away, r.down_result, True, cores=True
    )
    down.start()
    need("third", "slopes")

    def up_grad(number, carry):
        block, side = lax.div(number, 2), lax.rem(number, 2)
        lanes = lanes_at(side * depth, depth)
        left = r.third[:, lanes_at(block * share, share)]
        value = dot(left, r.slopes[:, lanes], TN).astype(BF16)
        at = pl.ds(lax.div(block, 2) * 2, 2)
        r.up_full[:, lax.rem(block, 2), at, :, lanes] = value.reshape(4, 2, share // 8, depth)
        return carry

    lax.fori_loop(0, 8, up_grad, 0)
    load(late)
    down.turn((0,))
    up = Sum(links, place, r.up_full, r.up_into, r.up_away, r.up_result, True, cores=True)
    up.start()
    need("sums")
    sum_third.last(after_third)
    for hop in range(1, STEPS):
        other = lax.rem(p.c + STEPS - hop, STEPS)
        links.take(peak_base + hop, r.peaks_ctx.at[pl.ds(other, 1)], (p.s, other))
    best = []
    for group in range(groups):
        tile = r.peaks_ctx[group]
        for owner in range(group + groups, STEPS, groups):
            tile = jnp.maximum(tile, r.peaks_ctx[owner])
        best.append(tile)
    everyone = best[0]
    for tile in best[1:]:
        everyone = jnp.maximum(everyone, tile)
    mine = jnp.concatenate([tile[0:2] for tile in best] + [everyone[2 : 2 + held]], axis=0)
    r.peaks_seq[pl.ds(p.s, 1)] = mine[None]
    peak_seq = links.slots(3)
    own_peak = r.peaks_seq.at[pl.ds(p.s, 1)]
    for hop, other in enumerate((p.far, p.opp, p.sib)):
        links.push(peak_seq + hop, own_peak, own_peak, (other, p.c))

    up.turn((0,))
    get_cross.forward_all()
    down.turn((2,))
    need("w_co", "cross", "query", "kvs", "w_cq", "second")
    get_cross.finish_all()
    up.turn((2,))

    def cross_back(slot, carry):
        at = rows_at(slot * rows, rows)
        grad_rows = dot(r.cross_branch[at], r.w_co[...], NT).astype(BF16)
        live = lax.broadcasted_iota(jnp.int32, (keys, 1), 0) < r.lens[pl.ds(slot, 1)][0, 4:5, 0:1]
        for head in range(held):
            cut = slice(head * HD, (head + 1) * HD)
            vcut = slice(width + head * HD, width + (head + 1) * HD)
            asked, grad = r.query[at, cut], grad_rows[:, cut]
            key = r.kvs[slot, :, cut]
            scores = dot(key, asked, NT) * SCALE
            probs = softmax_columns(jnp.where(live, scores, masked_score))
            dprobs = dot(r.kvs[slot, :, vcut], grad, NT)
            delta = jnp.sum(probs * dprobs, axis=0, keepdims=True)
            dscores = (probs * (dprobs - delta)).astype(BF16)
            r.dquery[at, cut] = (dot(dscores, key, TN) * SCALE).astype(BF16)
            shape = (4, 2, source_rows, HD)
            r.dkv_full[slot, :, :, :, cut] = (
                (dot(dscores, asked) * SCALE).astype(BF16).reshape(shape)
            )
            r.dkv_full[slot, :, :, :, vcut] = (
                dot(probs.astype(BF16), grad).astype(BF16).reshape(shape)
            )
        return carry

    lax.fori_loop(0, 4, cross_back, 0)
    dkv = Sum(links, place, r.dkv_full, r.dkv_into, r.dkv_away, r.dkv_result)
    need("third_part")
    sum_output = Reduce(
        links, flat, r.rs_out.at[2], r.rs_in.at[2], rows, stored(r.third_part)
    )
    sum_output.first()
    down.turn((1,))
    up.turn((1,))
    dkv.start()

    get_self = Gather(links, (p.seq,) * PIECES, r.self_branch, rows)

    def after_second(piece, total):
        cut = slice(piece * step, (piece + 1) * step)
        hat, inverse = norm_terms_of(r.sums[0, cut])
        back, gain, bias = norm_backward(total, hat, inverse, r.gain[1:2])
        add_norms(1, gain, bias)
        value = r.grad_sum[cut] + back
        r.grad_sum[cut] = value
        r.self_branch[rows_at(p.s * rows + piece * step, step)] = value.astype(BF16)
        get_self.start(piece)

    def cross_rows(number, carry):
        lanes = lanes_at(number * 256, 256)
        r.part[:, lanes] = dot(r.dquery[...], r.w_cq[rows_at(number * 256, 256)], NT).astype(BF16)
        return carry

    lax.fori_loop(0, depth // 256, cross_rows, 0)
    Reduce(
        links, (p.seq,) * PIECES, r.rs_out.at[1], r.rs_in.at[1], rows, stored(r.part)
    ).run(after_second)

    def row_grad(left, right, full):
        def one(part, carry):
            lanes = lanes_at(part * 128, 128)
            value = dot(left[:, lanes], right[...], TN).astype(BF16)
            full[pl.ds(part * 2, 2)] = value.reshape((2, 2) + full.shape[2:])
            return carry

        lax.fori_loop(0, left.shape[1] // 128, one, 0)

    def column_grad(left, right, full):
        def one(block, carry):
            lanes = lanes_at(block * share, share)
            value = dot(left[:, lanes], right(), TN).astype(BF16)
            full[pl.ds(block, 1)] = value.reshape((1,) + full.shape[1:])
            return carry

        lax.fori_loop(0, 4, one, 0)

    row_grad(r.cross, r.cross_branch, r.co_full)
    get_self.forward_all()
    column_grad(r.second, lambda: r.dquery[...], r.cq_full)
    get_self.finish_all()

    need("w_out", "heads", "mix")

    def mix_back(slot, carry):
        value = dot(r.self_branch[rows_at(slot * rows, rows)], r.w_out[...], NT).astype(BF16)
        for group in range(groups):
            r.gsent[slot * groups + group] = value[:, group * pair_width : (group + 1) * pair_width]
        return carry

    lax.fori_loop(0, 4, mix_back, 0)
    a2a = links.slots(STEPS)
    mine_rows = rows_at(p.c * rows, rows)
    for hop in range(1, STEPS):
        other = lax.rem(p.c + hop, STEPS)
        links.push(a2a + hop, r.gsent.at[other], r.gheads.at[mine_rows], (p.s, other))
    r.gheads[mine_rows] = r.gsent[p.c]
    my_slot, my_group = lax.div(p.c, groups), lax.rem(p.c, groups)
    length = r.lens[pl.ds(my_slot, 1)][0, 0:1, 0:1]
    for owner in range(STEPS):
        pos = row_positions(r.table, owner, half)
        pos = jnp.where(pos < length, pos, STEPS * rows)
        r.key_pos[owner * rows : (owner + 1) * rows] = jnp.broadcast_to(pos, (rows, 128))
    sum_output.second()
    dkv.turn()
    row_grad(r.mix, r.self_branch, r.so_full)
    co = Sum(links, place, r.co_full, r.co_into, r.co_away, r.co_result, True)
    cq = Sum(links, place, r.cq_full, r.cq_into, r.cq_away, r.cq_result)
    so = Sum(links, place, r.so_full, r.so_into, r.so_away, r.so_result, True)
    for job in (co, cq, so):
        job.start()
    for hop in range(1, STEPS):
        other = lax.rem(p.c + STEPS - hop, STEPS)
        links.take(a2a + hop, r.gheads.at[rows_at(other * rows, rows)], (p.s, other))

    slot_rows = rows_at(my_slot * rows, rows)
    group_lanes = lanes_at(my_group * pair_width, pair_width)
    back_q, back_kv = links.slots(STEPS), links.slots(STEPS)

    def q_copy(owner):
        at = rows_at(owner * rows, rows)
        return links.copy(
            back_q + p.c, r.dq_own.at[at], r.dproj.at[0, slot_rows, group_lanes], (p.s, owner)
        )

    def kv_copy(owner):
        at = rows_at(owner * rows, rows)
        return links.copy(
            back_kv + p.c,
            r.dkv_own.at[:, at],
            r.dproj.at[pl.ds(1, 2), slot_rows, group_lanes],
            (p.s, owner),
        )

    def attend_back(block, carry):
        at = rows_at(block * 2 * rows, 2 * rows)
        asked_pos = jnp.concatenate(
            [
                column_positions(r.table, 2 * block, half),
                column_positions(r.table, 2 * block + 1, half),
            ],
            axis=1,
        )
        key_pos = r.key_pos[...]
        allowed = jnp.concatenate([key_pos] * (2 * rows // 128), axis=1) <= asked_pos
        for head in range(pair_width // HD):
            cut = slice(head * HD, (head + 1) * HD)
            asked, grad = r.heads[0, at, cut], r.gheads[at, cut]
            key = r.heads[1, :, cut]
            scores = dot(key, asked, NT) * SCALE
            probs = softmax_columns(jnp.where(allowed, scores, masked_score))
            dprobs = dot(r.heads[2, :, cut], grad, NT)
            delta = jnp.sum(probs * dprobs, axis=0, keepdims=True)
            dscores = (probs * (dprobs - delta)).astype(BF16)
            r.dq_own[at, cut] = (dot(dscores, key, TN) * SCALE).astype(BF16)
            if block == 0:
                r.acc[0, :, cut] = dot(dscores, asked)
                r.acc[1, :, cut] = dot(probs.astype(BF16), grad)
            else:
                r.acc[0, :, cut] += dot(dscores, asked)
                r.acc[1, :, cut] += dot(probs.astype(BF16), grad)
        return carry

    for block in range(STEPS // 2):
        attend_back(block, 0)
        for owner in (2 * block, 2 * block + 1):
            pl.when(p.c != owner)(q_copy(owner).start)
    for owner in range(STEPS):
        at = rows_at(owner * rows, rows)
        r.dkv_own[0, at] = (r.acc[0, at] * SCALE).astype(BF16)
        r.dkv_own[1, at] = r.acc[1, at].astype(BF16)
        pl.when(p.c != owner)(kv_copy(owner).start)
    r.dproj[0, slot_rows, group_lanes] = r.dq_own[mine_rows]
    r.dproj[pl.ds(1, 2), slot_rows, group_lanes] = r.dkv_own[:, mine_rows]

    need("w_ckv", "source")
    dkv.finish()
    r.dsource[...] = r.dkv_result[...].reshape(4 * source_rows, 2 * width)
    column_grad(r.source, lambda: r.dsource[...], r.ckv_full)
    ckv = Sum(links, place, r.ckv_full, r.ckv_into, r.ckv_away, r.ckv_result)
    ckv.start()

    def source_partial(block, piece):
        return dot(r.dsource[rows_at(block * source_rows, source_rows)], r.w_ckv[...], NT)

    def after_encoder(piece, total):
        r.grad_source[...] = total

    Reduce(links, (p.seq,), r.enc_out, r.enc_in, source_rows, source_partial).run(after_encoder)

    def after_output(piece, total):
        cut = slice(piece * step, (piece + 1) * step)
        valid = own_rows[cut] < r.target[0]
        r.output[cut] = jnp.where(valid, r.sums[1, cut] + total, 0.0).astype(BF16)

    sum_output.last(after_output)
    for job in (co, cq, so):
        job.turn()
    need("w_qkv", "first")
    for owner in range(STEPS):

        @pl.when(p.c != owner)
        def _():
            at = pl.ds((owner // groups) * rows, rows)
            lane = lanes_at((owner % groups) * pair_width, pair_width)
            links.take(back_q + owner, r.dproj.at[0, at, lane], (p.s, owner))
            links.take(back_kv + owner, r.dproj.at[pl.ds(1, 2), at, lane], (p.s, owner))

    def first_rows(number, carry):
        at = rows_at(number * 256, 256)
        total = dot(r.dproj[0], r.w_qkv[at, :width], NT)
        total += dot(r.dproj[1], r.w_qkv[at, width : 2 * width], NT)
        total += dot(r.dproj[2], r.w_qkv[at, 2 * width :], NT)
        r.part[:, lanes_at(number * 256, 256)] = total.astype(BF16)
        return carry

    lax.fori_loop(0, depth // 256, first_rows, 0)

    def after_first(piece, total):
        cut = slice(piece * step, (piece + 1) * step)
        hat, inverse = norm_terms_of(r.tokens[0, cut].astype(F32))
        back, gain, bias = norm_backward(total, hat, inverse, r.gain[0:1])
        add_norms(0, gain, bias)
        r.grad_inputs[cut] = r.grad_sum[cut] + back

    def qkv_grad(block, carry):
        lanes = lanes_at(block * share, share)
        left = r.first[:, lanes]
        for part in range(3):
            value = dot(left, r.dproj[part], TN).astype(BF16)
            r.qkv_full[pl.ds(block, 1), :, :, :, part * width : (part + 1) * width] = value.reshape(
                (1,) + r.qkv_full.shape[1:4] + (width,)
            )
        return carry

    lax.fori_loop(0, 4, qkv_grad, 0)
    qkv = Sum(links, place, r.qkv_full, r.qkv_into, r.qkv_away, r.qkv_result)
    qkv.start()
    sum_first = Reduce(
        links, (p.seq,) * PIECES, r.rs_out.at[3], r.rs_in.at[3], rows, stored(r.part)
    )
    sum_first.first()
    sum_first.second()
    ckv.turn((0, 2))
    qkv.turn((0, 2))
    sum_first.last(after_first)

    norm_seq, norm_ctx = links.slots(3), links.slots(STEPS)
    others = (p.far, p.opp, p.sib)
    for hop, other in enumerate(others):
        links.push(
            norm_seq + hop,
            r.norms.at[:, lanes_at(other * share, share)],
            r.norms_seq.at[pl.ds(p.s, 1)].at[0],
            (other, p.c),
        )
    ckv.turn((1, 3))
    total = r.norms[:, lanes_at(p.s * share, share)]
    for hop, other in enumerate(others):
        links.take(norm_seq + hop, r.norms_seq.at[pl.ds(other, 1)].at[0], (other, p.c))
        total = total + r.norms_seq[pl.ds(other, 1)][0]
    r.norms_ctx[pl.ds(p.c, 1)] = total[None]
    own_norms = r.norms_ctx.at[pl.ds(p.c, 1)]
    for hop in range(1, STEPS):
        links.push(norm_ctx + hop, own_norms, own_norms, (p.s, lax.rem(p.c + hop, STEPS)))
    qkv.turn((1, 3))
    sums = {}
    for job in (up, down):
        job.turn((3,))
        job.finish()
    sums["up"] = Exchange(links, p.flat, r.up_result, r.up_taken)
    sums["up"].start()
    keeps, swapped = p.k == p.y, links.slots(1)
    links.push(swapped, r.down_result, r.down_taken, (p.sib, p.pair), p.k != p.y)

    @pl.when(keeps)
    def _():
        r.down_taken[...] = r.down_result[...]

    for job in (co, so):
        job.finish()
    for name, job in (("cq", cq), ("ckv", ckv), ("qkv", qkv)):
        job.finish()
        sums[name] = Exchange(links, p.seq, getattr(r, name + "_result"), getattr(r, name + "_taken"))
        sums[name].start()
    for hop in range(1, STEPS):
        other = lax.rem(p.c + STEPS - hop, STEPS)
        links.take(norm_ctx + hop, r.norms_ctx.at[pl.ds(other, 1)], (p.s, other))
    total = r.norms_ctx[0]
    for owner in range(1, STEPS):
        total = total + r.norms_ctx[owner]
    r.norm_sum[...] = total
    for hop, other in enumerate(others):
        links.take(peak_seq + hop, r.peaks_seq.at[pl.ds(other, 1)], (other, p.c))
    for job in sums.values():
        job.finish()
    links.take(swapped, r.down_taken, (p.sib, p.pair), p.k != p.y)
    for owner in range(STEPS):
        pl.when(p.c != owner)(q_copy(owner).wait_send)
        pl.when(p.c != owner)(kv_copy(owner).wait_send)
    links.finish()


def backward_call(kept, given):
    rows, depth = given["tokens"].shape[1:]
    width = kept["w_cq"].shape[1]
    source_rows = kept["source"].shape[0] // 4
    keys = kept["kvs"].shape[1]
    share = depth // 32
    hidden = kept["hidden"].shape[1]
    any_space = pl.BlockSpec(memory_space=pl.ANY)
    vmem = pl.BlockSpec(memory_space=pltpu.VMEM)
    smem = pl.BlockSpec(memory_space=pltpu.SMEM)
    inputs = dict(
        table=(smem, given["table"]),
        target=(smem, given["target"]),
        tokens=(vmem, given["tokens"]),
        cotangent=(vmem, given["cotangent"]),
        gain=(vmem, given["gain"]),
        peak=(vmem, kept["peak"]),
        lens=(vmem, kept["lens"]),
        grad_third=(vmem, kept["grad_third"]),
    )
    loaded = dict(
        hidden=kept["hidden"],
        branch=kept["branch"],
        third=kept["third"],
        slopes=kept["slopes"],
        third_part=kept["third_part"],
        sums=kept["sums"],
        w_co=given["cross_out"],
        cross=kept["cross"],
        query=kept["query"],
        kvs=kept["kvs"],
        w_cq=kept["w_cq"],
        second=kept["second"],
        w_out=given["self_out"],
        heads=kept["heads"],
        mix=kept["mix"],
        w_ckv=kept["w_ckv"],
        source=kept["source"],
        w_qkv=kept["w_qkv"],
        first=kept["first"],
    )
    for name, value in loaded.items():
        inputs[name + "_hbm"] = (any_space, value)
    outs = dict(
        output=((rows, depth), BF16),
        grad_inputs=((rows, depth), F32),
        grad_source=((source_rows, depth), F32),
        down_taken=((hidden // (8 * share), share, depth), BF16),
        co_result=((1, share, depth), BF16),
        so_result=((1, share, depth), BF16),
        up_taken=((4, share, hidden), BF16),
        cq_taken=((4, share, width), BF16),
        ckv_taken=((4, share, 2 * width), BF16),
        qkv_taken=((4, share, 3 * width), BF16),
        norm_sum=((8, depth // 4), F32),
        peaks_seq=((4, 8, 128), F32),
    )
    down_blocks = hidden // (8 * share)
    scratch = {
        name: (value.shape, value.dtype)
        for name, value in loaded.items()
        if name not in ("third_part", "second", "first")
    }
    scratch |= dict(
        down_full=((4, 2, down_blocks, share, depth), BF16),
        up_full=((4, 2, 4, share, hidden), BF16),
        down_into=((4, down_blocks, share, depth), BF16),
        down_away=((3, down_blocks, share, depth), BF16),
        down_result=((down_blocks, share, depth), BF16),
        up_into=((4, 4, share, hidden), BF16),
        up_away=((3, 4, share, hidden), BF16),
        up_result=((4, share, hidden), BF16),
        peaks_ctx=((8, 8, 128), F32),
        norms=((8, depth), F32),
        norms_seq=((4, 8, depth // 4), F32),
        norms_ctx=((8, 8, depth // 4), F32),
        cross_branch=((4 * rows, depth), BF16),
        self_branch=((4 * rows, depth), BF16),
        grad_sum=((rows, depth), F32),
        rs_out=((4, 3, rows, depth), BF16),
        rs_in=((4, 3, rows, depth), BF16),
        enc_out=((3, source_rows, depth), BF16),
        enc_in=((3, source_rows, depth), BF16),
        dquery=((4 * rows, width), BF16),
        dsource=((4 * source_rows, 2 * width), BF16),
        gsent=((8, rows, 128), BF16),
        gheads=((8 * rows, 128), BF16),
        key_pos=((8 * rows, 128), jnp.int32),
        acc=((2, 8 * rows, 128), F32),
        dq_own=((8 * rows, 128), BF16),
        dkv_own=((2, 8 * rows, 128), BF16),
        dproj=((3, 4 * rows, width), BF16),
    )
    for name in ("co", "so"):
        scratch[name + "_full"] = ((4, 2, 1, share, depth), BF16)
        scratch[name + "_into"] = ((4, 1, share, depth), BF16)
        scratch[name + "_away"] = ((3, 1, share, depth), BF16)
    for name, columns, r in (
        ("cq", width, share),
        ("ckv", 2 * width, share),
        ("qkv", 3 * width, share),
        ("dkv", 2 * width, source_rows),
    ):
        scratch[name + "_full"] = ((4, 4, 2, r, columns), BF16)
        scratch[name + "_into"] = ((4, 4, r, columns), BF16)
        scratch[name + "_away"] = ((3, 4, r, columns), BF16)
        scratch[name + "_result"] = ((4, r, columns), BF16)
    sems = dict(send_sem=224, recv_sem=224, local_sem=4, load_sem=len(loaded))
    names = list(inputs) + list(outs) + list(scratch) + list(sems)

    def kernel(*refs):
        held = dict(zip(names, refs), loaded=tuple(loaded))
        backward_body(type("Refs", (), held))

    made = pl.pallas_call(
        kernel,
        in_specs=[spec for spec, _ in inputs.values()],
        out_specs=[vmem] * len(outs),
        out_shape=[jax.ShapeDtypeStruct(*shape) for shape in outs.values()],
        scratch_shapes=[pltpu.VMEM(*shape) for shape in scratch.values()]
        + [pltpu.SemaphoreType.DMA((count,)) for count in sems.values()],
        compiler_params=pltpu.CompilerParams(
            collective_id=1, has_side_effects=True, vmem_limit_bytes=61 * 2**20
        ),
        name="backward",
    )(*[value for _, value in inputs.values()])
    return dict(zip(outs, made))


def finish_kernel(
    clip_ref,
    peaks_ref,
    norm_ref,
    qkv_w,
    cq_w,
    ckv_w,
    output_ref,
    inputs_ref,
    source_ref,
    down_ref,
    co_ref,
    so_ref,
    up_ref,
    cq_ref,
    ckv_ref,
    qkv_ref,
    output_out,
    inputs_out,
    source_out,
    qkv_out,
    so_out,
    cq_out,
    ckv_out,
    co_out,
    up_out,
    down_out,
    gain_out,
    bias_out,
    self_out,
    cross_out,
):
    output_out[0] = output_ref[...]
    inputs_out[0] = inputs_ref[...]
    source_out[0] = source_ref[...]
    share = so_out.shape[0]
    so_out[...] = so_ref[0].astype(F32)
    co_out[...] = co_ref[0].astype(F32)
    for block in range(down_ref.shape[0]):
        down_out[block * share : (block + 1) * share] = down_ref[block].astype(F32)

    def columns(out, taken, parts):
        whole, width = out.shape[1] // parts, out.shape[1] // (4 * parts)
        for owner in range(4):
            for part in range(parts):
                at = part * whole + owner * width
                out[:, at : at + width] = taken[owner, :, part * width : (part + 1) * width].astype(
                    F32
                )

    columns(up_out, up_ref, 1)
    columns(cq_out, cq_ref, 1)
    columns(ckv_out, ckv_ref, 2)
    columns(qkv_out, qkv_ref, 3)
    spread = gain_out.shape[1]
    turned = pltpu.roll(norm_ref[...], norm_ref.shape[1] - lax.axis_index("ctx") * spread, 1)
    gain_out[...] = turned[0:3, :spread]
    bias_out[...] = turned[3:6, :spread]
    lane = lax.broadcasted_iota(jnp.int32, (1, 128), 1)
    held = peaks_ref.shape[1] // 2
    for owner in range(4):
        for two in range(held // 2):
            head = owner * held + two * 2
            at = slice(head * HD, head * HD + 128)
            for kind, jobs in (
                (0, ((self_out, qkv_w, 0, 0), (self_out, qkv_w, H * HD, H * HD))),
                (1, ((cross_out, cq_w, 0, 0), (cross_out, ckv_w, 0, H * HD))),
            ):
                top = [peaks_ref[owner, kind * held + two * 2 + i : kind * held + two * 2 + i + 1] for i in (0, 1)]
                limit = [clip_ref[kind, head + i] for i in (0, 1)]
                limits = jnp.where(lane < HD, limit[0], limit[1])
                tops = jnp.where(lane < HD, top[0], top[1])
                factor = jnp.sqrt(limits / jnp.maximum(tops, limits))
                for out, weight, start, goal in jobs:
                    out[:, goal + head * HD : goal + head * HD + 128] = (
                        weight[:, start + head * HD : start + head * HD + 128].astype(F32) * factor
                    ).astype(BF16)


def finish_call(made, given):
    rows, depth = given["tokens"].shape[1:]
    hidden = given["mlp_up"].shape[1]
    source_rows, share = made["grad_source"].shape[0], made["so_result"].shape[1]
    columns = H * HD
    weight_rows = given["self_qkv"].shape[0]
    shapes = [
        ((1, rows, depth), BF16),
        ((1, rows, depth), F32),
        ((1, source_rows, depth), F32),
        ((share, 3 * columns), F32),
        ((share, depth), F32),
        ((share, columns), F32),
        ((share, 2 * columns), F32),
        ((share, depth), F32),
        ((share, hidden), F32),
        ((hidden // 32, depth), F32),
        ((3, share), F32),
        ((3, share), F32),
        ((weight_rows, 2 * columns), BF16),
        ((weight_rows, 2 * columns), BF16),
    ]
    vmem = pl.BlockSpec(memory_space=pltpu.VMEM)
    return pl.pallas_call(
        finish_kernel,
        in_specs=[pl.BlockSpec(memory_space=pltpu.SMEM)] + [vmem] * 15,
        out_specs=[vmem] * len(shapes),
        out_shape=[jax.ShapeDtypeStruct(*shape) for shape in shapes],
        compiler_params=pltpu.CompilerParams(vmem_limit_bytes=61 * 2**20),
        name="finish",
    )(
        given["clip"],
        made["peaks_seq"],
        made["norm_sum"],
        given["self_qkv"],
        given["cross_q"],
        given["cross_kv"],
        made["output"],
        made["grad_inputs"],
        made["grad_source"],
        made["down_taken"],
        made["co_result"],
        made["so_result"],
        made["up_taken"],
        made["cq_taken"],
        made["ckv_taken"],
        made["qkv_taken"],
    )


def fast_device(
    tokens,
    encoder_states,
    cotangent,
    target_lengths,
    source_lengths,
    block_table,
    self_qkv,
    self_out,
    cross_q,
    cross_kv,
    cross_out,
    mlp_up,
    mlp_down,
    norm_gain,
    norm_bias,
    clip_limit,
):
    kept = forward_call(
        block_table,
        target_lengths,
        source_lengths,
        tokens,
        encoder_states,
        cotangent,
        self_qkv,
        self_out,
        cross_q,
        cross_kv,
        cross_out,
        mlp_up,
        mlp_down,
        norm_gain,
        norm_bias,
    )
    given = dict(
        table=block_table,
        target=target_lengths,
        tokens=tokens,
        cotangent=cotangent,
        gain=norm_gain,
        cross_out=cross_out,
        self_out=self_out,
        self_qkv=self_qkv,
        cross_q=cross_q,
        cross_kv=cross_kv,
        mlp_up=mlp_up,
        clip=clip_limit,
    )
    made = backward_call(kept, given)
    held = H // 4
    tops = made["peaks_seq"][:, :, 0].reshape(4, 2, held).transpose(1, 0, 2).reshape(2, H)
    return (*finish_call(made, given), tops)


def solution(mesh):
    body = fast_device if fast_fits(mesh) else general_device
    return jax.shard_map(
        body,
        mesh=mesh,
        in_specs=(
            P("seq", "ctx", None),
            P("seq", "ctx", None),
            P("seq", "ctx", None),
            P("seq"),
            P("seq"),
            P(),
            P("seq", None),
            P("seq", None),
            P("seq", None),
            P("seq", None),
            P("seq", None),
            P("seq", None),
            P("seq", None),
            P(),
            P(),
            P(),
        ),
        out_specs=(
            P("seq", "ctx", None),
            P("seq", "ctx", None),
            P("seq", "ctx", None),
            P(("seq", "ctx"), None),
            P(("seq", "ctx"), None),
            P(("seq", "ctx"), None),
            P(("seq", "ctx"), None),
            P(("seq", "ctx"), None),
            P(("seq", "ctx"), None),
            P(("seq", "ctx"), None),
            P(None, ("seq", "ctx")),
            P(None, ("seq", "ctx")),
            P("seq", None),
            P("seq", None),
            P(),
        ),
        check_vma=False,
    )
```

```python
import functools

import jax
import jax.numpy as jnp
from jax import lax
from jax.experimental import pallas as pl
from jax.experimental.pallas import tpu as pltpu
from jax.sharding import PartitionSpec as P

H = 16
HD = 64


masked_score = -1000000000.0
norm_eps = 1e-05


def block_size(count):
    return max((step for step in range(1, min(count, 512) + 1) if count % step == 0))


def layer_norm(values, gain, bias):
    centered = values - jnp.mean(values, axis=-1, keepdims=True)
    spread = jnp.mean(centered * centered, axis=-1, keepdims=True)
    return centered * lax.rsqrt(spread + norm_eps) * gain + bias


def allowed_pairs(query_pos, key_pos, key_limit, causal):
    allowed = jnp.broadcast_to(
        (key_pos < key_limit)[None, :], (query_pos.shape[0], key_pos.shape[0])
    )
    if causal:
        allowed = allowed & (key_pos[None, :] <= query_pos[:, None])
    return allowed


def head_scores(query_heads, key_rows):
    key_heads = key_rows.reshape(key_rows.shape[0], H, HD)
    return jnp.einsum(
        "qhd,khd->hqk", query_heads, key_heads, preferred_element_type=jnp.float32
    ) * HD ** (-0.5)


def softmax_stats(query_heads, kv_rows, key_pos, query_pos, query_ok, key_limit, causal):
    count = kv_rows.shape[0]
    step = block_size(count)
    width = H * HD
    rows = query_heads.shape[0]

    def softmax_visit(carry, block):
        top, total, peak = carry
        block_rows, block_pos = block
        allowed = allowed_pairs(query_pos, block_pos, key_limit, causal)
        scores = jnp.where(
            allowed[None], head_scores(query_heads, block_rows[:, :width]), masked_score
        )
        new_top = jnp.maximum(top, jnp.max(scores, axis=-1))
        total = total * jnp.exp(top - new_top) + jnp.sum(
            jnp.exp(scores - new_top[..., None]), axis=-1
        )
        counted = jnp.where((allowed & query_ok[:, None])[None], scores, masked_score)
        peak = jnp.maximum(peak, jnp.max(counted, axis=(1, 2)))
        return ((new_top, total, peak), None)

    start = (
        jnp.full((H, rows), -jnp.inf, jnp.float32),
        jnp.zeros((H, rows), jnp.float32),
        jnp.full((H,), masked_score, jnp.float32),
    )
    blocks = (kv_rows.reshape(count // step, step, 2 * width), key_pos.reshape(count // step, step))
    return lax.scan(softmax_visit, start, blocks)[0]


def attend_values(query_heads, kv_rows, key_pos, query_pos, key_limit, causal, top, total):
    count = kv_rows.shape[0]
    step = block_size(count)
    width = H * HD
    rows = query_heads.shape[0]

    def attend_visit(acc, block):
        block_rows, block_pos = block
        allowed = allowed_pairs(query_pos, block_pos, key_limit, causal)
        scores = jnp.where(
            allowed[None], head_scores(query_heads, block_rows[:, :width]), masked_score
        )
        weights = (jnp.exp(scores - top[..., None]) / total[..., None]).astype(jnp.bfloat16)
        value_heads = block_rows[:, width:].reshape(step, H, HD)
        return (
            acc
            + jnp.einsum("hqk,khd->qhd", weights, value_heads, preferred_element_type=jnp.float32),
            None,
        )

    blocks = (kv_rows.reshape(count // step, step, 2 * width), key_pos.reshape(count // step, step))
    acc = lax.scan(attend_visit, jnp.zeros((rows, H, HD), jnp.float32), blocks)[0]
    return acc.reshape(rows, width)


def query_grads(
    query_heads, kv_rows, key_pos, query_pos, key_limit, causal, top, total, grad_heads, delta
):
    count = kv_rows.shape[0]
    step = block_size(count)
    width = H * HD
    rows = query_heads.shape[0]

    def query_visit(acc, block):
        block_rows, block_pos = block
        allowed = allowed_pairs(query_pos, block_pos, key_limit, causal)
        scores = jnp.where(
            allowed[None], head_scores(query_heads, block_rows[:, :width]), masked_score
        )
        probs = jnp.exp(scores - top[..., None]) / total[..., None]
        value_heads = block_rows[:, width:].reshape(step, H, HD)
        dprobs = jnp.einsum(
            "qhd,khd->hqk", grad_heads, value_heads, preferred_element_type=jnp.float32
        )
        dscores = (probs * (dprobs - delta[..., None])).astype(jnp.bfloat16)
        key_heads = block_rows[:, :width].reshape(step, H, HD)
        return (
            acc
            + jnp.einsum("hqk,khd->qhd", dscores, key_heads, preferred_element_type=jnp.float32),
            None,
        )

    blocks = (kv_rows.reshape(count // step, step, 2 * width), key_pos.reshape(count // step, step))
    acc = lax.scan(query_visit, jnp.zeros((rows, H, HD), jnp.float32), blocks)[0]
    return acc.reshape(rows, width) * HD ** (-0.5)


def key_grads(
    query_heads,
    kv_rows,
    key_pos,
    query_pos,
    key_limit,
    causal,
    top,
    total,
    grad_heads,
    delta,
    start,
    count,
):
    step = block_size(count)
    width = H * HD

    def piece(index):
        offset = start + index * step
        block_rows = lax.dynamic_slice_in_dim(kv_rows, offset, step, 0)
        block_pos = lax.dynamic_slice_in_dim(key_pos, offset, step, 0)
        allowed = allowed_pairs(query_pos, block_pos, key_limit, causal)
        scores = jnp.where(
            allowed[None], head_scores(query_heads, block_rows[:, :width]), masked_score
        )
        probs = jnp.exp(scores - top[..., None]) / total[..., None]
        value_heads = block_rows[:, width:].reshape(step, H, HD)
        dprobs = jnp.einsum(
            "qhd,khd->hqk", grad_heads, value_heads, preferred_element_type=jnp.float32
        )
        dscores = (probs * (dprobs - delta[..., None])).astype(jnp.bfloat16)
        dkeys = jnp.einsum(
            "hqk,qhd->khd", dscores, query_heads, preferred_element_type=jnp.float32
        ).reshape(step, width) * HD ** (-0.5)
        dvalues = jnp.einsum(
            "hqk,qhd->khd",
            probs.astype(jnp.bfloat16),
            grad_heads,
            preferred_element_type=jnp.float32,
        ).reshape(step, width)
        return jnp.concatenate([dkeys, dvalues], axis=1)

    return lax.map(piece, jnp.arange(count // step, dtype=jnp.int32)).reshape(count, 2 * width)


def split_rows(grad, seq_count, ctx_count):
    return grad.reshape(
        (seq_count, ctx_count, grad.shape[0] // (seq_count * ctx_count)) + grad.shape[1:]
    )


def join_rows(grad):
    return grad.reshape((grad.shape[2],) + grad.shape[3:])


def general_device(
    tokens,
    encoder_states,
    cotangent,
    target_lengths,
    source_lengths,
    block_table,
    self_qkv,
    self_out,
    cross_q,
    cross_kv,
    cross_out,
    mlp_up,
    mlp_down,
    norm_gain,
    norm_bias,
    clip_limit,
):
    rows = tokens.shape[1]
    width = H * HD
    half = rows // 2
    source_rows = encoder_states.shape[1]
    seq_count = lax.axis_size("seq")
    ctx_count = lax.axis_size("ctx")
    all_positions = (
        block_table[:, :, None] * half + jnp.arange(half, dtype=jnp.int32)[None, None, :]
    ).reshape(-1)
    own_positions = lax.dynamic_slice_in_dim(all_positions, lax.axis_index("ctx") * rows, rows, 0)
    length = target_lengths[0]
    source_length = source_lengths[0]
    query_ok = own_positions < length
    valid_rows = query_ok[:, None]
    source_positions = jnp.arange(source_rows * ctx_count, dtype=jnp.int32)
    w_qkv, w_out, w_cq, w_ckv, w_co = (
        lax.all_gather(self_qkv, "seq", axis=0, tiled=True),
        lax.all_gather(self_out, "seq", axis=0, tiled=True),
        lax.all_gather(cross_q, "seq", axis=0, tiled=True),
        lax.all_gather(cross_kv, "seq", axis=0, tiled=True),
        lax.all_gather(cross_out, "seq", axis=0, tiled=True),
    )
    inputs = tokens[0].astype(jnp.float32)
    first_norm, first_back = jax.vjp(layer_norm, inputs, norm_gain[0], norm_bias[0])
    first_low = first_norm.astype(jnp.bfloat16)
    projected = jnp.dot(first_low, w_qkv, preferred_element_type=jnp.float32).astype(jnp.bfloat16)
    self_query = projected[:, :width].reshape(rows, H, HD)
    source_kv = jnp.dot(encoder_states[0], w_ckv, preferred_element_type=jnp.float32).astype(
        jnp.bfloat16
    )
    self_kv, cross_kvs = (
        lax.all_gather(projected[:, width:], "ctx", axis=0, tiled=True),
        lax.all_gather(source_kv, "ctx", axis=0, tiled=True),
    )
    self_top, self_total, self_peak = softmax_stats(
        self_query, self_kv, all_positions, own_positions, query_ok, length, True
    )
    self_mix = attend_values(
        self_query, self_kv, all_positions, own_positions, length, True, self_top, self_total
    )
    self_low = self_mix.astype(jnp.bfloat16)
    first_sum = inputs + jnp.dot(self_low, w_out, preferred_element_type=jnp.float32)
    second_norm, second_back = jax.vjp(layer_norm, first_sum, norm_gain[1], norm_bias[1])
    second_low = second_norm.astype(jnp.bfloat16)
    cross_rows = jnp.dot(second_low, w_cq, preferred_element_type=jnp.float32).astype(jnp.bfloat16)
    cross_query = cross_rows.reshape(rows, H, HD)
    cross_top, cross_total, cross_peak = softmax_stats(
        cross_query, cross_kvs, source_positions, own_positions, query_ok, source_length, False
    )
    cross_mix = attend_values(
        cross_query,
        cross_kvs,
        source_positions,
        own_positions,
        source_length,
        False,
        cross_top,
        cross_total,
    )
    cross_low = cross_mix.astype(jnp.bfloat16)
    second_sum = first_sum + jnp.dot(cross_low, w_co, preferred_element_type=jnp.float32)
    third_norm, third_back = jax.vjp(layer_norm, second_sum, norm_gain[2], norm_bias[2])
    third_low = third_norm.astype(jnp.bfloat16)
    w_up, w_down = (
        lax.all_gather(mlp_up, "seq", axis=0, tiled=True),
        lax.all_gather(mlp_down, "seq", axis=0, tiled=True),
    )
    hidden_pre = jnp.dot(third_low, w_up, preferred_element_type=jnp.float32)
    hidden_act, gelu_back = jax.vjp(jax.nn.gelu, hidden_pre)
    hidden_low = hidden_act.astype(jnp.bfloat16)
    third_sum = second_sum + jnp.dot(hidden_low, w_down, preferred_element_type=jnp.float32)
    output_rows = jnp.where(valid_rows, third_sum, 0.0).astype(jnp.bfloat16)
    peaks = lax.pmax(jnp.stack([self_peak, cross_peak]), ("seq", "ctx"))
    grad_rows = jnp.where(valid_rows, cotangent[0].astype(jnp.float32), 0.0)
    mlp_branch = grad_rows.astype(jnp.bfloat16)
    grad_down = jnp.einsum("rf,rd->fd", hidden_low, mlp_branch, preferred_element_type=jnp.float32)
    grad_act = jnp.einsum("rd,fd->rf", mlp_branch, w_down, preferred_element_type=jnp.float32)
    grad_pre = gelu_back(grad_act)[0].astype(jnp.bfloat16)
    grad_up = jnp.einsum("rd,rf->df", third_low, grad_pre, preferred_element_type=jnp.float32)
    back_third, gain_three, bias_three = third_back(
        jnp.einsum("rf,df->rd", grad_pre, w_up, preferred_element_type=jnp.float32)
    )
    up_part, down_part = (
        lax.psum_scatter(
            split_rows(grad_up, seq_count, ctx_count).astype(jnp.bfloat16),
            "ctx",
            scatter_dimension=1,
            tiled=True,
        ).astype(jnp.float32),
        lax.psum_scatter(
            split_rows(grad_down, seq_count, ctx_count).astype(jnp.bfloat16),
            "ctx",
            scatter_dimension=1,
            tiled=True,
        ).astype(jnp.float32),
    )
    up_shard, down_shard = (
        lax.psum_scatter(
            up_part.astype(jnp.bfloat16), "seq", scatter_dimension=0, tiled=True
        ).astype(jnp.float32),
        lax.psum_scatter(
            down_part.astype(jnp.bfloat16), "seq", scatter_dimension=0, tiled=True
        ).astype(jnp.float32),
    )
    grad_second = grad_rows + back_third
    cross_branch = grad_second.astype(jnp.bfloat16)
    grad_co = jnp.einsum("rd,re->de", cross_low, cross_branch, preferred_element_type=jnp.float32)
    cross_heads_grad = (
        jnp.einsum("re,de->rd", cross_branch, w_co, preferred_element_type=jnp.float32)
        .astype(jnp.bfloat16)
        .reshape(rows, H, HD)
    )
    cross_delta = jnp.einsum(
        "qhd,qhd->hq", cross_heads_grad.astype(jnp.float32), cross_mix.reshape(rows, H, HD)
    )
    grad_cross_rows = query_grads(
        cross_query,
        cross_kvs,
        source_positions,
        own_positions,
        source_length,
        False,
        cross_top,
        cross_total,
        cross_heads_grad,
        cross_delta,
    ).astype(jnp.bfloat16)
    grad_source_kv = lax.psum_scatter(
        key_grads(
            cross_query,
            cross_kvs,
            source_positions,
            own_positions,
            source_length,
            False,
            cross_top,
            cross_total,
            cross_heads_grad,
            cross_delta,
            jnp.int32(0),
            source_rows * lax.axis_size("ctx"),
        ).astype(jnp.bfloat16),
        "ctx",
        scatter_dimension=0,
        tiled=True,
    )
    grad_cq = jnp.einsum(
        "rd,re->de", second_low, grad_cross_rows, preferred_element_type=jnp.float32
    )
    grad_ckv = jnp.einsum(
        "sd,se->de", encoder_states[0], grad_source_kv, preferred_element_type=jnp.float32
    )
    grad_source = jnp.einsum("se,de->sd", grad_source_kv, w_ckv, preferred_element_type=jnp.float32)
    back_second, gain_two, bias_two = second_back(
        jnp.einsum("re,de->rd", grad_cross_rows, w_cq, preferred_element_type=jnp.float32)
    )
    grad_first = grad_second + back_second
    self_branch = grad_first.astype(jnp.bfloat16)
    grad_so = jnp.einsum("rd,re->de", self_low, self_branch, preferred_element_type=jnp.float32)
    self_heads_grad = (
        jnp.einsum("re,de->rd", self_branch, w_out, preferred_element_type=jnp.float32)
        .astype(jnp.bfloat16)
        .reshape(rows, H, HD)
    )
    self_delta = jnp.einsum(
        "qhd,qhd->hq", self_heads_grad.astype(jnp.float32), self_mix.reshape(rows, H, HD)
    )
    grad_query = query_grads(
        self_query,
        self_kv,
        all_positions,
        own_positions,
        length,
        True,
        self_top,
        self_total,
        self_heads_grad,
        self_delta,
    ).astype(jnp.bfloat16)
    grad_kv = lax.psum_scatter(
        key_grads(
            self_query,
            self_kv,
            all_positions,
            own_positions,
            length,
            True,
            self_top,
            self_total,
            self_heads_grad,
            self_delta,
            jnp.int32(0),
            rows * lax.axis_size("ctx"),
        ).astype(jnp.bfloat16),
        "ctx",
        scatter_dimension=0,
        tiled=True,
    )
    grad_projected = jnp.concatenate([grad_query, grad_kv], axis=1)
    grad_qkv = jnp.einsum(
        "rd,re->de", first_low, grad_projected, preferred_element_type=jnp.float32
    )
    back_first, gain_one, bias_one = first_back(
        jnp.einsum("re,de->rd", grad_projected, w_qkv, preferred_element_type=jnp.float32)
    )
    grad_inputs = grad_first + back_first
    norm_terms = jnp.stack([gain_one, gain_two, gain_three, bias_one, bias_two, bias_three], axis=1)
    qkv_part, out_part, cq_part, ckv_part, co_part, norm_part = (
        lax.psum_scatter(
            split_rows(grad_qkv, seq_count, ctx_count).astype(jnp.bfloat16),
            "ctx",
            scatter_dimension=1,
            tiled=True,
        ).astype(jnp.float32),
        lax.psum_scatter(
            split_rows(grad_so, seq_count, ctx_count).astype(jnp.bfloat16),
            "ctx",
            scatter_dimension=1,
            tiled=True,
        ).astype(jnp.float32),
        lax.psum_scatter(
            split_rows(grad_cq, seq_count, ctx_count).astype(jnp.bfloat16),
            "ctx",
            scatter_dimension=1,
            tiled=True,
        ).astype(jnp.float32),
        lax.psum_scatter(
            split_rows(grad_ckv, seq_count, ctx_count).astype(jnp.bfloat16),
            "ctx",
            scatter_dimension=1,
            tiled=True,
        ).astype(jnp.float32),
        lax.psum_scatter(
            split_rows(grad_co, seq_count, ctx_count).astype(jnp.bfloat16),
            "ctx",
            scatter_dimension=1,
            tiled=True,
        ).astype(jnp.float32),
        lax.psum_scatter(
            split_rows(norm_terms, seq_count, ctx_count).astype(jnp.bfloat16),
            "ctx",
            scatter_dimension=1,
            tiled=True,
        ).astype(jnp.float32),
    )
    qkv_shard, out_shard, cq_shard, ckv_shard, co_shard, norm_shard = (
        lax.psum_scatter(
            qkv_part.astype(jnp.bfloat16), "seq", scatter_dimension=0, tiled=True
        ).astype(jnp.float32),
        lax.psum_scatter(
            out_part.astype(jnp.bfloat16), "seq", scatter_dimension=0, tiled=True
        ).astype(jnp.float32),
        lax.psum_scatter(
            cq_part.astype(jnp.bfloat16), "seq", scatter_dimension=0, tiled=True
        ).astype(jnp.float32),
        lax.psum_scatter(
            ckv_part.astype(jnp.bfloat16), "seq", scatter_dimension=0, tiled=True
        ).astype(jnp.float32),
        lax.psum_scatter(
            co_part.astype(jnp.bfloat16), "seq", scatter_dimension=0, tiled=True
        ).astype(jnp.float32),
        lax.psum_scatter(
            norm_part.astype(jnp.bfloat16), "seq", scatter_dimension=0, tiled=True
        ).astype(jnp.float32),
    )
    norm_shard = join_rows(norm_shard)
    factors = jnp.sqrt(clip_limit / jnp.maximum(peaks, clip_limit))
    columns = jnp.repeat(factors, HD, axis=1)
    qkv_wide = self_qkv.astype(jnp.float32)
    clipped_self = jnp.concatenate(
        [qkv_wide[:, :width] * columns[0], qkv_wide[:, width : 2 * width] * columns[0]], axis=1
    ).astype(jnp.bfloat16)
    clipped_cross = jnp.concatenate(
        [
            cross_q.astype(jnp.float32) * columns[1],
            cross_kv[:, :width].astype(jnp.float32) * columns[1],
        ],
        axis=1,
    ).astype(jnp.bfloat16)
    return (
        output_rows[None],
        grad_inputs[None],
        grad_source[None],
        join_rows(qkv_shard),
        join_rows(out_shard),
        join_rows(cq_shard),
        join_rows(ckv_shard),
        join_rows(co_shard),
        join_rows(up_shard),
        join_rows(down_shard),
        norm_shard[:, :3].T,
        norm_shard[:, 3:].T,
        clipped_self,
        clipped_cross,
        peaks,
    )


F32 = jnp.float32
BF16 = jnp.bfloat16
SCALE = HD**-0.5


def fast_fits(mesh):
    seq_count, ctx_count = mesh.shape["seq"], mesh.shape["ctx"]
    if H % seq_count or H % ctx_count:
        return False
    held, pair = H // seq_count, H // ctx_count
    return held % pair == 0 and seq_count * (held // pair) == ctx_count and pair * HD == 128


def dot(left, right, contract=((1,), (0,))):
    return lax.dot_general(left, right, (contract, ((), ())), preferred_element_type=F32)


NT = ((1,), (1,))
TN = ((0,), (0,))


def norm_forward(values, gain, bias):
    centered = values - jnp.mean(values, axis=-1, keepdims=True)
    spread = jnp.mean(centered * centered, axis=-1, keepdims=True)
    inverse = lax.rsqrt(spread + norm_eps)
    hat = centered * inverse
    return hat, inverse, (hat * gain + bias).astype(BF16)


def norm_backward(grad, hat, inverse, gain):
    scaled = grad * gain
    inner = jnp.mean(scaled, axis=-1, keepdims=True)
    outer = jnp.mean(scaled * hat, axis=-1, keepdims=True)
    return (
        (scaled - inner - hat * outer) * inverse,
        jnp.sum(grad * hat, axis=0),
        jnp.sum(grad, axis=0),
    )


MESH = pl.DeviceIdType.MESH


class Links:
    def __init__(self, send, recv, local):
        self.send, self.recv, self.local = send, recv, local
        self.count, self.local_count = 0, 0
        self.sends, self.saves = [], []

    def slots(self, count):
        start = self.count
        self.count += count
        return start

    def copy(self, index, src, dst, device):
        return pltpu.make_async_remote_copy(
            src_ref=src,
            dst_ref=dst,
            send_sem=self.send.at[index],
            recv_sem=self.recv.at[index],
            device_id=device,
            device_id_type=MESH,
        )

    def push(self, index, src, dst, device, when=None):
        made = self.copy(index, src, dst, device)
        if when is None:
            made.start()
        else:
            pl.when(when)(made.start)
        self.sends.append((made, when))

    def take(self, index, dst, device, when=None):
        made = self.copy(index, dst, dst, device)
        if when is None:
            made.wait_recv()
        else:
            pl.when(when)(made.wait_recv)

    def save(self, src, dst):
        made = pltpu.make_async_copy(src, dst, self.local.at[self.local_count])
        self.local_count += 1
        made.start()
        self.saves.append(made)
        return made

    def finish(self):
        for made, when in self.sends:
            if when is None:
                made.wait_send()
            else:
                pl.when(when)(made.wait_send)
        for made in self.saves:
            made.wait()
        self.sends, self.saves = [], []


class Team:
    def __init__(self, own, near, far, opp):
        self.own, self.near, self.far, self.opp = own, near, far, opp

    def turned(self):
        return Team(self.own, self.far, self.near, self.opp)


class Place:
    def __init__(self):
        self.s, self.c = lax.axis_index("seq"), lax.axis_index("ctx")
        self.k, self.x = lax.rem(self.s, 2), lax.div(self.s, 2)
        self.y, self.z = lax.rem(self.c, 2), lax.div(self.c, 2)
        self.sib = self.s + 1 - 2 * self.k
        self.far = lax.rem(self.s + 2, 4)
        self.opp = lax.rem(self.sib + 2, 4)
        self.pair = self.c + 1 - 2 * self.y
        other = 1 - self.x
        self.low, self.high = lax.rem(self.z, 2), lax.div(self.z, 2)
        self.beside = (self.z + 1 - 2 * self.low) * 2 + self.y
        self.over = lax.rem(self.z + 2, 4) * 2 + self.y
        self.seq = Team(
            self.s,
            ((self.sib, self.c), self.sib),
            ((self.far, self.c), self.far),
            ((self.opp, self.c), self.opp),
        )
        self.flat = Team(
            self.x * 2 + self.low,
            ((self.s, self.beside), self.x * 2 + 1 - self.low),
            ((self.far, self.c), other * 2 + self.low),
            ((self.far, self.beside), other * 2 + 1 - self.low),
        )

    def greet(self):
        barrier = pltpu.get_barrier_semaphore()
        for other in (self.sib, self.far, self.opp):
            pl.semaphore_signal(barrier, inc=1, device_id=(other, self.c), device_id_type=MESH)
        for step in range(1, 8):
            pl.semaphore_signal(
                barrier,
                inc=1,
                device_id=(self.s, lax.rem(self.c + step, 8)),
                device_id_type=MESH,
            )
        for other in ((self.far, self.beside), (self.sib, self.beside)):
            pl.semaphore_signal(barrier, inc=1, device_id=other, device_id_type=MESH)

    def meet(self):
        pl.semaphore_wait(pltpu.get_barrier_semaphore(), 12)


def rows_at(start, count):
    return pl.ds(pl.multiple_of(start, 16), count)


def lanes_at(start, count):
    return pl.ds(pl.multiple_of(start, 128), count)


class Columns:
    def __init__(self, links, place, weight, dest, parts, pieces=1):
        self.links, self.place, self.weight, self.dest = links, place, weight, dest
        rows, columns = weight.shape
        self.rows, self.whole, self.width = rows, columns // parts, columns // (4 * parts)
        self.step = rows // pieces
        self.jobs = [(part, piece) for piece in range(pieces) for part in range(parts)]
        self.base = {job: links.slots(5) for job in self.jobs}
        self.mine = place.k == place.y

    def source(self, job, target):
        part, piece = job
        return self.weight.at[
            pl.ds(piece * self.step, self.step),
            lanes_at(part * self.whole + target * self.width, self.width),
        ]

    def land(self, job, owner):
        part, piece = job
        return self.dest.at[
            rows_at(owner * self.rows + piece * self.step, self.step),
            pl.ds(part * self.width, self.width),
        ]

    def start(self, jobs=None):
        p = self.place
        for job in self.jobs if jobs is None else jobs:
            base = self.base[job]
            land = self.land(job, p.s)
            self.links.push(base, self.source(job, p.far), land, (p.far, p.c), self.mine)
            self.links.push(base + 1, self.source(job, p.opp), land, (p.opp, p.c), self.mine)
            self.links.push(base + 2, self.source(job, p.sib), land, (p.sib, p.c))
            self.links.save(self.source(job, p.s), land)

    def relay(self, jobs=None):
        p = self.place
        came = lax.rem(p.x + 1, 2) * 2 + p.y
        for job in self.jobs if jobs is None else jobs:
            base = self.base[job]
            land = self.land(job, came)
            self.links.take(base, land, (p.far, p.c), p.k == p.y)
            self.links.take(base + 1, land, (p.opp, p.c), p.k != p.y)
            self.links.push(base + 3, land, land, (p.s, p.pair))

    def finish(self):
        p = self.place
        for job in self.jobs:
            base = self.base[job]
            self.links.take(base + 2, self.land(job, p.sib), (p.sib, p.c))
            self.links.take(
                base + 3,
                self.land(job, lax.rem(p.x + 1, 2) * 2 + 1 - p.y),
                (p.s, p.pair),
            )


class Gather:
    def __init__(self, links, teams, dest, rows):
        self.links, self.teams, self.dest, self.rows = links, teams, dest, rows
        self.step = rows // len(teams)
        self.base = [links.slots(3) for _ in teams]

    def land(self, piece, owner):
        return self.dest.at[rows_at(owner * self.rows + piece * self.step, self.step)]

    def start(self, piece=0):
        t, base = self.teams[piece], self.base[piece]
        land = self.land(piece, t.own)
        self.links.push(base, land, land, t.far[0])
        self.links.push(base + 1, land, land, t.near[0])

    def forward(self, piece=0):
        t, base = self.teams[piece], self.base[piece]
        land = self.land(piece, t.far[1])
        self.links.take(base, land, t.far[0])
        self.links.push(base + 2, land, land, t.near[0])

    def finish(self, piece=0):
        t, base = self.teams[piece], self.base[piece]
        self.links.take(base + 1, self.land(piece, t.near[1]), t.near[0])
        self.links.take(base + 2, self.land(piece, t.opp[1]), t.near[0])

    def start_all(self):
        for piece in range(len(self.teams)):
            self.start(piece)

    def forward_all(self):
        for piece in range(len(self.teams)):
            self.forward(piece)

    def finish_all(self):
        for piece in range(len(self.teams)):
            self.finish(piece)


class Reduce:
    def __init__(self, links, teams, out, into, rows, partial):
        self.links, self.teams, self.out, self.into, self.partial = links, teams, out, into, partial
        self.step = rows // len(teams)
        self.base = [links.slots(3) for _ in teams]
        self.cut = [pl.ds(piece * self.step, self.step) for piece in range(len(teams))]

    def pieces(self):
        return [(piece, t, self.base[piece], self.cut[piece]) for piece, t in enumerate(self.teams)]

    def first(self):
        for piece, t, base, cut in self.pieces():
            self.out[0, cut] = self.partial(t.opp[1], piece).astype(BF16)
            self.links.push(base, self.out.at[0, cut], self.into.at[0, cut], t.near[0])
        for piece, t, base, cut in self.pieces():
            self.out[1, cut] = self.partial(t.near[1], piece).astype(BF16)
            self.links.push(base + 2, self.out.at[1, cut], self.into.at[1, cut], t.near[0])

    def second(self):
        for piece, t, base, cut in self.pieces():
            held = self.partial(t.far[1], piece).astype(F32)
            self.links.take(base, self.into.at[0, cut], t.near[0])
            self.out[2, cut] = (held + self.into[0, cut].astype(F32)).astype(BF16)
            self.links.push(base + 1, self.out.at[2, cut], self.into.at[2, cut], t.far[0])

    def last(self, then):
        for piece, t, base, cut in self.pieces():
            held = self.partial(t.own, piece).astype(F32)
            self.links.take(base + 2, self.into.at[1, cut], t.near[0])
            held = held + self.into[1, cut].astype(F32)
            self.links.take(base + 1, self.into.at[2, cut], t.far[0])
            then(piece, held + self.into[2, cut].astype(F32))

    def run(self, then):
        self.first()
        self.second()
        self.last(then)


class Shared:
    def __init__(self, links, place, weight, dest, pieces):
        self.links, self.place, self.weight, self.dest = links, place, weight, dest
        self.rows, self.width = weight.shape[0], weight.shape[1] // 4
        self.step = self.rows // pieces
        self.jobs = range(pieces)
        self.base = [links.slots(3) for _ in self.jobs]

    def source(self, job, slice_index):
        return self.weight.at[
            pl.ds(job * self.step, self.step), lanes_at(slice_index * self.width, self.width)
        ]

    def land(self, job, owner):
        return self.dest.at[rows_at(owner * self.rows + job * self.step, self.step)]

    def start(self, jobs):
        p = self.place
        for job in jobs:
            land = self.land(job, p.s)
            self.links.push(self.base[job], self.source(job, p.flat.far[1]), land, (p.far, p.c))
            self.links.push(self.base[job] + 1, self.source(job, p.flat.own), land, (p.sib, p.c))
            self.links.save(self.source(job, p.flat.own), land)

    def forward(self, jobs):
        p = self.place
        for job in jobs:
            land = self.land(job, p.far)
            self.links.take(self.base[job], land, (p.far, p.c))
            self.links.push(self.base[job] + 2, land, land, (p.sib, p.c))

    def finish(self):
        p = self.place
        for job in self.jobs:
            self.links.take(self.base[job] + 1, self.land(job, p.sib), (p.sib, p.c))
            self.links.take(self.base[job] + 2, self.land(job, p.opp), (p.sib, p.c))


def gelu_pair(value):
    rate = 0.7978845608028654
    square = value * value
    bent = jnp.tanh(rate * value * (1.0 + 0.044715 * square))
    half = 0.5 * (1.0 + bent)
    slope = half + 0.5 * value * (1.0 - bent * bent) * (rate * (1.0 + 0.134145 * square))
    return value * half, slope


def row_positions(table_ref, owner, half):
    place = lax.broadcasted_iota(jnp.int32, (2 * half, 1), 0)
    pair = table_ref[pl.ds(owner, 1)]
    first, second = pair[:, 0:1] * half, pair[:, 1:2] * half - half
    return place + jnp.where(place < half, first, second)


def column_positions(table_ref, owner, half):
    place = lax.broadcasted_iota(jnp.int32, (1, 2 * half), 1)
    pair = table_ref[pl.ds(owner, 1)]
    first, second = pair[:, 0:1] * half, pair[:, 1:2] * half - half
    return place + jnp.where(place < half, first, second)


def softmax_rows(scores):
    top = jnp.max(scores, axis=-1, keepdims=True)
    expos = jnp.exp(scores - top)
    return expos * (1.0 / jnp.sum(expos, axis=-1, keepdims=True)), top


def softmax_columns(scores):
    expos = jnp.exp(scores - jnp.max(scores, axis=0, keepdims=True))
    return expos * (1.0 / jnp.sum(expos, axis=0, keepdims=True))


PIECES = 2
STEPS = 8


def forward_kernel(
    table_ref,
    target_ref,
    source_ref,
    tokens_ref,
    encoder_ref,
    cotangent_ref,
    qkv_ref,
    out_ref,
    cq_ref,
    ckv_ref,
    co_ref,
    up_ref,
    down_ref,
    gain_ref,
    bias_ref,
    first_out,
    second_out,
    third_out,
    branch_out,
    source_out,
    w_qkv_out,
    w_cq_out,
    w_ckv_out,
    hidden_out,
    slopes_out,
    grad_third_out,
    third_part_out,
    heads_out,
    mix_out,
    query_out,
    kvs_out,
    cross_out_ref,
    sums_out,
    peak_out,
    lens_out,
    first,
    second,
    third,
    branch,
    source,
    w_qkv,
    w_cq,
    w_ckv,
    sent,
    heads,
    mix_own,
    mix,
    query,
    kv_own,
    kvs,
    cross,
    sums,
    columns,
    lens,
    rs_out,
    rs_in,
    part,
    w_up,
    w_down,
    hidden,
    slopes,
    grad_third,
    third_part,
    send_sem,
    recv_sem,
    local_sem,
):
    place, links = Place(), Links(send_sem, recv_sem, local_sem)
    p = place
    rows = tokens_ref.shape[1]
    source_rows = encoder_ref.shape[1]
    half = rows // 2
    width = w_cq.shape[1]
    pair_width = heads.shape[2]
    held = width // HD
    groups = width // pair_width
    place.greet()
    own = rows_at(p.s * rows, rows)
    inputs = tokens_ref[0].astype(F32)
    first[own] = norm_forward(inputs, gain_ref[0:1], bias_ref[0:1])[2]
    place.meet()

    get_qkv = Columns(links, place, qkv_ref, w_qkv, 3)
    get_qkv.start()
    get_first = Gather(links, (p.seq,), first, rows)
    get_first.start()
    source[rows_at(p.s * source_rows, source_rows)] = encoder_ref[0]
    get_source = Gather(links, (p.seq,), source, source_rows)
    get_source.start()
    place_lens = links.slots(3)
    line = lax.broadcasted_iota(jnp.int32, (8, 128), 0)
    lens[pl.ds(p.s, 1)] = jnp.where(line < 4, target_ref[0], source_ref[0])[None]
    own_lens = lens.at[pl.ds(p.s, 1)]
    for step, other in enumerate((p.far, p.opp, p.sib)):
        links.push(place_lens + step, own_lens, own_lens, (other, p.c))
    for owner in range(STEPS):
        columns[:, owner * rows : (owner + 1) * rows] = column_positions(table_ref, owner, half)
    own_rows = row_positions(table_ref, p.c, half)
    valid = own_rows < target_ref[0]
    own_flat = p.flat.own * rows
    branch[rows_at(own_flat, rows)] = jnp.where(valid, cotangent_ref[0].astype(F32), 0.0).astype(BF16)
    get_cq = Columns(links, place, cq_ref, w_cq, 1)
    get_ckv = Columns(links, place, ckv_ref, w_ckv, 2)
    get_up = Shared(links, place, up_ref, w_up, 4)
    flat = (p.flat, p.flat.turned())

    get_qkv.relay()
    get_first.forward()
    get_source.forward()
    get_first.finish()
    get_source.finish()
    for made in links.saves:
        made.wait()
    links.saves = []
    get_qkv.finish()
    links.save(first, first_out)
    links.save(w_qkv, w_qkv_out)
    links.save(source, source_out)
    for step, other in enumerate((p.far, p.opp, p.sib)):
        links.take(place_lens + step, lens.at[pl.ds(other, 1)], (other, p.c))
    links.save(lens, lens_out)

    def project(block, carry):
        value = dot(first[rows_at(block * rows, rows)], w_qkv[...]).astype(BF16)
        for group in range(groups):
            for part in range(3):
                at = part * width + group * pair_width
                sent[block * groups + group, part] = value[:, at : at + pair_width]
        return carry

    lax.fori_loop(0, 4, project, 0)
    a2a = links.slots(STEPS)
    mine = rows_at(p.c * rows, rows)
    for step in range(1, STEPS):
        other = lax.rem(p.c + step, STEPS)
        links.push(a2a + step, sent.at[other], heads.at[:, mine], (p.s, other))
    keep = pltpu.make_async_copy(sent.at[p.c], heads.at[:, mine], local_sem.at[STEPS * 8 - 1])
    keep.start()
    get_cq.start()
    get_ckv.start()
    get_up.start((0, 1))
    keeps = p.k == p.low
    get_down = links.slots(1)
    links.push(get_down, down_ref, w_down, (p.sib, p.c), keeps)
    own_down = pltpu.make_async_copy(down_ref, w_down, local_sem.at[STEPS * 8 - 2])
    pl.when(keeps)(own_down.start)
    get_branch = Gather(links, flat, branch, rows)
    get_branch.start_all()
    keep.wait()
    get_cq.relay()
    get_ckv.relay()
    for step in range(1, STEPS):
        other = lax.rem(p.c + STEPS - step, STEPS)
        links.take(a2a + step, heads.at[:, rows_at(other * rows, rows)], (p.s, other))
    links.save(heads, heads_out)

    my_slot = lax.div(p.c, groups)
    my_group = lax.rem(p.c, groups)
    length = lens[pl.ds(my_slot, 1)][0, 0:1, 0:1]
    back = links.slots(STEPS)
    slot_rows = rows_at(my_slot * rows, rows)
    group_lanes = lanes_at(my_group * pair_width, pair_width)

    def back_copy(owner):
        return links.copy(
            back + p.c, mix_own.at[rows_at(owner * rows, rows)], mix.at[slot_rows, group_lanes], (p.s, owner)
        )

    columns[...] = jnp.where(columns[...] < length, columns[...], STEPS * rows)

    def attend(block, peaks):
        at = rows_at(block * 2 * rows, 2 * rows)
        row_pos = jnp.concatenate(
            [row_positions(table_ref, 2 * block, half), row_positions(table_ref, 2 * block + 1, half)], axis=0
        )
        allowed = columns[...] <= row_pos
        ok = row_pos < length
        tops = []
        for head in range(pair_width // HD):
            cut = slice(head * HD, (head + 1) * HD)
            scores = dot(heads[0, at, cut], heads[1, :, cut], NT) * SCALE
            probs, top = softmax_rows(jnp.where(allowed, scores, masked_score))
            mix_own[at, cut] = dot(probs.astype(BF16), heads[2, :, cut]).astype(BF16)
            peak = jnp.max(jnp.where(ok, top, masked_score), axis=0, keepdims=True)
            tops.append(jnp.maximum(peaks[head], peak))
        return tuple(tops)

    low = jnp.full((1, 1), masked_score, F32)
    peaks = (low, low)
    for block in range(STEPS // 2):
        peaks = attend(block, peaks)
        for owner in (2 * block, 2 * block + 1):
            pl.when(p.c != owner)(back_copy(owner).start)
    for head in range(2):
        peak_out[head : head + 1] = jnp.broadcast_to(peaks[head], (1, 128))
    mix[slot_rows, group_lanes] = mix_own[mine]

    get_cq.finish()
    get_ckv.finish()
    for made in links.saves:
        made.wait()
    links.saves = []
    links.save(w_cq, w_cq_out)
    links.save(w_ckv, w_ckv_out)
    value = dot(source[...], w_ckv[...]).astype(BF16)
    for slot in range(4):
        kv_own[slot] = value[slot * source_rows : (slot + 1) * source_rows]
    own_keys = rows_at(p.c * source_rows, source_rows)
    kvs[:, own_keys] = kv_own[...]
    along, across = links.slots(4), links.slots(4)
    links.push(across, kv_own, kvs.at[:, own_keys], (p.s, p.pair))
    for step in range(1, 4):
        other = lax.rem(p.z + step, 4) * 2 + p.y
        links.push(along + step, kv_own, kvs.at[:, own_keys], (p.s, other))
    get_up.forward((0, 1))
    get_branch.forward_all()

    for owner in range(STEPS):

        @pl.when(p.c != owner)
        def _():
            lane = lanes_at((owner % groups) * pair_width, pair_width)
            links.take(
                back + owner, mix.at[pl.ds((owner // groups) * rows, rows), lane], (p.s, owner)
            )

    links.save(mix, mix_out)

    def boundary(index, left, weight, base, gather, start):
        step = rows // PIECES

        def tile(number, carry):
            lanes = lanes_at(number * 256, 256)
            part[:, lanes] = dot(left[...], weight[:, lanes]).astype(BF16)
            return carry

        lax.fori_loop(0, part.shape[1] // 256, tile, 0)

        def then(piece, total):
            cut = pl.ds(piece * step, step)
            value = base(piece) + total
            sums[index, cut] = value
            gather.dest[rows_at(start + piece * step, step)] = norm_forward(
                value, gain_ref[index + 1 : index + 2], bias_ref[index + 1 : index + 2]
            )[2]
            gather.start(piece)

        Reduce(
            links,
            (p.seq,) * PIECES,
            rs_out.at[index],
            rs_in.at[index],
            rows,
            lambda block, piece: part[rows_at(block * rows + piece * step, step)],
        ).run(then)

    step = rows // PIECES
    get_second = Gather(links, (p.seq,) * PIECES, second, rows)
    boundary(
        0,
        mix,
        out_ref,
        lambda piece: tokens_ref[0, piece * step : (piece + 1) * step].astype(F32),
        get_second,
        p.s * rows,
    )
    for hop in range(1, 4):
        other = lax.rem(p.z + 4 - hop, 4) * 2 + p.y
        land = kvs.at[:, rows_at(other * source_rows, source_rows)]
        links.take(along + hop, land, (p.s, other))
        links.push(across + hop, land, land, (p.s, p.pair))
    get_up.start((2, 3))
    get_second.forward_all()
    get_second.finish_all()
    links.save(second, second_out)
    for hop in range(4):
        other = lax.rem(p.z + 4 - hop, 4) * 2 + 1 - p.y
        land = kvs.at[:, rows_at(other * source_rows, source_rows)]
        links.take(across + hop, land, (p.s, p.pair))
    links.save(kvs, kvs_out)

    keys = kvs.shape[1]

    def cross_attend(slot, peaks):
        at = rows_at(slot * rows, rows)
        asked = dot(second[at], w_cq[...]).astype(BF16)
        query[at] = asked
        limits = lens[pl.ds(slot, 1)]
        live = lax.broadcasted_iota(jnp.int32, (1, keys), 1) < limits[0, 4:5, 0:1]
        ok = own_rows < limits[0, 0:1, 0:1]
        tops = []
        for head in range(held):
            cut = slice(head * HD, (head + 1) * HD)
            vcut = slice(width + head * HD, width + (head + 1) * HD)
            scores = dot(asked[:, cut], kvs[slot, :, cut], NT) * SCALE
            probs, top = softmax_rows(jnp.where(live, scores, masked_score))
            cross[at, cut] = dot(probs.astype(BF16), kvs[slot, :, vcut]).astype(BF16)
            peak = jnp.max(jnp.where(ok, top, masked_score), axis=0, keepdims=True)
            tops.append(jnp.maximum(peaks[head], peak))
        return tuple(tops)

    peaks = lax.fori_loop(0, 4, cross_attend, (low,) * held)
    for head in range(held):
        peak_out[2 + head : 3 + head] = jnp.broadcast_to(peaks[head], (1, 128))
    links.save(query, query_out)
    links.save(cross, cross_out_ref)
    get_up.forward((2, 3))
    get_branch.finish_all()
    links.save(branch, branch_out)
    get_third = Gather(links, flat, third, rows)
    boundary(
        1,
        cross,
        co_ref,
        lambda piece: sums[0, piece * step : (piece + 1) * step],
        get_third,
        own_flat,
    )
    links.save(sums, sums_out)
    get_third.forward_all()
    get_up.finish()
    for made in links.saves:
        made.wait()
    links.saves = []
    pl.when(keeps)(own_down.wait)
    links.take(get_down, w_down, (p.sib, p.c), p.k != p.low)
    get_third.finish_all()
    links.save(third, third_out)

    def units(number, carry):
        lanes = lanes_at(number * 256, 256)
        value, slope = gelu_pair(dot(third[...], w_up[:, lanes]))
        hidden[:, lanes] = value.astype(BF16)
        grad = dot(branch[...], w_down[rows_at(number * 256, 256)], NT)
        slopes[:, lanes] = (grad * slope).astype(BF16)
        return carry

    lax.fori_loop(0, w_up.shape[1] // 256, units, 0, unroll=2)
    links.save(hidden, hidden_out)
    links.save(slopes, slopes_out)

    def back_rows(number, carry):
        lanes = lanes_at(number * 256, 256)
        grad_third[:, lanes] = dot(slopes[...], w_up[rows_at(number * 256, 256)], NT).astype(BF16)
        third_part[:, lanes] = dot(hidden[...], w_down[:, lanes]).astype(BF16)
        return carry

    lax.fori_loop(0, third.shape[1] // 256, back_rows, 0, unroll=2)
    links.save(grad_third, grad_third_out)
    links.save(third_part, third_part_out)
    for owner in range(STEPS):
        pl.when(p.c != owner)(back_copy(owner).wait_send)
    links.finish()


def forward_call(
    table, targets, sources, tokens, encoder, cotangent, qkv, out, cq, ckv, co, up, down, gain, bias
):
    rows, width = tokens.shape[1], out.shape[0]
    source_rows = encoder.shape[1]
    depth = tokens.shape[2]
    keys = 8 * source_rows
    any_space = pl.BlockSpec(memory_space=pl.ANY)
    vmem = pl.BlockSpec(memory_space=pltpu.VMEM)
    smem = pl.BlockSpec(memory_space=pltpu.SMEM)
    shapes = dict(
        first=((4 * rows, depth), BF16),
        second=((4 * rows, depth), BF16),
        third=((4 * rows, depth), BF16),
        branch=((4 * rows, depth), BF16),
        source=((4 * source_rows, depth), BF16),
        w_qkv=((depth, 3 * width), BF16),
        w_cq=((depth, width), BF16),
        w_ckv=((depth, 2 * width), BF16),
        hidden=((4 * rows, up.shape[1] // 4), BF16),
        slopes=((4 * rows, up.shape[1] // 4), BF16),
        grad_third=((4 * rows, depth), BF16),
        third_part=((4 * rows, depth), BF16),
        heads=((3, 8 * rows, 128), BF16),
        mix=((4 * rows, width), BF16),
        query=((4 * rows, width), BF16),
        kvs=((4, keys, 2 * width), BF16),
        cross=((4 * rows, width), BF16),
        sums=((2, rows, depth), F32),
        peak=((8, 128), F32),
        lens=((4, 8, 128), jnp.int32),
    )
    scratch = [
        shapes[name]
        for name in ("first", "second", "third", "branch", "source", "w_qkv", "w_cq", "w_ckv")
    ] + [
        ((8, 3, rows, 128), BF16),
        shapes["heads"],
        ((8 * rows, 128), BF16),
        shapes["mix"],
        shapes["query"],
        ((4, source_rows, 2 * width), BF16),
        shapes["kvs"],
        shapes["cross"],
        shapes["sums"],
        ((1, 8 * rows), jnp.int32),
        shapes["lens"],
        ((2, 3, rows, depth), BF16),
        ((2, 3, rows, depth), BF16),
        ((4 * rows, depth), BF16),
        ((depth, up.shape[1] // 4), BF16),
        (down.shape, BF16),
        shapes["hidden"],
        shapes["slopes"],
        shapes["grad_third"],
        shapes["third_part"],
    ]
    made = pl.pallas_call(
        forward_kernel,
        in_specs=[vmem] + [smem] * 2
        + [vmem] * 3
        + [any_space, vmem, any_space, any_space, vmem, any_space, any_space]
        + [vmem] * 2,
        out_specs=[vmem if name == "peak" else any_space for name in shapes],
        out_shape=[jax.ShapeDtypeStruct(*shape) for shape in shapes.values()],
        scratch_shapes=[pltpu.VMEM(*shape) for shape in scratch]
        + [
            pltpu.SemaphoreType.DMA((128,)),
            pltpu.SemaphoreType.DMA((128,)),
            pltpu.SemaphoreType.DMA((64,)),
        ],
        compiler_params=pltpu.CompilerParams(
            collective_id=0, has_side_effects=True, vmem_limit_bytes=61 * 2**20
        ),
        name="forward",
    )(table, targets, sources, tokens, encoder, cotangent, qkv, out, cq, ckv, co, up, down, gain, bias)
    return dict(zip(shapes, made))


class Sum:
    def __init__(self, links, place, full, into, away, result, lead=False):
        self.links, self.place, self.full = links, place, full
        self.half = place.y
        self.other = (place.s, place.pair)
        self.into, self.away, self.result, self.lead = into, away, result, lead
        self.base = links.slots(7)
        self.near = place.z + 1 - 2 * lax.rem(place.z, 2)
        self.across = lax.rem(place.z + 2, 4)
        self.order = (lax.rem(self.near + 2, 4), self.across, self.near, place.z)

    def start(self, turns=(0, 1, 2, 3)):
        for turn in turns:
            to = self.order[turn]
            give = 1 - self.half
            src = self.full.at[to, give] if self.lead else self.full.at[:, to, give]
            self.links.push(self.base + turn, src, self.into.at[to], self.other)

    def turn(self, turns=(0, 1, 2, 3)):
        p, links, into, away = self.place, self.links, self.into, self.away
        for turn in turns:
            to = self.order[turn]
            links.take(self.base + turn, into.at[to], self.other)
            if turn == 1:
                links.take(self.base + 4, away.at[0], (p.s, self.near * 2 + p.y))

            def add(a, carry):
                mine = self.full[to, self.half, a] if self.lead else self.full[a, to, self.half]
                total = mine.astype(F32) + into[to, a].astype(F32)
                if turn == 1:
                    total = total + away[0, a].astype(F32)
                into[to, a] = total.astype(BF16)
                return carry

            if turn < 3:
                lax.fori_loop(0, into.shape[1], add, 0)
                goal = self.across if turn == 1 else self.near
                links.push(
                    self.base + 4 + turn, into.at[to], away.at[turn], (p.s, goal * 2 + p.y)
                )

    def finish(self):
        p, links, into, away = self.place, self.links, self.into, self.away
        links.take(self.base + 5, away.at[1], (p.s, self.across * 2 + p.y))
        links.take(self.base + 6, away.at[2], (p.s, self.near * 2 + p.y))

        def add(a, carry):
            mine = self.full[p.z, self.half, a] if self.lead else self.full[a, p.z, self.half]
            total = mine.astype(F32) + into[p.z, a].astype(F32)
            total = total + (away[1, a].astype(F32) + away[2, a].astype(F32))
            self.result[a] = total.astype(BF16)
            return carry

        lax.fori_loop(0, into.shape[1], add, 0)


class SumChip:
    def __init__(self, links, place, full, into, along, away, result):
        self.links, self.place, self.full, self.into = links, place, full, into
        self.along, self.away, self.result = along, away, result
        self.base = links.slots(7)
        self.high = (1 - place.high, place.high)

    def start(self):
        p = self.place
        for turn in range(4):
            high, y = self.high[turn // 2], (1 - p.y, p.y)[turn % 2]
            src, dst = self.full.at[high, y, 1 - p.k], self.into.at[high, y]
            self.links.push(self.base + turn, src, dst, (p.sib, p.c))

    def total(self, turn, extra, store):
        p, full, into = self.place, self.full, self.into
        high, y = self.high[turn // 2], (1 - p.y, p.y)[turn % 2]
        self.links.take(self.base + turn, into.at[high, y], (p.sib, p.c))

        def add(a, carry):
            value = full[high, y, p.k, a].astype(F32) + into[high, y, a].astype(F32)
            for part in extra:
                value = value + part[a].astype(F32)
            store[a] = value.astype(BF16)
            return carry

        lax.fori_loop(0, into.shape[2], add, 0)

    def across_y(self):
        p = self.place
        for step in range(2):
            held = self.into.at[self.high[step], 1 - p.y]
            self.total(2 * step, (), held)
            self.links.push(self.base + 4 + step, held, self.along.at[step], (p.s, p.pair))

    def across_z(self):
        p = self.place
        self.links.take(self.base + 4, self.along.at[0], (p.s, p.pair))
        held = self.into.at[self.high[0], p.y]
        self.total(1, (self.along.at[0],), held)
        self.links.push(self.base + 6, held, self.away, (p.s, p.over))

    def finish(self):
        p = self.place
        self.links.take(self.base + 5, self.along.at[1], (p.s, p.pair))
        self.links.take(self.base + 6, self.away, (p.s, p.over))
        self.total(3, (self.along.at[1], self.away), self.result)


class Exchange:
    def __init__(self, links, team, result, taken):
        self.links, self.team, self.result, self.taken = links, team, result, taken
        self.base = links.slots(3)
        self.others = (team.far, team.opp, team.near)

    def start(self):
        own = pl.ds(self.team.own, 1)
        for step, (device, index) in enumerate(self.others):
            src = self.result.at[pl.ds(index, 1)]
            self.links.push(self.base + step, src, self.taken.at[own], device)
        self.taken[own] = self.result[own]

    def finish(self):
        for step, (device, index) in enumerate(self.others):
            self.links.take(self.base + step, self.taken.at[pl.ds(index, 1)], device)


def norm_terms_of(values):
    centered = values - jnp.mean(values, axis=-1, keepdims=True)
    spread = jnp.mean(centered * centered, axis=-1, keepdims=True)
    inverse = lax.rsqrt(spread + norm_eps)
    return centered * inverse, inverse


def backward_body(r):
    place, links = Place(), Links(r.send_sem, r.recv_sem, r.local_sem)
    p = place
    rows = r.tokens.shape[1]
    half = rows // 2
    width = r.w_cq.shape[1]
    source_rows = r.source.shape[0] // 4
    keys = r.kvs.shape[1]
    pair_width = r.heads.shape[2]
    held, groups = width // HD, width // pair_width
    depth = r.tokens.shape[2]
    step = rows // PIECES
    share = depth // 4

    loads = {}

    def load(names):
        for name in names:
            at = r.load_sem.at[r.loaded.index(name)]
            loads[name] = pltpu.make_async_copy(getattr(r, name + "_hbm"), getattr(r, name), at)
            loads[name].start()

    r.part, r.third_part = r.hidden.at[:, :depth], r.hidden.at[:, depth : 2 * depth]
    r.second, r.first = r.slopes.at[:, :depth], r.slopes.at[:, depth : 2 * depth]
    soon = ("hidden", "branch", "third", "slopes", "sums")
    late = ("third_part", "second", "first")
    load(soon)

    def need(*wanted):
        for name in wanted:
            loads.pop(name).wait()

    place.greet()
    place.meet()
    r.peaks_ctx[pl.ds(p.c, 1)] = r.peak[...][None]
    peak_base = links.slots(STEPS)
    own_peak = r.peaks_ctx.at[pl.ds(p.c, 1)]
    for hop in range(1, STEPS):
        links.push(peak_base + hop, own_peak, own_peak, (p.s, lax.rem(p.c + hop, STEPS)))

    own_rows = row_positions(r.table, p.c, half)
    r.norms[...] = jnp.zeros_like(r.norms)

    def add_norms(index, gain, bias):
        r.norms[index : index + 1] += gain[None]
        r.norms[index + 3 : index + 4] += bias[None]

    get_cross = Gather(links, (p.seq,) * PIECES, r.cross_branch, rows)

    def after_third(piece, total):
        cut = slice(piece * step, (piece + 1) * step)
        hat, inverse = norm_terms_of(r.sums[1, cut])
        back, gain, bias = norm_backward(total, hat, inverse, r.gain[2:3])
        add_norms(2, gain, bias)
        valid = own_rows[cut] < r.target[0]
        value = jnp.where(valid, r.cotangent[0, cut].astype(F32), 0.0) + back
        r.grad_sum[cut] = value
        r.cross_branch[rows_at(p.s * rows + piece * step, step)] = value.astype(BF16)
        get_cross.start(piece)

    def stored(ref):
        return lambda block, piece: ref[rows_at(block * rows + piece * step, step)].astype(F32)

    flat = (p.flat, p.flat.turned())
    sum_third = Reduce(
        links, flat, r.rs_out.at[0], r.rs_in.at[0], rows, stored(r.grad_third)
    )
    sum_third.first()

    def down_grad(block, carry):
        value = dot(r.hidden[:, lanes_at(block * 256, 256)], r.branch[...], TN).astype(BF16)
        place_of = (lax.div(block, 4), lax.rem(block, 2), lax.rem(lax.div(block, 2), 2))
        r.down_full[place_of] = value.reshape(r.down_full.shape[3:])
        return carry

    need("hidden", "branch")
    lax.fori_loop(0, 3, down_grad, 0)
    sum_third.second()
    load([name for name in r.loaded if name not in soon + late])
    lax.fori_loop(3, 8, down_grad, 0)
    down = SumChip(
        links, place, r.down_full, r.down_into, r.down_along, r.down_away, r.down_result
    )
    down.start()
    need("third", "slopes")

    def up_grad(number, carry):
        block, side = lax.div(number, 2), lax.rem(number, 2)
        lanes = lanes_at(side * depth, depth)
        left = r.third[:, lanes_at(block * share, share)]
        value = dot(left, r.slopes[:, lanes], TN).astype(BF16)
        value = value.reshape(2, 2, 2, share // 8, depth)
        for low in range(2):
            at = lax.div(block, 2) * 2 + low
            r.up_full[:, :, lax.rem(block, 2), at, :, lanes] = value[:, low]
        return carry

    lax.fori_loop(0, 8, up_grad, 0)
    load(late)
    down.across_y()
    up = SumChip(links, place, r.up_full, r.up_into, r.up_along, r.up_away, r.up_result)
    up.start()
    up.across_y()
    need("sums")
    sum_third.last(after_third)
    for hop in range(1, STEPS):
        other = lax.rem(p.c + STEPS - hop, STEPS)
        links.take(peak_base + hop, r.peaks_ctx.at[pl.ds(other, 1)], (p.s, other))
    best = []
    for group in range(groups):
        tile = r.peaks_ctx[group]
        for owner in range(group + groups, STEPS, groups):
            tile = jnp.maximum(tile, r.peaks_ctx[owner])
        best.append(tile)
    everyone = best[0]
    for tile in best[1:]:
        everyone = jnp.maximum(everyone, tile)
    mine = jnp.concatenate([tile[0:2] for tile in best] + [everyone[2 : 2 + held]], axis=0)
    r.peaks_seq[pl.ds(p.s, 1)] = mine[None]
    peak_seq = links.slots(3)
    own_peak = r.peaks_seq.at[pl.ds(p.s, 1)]
    for hop, other in enumerate((p.far, p.opp, p.sib)):
        links.push(peak_seq + hop, own_peak, own_peak, (other, p.c))

    get_cross.forward_all()
    down.across_z()
    need("w_co", "cross", "query", "kvs", "w_cq", "second")
    get_cross.finish_all()

    def cross_back(slot, carry):
        at = rows_at(slot * rows, rows)
        grad_rows = dot(r.cross_branch[at], r.w_co[...], NT).astype(BF16)
        live = lax.broadcasted_iota(jnp.int32, (keys, 1), 0) < r.lens[pl.ds(slot, 1)][0, 4:5, 0:1]
        for head in range(held):
            cut = slice(head * HD, (head + 1) * HD)
            vcut = slice(width + head * HD, width + (head + 1) * HD)
            asked, grad = r.query[at, cut], grad_rows[:, cut]
            key = r.kvs[slot, :, cut]
            scores = dot(key, asked, NT) * SCALE
            probs = softmax_columns(jnp.where(live, scores, masked_score))
            dprobs = dot(r.kvs[slot, :, vcut], grad, NT)
            delta = jnp.sum(probs * dprobs, axis=0, keepdims=True)
            dscores = (probs * (dprobs - delta)).astype(BF16)
            r.dquery[at, cut] = (dot(dscores, key, TN) * SCALE).astype(BF16)
            shape = (4, 2, source_rows, HD)
            r.dkv_full[slot, :, :, :, cut] = (
                (dot(dscores, asked) * SCALE).astype(BF16).reshape(shape)
            )
            r.dkv_full[slot, :, :, :, vcut] = (
                dot(probs.astype(BF16), grad).astype(BF16).reshape(shape)
            )
        return carry

    lax.fori_loop(0, 4, cross_back, 0)
    dkv = Sum(links, place, r.dkv_full, r.dkv_into, r.dkv_away, r.dkv_result)
    need("third_part")
    sum_output = Reduce(
        links, flat, r.rs_out.at[2], r.rs_in.at[2], rows, stored(r.third_part)
    )
    sum_output.first()

    get_self = Gather(links, (p.seq,) * PIECES, r.self_branch, rows)

    def after_second(piece, total):
        cut = slice(piece * step, (piece + 1) * step)
        hat, inverse = norm_terms_of(r.sums[0, cut])
        back, gain, bias = norm_backward(total, hat, inverse, r.gain[1:2])
        add_norms(1, gain, bias)
        value = r.grad_sum[cut] + back
        r.grad_sum[cut] = value
        r.self_branch[rows_at(p.s * rows + piece * step, step)] = value.astype(BF16)
        get_self.start(piece)

    def cross_rows(number, carry):
        lanes = lanes_at(number * 256, 256)
        r.part[:, lanes] = dot(r.dquery[...], r.w_cq[rows_at(number * 256, 256)], NT).astype(BF16)
        return carry

    lax.fori_loop(0, depth // 256, cross_rows, 0)
    Reduce(
        links, (p.seq,) * PIECES, r.rs_out.at[1], r.rs_in.at[1], rows, stored(r.part)
    ).run(after_second)

    def row_grad(left, right, full):
        def one(part, carry):
            lanes = lanes_at(part * 128, 128)
            value = dot(left[:, lanes], right[...], TN).astype(BF16)
            full[pl.ds(part * 2, 2)] = value.reshape((2, 2) + full.shape[2:])
            return carry

        lax.fori_loop(0, left.shape[1] // 128, one, 0)

    def column_grad(left, right, full):
        def one(block, carry):
            lanes = lanes_at(block * share, share)
            value = dot(left[:, lanes], right(), TN).astype(BF16)
            full[pl.ds(block, 1)] = value.reshape((1,) + full.shape[1:])
            return carry

        lax.fori_loop(0, 4, one, 0)

    row_grad(r.cross, r.cross_branch, r.co_full)
    get_self.forward_all()
    column_grad(r.second, lambda: r.dquery[...], r.cq_full)
    get_self.finish_all()

    need("w_out", "heads", "mix")

    def mix_back(slot, carry):
        value = dot(r.self_branch[rows_at(slot * rows, rows)], r.w_out[...], NT).astype(BF16)
        for group in range(groups):
            r.gsent[slot * groups + group] = value[:, group * pair_width : (group + 1) * pair_width]
        return carry

    lax.fori_loop(0, 4, mix_back, 0)
    a2a = links.slots(STEPS)
    mine_rows = rows_at(p.c * rows, rows)
    for hop in range(1, STEPS):
        other = lax.rem(p.c + hop, STEPS)
        links.push(a2a + hop, r.gsent.at[other], r.gheads.at[mine_rows], (p.s, other))
    r.gheads[mine_rows] = r.gsent[p.c]
    my_slot, my_group = lax.div(p.c, groups), lax.rem(p.c, groups)
    length = r.lens[pl.ds(my_slot, 1)][0, 0:1, 0:1]
    for owner in range(STEPS):
        pos = row_positions(r.table, owner, half)
        pos = jnp.where(pos < length, pos, STEPS * rows)
        r.key_pos[owner * rows : (owner + 1) * rows] = jnp.broadcast_to(pos, (rows, 128))
    co = Sum(links, place, r.co_full, r.co_into, r.co_away, r.co_result, True)
    cq = Sum(links, place, r.cq_full, r.cq_into, r.cq_away, r.cq_result)
    so = Sum(links, place, r.so_full, r.so_into, r.so_away, r.so_result, True)
    row_grad(r.mix, r.self_branch, r.so_full)
    for job in (dkv, cq, co, so):
        job.start()
    sum_output.second()
    up.across_z()
    for hop in range(1, STEPS):
        other = lax.rem(p.c + STEPS - hop, STEPS)
        links.take(a2a + hop, r.gheads.at[rows_at(other * rows, rows)], (p.s, other))

    slot_rows = rows_at(my_slot * rows, rows)
    group_lanes = lanes_at(my_group * pair_width, pair_width)
    back_q, back_kv = links.slots(STEPS), links.slots(STEPS)

    def q_copy(owner):
        at = rows_at(owner * rows, rows)
        return links.copy(
            back_q + p.c, r.dq_own.at[at], r.dproj.at[0, slot_rows, group_lanes], (p.s, owner)
        )

    def kv_copy(owner):
        at = rows_at(owner * rows, rows)
        return links.copy(
            back_kv + p.c,
            r.dkv_own.at[:, at],
            r.dproj.at[pl.ds(1, 2), slot_rows, group_lanes],
            (p.s, owner),
        )

    def attend_back(block, carry):
        at = rows_at(block * 2 * rows, 2 * rows)
        asked_pos = jnp.concatenate(
            [
                column_positions(r.table, 2 * block, half),
                column_positions(r.table, 2 * block + 1, half),
            ],
            axis=1,
        )
        key_pos = r.key_pos[...]
        allowed = jnp.concatenate([key_pos] * (2 * rows // 128), axis=1) <= asked_pos
        for head in range(pair_width // HD):
            cut = slice(head * HD, (head + 1) * HD)
            asked, grad = r.heads[0, at, cut], r.gheads[at, cut]
            key = r.heads[1, :, cut]
            scores = dot(key, asked, NT) * SCALE
            probs = softmax_columns(jnp.where(allowed, scores, masked_score))
            dprobs = dot(r.heads[2, :, cut], grad, NT)
            delta = jnp.sum(probs * dprobs, axis=0, keepdims=True)
            dscores = (probs * (dprobs - delta)).astype(BF16)
            r.dq_own[at, cut] = (dot(dscores, key, TN) * SCALE).astype(BF16)
            if block == 0:
                r.acc[0, :, cut] = dot(dscores, asked)
                r.acc[1, :, cut] = dot(probs.astype(BF16), grad)
            else:
                r.acc[0, :, cut] += dot(dscores, asked)
                r.acc[1, :, cut] += dot(probs.astype(BF16), grad)
        return carry

    for block in range(STEPS // 2):
        attend_back(block, 0)
        for owner in (2 * block, 2 * block + 1):
            pl.when(p.c != owner)(q_copy(owner).start)
    for owner in range(STEPS):
        at = rows_at(owner * rows, rows)
        r.dkv_own[0, at] = (r.acc[0, at] * SCALE).astype(BF16)
        r.dkv_own[1, at] = r.acc[1, at].astype(BF16)
        pl.when(p.c != owner)(kv_copy(owner).start)
    r.dproj[0, slot_rows, group_lanes] = r.dq_own[mine_rows]
    r.dproj[pl.ds(1, 2), slot_rows, group_lanes] = r.dkv_own[:, mine_rows]

    dkv.turn((0, 2))
    cq.turn((0, 2))
    def after_output(piece, total):
        cut = slice(piece * step, (piece + 1) * step)
        valid = own_rows[cut] < r.target[0]
        r.output[cut] = jnp.where(valid, r.sums[1, cut] + total, 0.0).astype(BF16)

    sum_output.last(after_output)
    dkv.turn((1, 3))
    cq.turn((1, 3))
    for job in (co, so):
        job.turn((0, 2))
    need("w_ckv", "source")
    dkv.finish()
    r.dsource[...] = r.dkv_result[...].reshape(4 * source_rows, 2 * width)
    column_grad(r.source, lambda: r.dsource[...], r.ckv_full)
    ckv = Sum(links, place, r.ckv_full, r.ckv_into, r.ckv_away, r.ckv_result)
    ckv.start()

    def source_partial(block, piece):
        return dot(r.dsource[rows_at(block * source_rows, source_rows)], r.w_ckv[...], NT)

    def after_encoder(piece, total):
        r.grad_source[...] = total

    Reduce(links, (p.seq,), r.enc_out, r.enc_in, source_rows, source_partial).run(after_encoder)

    need("w_qkv", "first")
    for owner in range(STEPS):

        @pl.when(p.c != owner)
        def _():
            at = pl.ds((owner // groups) * rows, rows)
            lane = lanes_at((owner % groups) * pair_width, pair_width)
            links.take(back_q + owner, r.dproj.at[0, at, lane], (p.s, owner))
            links.take(back_kv + owner, r.dproj.at[pl.ds(1, 2), at, lane], (p.s, owner))

    def first_rows(number, carry):
        at = rows_at(number * 256, 256)
        total = dot(r.dproj[0], r.w_qkv[at, :width], NT)
        total += dot(r.dproj[1], r.w_qkv[at, width : 2 * width], NT)
        total += dot(r.dproj[2], r.w_qkv[at, 2 * width :], NT)
        r.part[:, lanes_at(number * 256, 256)] = total.astype(BF16)
        return carry

    lax.fori_loop(0, depth // 256, first_rows, 0)

    def after_first(piece, total):
        cut = slice(piece * step, (piece + 1) * step)
        hat, inverse = norm_terms_of(r.tokens[0, cut].astype(F32))
        back, gain, bias = norm_backward(total, hat, inverse, r.gain[0:1])
        add_norms(0, gain, bias)
        r.grad_inputs[cut] = r.grad_sum[cut] + back

    def qkv_grad(block, carry):
        lanes = lanes_at(block * share, share)
        left = r.first[:, lanes]
        for part in range(3):
            value = dot(left, r.dproj[part], TN).astype(BF16)
            r.qkv_full[pl.ds(block, 1), :, :, :, part * width : (part + 1) * width] = value.reshape(
                (1,) + r.qkv_full.shape[1:4] + (width,)
            )
        return carry

    lax.fori_loop(0, 4, qkv_grad, 0)
    qkv = Sum(links, place, r.qkv_full, r.qkv_into, r.qkv_away, r.qkv_result)
    qkv.start()
    sum_first = Reduce(
        links, (p.seq,) * PIECES, r.rs_out.at[3], r.rs_in.at[3], rows, stored(r.part)
    )
    sum_first.first()
    sum_first.second()
    for job in (co, so):
        job.turn((1, 3))
    ckv.turn((0, 2))
    qkv.turn((0, 2))
    sum_first.last(after_first)

    norm_seq, norm_ctx = links.slots(3), links.slots(STEPS)
    others = (p.far, p.opp, p.sib)
    for hop, other in enumerate(others):
        links.push(
            norm_seq + hop,
            r.norms.at[:, lanes_at(other * share, share)],
            r.norms_seq.at[pl.ds(p.s, 1)].at[0],
            (other, p.c),
        )
    ckv.turn((1, 3))
    total = r.norms[:, lanes_at(p.s * share, share)]
    for hop, other in enumerate(others):
        links.take(norm_seq + hop, r.norms_seq.at[pl.ds(other, 1)].at[0], (other, p.c))
        total = total + r.norms_seq[pl.ds(other, 1)][0]
    r.norms_ctx[pl.ds(p.c, 1)] = total[None]
    own_norms = r.norms_ctx.at[pl.ds(p.c, 1)]
    for hop in range(1, STEPS):
        links.push(norm_ctx + hop, own_norms, own_norms, (p.s, lax.rem(p.c + hop, STEPS)))
    qkv.turn((1, 3))
    sums = {}
    for job in (up, down):
        job.finish()
    sums["up"] = Exchange(links, p.flat, r.up_result, r.up_taken)
    sums["up"].start()
    keeps, swapped = p.k == p.low, links.slots(1)
    links.push(swapped, r.down_result, r.down_taken, (p.sib, p.beside), p.k != p.low)

    @pl.when(keeps)
    def _():
        r.down_taken[...] = r.down_result[...]

    for job in (co, so):
        job.finish()
    for name, job in (("cq", cq), ("ckv", ckv), ("qkv", qkv)):
        job.finish()
        sums[name] = Exchange(links, p.seq, getattr(r, name + "_result"), getattr(r, name + "_taken"))
        sums[name].start()
    for hop in range(1, STEPS):
        other = lax.rem(p.c + STEPS - hop, STEPS)
        links.take(norm_ctx + hop, r.norms_ctx.at[pl.ds(other, 1)], (p.s, other))
    total = r.norms_ctx[0]
    for owner in range(1, STEPS):
        total = total + r.norms_ctx[owner]
    r.norm_sum[...] = total
    for hop, other in enumerate(others):
        links.take(peak_seq + hop, r.peaks_seq.at[pl.ds(other, 1)], (other, p.c))
    for job in sums.values():
        job.finish()
    links.take(swapped, r.down_taken, (p.sib, p.beside), p.k != p.low)
    for owner in range(STEPS):
        pl.when(p.c != owner)(q_copy(owner).wait_send)
        pl.when(p.c != owner)(kv_copy(owner).wait_send)
    links.finish()


def backward_call(kept, given):
    rows, depth = given["tokens"].shape[1:]
    width = kept["w_cq"].shape[1]
    source_rows = kept["source"].shape[0] // 4
    keys = kept["kvs"].shape[1]
    share = depth // 32
    hidden = kept["hidden"].shape[1]
    any_space = pl.BlockSpec(memory_space=pl.ANY)
    vmem = pl.BlockSpec(memory_space=pltpu.VMEM)
    smem = pl.BlockSpec(memory_space=pltpu.SMEM)
    inputs = dict(
        table=(vmem, given["table"]),
        target=(smem, given["target"]),
        tokens=(vmem, given["tokens"]),
        cotangent=(vmem, given["cotangent"]),
        gain=(vmem, given["gain"]),
        peak=(vmem, kept["peak"]),
        lens=(vmem, kept["lens"]),
        grad_third=(vmem, kept["grad_third"]),
    )
    loaded = dict(
        hidden=kept["hidden"],
        branch=kept["branch"],
        third=kept["third"],
        slopes=kept["slopes"],
        third_part=kept["third_part"],
        sums=kept["sums"],
        w_co=given["cross_out"],
        cross=kept["cross"],
        query=kept["query"],
        kvs=kept["kvs"],
        w_cq=kept["w_cq"],
        second=kept["second"],
        w_out=given["self_out"],
        heads=kept["heads"],
        mix=kept["mix"],
        w_ckv=kept["w_ckv"],
        source=kept["source"],
        w_qkv=kept["w_qkv"],
        first=kept["first"],
    )
    for name, value in loaded.items():
        inputs[name + "_hbm"] = (any_space, value)
    outs = dict(
        output=((rows, depth), BF16),
        grad_inputs=((rows, depth), F32),
        grad_source=((source_rows, depth), F32),
        down_taken=((hidden // (8 * share), share, depth), BF16),
        co_result=((1, share, depth), BF16),
        so_result=((1, share, depth), BF16),
        up_taken=((4, share, hidden), BF16),
        cq_taken=((4, share, width), BF16),
        ckv_taken=((4, share, 2 * width), BF16),
        qkv_taken=((4, share, 3 * width), BF16),
        norm_sum=((8, depth // 4), F32),
        peaks_seq=((4, 8, 128), F32),
    )
    down_blocks = hidden // (8 * share)
    scratch = {
        name: (value.shape, value.dtype)
        for name, value in loaded.items()
        if name not in ("third_part", "second", "first")
    }
    scratch |= dict(
        down_full=((2, 2, 2, down_blocks, share, depth), BF16),
        up_full=((2, 2, 2, 4, share, hidden), BF16),
        down_into=((2, 2, down_blocks, share, depth), BF16),
        down_along=((2, down_blocks, share, depth), BF16),
        down_away=((down_blocks, share, depth), BF16),
        down_result=((down_blocks, share, depth), BF16),
        up_into=((2, 2, 4, share, hidden), BF16),
        up_along=((2, 4, share, hidden), BF16),
        up_away=((4, share, hidden), BF16),
        up_result=((4, share, hidden), BF16),
        peaks_ctx=((8, 8, 128), F32),
        norms=((8, depth), F32),
        norms_seq=((4, 8, depth // 4), F32),
        norms_ctx=((8, 8, depth // 4), F32),
        cross_branch=((4 * rows, depth), BF16),
        self_branch=((4 * rows, depth), BF16),
        grad_sum=((rows, depth), F32),
        rs_out=((4, 3, rows, depth), BF16),
        rs_in=((4, 3, rows, depth), BF16),
        enc_out=((3, source_rows, depth), BF16),
        enc_in=((3, source_rows, depth), BF16),
        dquery=((4 * rows, width), BF16),
        dsource=((4 * source_rows, 2 * width), BF16),
        gsent=((8, rows, 128), BF16),
        gheads=((8 * rows, 128), BF16),
        key_pos=((8 * rows, 128), jnp.int32),
        acc=((2, 8 * rows, 128), F32),
        dq_own=((8 * rows, 128), BF16),
        dkv_own=((2, 8 * rows, 128), BF16),
        dproj=((3, 4 * rows, width), BF16),
    )
    for name in ("co", "so"):
        scratch[name + "_full"] = ((4, 2, 1, share, depth), BF16)
        scratch[name + "_into"] = ((4, 1, share, depth), BF16)
        scratch[name + "_away"] = ((3, 1, share, depth), BF16)
    for name, columns, r in (
        ("cq", width, share),
        ("ckv", 2 * width, share),
        ("qkv", 3 * width, share),
        ("dkv", 2 * width, source_rows),
    ):
        scratch[name + "_full"] = ((4, 4, 2, r, columns), BF16)
        scratch[name + "_into"] = ((4, 4, r, columns), BF16)
        scratch[name + "_away"] = ((3, 4, r, columns), BF16)
        scratch[name + "_result"] = ((4, r, columns), BF16)
    sems = dict(send_sem=224, recv_sem=224, local_sem=4, load_sem=len(loaded))
    names = list(inputs) + list(outs) + list(scratch) + list(sems)

    def kernel(*refs):
        held = dict(zip(names, refs), loaded=tuple(loaded))
        backward_body(type("Refs", (), held))

    made = pl.pallas_call(
        kernel,
        in_specs=[spec for spec, _ in inputs.values()],
        out_specs=[vmem] * len(outs),
        out_shape=[jax.ShapeDtypeStruct(*shape) for shape in outs.values()],
        scratch_shapes=[pltpu.VMEM(*shape) for shape in scratch.values()]
        + [pltpu.SemaphoreType.DMA((count,)) for count in sems.values()],
        compiler_params=pltpu.CompilerParams(
            collective_id=1, has_side_effects=True, vmem_limit_bytes=61 * 2**20
        ),
        name="backward",
    )(*[value for _, value in inputs.values()])
    return dict(zip(outs, made))


def finish_kernel(
    clip_ref,
    peaks_ref,
    norm_ref,
    qkv_w,
    cq_w,
    ckv_w,
    output_ref,
    inputs_ref,
    source_ref,
    down_ref,
    co_ref,
    so_ref,
    up_ref,
    cq_ref,
    ckv_ref,
    qkv_ref,
    output_out,
    inputs_out,
    source_out,
    qkv_out,
    so_out,
    cq_out,
    ckv_out,
    co_out,
    up_out,
    down_out,
    gain_out,
    bias_out,
    self_out,
    cross_out,
    peaks_out,
):
    output_out[0] = output_ref[...]
    inputs_out[0] = inputs_ref[...]
    source_out[0] = source_ref[...]
    share = so_out.shape[0]
    so_out[...] = so_ref[0].astype(F32)
    co_out[...] = co_ref[0].astype(F32)
    for block in range(down_ref.shape[0]):
        down_out[block * share : (block + 1) * share] = down_ref[block].astype(F32)

    def columns(out, taken, parts):
        whole, width = out.shape[1] // parts, out.shape[1] // (4 * parts)
        for owner in range(4):
            for part in range(parts):
                at = part * whole + owner * width
                out[:, at : at + width] = taken[owner, :, part * width : (part + 1) * width].astype(
                    F32
                )

    columns(up_out, up_ref, 1)
    columns(cq_out, cq_ref, 1)
    columns(ckv_out, ckv_ref, 2)
    columns(qkv_out, qkv_ref, 3)
    spread = gain_out.shape[1]
    turned = pltpu.roll(norm_ref[...], norm_ref.shape[1] - lax.axis_index("ctx") * spread, 1)
    gain_out[...] = turned[0:3, :spread]
    bias_out[...] = turned[3:6, :spread]
    lane = lax.broadcasted_iota(jnp.int32, (1, 128), 1)
    held = peaks_ref.shape[1] // 2
    for kind in range(2):
        tops = jnp.zeros((1, 128), F32)
        for head in range(H):
            at = kind * held + head % held
            tops = jnp.where(lane == head, peaks_ref[head // held, at : at + 1], tops)
        peaks_out[kind : kind + 1] = tops[:, :H]
    for owner in range(4):
        for two in range(held // 2):
            head = owner * held + two * 2
            at = slice(head * HD, head * HD + 128)
            for kind, jobs in (
                (0, ((self_out, qkv_w, 0, 0), (self_out, qkv_w, H * HD, H * HD))),
                (1, ((cross_out, cq_w, 0, 0), (cross_out, ckv_w, 0, H * HD))),
            ):
                top = [peaks_ref[owner, kind * held + two * 2 + i : kind * held + two * 2 + i + 1] for i in (0, 1)]
                limit = [clip_ref[kind, head + i] for i in (0, 1)]
                limits = jnp.where(lane < HD, limit[0], limit[1])
                tops = jnp.where(lane < HD, top[0], top[1])
                factor = jnp.sqrt(limits / jnp.maximum(tops, limits))
                for out, weight, start, goal in jobs:
                    out[:, goal + head * HD : goal + head * HD + 128] = (
                        weight[:, start + head * HD : start + head * HD + 128].astype(F32) * factor
                    ).astype(BF16)


def finish_call(made, given):
    rows, depth = given["tokens"].shape[1:]
    hidden = given["mlp_up"].shape[1]
    source_rows, share = made["grad_source"].shape[0], made["so_result"].shape[1]
    columns = H * HD
    weight_rows = given["self_qkv"].shape[0]
    shapes = [
        ((1, rows, depth), BF16),
        ((1, rows, depth), F32),
        ((1, source_rows, depth), F32),
        ((share, 3 * columns), F32),
        ((share, depth), F32),
        ((share, columns), F32),
        ((share, 2 * columns), F32),
        ((share, depth), F32),
        ((share, hidden), F32),
        ((hidden // 32, depth), F32),
        ((3, share), F32),
        ((3, share), F32),
        ((weight_rows, 2 * columns), BF16),
        ((weight_rows, 2 * columns), BF16),
        ((2, H), F32),
    ]
    vmem = pl.BlockSpec(memory_space=pltpu.VMEM)
    return pl.pallas_call(
        finish_kernel,
        in_specs=[pl.BlockSpec(memory_space=pltpu.SMEM)] + [vmem] * 15,
        out_specs=[vmem] * len(shapes),
        out_shape=[jax.ShapeDtypeStruct(*shape) for shape in shapes],
        compiler_params=pltpu.CompilerParams(vmem_limit_bytes=61 * 2**20),
        name="finish",
    )(
        given["clip"],
        made["peaks_seq"],
        made["norm_sum"],
        given["self_qkv"],
        given["cross_q"],
        given["cross_kv"],
        made["output"],
        made["grad_inputs"],
        made["grad_source"],
        made["down_taken"],
        made["co_result"],
        made["so_result"],
        made["up_taken"],
        made["cq_taken"],
        made["ckv_taken"],
        made["qkv_taken"],
    )


def fast_device(
    tokens,
    encoder_states,
    cotangent,
    target_lengths,
    source_lengths,
    block_table,
    self_qkv,
    self_out,
    cross_q,
    cross_kv,
    cross_out,
    mlp_up,
    mlp_down,
    norm_gain,
    norm_bias,
    clip_limit,
):
    kept = forward_call(
        block_table,
        target_lengths,
        source_lengths,
        tokens,
        encoder_states,
        cotangent,
        self_qkv,
        self_out,
        cross_q,
        cross_kv,
        cross_out,
        mlp_up,
        mlp_down,
        norm_gain,
        norm_bias,
    )
    given = dict(
        table=block_table,
        target=target_lengths,
        tokens=tokens,
        cotangent=cotangent,
        gain=norm_gain,
        cross_out=cross_out,
        self_out=self_out,
        self_qkv=self_qkv,
        cross_q=cross_q,
        cross_kv=cross_kv,
        mlp_up=mlp_up,
        clip=clip_limit,
    )
    made = backward_call(kept, given)
    return tuple(finish_call(made, given))


def solution(mesh):
    body = fast_device if fast_fits(mesh) else general_device
    return jax.shard_map(
        body,
        mesh=mesh,
        in_specs=(
            P("seq", "ctx", None),
            P("seq", "ctx", None),
            P("seq", "ctx", None),
            P("seq"),
            P("seq"),
            P(),
            P("seq", None),
            P("seq", None),
            P("seq", None),
            P("seq", None),
            P("seq", None),
            P("seq", None),
            P("seq", None),
            P(),
            P(),
            P(),
        ),
        out_specs=(
            P("seq", "ctx", None),
            P("seq", "ctx", None),
            P("seq", "ctx", None),
            P(("seq", "ctx"), None),
            P(("seq", "ctx"), None),
            P(("seq", "ctx"), None),
            P(("seq", "ctx"), None),
            P(("seq", "ctx"), None),
            P(("seq", "ctx"), None),
            P(("seq", "ctx"), None),
            P(None, ("seq", "ctx")),
            P(None, ("seq", "ctx")),
            P("seq", None),
            P("seq", None),
            P(),
        ),
        check_vma=False,
    )
```

```python
import functools

import jax
import jax.numpy as jnp
from jax import lax
from jax.experimental import pallas as pl
from jax.experimental.pallas import tpu as pltpu
from jax.sharding import PartitionSpec as P

SEQ, CTX = "seq", "ctx"
ROWS_OUT, ROWS_BACK = "rd,re->de", "re,de->rd"
SCORES, MIXED = "qhd,khd->hqk", "hqk,khd->qhd"
H = 16
HD = 64


masked_score = -1000000000.0
norm_eps = 1e-05


def block_size(count):
    return max((step for step in range(1, min(count, 512) + 1) if count % step == 0))


def layer_norm(values, gain, bias):
    centered = values - jnp.mean(values, axis=-1, keepdims=True)
    spread = jnp.mean(centered * centered, axis=-1, keepdims=True)
    return centered * lax.rsqrt(spread + norm_eps) * gain + bias


def allowed_pairs(query_pos, key_pos, key_limit, causal):
    allowed = jnp.broadcast_to(
        (key_pos < key_limit)[None, :], (query_pos.shape[0], key_pos.shape[0])
    )
    if causal:
        allowed = allowed & (key_pos[None, :] <= query_pos[:, None])
    return allowed


def head_scores(query_heads, key_rows):
    key_heads = key_rows.reshape(key_rows.shape[0], H, HD)
    return jnp.einsum(
        SCORES, query_heads, key_heads, preferred_element_type=jnp.float32
    ) * HD ** (-0.5)


def softmax_stats(query_heads, kv_rows, key_pos, query_pos, query_ok, key_limit, causal):
    count = kv_rows.shape[0]
    step = block_size(count)
    width = H * HD
    rows = query_heads.shape[0]

    def softmax_visit(carry, block):
        top, total, peak = carry
        block_rows, block_pos = block
        allowed = allowed_pairs(query_pos, block_pos, key_limit, causal)
        scores = jnp.where(
            allowed[None], head_scores(query_heads, block_rows[:, :width]), masked_score
        )
        new_top = jnp.maximum(top, jnp.max(scores, axis=-1))
        total = total * jnp.exp(top - new_top) + jnp.sum(
            jnp.exp(scores - new_top[..., None]), axis=-1
        )
        counted = jnp.where((allowed & query_ok[:, None])[None], scores, masked_score)
        peak = jnp.maximum(peak, jnp.max(counted, axis=(1, 2)))
        return ((new_top, total, peak), None)

    start = (
        jnp.full((H, rows), -jnp.inf, jnp.float32),
        jnp.zeros((H, rows), jnp.float32),
        jnp.full((H,), masked_score, jnp.float32),
    )
    blocks = (kv_rows.reshape(count // step, step, 2 * width), key_pos.reshape(count // step, step))
    return lax.scan(softmax_visit, start, blocks)[0]


def attend_values(query_heads, kv_rows, key_pos, query_pos, key_limit, causal, top, total):
    count = kv_rows.shape[0]
    step = block_size(count)
    width = H * HD
    rows = query_heads.shape[0]

    def attend_visit(acc, block):
        block_rows, block_pos = block
        allowed = allowed_pairs(query_pos, block_pos, key_limit, causal)
        scores = jnp.where(
            allowed[None], head_scores(query_heads, block_rows[:, :width]), masked_score
        )
        weights = (jnp.exp(scores - top[..., None]) / total[..., None]).astype(jnp.bfloat16)
        value_heads = block_rows[:, width:].reshape(step, H, HD)
        return (
            acc
            + jnp.einsum(MIXED, weights, value_heads, preferred_element_type=jnp.float32),
            None,
        )

    blocks = (kv_rows.reshape(count // step, step, 2 * width), key_pos.reshape(count // step, step))
    acc = lax.scan(attend_visit, jnp.zeros((rows, H, HD), jnp.float32), blocks)[0]
    return acc.reshape(rows, width)


def query_grads(
    query_heads, kv_rows, key_pos, query_pos, key_limit, causal, top, total, grad_heads, delta
):
    count = kv_rows.shape[0]
    step = block_size(count)
    width = H * HD
    rows = query_heads.shape[0]

    def query_visit(acc, block):
        block_rows, block_pos = block
        allowed = allowed_pairs(query_pos, block_pos, key_limit, causal)
        scores = jnp.where(
            allowed[None], head_scores(query_heads, block_rows[:, :width]), masked_score
        )
        probs = jnp.exp(scores - top[..., None]) / total[..., None]
        value_heads = block_rows[:, width:].reshape(step, H, HD)
        dprobs = jnp.einsum(
            SCORES, grad_heads, value_heads, preferred_element_type=jnp.float32
        )
        dscores = (probs * (dprobs - delta[..., None])).astype(jnp.bfloat16)
        key_heads = block_rows[:, :width].reshape(step, H, HD)
        return (
            acc
            + jnp.einsum(MIXED, dscores, key_heads, preferred_element_type=jnp.float32),
            None,
        )

    blocks = (kv_rows.reshape(count // step, step, 2 * width), key_pos.reshape(count // step, step))
    acc = lax.scan(query_visit, jnp.zeros((rows, H, HD), jnp.float32), blocks)[0]
    return acc.reshape(rows, width) * HD ** (-0.5)


def key_grads(
    query_heads,
    kv_rows,
    key_pos,
    query_pos,
    key_limit,
    causal,
    top,
    total,
    grad_heads,
    delta,
    start,
    count,
):
    step = block_size(count)
    width = H * HD

    def piece(index):
        offset = start + index * step
        block_rows = lax.dynamic_slice_in_dim(kv_rows, offset, step, 0)
        block_pos = lax.dynamic_slice_in_dim(key_pos, offset, step, 0)
        allowed = allowed_pairs(query_pos, block_pos, key_limit, causal)
        scores = jnp.where(
            allowed[None], head_scores(query_heads, block_rows[:, :width]), masked_score
        )
        probs = jnp.exp(scores - top[..., None]) / total[..., None]
        value_heads = block_rows[:, width:].reshape(step, H, HD)
        dprobs = jnp.einsum(
            SCORES, grad_heads, value_heads, preferred_element_type=jnp.float32
        )
        dscores = (probs * (dprobs - delta[..., None])).astype(jnp.bfloat16)
        dkeys = jnp.einsum(
            "hqk,qhd->khd", dscores, query_heads, preferred_element_type=jnp.float32
        ).reshape(step, width) * HD ** (-0.5)
        dvalues = jnp.einsum(
            "hqk,qhd->khd",
            probs.astype(jnp.bfloat16),
            grad_heads,
            preferred_element_type=jnp.float32,
        ).reshape(step, width)
        return jnp.concatenate([dkeys, dvalues], axis=1)

    return lax.map(piece, jnp.arange(count // step, dtype=jnp.int32)).reshape(count, 2 * width)


def split_rows(grad, seq_count, ctx_count):
    return grad.reshape(
        (seq_count, ctx_count, grad.shape[0] // (seq_count * ctx_count)) + grad.shape[1:]
    )


def join_rows(grad):
    return grad.reshape((grad.shape[2],) + grad.shape[3:])


def general_device(
    tokens,
    encoder_states,
    cotangent,
    target_lengths,
    source_lengths,
    block_table,
    self_qkv,
    self_out,
    cross_q,
    cross_kv,
    cross_out,
    mlp_up,
    mlp_down,
    norm_gain,
    norm_bias,
    clip_limit,
):
    rows = tokens.shape[1]
    width = H * HD
    half = rows // 2
    source_rows = encoder_states.shape[1]
    seq_count = lax.axis_size(SEQ)
    ctx_count = lax.axis_size(CTX)
    all_positions = (
        block_table[:, :, None] * half + jnp.arange(half, dtype=jnp.int32)[None, None, :]
    ).reshape(-1)
    own_positions = lax.dynamic_slice_in_dim(all_positions, lax.axis_index(CTX) * rows, rows, 0)
    length = target_lengths[0]
    source_length = source_lengths[0]
    query_ok = own_positions < length
    valid_rows = query_ok[:, None]
    source_positions = jnp.arange(source_rows * ctx_count, dtype=jnp.int32)
    w_qkv, w_out, w_cq, w_ckv, w_co = (
        lax.all_gather(self_qkv, SEQ, axis=0, tiled=True),
        lax.all_gather(self_out, SEQ, axis=0, tiled=True),
        lax.all_gather(cross_q, SEQ, axis=0, tiled=True),
        lax.all_gather(cross_kv, SEQ, axis=0, tiled=True),
        lax.all_gather(cross_out, SEQ, axis=0, tiled=True),
    )
    inputs = tokens[0].astype(jnp.float32)
    first_norm, first_back = jax.vjp(layer_norm, inputs, norm_gain[0], norm_bias[0])
    first_low = first_norm.astype(jnp.bfloat16)
    projected = jnp.dot(first_low, w_qkv, preferred_element_type=jnp.float32).astype(jnp.bfloat16)
    self_query = projected[:, :width].reshape(rows, H, HD)
    source_kv = jnp.dot(encoder_states[0], w_ckv, preferred_element_type=jnp.float32).astype(
        jnp.bfloat16
    )
    self_kv, cross_kvs = (
        lax.all_gather(projected[:, width:], CTX, axis=0, tiled=True),
        lax.all_gather(source_kv, CTX, axis=0, tiled=True),
    )
    self_top, self_total, self_peak = softmax_stats(
        self_query, self_kv, all_positions, own_positions, query_ok, length, True
    )
    self_mix = attend_values(
        self_query, self_kv, all_positions, own_positions, length, True, self_top, self_total
    )
    self_low = self_mix.astype(jnp.bfloat16)
    first_sum = inputs + jnp.dot(self_low, w_out, preferred_element_type=jnp.float32)
    second_norm, second_back = jax.vjp(layer_norm, first_sum, norm_gain[1], norm_bias[1])
    second_low = second_norm.astype(jnp.bfloat16)
    cross_rows = jnp.dot(second_low, w_cq, preferred_element_type=jnp.float32).astype(jnp.bfloat16)
    cross_query = cross_rows.reshape(rows, H, HD)
    cross_top, cross_total, cross_peak = softmax_stats(
        cross_query, cross_kvs, source_positions, own_positions, query_ok, source_length, False
    )
    cross_mix = attend_values(
        cross_query,
        cross_kvs,
        source_positions,
        own_positions,
        source_length,
        False,
        cross_top,
        cross_total,
    )
    cross_low = cross_mix.astype(jnp.bfloat16)
    second_sum = first_sum + jnp.dot(cross_low, w_co, preferred_element_type=jnp.float32)
    third_norm, third_back = jax.vjp(layer_norm, second_sum, norm_gain[2], norm_bias[2])
    third_low = third_norm.astype(jnp.bfloat16)
    w_up, w_down = (
        lax.all_gather(mlp_up, SEQ, axis=0, tiled=True),
        lax.all_gather(mlp_down, SEQ, axis=0, tiled=True),
    )
    hidden_pre = jnp.dot(third_low, w_up, preferred_element_type=jnp.float32)
    hidden_act, gelu_back = jax.vjp(jax.nn.gelu, hidden_pre)
    hidden_low = hidden_act.astype(jnp.bfloat16)
    third_sum = second_sum + jnp.dot(hidden_low, w_down, preferred_element_type=jnp.float32)
    output_rows = jnp.where(valid_rows, third_sum, 0.0).astype(jnp.bfloat16)
    peaks = lax.pmax(jnp.stack([self_peak, cross_peak]), (SEQ, CTX))
    grad_rows = jnp.where(valid_rows, cotangent[0].astype(jnp.float32), 0.0)
    mlp_branch = grad_rows.astype(jnp.bfloat16)
    grad_down = jnp.einsum("rf,rd->fd", hidden_low, mlp_branch, preferred_element_type=jnp.float32)
    grad_act = jnp.einsum("rd,fd->rf", mlp_branch, w_down, preferred_element_type=jnp.float32)
    grad_pre = gelu_back(grad_act)[0].astype(jnp.bfloat16)
    grad_up = jnp.einsum("rd,rf->df", third_low, grad_pre, preferred_element_type=jnp.float32)
    back_third, gain_three, bias_three = third_back(
        jnp.einsum("rf,df->rd", grad_pre, w_up, preferred_element_type=jnp.float32)
    )
    up_part, down_part = (
        lax.psum_scatter(
            split_rows(grad_up, seq_count, ctx_count).astype(jnp.bfloat16),
            CTX,
            scatter_dimension=1,
            tiled=True,
        ).astype(jnp.float32),
        lax.psum_scatter(
            split_rows(grad_down, seq_count, ctx_count).astype(jnp.bfloat16),
            CTX,
            scatter_dimension=1,
            tiled=True,
        ).astype(jnp.float32),
    )
    up_shard, down_shard = (
        lax.psum_scatter(
            up_part.astype(jnp.bfloat16), SEQ, scatter_dimension=0, tiled=True
        ).astype(jnp.float32),
        lax.psum_scatter(
            down_part.astype(jnp.bfloat16), SEQ, scatter_dimension=0, tiled=True
        ).astype(jnp.float32),
    )
    grad_second = grad_rows + back_third
    cross_branch = grad_second.astype(jnp.bfloat16)
    grad_co = jnp.einsum(ROWS_OUT, cross_low, cross_branch, preferred_element_type=jnp.float32)
    cross_heads_grad = (
        jnp.einsum(ROWS_BACK, cross_branch, w_co, preferred_element_type=jnp.float32)
        .astype(jnp.bfloat16)
        .reshape(rows, H, HD)
    )
    cross_delta = jnp.einsum(
        "qhd,qhd->hq", cross_heads_grad.astype(jnp.float32), cross_mix.reshape(rows, H, HD)
    )
    grad_cross_rows = query_grads(
        cross_query,
        cross_kvs,
        source_positions,
        own_positions,
        source_length,
        False,
        cross_top,
        cross_total,
        cross_heads_grad,
        cross_delta,
    ).astype(jnp.bfloat16)
    grad_source_kv = lax.psum_scatter(
        key_grads(
            cross_query,
            cross_kvs,
            source_positions,
            own_positions,
            source_length,
            False,
            cross_top,
            cross_total,
            cross_heads_grad,
            cross_delta,
            jnp.int32(0),
            source_rows * lax.axis_size(CTX),
        ).astype(jnp.bfloat16),
        CTX,
        scatter_dimension=0,
        tiled=True,
    )
    grad_cq = jnp.einsum(
        ROWS_OUT, second_low, grad_cross_rows, preferred_element_type=jnp.float32
    )
    grad_ckv = jnp.einsum(
        "sd,se->de", encoder_states[0], grad_source_kv, preferred_element_type=jnp.float32
    )
    grad_source = jnp.einsum("se,de->sd", grad_source_kv, w_ckv, preferred_element_type=jnp.float32)
    back_second, gain_two, bias_two = second_back(
        jnp.einsum(ROWS_BACK, grad_cross_rows, w_cq, preferred_element_type=jnp.float32)
    )
    grad_first = grad_second + back_second
    self_branch = grad_first.astype(jnp.bfloat16)
    grad_so = jnp.einsum(ROWS_OUT, self_low, self_branch, preferred_element_type=jnp.float32)
    self_heads_grad = (
        jnp.einsum(ROWS_BACK, self_branch, w_out, preferred_element_type=jnp.float32)
        .astype(jnp.bfloat16)
        .reshape(rows, H, HD)
    )
    self_delta = jnp.einsum(
        "qhd,qhd->hq", self_heads_grad.astype(jnp.float32), self_mix.reshape(rows, H, HD)
    )
    grad_query = query_grads(
        self_query,
        self_kv,
        all_positions,
        own_positions,
        length,
        True,
        self_top,
        self_total,
        self_heads_grad,
        self_delta,
    ).astype(jnp.bfloat16)
    grad_kv = lax.psum_scatter(
        key_grads(
            self_query,
            self_kv,
            all_positions,
            own_positions,
            length,
            True,
            self_top,
            self_total,
            self_heads_grad,
            self_delta,
            jnp.int32(0),
            rows * lax.axis_size(CTX),
        ).astype(jnp.bfloat16),
        CTX,
        scatter_dimension=0,
        tiled=True,
    )
    grad_projected = jnp.concatenate([grad_query, grad_kv], axis=1)
    grad_qkv = jnp.einsum(
        ROWS_OUT, first_low, grad_projected, preferred_element_type=jnp.float32
    )
    back_first, gain_one, bias_one = first_back(
        jnp.einsum(ROWS_BACK, grad_projected, w_qkv, preferred_element_type=jnp.float32)
    )
    grad_inputs = grad_first + back_first
    norm_terms = jnp.stack([gain_one, gain_two, gain_three, bias_one, bias_two, bias_three], axis=1)
    qkv_part, out_part, cq_part, ckv_part, co_part, norm_part = (
        lax.psum_scatter(
            split_rows(grad_qkv, seq_count, ctx_count).astype(jnp.bfloat16),
            CTX,
            scatter_dimension=1,
            tiled=True,
        ).astype(jnp.float32),
        lax.psum_scatter(
            split_rows(grad_so, seq_count, ctx_count).astype(jnp.bfloat16),
            CTX,
            scatter_dimension=1,
            tiled=True,
        ).astype(jnp.float32),
        lax.psum_scatter(
            split_rows(grad_cq, seq_count, ctx_count).astype(jnp.bfloat16),
            CTX,
            scatter_dimension=1,
            tiled=True,
        ).astype(jnp.float32),
        lax.psum_scatter(
            split_rows(grad_ckv, seq_count, ctx_count).astype(jnp.bfloat16),
            CTX,
            scatter_dimension=1,
            tiled=True,
        ).astype(jnp.float32),
        lax.psum_scatter(
            split_rows(grad_co, seq_count, ctx_count).astype(jnp.bfloat16),
            CTX,
            scatter_dimension=1,
            tiled=True,
        ).astype(jnp.float32),
        lax.psum_scatter(
            split_rows(norm_terms, seq_count, ctx_count).astype(jnp.bfloat16),
            CTX,
            scatter_dimension=1,
            tiled=True,
        ).astype(jnp.float32),
    )
    qkv_shard, out_shard, cq_shard, ckv_shard, co_shard, norm_shard = (
        lax.psum_scatter(
            qkv_part.astype(jnp.bfloat16), SEQ, scatter_dimension=0, tiled=True
        ).astype(jnp.float32),
        lax.psum_scatter(
            out_part.astype(jnp.bfloat16), SEQ, scatter_dimension=0, tiled=True
        ).astype(jnp.float32),
        lax.psum_scatter(
            cq_part.astype(jnp.bfloat16), SEQ, scatter_dimension=0, tiled=True
        ).astype(jnp.float32),
        lax.psum_scatter(
            ckv_part.astype(jnp.bfloat16), SEQ, scatter_dimension=0, tiled=True
        ).astype(jnp.float32),
        lax.psum_scatter(
            co_part.astype(jnp.bfloat16), SEQ, scatter_dimension=0, tiled=True
        ).astype(jnp.float32),
        lax.psum_scatter(
            norm_part.astype(jnp.bfloat16), SEQ, scatter_dimension=0, tiled=True
        ).astype(jnp.float32),
    )
    norm_shard = join_rows(norm_shard)
    factors = jnp.sqrt(clip_limit / jnp.maximum(peaks, clip_limit))
    columns = jnp.repeat(factors, HD, axis=1)
    qkv_wide = self_qkv.astype(jnp.float32)
    clipped_self = jnp.concatenate(
        [qkv_wide[:, :width] * columns[0], qkv_wide[:, width : 2 * width] * columns[0]], axis=1
    ).astype(jnp.bfloat16)
    clipped_cross = jnp.concatenate(
        [
            cross_q.astype(jnp.float32) * columns[1],
            cross_kv[:, :width].astype(jnp.float32) * columns[1],
        ],
        axis=1,
    ).astype(jnp.bfloat16)
    return (
        output_rows[None],
        grad_inputs[None],
        grad_source[None],
        join_rows(qkv_shard),
        join_rows(out_shard),
        join_rows(cq_shard),
        join_rows(ckv_shard),
        join_rows(co_shard),
        join_rows(up_shard),
        join_rows(down_shard),
        norm_shard[:, :3].T,
        norm_shard[:, 3:].T,
        clipped_self,
        clipped_cross,
        peaks,
    )


F32 = jnp.float32
BF16 = jnp.bfloat16
SCALE = HD**-0.5


def fast_fits(mesh):
    seq_count, ctx_count = mesh.shape[SEQ], mesh.shape[CTX]
    if H % seq_count or H % ctx_count:
        return False
    held, pair = H // seq_count, H // ctx_count
    return held % pair == 0 and seq_count * (held // pair) == ctx_count and pair * HD == 128


def dot(left, right, contract=((1,), (0,))):
    return lax.dot_general(left, right, (contract, ((), ())), preferred_element_type=F32)


NT = ((1,), (1,))
TN = ((0,), (0,))


def norm_forward(values, gain, bias):
    centered = values - jnp.mean(values, axis=-1, keepdims=True)
    spread = jnp.mean(centered * centered, axis=-1, keepdims=True)
    inverse = lax.rsqrt(spread + norm_eps)
    hat = centered * inverse
    return hat, inverse, (hat * gain + bias).astype(BF16)


def norm_backward(grad, hat, inverse, gain):
    scaled = grad * gain
    inner = jnp.mean(scaled, axis=-1, keepdims=True)
    outer = jnp.mean(scaled * hat, axis=-1, keepdims=True)
    return (
        (scaled - inner - hat * outer) * inverse,
        jnp.sum(grad * hat, axis=0),
        jnp.sum(grad, axis=0),
    )


MESH = pl.DeviceIdType.MESH


class Links:
    def __init__(self, send, recv, local):
        self.send, self.recv, self.local = send, recv, local
        self.count, self.local_count = 0, 0
        self.sends, self.saves = [], []

    def slots(self, count):
        start = self.count
        self.count += count
        return start

    def copy(self, index, src, dst, device):
        return pltpu.make_async_remote_copy(
            src_ref=src,
            dst_ref=dst,
            send_sem=self.send.at[index],
            recv_sem=self.recv.at[index],
            device_id=device,
            device_id_type=MESH,
        )

    def push(self, index, src, dst, device, when=None):
        made = self.copy(index, src, dst, device)
        if when is None:
            made.start()
        else:
            pl.when(when)(made.start)
        self.sends.append((made, when))

    def take(self, index, dst, device, when=None):
        made = self.copy(index, dst, dst, device)
        if when is None:
            made.wait_recv()
        else:
            pl.when(when)(made.wait_recv)

    def save(self, src, dst):
        made = pltpu.make_async_copy(src, dst, self.local.at[self.local_count])
        self.local_count += 1
        made.start()
        self.saves.append(made)
        return made

    def finish(self):
        for made, when in self.sends:
            if when is None:
                made.wait_send()
            else:
                pl.when(when)(made.wait_send)
        for made in self.saves:
            made.wait()
        self.sends, self.saves = [], []


class Team:
    def __init__(self, own, near, far, opp):
        self.own, self.near, self.far, self.opp = own, near, far, opp

    def turned(self):
        return Team(self.own, self.far, self.near, self.opp)


class Place:
    def __init__(self):
        self.s, self.c = lax.axis_index(SEQ), lax.axis_index(CTX)
        self.k, self.x = lax.rem(self.s, 2), lax.div(self.s, 2)
        self.y, self.z = lax.rem(self.c, 2), lax.div(self.c, 2)
        self.sib = self.s + 1 - 2 * self.k
        self.far = lax.rem(self.s + 2, 4)
        self.opp = lax.rem(self.sib + 2, 4)
        self.pair = self.c + 1 - 2 * self.y
        other = 1 - self.x
        self.low, self.high = lax.rem(self.z, 2), lax.div(self.z, 2)
        self.beside = (self.z + 1 - 2 * self.low) * 2 + self.y
        self.over = lax.rem(self.z + 2, 4) * 2 + self.y
        self.seq = Team(
            self.s,
            ((self.sib, self.c), self.sib),
            ((self.far, self.c), self.far),
            ((self.opp, self.c), self.opp),
        )
        self.flat = Team(
            self.x * 2 + self.low,
            ((self.s, self.beside), self.x * 2 + 1 - self.low),
            ((self.far, self.c), other * 2 + self.low),
            ((self.far, self.beside), other * 2 + 1 - self.low),
        )

    def greet(self):
        barrier = pltpu.get_barrier_semaphore()
        for other in (self.sib, self.far, self.opp):
            pl.semaphore_signal(barrier, inc=1, device_id=(other, self.c), device_id_type=MESH)
        for step in range(1, 8):
            pl.semaphore_signal(
                barrier,
                inc=1,
                device_id=(self.s, lax.rem(self.c + step, 8)),
                device_id_type=MESH,
            )
        for other in ((self.far, self.beside), (self.sib, self.beside)):
            pl.semaphore_signal(barrier, inc=1, device_id=other, device_id_type=MESH)

    def meet(self):
        pl.semaphore_wait(pltpu.get_barrier_semaphore(), 12)


def rows_at(start, count):
    return pl.ds(pl.multiple_of(start, 16), count)


def lanes_at(start, count):
    return pl.ds(pl.multiple_of(start, 128), count)


class Columns:
    def __init__(self, links, place, weight, dest, parts, pieces=1):
        self.links, self.place, self.weight, self.dest = links, place, weight, dest
        rows, columns = weight.shape
        self.rows, self.whole, self.width = rows, columns // parts, columns // (4 * parts)
        self.step = rows // pieces
        self.jobs = [(part, piece) for piece in range(pieces) for part in range(parts)]
        self.base = {job: links.slots(5) for job in self.jobs}
        self.mine = place.k == place.y

    def source(self, job, target):
        part, piece = job
        return self.weight.at[
            pl.ds(piece * self.step, self.step),
            lanes_at(part * self.whole + target * self.width, self.width),
        ]

    def land(self, job, owner):
        part, piece = job
        return self.dest.at[
            rows_at(owner * self.rows + piece * self.step, self.step),
            pl.ds(part * self.width, self.width),
        ]

    def start(self, jobs=None):
        p = self.place
        for job in self.jobs if jobs is None else jobs:
            base = self.base[job]
            land = self.land(job, p.s)
            self.links.push(base, self.source(job, p.far), land, (p.far, p.c), self.mine)
            self.links.push(base + 1, self.source(job, p.opp), land, (p.opp, p.c), self.mine)
            self.links.push(base + 2, self.source(job, p.sib), land, (p.sib, p.c))
            self.links.save(self.source(job, p.s), land)

    def relay(self, jobs=None):
        p = self.place
        came = lax.rem(p.x + 1, 2) * 2 + p.y
        for job in self.jobs if jobs is None else jobs:
            base = self.base[job]
            land = self.land(job, came)
            self.links.take(base, land, (p.far, p.c), p.k == p.y)
            self.links.take(base + 1, land, (p.opp, p.c), p.k != p.y)
            self.links.push(base + 3, land, land, (p.s, p.pair))

    def finish(self):
        p = self.place
        for job in self.jobs:
            base = self.base[job]
            self.links.take(base + 2, self.land(job, p.sib), (p.sib, p.c))
            self.links.take(
                base + 3,
                self.land(job, lax.rem(p.x + 1, 2) * 2 + 1 - p.y),
                (p.s, p.pair),
            )


class Gather:
    def __init__(self, links, teams, dest, rows):
        self.links, self.teams, self.dest, self.rows = links, teams, dest, rows
        self.step = rows // len(teams)
        self.base = [links.slots(3) for _ in teams]

    def land(self, piece, owner):
        return self.dest.at[rows_at(owner * self.rows + piece * self.step, self.step)]

    def start(self, piece=0):
        t, base = self.teams[piece], self.base[piece]
        land = self.land(piece, t.own)
        self.links.push(base, land, land, t.far[0])
        self.links.push(base + 1, land, land, t.near[0])

    def forward(self, piece=0):
        t, base = self.teams[piece], self.base[piece]
        land = self.land(piece, t.far[1])
        self.links.take(base, land, t.far[0])
        self.links.push(base + 2, land, land, t.near[0])

    def finish(self, piece=0):
        t, base = self.teams[piece], self.base[piece]
        self.links.take(base + 1, self.land(piece, t.near[1]), t.near[0])
        self.links.take(base + 2, self.land(piece, t.opp[1]), t.near[0])

    def start_all(self):
        for piece in range(len(self.teams)):
            self.start(piece)

    def forward_all(self):
        for piece in range(len(self.teams)):
            self.forward(piece)

    def finish_all(self):
        for piece in range(len(self.teams)):
            self.finish(piece)


class Reduce:
    def __init__(self, links, teams, out, into, rows, partial):
        self.links, self.teams, self.out, self.into, self.partial = links, teams, out, into, partial
        self.step = rows // len(teams)
        self.base = [links.slots(3) for _ in teams]
        self.cut = [pl.ds(piece * self.step, self.step) for piece in range(len(teams))]

    def pieces(self):
        return [(piece, t, self.base[piece], self.cut[piece]) for piece, t in enumerate(self.teams)]

    def first(self):
        for piece, t, base, cut in self.pieces():
            self.out[0, cut] = self.partial(t.opp[1], piece).astype(BF16)
            self.links.push(base, self.out.at[0, cut], self.into.at[0, cut], t.near[0])
        for piece, t, base, cut in self.pieces():
            self.out[1, cut] = self.partial(t.near[1], piece).astype(BF16)
            self.links.push(base + 2, self.out.at[1, cut], self.into.at[1, cut], t.near[0])

    def second(self):
        for piece, t, base, cut in self.pieces():
            held = self.partial(t.far[1], piece).astype(F32)
            self.links.take(base, self.into.at[0, cut], t.near[0])
            self.out[2, cut] = (held + self.into[0, cut].astype(F32)).astype(BF16)
            self.links.push(base + 1, self.out.at[2, cut], self.into.at[2, cut], t.far[0])

    def last(self, then):
        for piece, t, base, cut in self.pieces():
            held = self.partial(t.own, piece).astype(F32)
            self.links.take(base + 2, self.into.at[1, cut], t.near[0])
            held = held + self.into[1, cut].astype(F32)
            self.links.take(base + 1, self.into.at[2, cut], t.far[0])
            then(piece, held + self.into[2, cut].astype(F32))

    def run(self, then):
        self.first()
        self.second()
        self.last(then)


class Shared:
    def __init__(self, links, place, weight, dest, pieces):
        self.links, self.place, self.weight, self.dest = links, place, weight, dest
        self.rows, self.width = weight.shape[0], weight.shape[1] // 4
        self.step = self.rows // pieces
        self.jobs = range(pieces)
        self.base = [links.slots(3) for _ in self.jobs]

    def source(self, job, slice_index):
        return self.weight.at[
            pl.ds(job * self.step, self.step), lanes_at(slice_index * self.width, self.width)
        ]

    def land(self, job, owner):
        return self.dest.at[rows_at(owner * self.rows + job * self.step, self.step)]

    def start(self, jobs):
        p = self.place
        for job in jobs:
            land = self.land(job, p.s)
            self.links.push(self.base[job], self.source(job, p.flat.far[1]), land, (p.far, p.c))
            self.links.push(self.base[job] + 1, self.source(job, p.flat.own), land, (p.sib, p.c))
            self.links.save(self.source(job, p.flat.own), land)

    def forward(self, jobs):
        p = self.place
        for job in jobs:
            land = self.land(job, p.far)
            self.links.take(self.base[job], land, (p.far, p.c))
            self.links.push(self.base[job] + 2, land, land, (p.sib, p.c))

    def finish(self):
        p = self.place
        for job in self.jobs:
            self.links.take(self.base[job] + 1, self.land(job, p.sib), (p.sib, p.c))
            self.links.take(self.base[job] + 2, self.land(job, p.opp), (p.sib, p.c))


def gelu_pair(value):
    rate = 0.7978845608028654
    square = value * value
    bent = jnp.tanh(rate * value * (1.0 + 0.044715 * square))
    half = 0.5 * (1.0 + bent)
    slope = half + 0.5 * value * (1.0 - bent * bent) * (rate * (1.0 + 0.134145 * square))
    return value * half, slope


def row_positions(table_ref, owner, half):
    place = lax.broadcasted_iota(jnp.int32, (2 * half, 1), 0)
    pair = table_ref[pl.ds(owner, 1)]
    first, second = pair[:, 0:1] * half, pair[:, 1:2] * half - half
    return place + jnp.where(place < half, first, second)


def column_positions(table_ref, owner, half):
    place = lax.broadcasted_iota(jnp.int32, (1, 2 * half), 1)
    pair = table_ref[pl.ds(owner, 1)]
    first, second = pair[:, 0:1] * half, pair[:, 1:2] * half - half
    return place + jnp.where(place < half, first, second)


def softmax_rows(scores):
    top = jnp.max(scores, axis=-1, keepdims=True)
    expos = jnp.exp(scores - top)
    return expos * (1.0 / jnp.sum(expos, axis=-1, keepdims=True)), top


def softmax_columns(scores):
    expos = jnp.exp(scores - jnp.max(scores, axis=0, keepdims=True))
    return expos * (1.0 / jnp.sum(expos, axis=0, keepdims=True))


PIECES = 2
STEPS = 8


def forward_kernel(
    table_ref,
    target_ref,
    source_ref,
    tokens_ref,
    encoder_ref,
    cotangent_ref,
    qkv_ref,
    out_ref,
    cq_ref,
    ckv_ref,
    co_ref,
    up_ref,
    down_ref,
    gain_ref,
    bias_ref,
    first_out,
    second_out,
    third_out,
    branch_out,
    source_out,
    w_qkv_out,
    w_cq_out,
    w_ckv_out,
    hidden_out,
    slopes_out,
    grad_third_out,
    third_part_out,
    heads_out,
    mix_out,
    query_out,
    kvs_out,
    cross_out_ref,
    sums_out,
    peak_out,
    lens_out,
    first,
    second,
    third,
    branch,
    source,
    w_qkv,
    w_cq,
    w_ckv,
    sent,
    heads,
    mix_own,
    mix,
    query,
    kv_own,
    kvs,
    cross,
    sums,
    columns,
    lens,
    rs_out,
    rs_in,
    part,
    w_up,
    w_down,
    hidden,
    slopes,
    grad_third,
    third_part,
    send_sem,
    recv_sem,
    local_sem,
):
    place, links = Place(), Links(send_sem, recv_sem, local_sem)
    p = place
    rows = tokens_ref.shape[1]
    source_rows = encoder_ref.shape[1]
    half = rows // 2
    width = w_cq.shape[1]
    pair_width = heads.shape[2]
    held = width // HD
    groups = width // pair_width
    place.greet()
    own = rows_at(p.s * rows, rows)
    inputs = tokens_ref[0].astype(F32)
    first[own] = norm_forward(inputs, gain_ref[0:1], bias_ref[0:1])[2]
    place.meet()

    get_qkv = Columns(links, place, qkv_ref, w_qkv, 3)
    get_qkv.start()
    get_first = Gather(links, (p.seq,), first, rows)
    get_first.start()
    source[rows_at(p.s * source_rows, source_rows)] = encoder_ref[0]
    get_source = Gather(links, (p.seq,), source, source_rows)
    get_source.start()
    place_lens = links.slots(3)
    line = lax.broadcasted_iota(jnp.int32, (8, 128), 0)
    lens[pl.ds(p.s, 1)] = jnp.where(line < 4, target_ref[0], source_ref[0])[None]
    own_lens = lens.at[pl.ds(p.s, 1)]
    for step, other in enumerate((p.far, p.opp, p.sib)):
        links.push(place_lens + step, own_lens, own_lens, (other, p.c))
    for owner in range(STEPS):
        columns[:, owner * rows : (owner + 1) * rows] = column_positions(table_ref, owner, half)
    own_rows = row_positions(table_ref, p.c, half)
    valid = own_rows < target_ref[0]
    own_flat = p.flat.own * rows
    branch[rows_at(own_flat, rows)] = jnp.where(valid, cotangent_ref[0].astype(F32), 0.0).astype(BF16)
    get_cq = Columns(links, place, cq_ref, w_cq, 1)
    get_ckv = Columns(links, place, ckv_ref, w_ckv, 2)
    get_up = Shared(links, place, up_ref, w_up, 4)
    flat = (p.flat, p.flat.turned())

    get_qkv.relay()
    get_first.forward()
    get_source.forward()
    get_first.finish()
    get_source.finish()
    for made in links.saves:
        made.wait()
    links.saves = []
    get_qkv.finish()
    links.save(first, first_out)
    links.save(w_qkv, w_qkv_out)
    links.save(source, source_out)
    for step, other in enumerate((p.far, p.opp, p.sib)):
        links.take(place_lens + step, lens.at[pl.ds(other, 1)], (other, p.c))
    links.save(lens, lens_out)

    def project(block, carry):
        value = dot(first[rows_at(block * rows, rows)], w_qkv[...]).astype(BF16)
        for group in range(groups):
            for part in range(3):
                at = part * width + group * pair_width
                sent[block * groups + group, part] = value[:, at : at + pair_width]
        return carry

    lax.fori_loop(0, 4, project, 0)
    a2a = links.slots(STEPS)
    mine = rows_at(p.c * rows, rows)
    for step in range(1, STEPS):
        other = lax.rem(p.c + step, STEPS)
        links.push(a2a + step, sent.at[other], heads.at[:, mine], (p.s, other))
    keep = pltpu.make_async_copy(sent.at[p.c], heads.at[:, mine], local_sem.at[STEPS * 8 - 1])
    keep.start()
    get_cq.start()
    get_ckv.start()
    get_up.start((0, 1))
    keeps = p.k == p.low
    get_down = links.slots(1)
    links.push(get_down, down_ref, w_down, (p.sib, p.c), keeps)
    own_down = pltpu.make_async_copy(down_ref, w_down, local_sem.at[STEPS * 8 - 2])
    pl.when(keeps)(own_down.start)
    get_branch = Gather(links, flat, branch, rows)
    get_branch.start_all()
    keep.wait()
    get_cq.relay()
    get_ckv.relay()
    for step in range(1, STEPS):
        other = lax.rem(p.c + STEPS - step, STEPS)
        links.take(a2a + step, heads.at[:, rows_at(other * rows, rows)], (p.s, other))
    links.save(heads, heads_out)

    my_slot = lax.div(p.c, groups)
    my_group = lax.rem(p.c, groups)
    length = lens[pl.ds(my_slot, 1)][0, 0:1, 0:1]
    back = links.slots(STEPS)
    slot_rows = rows_at(my_slot * rows, rows)
    group_lanes = lanes_at(my_group * pair_width, pair_width)

    def back_copy(owner):
        return links.copy(
            back + p.c, mix_own.at[rows_at(owner * rows, rows)], mix.at[slot_rows, group_lanes], (p.s, owner)
        )

    columns[...] = jnp.where(columns[...] < length, columns[...], STEPS * rows)

    def attend(block, peaks):
        at = rows_at(block * 2 * rows, 2 * rows)
        row_pos = jnp.concatenate(
            [row_positions(table_ref, 2 * block, half), row_positions(table_ref, 2 * block + 1, half)], axis=0
        )
        allowed = columns[...] <= row_pos
        ok = row_pos < length
        tops = []
        for head in range(pair_width // HD):
            cut = slice(head * HD, (head + 1) * HD)
            scores = dot(heads[0, at, cut], heads[1, :, cut], NT) * SCALE
            probs, top = softmax_rows(jnp.where(allowed, scores, masked_score))
            mix_own[at, cut] = dot(probs.astype(BF16), heads[2, :, cut]).astype(BF16)
            peak = jnp.max(jnp.where(ok, top, masked_score), axis=0, keepdims=True)
            tops.append(jnp.maximum(peaks[head], peak))
        return tuple(tops)

    low = jnp.full((1, 1), masked_score, F32)
    peaks = (low, low)
    for block in range(STEPS // 2):
        peaks = attend(block, peaks)
        for owner in (2 * block, 2 * block + 1):
            pl.when(p.c != owner)(back_copy(owner).start)
    for head in range(2):
        peak_out[head : head + 1] = jnp.broadcast_to(peaks[head], (1, 128))
    mix[slot_rows, group_lanes] = mix_own[mine]

    get_cq.finish()
    get_ckv.finish()
    for made in links.saves:
        made.wait()
    links.saves = []
    links.save(w_cq, w_cq_out)
    links.save(w_ckv, w_ckv_out)
    value = dot(source[...], w_ckv[...]).astype(BF16)
    for slot in range(4):
        kv_own[slot] = value[slot * source_rows : (slot + 1) * source_rows]
    own_keys = rows_at(p.c * source_rows, source_rows)
    kvs[:, own_keys] = kv_own[...]
    along, across = links.slots(4), links.slots(4)
    links.push(across, kv_own, kvs.at[:, own_keys], (p.s, p.pair))
    for step in range(1, 4):
        other = lax.rem(p.z + step, 4) * 2 + p.y
        links.push(along + step, kv_own, kvs.at[:, own_keys], (p.s, other))
    get_up.forward((0, 1))
    get_branch.forward_all()

    for owner in range(STEPS):

        @pl.when(p.c != owner)
        def _():
            lane = lanes_at((owner % groups) * pair_width, pair_width)
            links.take(
                back + owner, mix.at[pl.ds((owner // groups) * rows, rows), lane], (p.s, owner)
            )

    links.save(mix, mix_out)

    def boundary(index, left, weight, base, gather, start):
        step = rows // PIECES

        def tile(number, carry):
            lanes = lanes_at(number * 256, 256)
            part[:, lanes] = dot(left[...], weight[:, lanes]).astype(BF16)
            return carry

        lax.fori_loop(0, part.shape[1] // 256, tile, 0)

        def then(piece, total):
            cut = pl.ds(piece * step, step)
            value = base(piece) + total
            sums[index, cut] = value
            gather.dest[rows_at(start + piece * step, step)] = norm_forward(
                value, gain_ref[index + 1 : index + 2], bias_ref[index + 1 : index + 2]
            )[2]
            gather.start(piece)

        Reduce(
            links,
            (p.seq,) * PIECES,
            rs_out.at[index],
            rs_in.at[index],
            rows,
            lambda block, piece: part[rows_at(block * rows + piece * step, step)],
        ).run(then)

    step = rows // PIECES
    get_second = Gather(links, (p.seq,) * PIECES, second, rows)
    boundary(
        0,
        mix,
        out_ref,
        lambda piece: tokens_ref[0, piece * step : (piece + 1) * step].astype(F32),
        get_second,
        p.s * rows,
    )
    for hop in range(1, 4):
        other = lax.rem(p.z + 4 - hop, 4) * 2 + p.y
        land = kvs.at[:, rows_at(other * source_rows, source_rows)]
        links.take(along + hop, land, (p.s, other))
        links.push(across + hop, land, land, (p.s, p.pair))
    get_up.start((2, 3))
    get_second.forward_all()
    get_second.finish_all()
    links.save(second, second_out)
    for hop in range(4):
        other = lax.rem(p.z + 4 - hop, 4) * 2 + 1 - p.y
        land = kvs.at[:, rows_at(other * source_rows, source_rows)]
        links.take(across + hop, land, (p.s, p.pair))
    links.save(kvs, kvs_out)

    keys = kvs.shape[1]

    def cross_attend(slot, peaks):
        at = rows_at(slot * rows, rows)
        asked = dot(second[at], w_cq[...]).astype(BF16)
        query[at] = asked
        limits = lens[pl.ds(slot, 1)]
        live = lax.broadcasted_iota(jnp.int32, (1, keys), 1) < limits[0, 4:5, 0:1]
        ok = own_rows < limits[0, 0:1, 0:1]
        tops = []
        for head in range(held):
            cut = slice(head * HD, (head + 1) * HD)
            vcut = slice(width + head * HD, width + (head + 1) * HD)
            scores = dot(asked[:, cut], kvs[slot, :, cut], NT) * SCALE
            probs, top = softmax_rows(jnp.where(live, scores, masked_score))
            cross[at, cut] = dot(probs.astype(BF16), kvs[slot, :, vcut]).astype(BF16)
            peak = jnp.max(jnp.where(ok, top, masked_score), axis=0, keepdims=True)
            tops.append(jnp.maximum(peaks[head], peak))
        return tuple(tops)

    peaks = lax.fori_loop(0, 4, cross_attend, (low,) * held)
    for head in range(held):
        peak_out[2 + head : 3 + head] = jnp.broadcast_to(peaks[head], (1, 128))
    links.save(query, query_out)
    links.save(cross, cross_out_ref)
    get_up.forward((2, 3))
    get_branch.finish_all()
    links.save(branch, branch_out)
    get_third = Gather(links, flat, third, rows)
    boundary(
        1,
        cross,
        co_ref,
        lambda piece: sums[0, piece * step : (piece + 1) * step],
        get_third,
        own_flat,
    )
    links.save(sums, sums_out)
    get_third.forward_all()
    get_up.finish()
    for made in links.saves:
        made.wait()
    links.saves = []
    pl.when(keeps)(own_down.wait)
    links.take(get_down, w_down, (p.sib, p.c), p.k != p.low)
    get_third.finish_all()
    links.save(third, third_out)

    def units(number, carry):
        lanes = lanes_at(number * 256, 256)
        value, slope = gelu_pair(dot(third[...], w_up[:, lanes]))
        hidden[:, lanes] = value.astype(BF16)
        grad = dot(branch[...], w_down[rows_at(number * 256, 256)], NT)
        slopes[:, lanes] = (grad * slope).astype(BF16)
        return carry

    lax.fori_loop(0, w_up.shape[1] // 256, units, 0, unroll=2)
    links.save(hidden, hidden_out)
    links.save(slopes, slopes_out)

    def back_rows(number, carry):
        lanes = lanes_at(number * 256, 256)
        grad_third[:, lanes] = dot(slopes[...], w_up[rows_at(number * 256, 256)], NT).astype(BF16)
        third_part[:, lanes] = dot(hidden[...], w_down[:, lanes]).astype(BF16)
        return carry

    lax.fori_loop(0, third.shape[1] // 256, back_rows, 0, unroll=2)
    links.save(grad_third, grad_third_out)
    links.save(third_part, third_part_out)
    for owner in range(STEPS):
        pl.when(p.c != owner)(back_copy(owner).wait_send)
    links.finish()


def forward_call(
    table, targets, sources, tokens, encoder, cotangent, qkv, out, cq, ckv, co, up, down, gain, bias
):
    rows, width = tokens.shape[1], out.shape[0]
    source_rows = encoder.shape[1]
    depth = tokens.shape[2]
    keys = 8 * source_rows
    any_space = pl.BlockSpec(memory_space=pl.ANY)
    vmem = pl.BlockSpec(memory_space=pltpu.VMEM)
    smem = pl.BlockSpec(memory_space=pltpu.SMEM)
    shapes = dict(
        first=((4 * rows, depth), BF16),
        second=((4 * rows, depth), BF16),
        third=((4 * rows, depth), BF16),
        branch=((4 * rows, depth), BF16),
        source=((4 * source_rows, depth), BF16),
        w_qkv=((depth, 3 * width), BF16),
        w_cq=((depth, width), BF16),
        w_ckv=((depth, 2 * width), BF16),
        hidden=((4 * rows, up.shape[1] // 4), BF16),
        slopes=((4 * rows, up.shape[1] // 4), BF16),
        grad_third=((4 * rows, depth), BF16),
        third_part=((4 * rows, depth), BF16),
        heads=((3, 8 * rows, 128), BF16),
        mix=((4 * rows, width), BF16),
        query=((4 * rows, width), BF16),
        kvs=((4, keys, 2 * width), BF16),
        cross=((4 * rows, width), BF16),
        sums=((2, rows, depth), F32),
        peak=((8, 128), F32),
        lens=((4, 8, 128), jnp.int32),
    )
    scratch = [
        shapes[name]
        for name in ("first", "second", "third", "branch", "source", "w_qkv", "w_cq", "w_ckv")
    ] + [
        ((8, 3, rows, 128), BF16),
        shapes["heads"],
        ((8 * rows, 128), BF16),
        shapes["mix"],
        shapes["query"],
        ((4, source_rows, 2 * width), BF16),
        shapes["kvs"],
        shapes["cross"],
        shapes["sums"],
        ((1, 8 * rows), jnp.int32),
        shapes["lens"],
        ((2, 3, rows, depth), BF16),
        ((2, 3, rows, depth), BF16),
        ((4 * rows, depth), BF16),
        ((depth, up.shape[1] // 4), BF16),
        (down.shape, BF16),
        shapes["hidden"],
        shapes["slopes"],
        shapes["grad_third"],
        shapes["third_part"],
    ]
    made = pl.pallas_call(
        forward_kernel,
        in_specs=[vmem] + [smem] * 2
        + [vmem] * 3
        + [any_space, vmem, any_space, any_space, vmem, any_space, any_space]
        + [vmem] * 2,
        out_specs=[vmem if name == "peak" else any_space for name in shapes],
        out_shape=[jax.ShapeDtypeStruct(*shape) for shape in shapes.values()],
        scratch_shapes=[pltpu.VMEM(*shape) for shape in scratch]
        + [
            pltpu.SemaphoreType.DMA((128,)),
            pltpu.SemaphoreType.DMA((128,)),
            pltpu.SemaphoreType.DMA((64,)),
        ],
        compiler_params=pltpu.CompilerParams(
            collective_id=0, has_side_effects=True, vmem_limit_bytes=61 * 2**20
        ),
        name="forward",
    )(table, targets, sources, tokens, encoder, cotangent, qkv, out, cq, ckv, co, up, down, gain, bias)
    return dict(zip(shapes, made))


class Sum:
    def __init__(self, links, place, full, into, away, result, lead=False):
        self.links, self.place, self.full = links, place, full
        self.half = place.y
        self.other = (place.s, place.pair)
        self.into, self.away, self.result, self.lead = into, away, result, lead
        self.base = links.slots(7)
        self.near = place.z + 1 - 2 * lax.rem(place.z, 2)
        self.across = lax.rem(place.z + 2, 4)
        self.order = (lax.rem(self.near + 2, 4), self.across, self.near, place.z)

    def start(self, turns=(0, 1, 2, 3)):
        for turn in turns:
            to = self.order[turn]
            give = 1 - self.half
            src = self.full.at[to, give] if self.lead else self.full.at[:, to, give]
            self.links.push(self.base + turn, src, self.into.at[to], self.other)

    def turn(self, turns=(0, 1, 2, 3)):
        p, links, into, away = self.place, self.links, self.into, self.away
        for turn in turns:
            to = self.order[turn]
            links.take(self.base + turn, into.at[to], self.other)
            if turn == 1:
                links.take(self.base + 4, away.at[0], (p.s, self.near * 2 + p.y))

            def add(a, carry):
                mine = self.full[to, self.half, a] if self.lead else self.full[a, to, self.half]
                total = mine.astype(F32) + into[to, a].astype(F32)
                if turn == 1:
                    total = total + away[0, a].astype(F32)
                into[to, a] = total.astype(BF16)
                return carry

            if turn < 3:
                lax.fori_loop(0, into.shape[1], add, 0)
                goal = self.across if turn == 1 else self.near
                links.push(
                    self.base + 4 + turn, into.at[to], away.at[turn], (p.s, goal * 2 + p.y)
                )

    def finish(self):
        p, links, into, away = self.place, self.links, self.into, self.away
        links.take(self.base + 5, away.at[1], (p.s, self.across * 2 + p.y))
        links.take(self.base + 6, away.at[2], (p.s, self.near * 2 + p.y))

        def add(a, carry):
            mine = self.full[p.z, self.half, a] if self.lead else self.full[a, p.z, self.half]
            total = mine.astype(F32) + into[p.z, a].astype(F32)
            total = total + (away[1, a].astype(F32) + away[2, a].astype(F32))
            self.result[a] = total.astype(BF16)
            return carry

        lax.fori_loop(0, into.shape[1], add, 0)


class SumChip:
    def __init__(self, links, place, full, into, along, away, result):
        self.links, self.place, self.full, self.into = links, place, full, into
        self.along, self.away, self.result = along, away, result
        self.base = links.slots(7)
        self.high = (1 - place.high, place.high)

    def start(self):
        p = self.place
        for turn in range(4):
            high, y = self.high[turn // 2], (1 - p.y, p.y)[turn % 2]
            src, dst = self.full.at[high, y, 1 - p.k], self.into.at[high, y]
            self.links.push(self.base + turn, src, dst, (p.sib, p.c))

    def total(self, turn, extra, store):
        p, full, into = self.place, self.full, self.into
        high, y = self.high[turn // 2], (1 - p.y, p.y)[turn % 2]
        self.links.take(self.base + turn, into.at[high, y], (p.sib, p.c))

        def add(a, carry):
            value = full[high, y, p.k, a].astype(F32) + into[high, y, a].astype(F32)
            for part in extra:
                value = value + part[a].astype(F32)
            store[a] = value.astype(BF16)
            return carry

        lax.fori_loop(0, into.shape[2], add, 0)

    def across_y(self):
        p = self.place
        for step in range(2):
            held = self.into.at[self.high[step], 1 - p.y]
            self.total(2 * step, (), held)
            self.links.push(self.base + 4 + step, held, self.along.at[step], (p.s, p.pair))

    def across_z(self):
        p = self.place
        self.links.take(self.base + 4, self.along.at[0], (p.s, p.pair))
        held = self.into.at[self.high[0], p.y]
        self.total(1, (self.along.at[0],), held)
        self.links.push(self.base + 6, held, self.away, (p.s, p.over))

    def finish(self):
        p = self.place
        self.links.take(self.base + 5, self.along.at[1], (p.s, p.pair))
        self.links.take(self.base + 6, self.away, (p.s, p.over))
        self.total(3, (self.along.at[1], self.away), self.result)


class Exchange:
    def __init__(self, links, team, result, taken):
        self.links, self.team, self.result, self.taken = links, team, result, taken
        self.base = links.slots(3)
        self.others = (team.far, team.opp, team.near)

    def start(self):
        own = pl.ds(self.team.own, 1)
        for step, (device, index) in enumerate(self.others):
            src = self.result.at[pl.ds(index, 1)]
            self.links.push(self.base + step, src, self.taken.at[own], device)
        self.taken[own] = self.result[own]

    def finish(self):
        for step, (device, index) in enumerate(self.others):
            self.links.take(self.base + step, self.taken.at[pl.ds(index, 1)], device)


def norm_terms_of(values):
    centered = values - jnp.mean(values, axis=-1, keepdims=True)
    spread = jnp.mean(centered * centered, axis=-1, keepdims=True)
    inverse = lax.rsqrt(spread + norm_eps)
    return centered * inverse, inverse


def backward_body(r):
    place, links = Place(), Links(r.send_sem, r.recv_sem, r.local_sem)
    p = place
    rows = r.tokens.shape[1]
    half = rows // 2
    width = r.w_cq.shape[1]
    source_rows = r.source.shape[0] // 4
    keys = r.kvs.shape[1]
    pair_width = r.heads.shape[2]
    held, groups = width // HD, width // pair_width
    depth = r.tokens.shape[2]
    step = rows // PIECES
    share = depth // 4

    loads = {}

    def load(names):
        for name in names:
            at = r.load_sem.at[r.loaded.index(name)]
            loads[name] = pltpu.make_async_copy(getattr(r, name + "_hbm"), getattr(r, name), at)
            loads[name].start()

    r.part, r.third_part = r.hidden.at[:, :depth], r.hidden.at[:, depth : 2 * depth]
    r.second, r.first = r.slopes.at[:, :depth], r.slopes.at[:, depth : 2 * depth]
    soon = ("hidden", "branch", "third", "slopes", "sums")
    late = ("third_part", "second", "first")
    load(soon)

    def need(*wanted):
        for name in wanted:
            loads.pop(name).wait()

    place.greet()
    place.meet()
    r.peaks_ctx[pl.ds(p.c, 1)] = r.peak[...][None]
    peak_base = links.slots(STEPS)
    own_peak = r.peaks_ctx.at[pl.ds(p.c, 1)]
    for hop in range(1, STEPS):
        links.push(peak_base + hop, own_peak, own_peak, (p.s, lax.rem(p.c + hop, STEPS)))

    own_rows = row_positions(r.table, p.c, half)
    r.norms[...] = jnp.zeros_like(r.norms)

    def add_norms(index, gain, bias):
        r.norms[index : index + 1] += gain[None]
        r.norms[index + 3 : index + 4] += bias[None]

    get_cross = Gather(links, (p.seq,) * PIECES, r.cross_branch, rows)

    def after_third(piece, total):
        cut = slice(piece * step, (piece + 1) * step)
        hat, inverse = norm_terms_of(r.sums[1, cut])
        back, gain, bias = norm_backward(total, hat, inverse, r.gain[2:3])
        add_norms(2, gain, bias)
        valid = own_rows[cut] < r.target[0]
        value = jnp.where(valid, r.cotangent[0, cut].astype(F32), 0.0) + back
        r.grad_sum[cut] = value
        r.cross_branch[rows_at(p.s * rows + piece * step, step)] = value.astype(BF16)
        get_cross.start(piece)

    def stored(ref):
        return lambda block, piece: ref[rows_at(block * rows + piece * step, step)].astype(F32)

    flat = (p.flat, p.flat.turned())
    sum_third = Reduce(
        links, flat, r.rs_out.at[0], r.rs_in.at[0], rows, stored(r.grad_third)
    )
    sum_third.first()

    def down_grad(block, carry):
        value = dot(r.hidden[:, lanes_at(block * 256, 256)], r.branch[...], TN).astype(BF16)
        place_of = (lax.div(block, 4), lax.rem(block, 2), lax.rem(lax.div(block, 2), 2))
        r.down_full[place_of] = value.reshape(r.down_full.shape[3:])
        return carry

    need("hidden", "branch")
    lax.fori_loop(0, 3, down_grad, 0)
    sum_third.second()
    load([name for name in r.loaded if name not in soon + late])
    lax.fori_loop(3, 8, down_grad, 0)
    down = SumChip(
        links, place, r.down_full, r.down_into, r.down_along, r.down_away, r.down_result
    )
    down.start()
    need("third", "slopes")

    def up_grad(number, carry):
        block, side = lax.div(number, 2), lax.rem(number, 2)
        lanes = lanes_at(side * depth, depth)
        left = r.third[:, lanes_at(block * share, share)]
        value = dot(left, r.slopes[:, lanes], TN).astype(BF16)
        value = value.reshape(2, 2, 2, share // 8, depth)
        for low in range(2):
            at = lax.div(block, 2) * 2 + low
            r.up_full[:, :, lax.rem(block, 2), at, :, lanes] = value[:, low]
        return carry

    lax.fori_loop(0, 8, up_grad, 0)
    load(late)
    down.across_y()
    up = SumChip(links, place, r.up_full, r.up_into, r.up_along, r.up_away, r.up_result)
    up.start()
    up.across_y()
    need("sums")
    sum_third.last(after_third)
    for hop in range(1, STEPS):
        other = lax.rem(p.c + STEPS - hop, STEPS)
        links.take(peak_base + hop, r.peaks_ctx.at[pl.ds(other, 1)], (p.s, other))
    best = []
    for group in range(groups):
        tile = r.peaks_ctx[group]
        for owner in range(group + groups, STEPS, groups):
            tile = jnp.maximum(tile, r.peaks_ctx[owner])
        best.append(tile)
    everyone = best[0]
    for tile in best[1:]:
        everyone = jnp.maximum(everyone, tile)
    mine = jnp.concatenate([tile[0:2] for tile in best] + [everyone[2 : 2 + held]], axis=0)
    r.peaks_seq[pl.ds(p.s, 1)] = mine[None]
    peak_seq = links.slots(3)
    own_peak = r.peaks_seq.at[pl.ds(p.s, 1)]
    for hop, other in enumerate((p.far, p.opp, p.sib)):
        links.push(peak_seq + hop, own_peak, own_peak, (other, p.c))

    get_cross.forward_all()
    down.across_z()
    need("w_co", "cross", "query", "kvs", "w_cq", "second")
    get_cross.finish_all()

    def cross_back(slot, carry):
        at = rows_at(slot * rows, rows)
        grad_rows = dot(r.cross_branch[at], r.w_co[...], NT).astype(BF16)
        live = lax.broadcasted_iota(jnp.int32, (keys, 1), 0) < r.lens[pl.ds(slot, 1)][0, 4:5, 0:1]
        for head in range(held):
            cut = slice(head * HD, (head + 1) * HD)
            vcut = slice(width + head * HD, width + (head + 1) * HD)
            asked, grad = r.query[at, cut], grad_rows[:, cut]
            key = r.kvs[slot, :, cut]
            scores = dot(key, asked, NT) * SCALE
            probs = softmax_columns(jnp.where(live, scores, masked_score))
            dprobs = dot(r.kvs[slot, :, vcut], grad, NT)
            delta = jnp.sum(probs * dprobs, axis=0, keepdims=True)
            dscores = (probs * (dprobs - delta)).astype(BF16)
            r.dquery[at, cut] = (dot(dscores, key, TN) * SCALE).astype(BF16)
            shape = (4, 2, source_rows, HD)
            r.dkv_full[slot, :, :, :, cut] = (
                (dot(dscores, asked) * SCALE).astype(BF16).reshape(shape)
            )
            r.dkv_full[slot, :, :, :, vcut] = (
                dot(probs.astype(BF16), grad).astype(BF16).reshape(shape)
            )
        return carry

    lax.fori_loop(0, 4, cross_back, 0)
    dkv = Sum(links, place, r.dkv_full, r.dkv_into, r.dkv_away, r.dkv_result)
    need("third_part")
    sum_output = Reduce(
        links, flat, r.rs_out.at[2], r.rs_in.at[2], rows, stored(r.third_part)
    )
    sum_output.first()

    get_self = Gather(links, (p.seq,) * PIECES, r.self_branch, rows)

    def after_second(piece, total):
        cut = slice(piece * step, (piece + 1) * step)
        hat, inverse = norm_terms_of(r.sums[0, cut])
        back, gain, bias = norm_backward(total, hat, inverse, r.gain[1:2])
        add_norms(1, gain, bias)
        value = r.grad_sum[cut] + back
        r.grad_sum[cut] = value
        r.self_branch[rows_at(p.s * rows + piece * step, step)] = value.astype(BF16)
        get_self.start(piece)

    def cross_rows(number, carry):
        lanes = lanes_at(number * 256, 256)
        r.part[:, lanes] = dot(r.dquery[...], r.w_cq[rows_at(number * 256, 256)], NT).astype(BF16)
        return carry

    lax.fori_loop(0, depth // 256, cross_rows, 0)
    Reduce(
        links, (p.seq,) * PIECES, r.rs_out.at[1], r.rs_in.at[1], rows, stored(r.part)
    ).run(after_second)

    def row_grad(left, right, full):
        def one(part, carry):
            lanes = lanes_at(part * 128, 128)
            value = dot(left[:, lanes], right[...], TN).astype(BF16)
            full[pl.ds(part * 2, 2)] = value.reshape((2, 2) + full.shape[2:])
            return carry

        lax.fori_loop(0, left.shape[1] // 128, one, 0)

    def column_grad(left, right, full):
        def one(block, carry):
            lanes = lanes_at(block * share, share)
            value = dot(left[:, lanes], right(), TN).astype(BF16)
            full[pl.ds(block, 1)] = value.reshape((1,) + full.shape[1:])
            return carry

        lax.fori_loop(0, 4, one, 0)

    row_grad(r.cross, r.cross_branch, r.co_full)
    get_self.forward_all()
    column_grad(r.second, lambda: r.dquery[...], r.cq_full)
    get_self.finish_all()

    need("w_out", "heads", "mix")

    def mix_back(slot, carry):
        value = dot(r.self_branch[rows_at(slot * rows, rows)], r.w_out[...], NT).astype(BF16)
        for group in range(groups):
            r.gsent[slot * groups + group] = value[:, group * pair_width : (group + 1) * pair_width]
        return carry

    lax.fori_loop(0, 4, mix_back, 0)
    a2a = links.slots(STEPS)
    mine_rows = rows_at(p.c * rows, rows)
    for hop in range(1, STEPS):
        other = lax.rem(p.c + hop, STEPS)
        links.push(a2a + hop, r.gsent.at[other], r.gheads.at[mine_rows], (p.s, other))
    r.gheads[mine_rows] = r.gsent[p.c]
    my_slot, my_group = lax.div(p.c, groups), lax.rem(p.c, groups)
    length = r.lens[pl.ds(my_slot, 1)][0, 0:1, 0:1]
    for owner in range(STEPS):
        pos = row_positions(r.table, owner, half)
        pos = jnp.where(pos < length, pos, STEPS * rows)
        r.key_pos[owner * rows : (owner + 1) * rows] = jnp.broadcast_to(pos, (rows, 128))
    co = Sum(links, place, r.co_full, r.co_into, r.co_away, r.co_result, True)
    cq = Sum(links, place, r.cq_full, r.cq_into, r.cq_away, r.cq_result)
    so = Sum(links, place, r.so_full, r.so_into, r.so_away, r.so_result, True)
    row_grad(r.mix, r.self_branch, r.so_full)
    for job in (dkv, cq, co, so):
        job.start()
    sum_output.second()
    up.across_z()
    for hop in range(1, STEPS):
        other = lax.rem(p.c + STEPS - hop, STEPS)
        links.take(a2a + hop, r.gheads.at[rows_at(other * rows, rows)], (p.s, other))

    slot_rows = rows_at(my_slot * rows, rows)
    group_lanes = lanes_at(my_group * pair_width, pair_width)
    back_q, back_kv = links.slots(STEPS), links.slots(STEPS)

    def q_copy(owner):
        at = rows_at(owner * rows, rows)
        return links.copy(
            back_q + p.c, r.dq_own.at[at], r.dproj.at[0, slot_rows, group_lanes], (p.s, owner)
        )

    def kv_copy(owner):
        at = rows_at(owner * rows, rows)
        return links.copy(
            back_kv + p.c,
            r.dkv_own.at[:, at],
            r.dproj.at[pl.ds(1, 2), slot_rows, group_lanes],
            (p.s, owner),
        )

    def attend_back(block, carry):
        at = rows_at(block * 2 * rows, 2 * rows)
        asked_pos = jnp.concatenate(
            [
                column_positions(r.table, 2 * block, half),
                column_positions(r.table, 2 * block + 1, half),
            ],
            axis=1,
        )
        key_pos = r.key_pos[...]
        allowed = jnp.concatenate([key_pos] * (2 * rows // 128), axis=1) <= asked_pos
        for head in range(pair_width // HD):
            cut = slice(head * HD, (head + 1) * HD)
            asked, grad = r.heads[0, at, cut], r.gheads[at, cut]
            key = r.heads[1, :, cut]
            scores = dot(key, asked, NT) * SCALE
            probs = softmax_columns(jnp.where(allowed, scores, masked_score))
            dprobs = dot(r.heads[2, :, cut], grad, NT)
            delta = jnp.sum(probs * dprobs, axis=0, keepdims=True)
            dscores = (probs * (dprobs - delta)).astype(BF16)
            r.dq_own[at, cut] = (dot(dscores, key, TN) * SCALE).astype(BF16)
            if block == 0:
                r.acc[0, :, cut] = dot(dscores, asked)
                r.acc[1, :, cut] = dot(probs.astype(BF16), grad)
            else:
                r.acc[0, :, cut] += dot(dscores, asked)
                r.acc[1, :, cut] += dot(probs.astype(BF16), grad)
        return carry

    for block in range(STEPS // 2):
        attend_back(block, 0)
        for owner in (2 * block, 2 * block + 1):
            pl.when(p.c != owner)(q_copy(owner).start)
    for owner in range(STEPS):
        at = rows_at(owner * rows, rows)
        r.dkv_own[0, at] = (r.acc[0, at] * SCALE).astype(BF16)
        r.dkv_own[1, at] = r.acc[1, at].astype(BF16)
        pl.when(p.c != owner)(kv_copy(owner).start)
    r.dproj[0, slot_rows, group_lanes] = r.dq_own[mine_rows]
    r.dproj[pl.ds(1, 2), slot_rows, group_lanes] = r.dkv_own[:, mine_rows]

    dkv.turn((0, 2))
    cq.turn((0, 2))
    def after_output(piece, total):
        cut = slice(piece * step, (piece + 1) * step)
        valid = own_rows[cut] < r.target[0]
        r.output[cut] = jnp.where(valid, r.sums[1, cut] + total, 0.0).astype(BF16)

    sum_output.last(after_output)
    dkv.turn((1, 3))
    cq.turn((1, 3))
    for job in (co, so):
        job.turn((0, 2))
    need("w_ckv", "source")
    dkv.finish()
    r.dsource[...] = r.dkv_result[...].reshape(4 * source_rows, 2 * width)
    column_grad(r.source, lambda: r.dsource[...], r.ckv_full)
    ckv = Sum(links, place, r.ckv_full, r.ckv_into, r.ckv_away, r.ckv_result)
    ckv.start()

    def source_partial(block, piece):
        return dot(r.dsource[rows_at(block * source_rows, source_rows)], r.w_ckv[...], NT)

    def after_encoder(piece, total):
        r.grad_source[...] = total

    Reduce(links, (p.seq,), r.enc_out, r.enc_in, source_rows, source_partial).run(after_encoder)

    need("w_qkv", "first")
    for owner in range(STEPS):

        @pl.when(p.c != owner)
        def _():
            at = pl.ds((owner // groups) * rows, rows)
            lane = lanes_at((owner % groups) * pair_width, pair_width)
            links.take(back_q + owner, r.dproj.at[0, at, lane], (p.s, owner))
            links.take(back_kv + owner, r.dproj.at[pl.ds(1, 2), at, lane], (p.s, owner))

    def first_rows(number, carry):
        at = rows_at(number * 256, 256)
        total = dot(r.dproj[0], r.w_qkv[at, :width], NT)
        total += dot(r.dproj[1], r.w_qkv[at, width : 2 * width], NT)
        total += dot(r.dproj[2], r.w_qkv[at, 2 * width :], NT)
        r.part[:, lanes_at(number * 256, 256)] = total.astype(BF16)
        return carry

    lax.fori_loop(0, depth // 256, first_rows, 0)

    def after_first(piece, total):
        cut = slice(piece * step, (piece + 1) * step)
        hat, inverse = norm_terms_of(r.tokens[0, cut].astype(F32))
        back, gain, bias = norm_backward(total, hat, inverse, r.gain[0:1])
        add_norms(0, gain, bias)
        r.grad_inputs[cut] = r.grad_sum[cut] + back

    def qkv_grad(block, carry):
        lanes = lanes_at(block * share, share)
        left = r.first[:, lanes]
        for part in range(3):
            value = dot(left, r.dproj[part], TN).astype(BF16)
            r.qkv_full[pl.ds(block, 1), :, :, :, part * width : (part + 1) * width] = value.reshape(
                (1,) + r.qkv_full.shape[1:4] + (width,)
            )
        return carry

    lax.fori_loop(0, 4, qkv_grad, 0)
    qkv = Sum(links, place, r.qkv_full, r.qkv_into, r.qkv_away, r.qkv_result)
    qkv.start()
    sum_first = Reduce(
        links, (p.seq,) * PIECES, r.rs_out.at[3], r.rs_in.at[3], rows, stored(r.part)
    )
    sum_first.first()
    sum_first.second()
    for job in (co, so):
        job.turn((1, 3))
    ckv.turn((0, 2))
    qkv.turn((0, 2))
    sum_first.last(after_first)

    norm_seq, norm_ctx = links.slots(3), links.slots(STEPS)
    others = (p.far, p.opp, p.sib)
    for hop, other in enumerate(others):
        links.push(
            norm_seq + hop,
            r.norms.at[:, lanes_at(other * share, share)],
            r.norms_seq.at[pl.ds(p.s, 1)].at[0],
            (other, p.c),
        )
    ckv.turn((1, 3))
    total = r.norms[:, lanes_at(p.s * share, share)]
    for hop, other in enumerate(others):
        links.take(norm_seq + hop, r.norms_seq.at[pl.ds(other, 1)].at[0], (other, p.c))
        total = total + r.norms_seq[pl.ds(other, 1)][0]
    r.norms_ctx[pl.ds(p.c, 1)] = total[None]
    own_norms = r.norms_ctx.at[pl.ds(p.c, 1)]
    for hop in range(1, STEPS):
        links.push(norm_ctx + hop, own_norms, own_norms, (p.s, lax.rem(p.c + hop, STEPS)))
    qkv.turn((1, 3))
    sums = {}
    for job in (up, down):
        job.finish()
    sums["up"] = Exchange(links, p.flat, r.up_result, r.up_taken)
    sums["up"].start()
    keeps, swapped = p.k == p.low, links.slots(1)
    links.push(swapped, r.down_result, r.down_taken, (p.sib, p.beside), p.k != p.low)

    @pl.when(keeps)
    def _():
        r.down_taken[...] = r.down_result[...]

    for job in (co, so):
        job.finish()
    for name, job in (("cq", cq), ("ckv", ckv), ("qkv", qkv)):
        job.finish()
        sums[name] = Exchange(links, p.seq, getattr(r, name + "_result"), getattr(r, name + "_taken"))
        sums[name].start()
    for hop in range(1, STEPS):
        other = lax.rem(p.c + STEPS - hop, STEPS)
        links.take(norm_ctx + hop, r.norms_ctx.at[pl.ds(other, 1)], (p.s, other))
    total = r.norms_ctx[0]
    for owner in range(1, STEPS):
        total = total + r.norms_ctx[owner]
    r.norm_sum[...] = total
    for hop, other in enumerate(others):
        links.take(peak_seq + hop, r.peaks_seq.at[pl.ds(other, 1)], (other, p.c))
    for job in sums.values():
        job.finish()
    links.take(swapped, r.down_taken, (p.sib, p.beside), p.k != p.low)
    for owner in range(STEPS):
        pl.when(p.c != owner)(q_copy(owner).wait_send)
        pl.when(p.c != owner)(kv_copy(owner).wait_send)
    links.finish()


def backward_call(kept, given):
    rows, depth = given["tokens"].shape[1:]
    width = kept["w_cq"].shape[1]
    source_rows = kept["source"].shape[0] // 4
    keys = kept["kvs"].shape[1]
    share = depth // 32
    hidden = kept["hidden"].shape[1]
    any_space = pl.BlockSpec(memory_space=pl.ANY)
    vmem = pl.BlockSpec(memory_space=pltpu.VMEM)
    smem = pl.BlockSpec(memory_space=pltpu.SMEM)
    inputs = dict(
        table=(vmem, given["table"]),
        target=(smem, given["target"]),
        tokens=(vmem, given["tokens"]),
        cotangent=(vmem, given["cotangent"]),
        gain=(vmem, given["gain"]),
        peak=(vmem, kept["peak"]),
        lens=(vmem, kept["lens"]),
        grad_third=(vmem, kept["grad_third"]),
    )
    loaded = dict(
        hidden=kept["hidden"],
        branch=kept["branch"],
        third=kept["third"],
        slopes=kept["slopes"],
        third_part=kept["third_part"],
        sums=kept["sums"],
        w_co=given["cross_out"],
        cross=kept["cross"],
        query=kept["query"],
        kvs=kept["kvs"],
        w_cq=kept["w_cq"],
        second=kept["second"],
        w_out=given["self_out"],
        heads=kept["heads"],
        mix=kept["mix"],
        w_ckv=kept["w_ckv"],
        source=kept["source"],
        w_qkv=kept["w_qkv"],
        first=kept["first"],
    )
    for name, value in loaded.items():
        inputs[name + "_hbm"] = (any_space, value)
    outs = dict(
        output=((rows, depth), BF16),
        grad_inputs=((rows, depth), F32),
        grad_source=((source_rows, depth), F32),
        down_taken=((hidden // (8 * share), share, depth), BF16),
        co_result=((1, share, depth), BF16),
        so_result=((1, share, depth), BF16),
        up_taken=((4, share, hidden), BF16),
        cq_taken=((4, share, width), BF16),
        ckv_taken=((4, share, 2 * width), BF16),
        qkv_taken=((4, share, 3 * width), BF16),
        norm_sum=((8, depth // 4), F32),
        peaks_seq=((4, 8, 128), F32),
    )
    down_blocks = hidden // (8 * share)
    scratch = {
        name: (value.shape, value.dtype)
        for name, value in loaded.items()
        if name not in ("third_part", "second", "first")
    }
    scratch |= dict(
        down_full=((2, 2, 2, down_blocks, share, depth), BF16),
        up_full=((2, 2, 2, 4, share, hidden), BF16),
        down_into=((2, 2, down_blocks, share, depth), BF16),
        down_along=((2, down_blocks, share, depth), BF16),
        down_away=((down_blocks, share, depth), BF16),
        down_result=((down_blocks, share, depth), BF16),
        up_into=((2, 2, 4, share, hidden), BF16),
        up_along=((2, 4, share, hidden), BF16),
        up_away=((4, share, hidden), BF16),
        up_result=((4, share, hidden), BF16),
        peaks_ctx=((8, 8, 128), F32),
        norms=((8, depth), F32),
        norms_seq=((4, 8, depth // 4), F32),
        norms_ctx=((8, 8, depth // 4), F32),
        cross_branch=((4 * rows, depth), BF16),
        self_branch=((4 * rows, depth), BF16),
        grad_sum=((rows, depth), F32),
        rs_out=((4, 3, rows, depth), BF16),
        rs_in=((4, 3, rows, depth), BF16),
        enc_out=((3, source_rows, depth), BF16),
        enc_in=((3, source_rows, depth), BF16),
        dquery=((4 * rows, width), BF16),
        dsource=((4 * source_rows, 2 * width), BF16),
        gsent=((8, rows, 128), BF16),
        gheads=((8 * rows, 128), BF16),
        key_pos=((8 * rows, 128), jnp.int32),
        acc=((2, 8 * rows, 128), F32),
        dq_own=((8 * rows, 128), BF16),
        dkv_own=((2, 8 * rows, 128), BF16),
        dproj=((3, 4 * rows, width), BF16),
    )
    for name in ("co", "so"):
        scratch[name + "_full"] = ((4, 2, 1, share, depth), BF16)
        scratch[name + "_into"] = ((4, 1, share, depth), BF16)
        scratch[name + "_away"] = ((3, 1, share, depth), BF16)
    for name, columns, r in (
        ("cq", width, share),
        ("ckv", 2 * width, share),
        ("qkv", 3 * width, share),
        ("dkv", 2 * width, source_rows),
    ):
        scratch[name + "_full"] = ((4, 4, 2, r, columns), BF16)
        scratch[name + "_into"] = ((4, 4, r, columns), BF16)
        scratch[name + "_away"] = ((3, 4, r, columns), BF16)
        scratch[name + "_result"] = ((4, r, columns), BF16)
    sems = dict(send_sem=224, recv_sem=224, local_sem=4, load_sem=len(loaded))
    names = list(inputs) + list(outs) + list(scratch) + list(sems)

    def kernel(*refs):
        held = dict(zip(names, refs), loaded=tuple(loaded))
        backward_body(type("Refs", (), held))

    made = pl.pallas_call(
        kernel,
        in_specs=[spec for spec, _ in inputs.values()],
        out_specs=[vmem] * len(outs),
        out_shape=[jax.ShapeDtypeStruct(*shape) for shape in outs.values()],
        scratch_shapes=[pltpu.VMEM(*shape) for shape in scratch.values()]
        + [pltpu.SemaphoreType.DMA((count,)) for count in sems.values()],
        compiler_params=pltpu.CompilerParams(
            collective_id=1, has_side_effects=True, vmem_limit_bytes=61 * 2**20
        ),
        name="backward",
    )(*[value for _, value in inputs.values()])
    return dict(zip(outs, made))


def finish_kernel(
    clip_ref,
    peaks_ref,
    norm_ref,
    qkv_w,
    cq_w,
    ckv_w,
    output_ref,
    inputs_ref,
    source_ref,
    down_ref,
    co_ref,
    so_ref,
    up_ref,
    cq_ref,
    ckv_ref,
    qkv_ref,
    output_out,
    inputs_out,
    source_out,
    qkv_out,
    so_out,
    cq_out,
    ckv_out,
    co_out,
    up_out,
    down_out,
    gain_out,
    bias_out,
    self_out,
    cross_out,
    peaks_out,
):
    output_out[0] = output_ref[...]
    inputs_out[0] = inputs_ref[...]
    source_out[0] = source_ref[...]
    share = so_out.shape[0]
    so_out[...] = so_ref[0].astype(F32)
    co_out[...] = co_ref[0].astype(F32)
    for block in range(down_ref.shape[0]):
        down_out[block * share : (block + 1) * share] = down_ref[block].astype(F32)

    def columns(out, taken, parts):
        whole, width = out.shape[1] // parts, out.shape[1] // (4 * parts)
        for owner in range(4):
            for part in range(parts):
                at = part * whole + owner * width
                out[:, at : at + width] = taken[owner, :, part * width : (part + 1) * width].astype(
                    F32
                )

    columns(up_out, up_ref, 1)
    columns(cq_out, cq_ref, 1)
    columns(ckv_out, ckv_ref, 2)
    columns(qkv_out, qkv_ref, 3)
    spread = gain_out.shape[1]
    turned = pltpu.roll(norm_ref[...], norm_ref.shape[1] - lax.axis_index(CTX) * spread, 1)
    gain_out[...] = turned[0:3, :spread]
    bias_out[...] = turned[3:6, :spread]
    lane = lax.broadcasted_iota(jnp.int32, (1, 128), 1)
    held = peaks_ref.shape[1] // 2
    for kind in range(2):
        tops = jnp.zeros((1, 128), F32)
        for head in range(H):
            at = kind * held + head % held
            tops = jnp.where(lane == head, peaks_ref[head // held, at : at + 1], tops)
        peaks_out[kind : kind + 1] = tops[:, :H]
    for owner in range(4):
        for two in range(held // 2):
            head = owner * held + two * 2
            at = slice(head * HD, head * HD + 128)
            for kind, jobs in (
                (0, ((self_out, qkv_w, 0, 0), (self_out, qkv_w, H * HD, H * HD))),
                (1, ((cross_out, cq_w, 0, 0), (cross_out, ckv_w, 0, H * HD))),
            ):
                top = [peaks_ref[owner, kind * held + two * 2 + i : kind * held + two * 2 + i + 1] for i in (0, 1)]
                limit = [clip_ref[kind, head + i] for i in (0, 1)]
                limits = jnp.where(lane < HD, limit[0], limit[1])
                tops = jnp.where(lane < HD, top[0], top[1])
                factor = jnp.sqrt(limits / jnp.maximum(tops, limits))
                for out, weight, start, goal in jobs:
                    out[:, goal + head * HD : goal + head * HD + 128] = (
                        weight[:, start + head * HD : start + head * HD + 128].astype(F32) * factor
                    ).astype(BF16)


def finish_call(made, given):
    rows, depth = given["tokens"].shape[1:]
    hidden = given["mlp_up"].shape[1]
    source_rows, share = made["grad_source"].shape[0], made["so_result"].shape[1]
    columns = H * HD
    weight_rows = given["self_qkv"].shape[0]
    shapes = [
        ((1, rows, depth), BF16),
        ((1, rows, depth), F32),
        ((1, source_rows, depth), F32),
        ((share, 3 * columns), F32),
        ((share, depth), F32),
        ((share, columns), F32),
        ((share, 2 * columns), F32),
        ((share, depth), F32),
        ((share, hidden), F32),
        ((hidden // 32, depth), F32),
        ((3, share), F32),
        ((3, share), F32),
        ((weight_rows, 2 * columns), BF16),
        ((weight_rows, 2 * columns), BF16),
        ((2, H), F32),
    ]
    vmem = pl.BlockSpec(memory_space=pltpu.VMEM)
    return pl.pallas_call(
        finish_kernel,
        in_specs=[pl.BlockSpec(memory_space=pltpu.SMEM)] + [vmem] * 15,
        out_specs=[vmem] * len(shapes),
        out_shape=[jax.ShapeDtypeStruct(*shape) for shape in shapes],
        compiler_params=pltpu.CompilerParams(vmem_limit_bytes=61 * 2**20),
        name="finish",
    )(
        given["clip"],
        made["peaks_seq"],
        made["norm_sum"],
        given["self_qkv"],
        given["cross_q"],
        given["cross_kv"],
        made["output"],
        made["grad_inputs"],
        made["grad_source"],
        made["down_taken"],
        made["co_result"],
        made["so_result"],
        made["up_taken"],
        made["cq_taken"],
        made["ckv_taken"],
        made["qkv_taken"],
    )


def fast_device(
    tokens,
    encoder_states,
    cotangent,
    target_lengths,
    source_lengths,
    block_table,
    self_qkv,
    self_out,
    cross_q,
    cross_kv,
    cross_out,
    mlp_up,
    mlp_down,
    norm_gain,
    norm_bias,
    clip_limit,
):
    kept = forward_call(
        block_table,
        target_lengths,
        source_lengths,
        tokens,
        encoder_states,
        cotangent,
        self_qkv,
        self_out,
        cross_q,
        cross_kv,
        cross_out,
        mlp_up,
        mlp_down,
        norm_gain,
        norm_bias,
    )
    given = dict(
        table=block_table,
        target=target_lengths,
        tokens=tokens,
        cotangent=cotangent,
        gain=norm_gain,
        cross_out=cross_out,
        self_out=self_out,
        self_qkv=self_qkv,
        cross_q=cross_q,
        cross_kv=cross_kv,
        mlp_up=mlp_up,
        clip=clip_limit,
    )
    made = backward_call(kept, given)
    return tuple(finish_call(made, given))


def solution(mesh):
    body = fast_device if fast_fits(mesh) else general_device
    return jax.shard_map(
        body,
        mesh=mesh,
        in_specs=(
            P(SEQ, CTX, None),
            P(SEQ, CTX, None),
            P(SEQ, CTX, None),
            P(SEQ),
            P(SEQ),
            P(),
            P(SEQ, None),
            P(SEQ, None),
            P(SEQ, None),
            P(SEQ, None),
            P(SEQ, None),
            P(SEQ, None),
            P(SEQ, None),
            P(),
            P(),
            P(),
        ),
        out_specs=(
            P(SEQ, CTX, None),
            P(SEQ, CTX, None),
            P(SEQ, CTX, None),
            P((SEQ, CTX), None),
            P((SEQ, CTX), None),
            P((SEQ, CTX), None),
            P((SEQ, CTX), None),
            P((SEQ, CTX), None),
            P((SEQ, CTX), None),
            P((SEQ, CTX), None),
            P(None, (SEQ, CTX)),
            P(None, (SEQ, CTX)),
            P(SEQ, None),
            P(SEQ, None),
            P(),
        ),
        check_vma=False,
    )
```
